32 devices in a mesh: rows: 16 (over z, y, x), tensor: 2 (over core).
Axes of the slice: x: 2, y: 2, z: 4, core: 2. Of those that a mesh axis runs over, the one named last changes fastest.
Arguments:
- byte_rows: bfloat16 [4096, 1472], P('rows'), may hold values from -6 to 6
- lengths: int32 [8], replicated, may hold values from 1 to 1024, 4096 in all
- keep_mask: int32 [4096], P('rows'), may hold values from 0 to 1, as said below
- w_delete: float32 [1472], replicated, may hold values from -0.0546875 to 0.0546875
- g_delete: float32 [1472], replicated, may hold values from 0.5 to 1.5
- g_attn: float32 [1472], replicated, may hold values from 0.5 to 1.5
- w_query: bfloat16 [1472, 384], P(None, 'tensor'), may hold values from -0.01953125 to 0.01953125
- w_key: bfloat16 [1472, 384], P(None, 'tensor'), may hold values from -0.15625 to 0.15625
- w_value: bfloat16 [1472, 384], P(None, 'tensor'), may hold values from -0.15625 to 0.15625
- w_out: bfloat16 [384, 1472], P('tensor'), may hold values from -1.75 to 1.75
- rel_bias: float32 [32, 6], P(None, 'tensor'), may hold values from -4 to 4
- g_ff: float32 [1472], replicated, may hold values from 0.5 to 1.5
- w_gate: bfloat16 [1472, 3584], P(None, ('rows', 'tensor')), may hold values from -0.15625 to 0.15625
- w_up: bfloat16 [1472, 3584], P(None, ('rows', 'tensor')), may hold values from -0.15625 to 0.15625
- w_down: bfloat16 [3584, 1472], P(('rows', 'tensor')), may hold values from -0.1875 to 0.1875
- out_cot: bfloat16 [3072, 1472], P('rows'), may hold values from -6 to 6
- gate_cot: float32 [4096], P('rows'), may hold values from -6 to 6
Outputs:
- block_out: bfloat16 [3072, 1472], P('rows')
- gate_out: float32 [4096], P('rows')
- grad_rows: float32 [4096, 1472], P('rows')
- grad_w_delete: float32 [1472], replicated
- grad_g_delete: float32 [1472], replicated
- grad_g_attn: float32 [1472], replicated
- grad_w_query: float32 [1472, 384], P(None, 'tensor')
- grad_w_key: float32 [1472, 384], P(None, 'tensor')
- grad_w_value: float32 [1472, 384], P(None, 'tensor')
- grad_w_out: float32 [384, 1472], P('tensor')
- grad_rel_bias: float32 [32, 6], P(None, 'tensor')
- grad_g_ff: float32 [1472], replicated
- grad_w_gate: float32 [1472, 3584], P(None, ('rows', 'tensor'))
- grad_w_up: float32 [1472, 3584], P(None, ('rows', 'tensor'))
- grad_w_down: float32 [3584, 1472], P(('rows', 'tensor'))
The draws below stay inside these ranges and needn't reach their ends.
Inputs may be any that keep to these rules, and one draw needn't show every extreme that they name: `keep_mask`: 3072 rows are kept in all. Each index of rows keeps between 128 and 256 of its rows, both ends reached in every draw. The rows kept by all indices below index m number m * 192 + e with |e| <= 32, and e = 32 and e = -32 are both reached in every draw.
All inputs are finite; a program needn't handle non-finite values.
Results may differ from the reference program's by a relative error of at most 0.014.
Values may be sent and summed in bfloat16 or wider, within the bound.
A program may use at most 256 MiB of HBM per device.

```python
import math
import jax
import jax.numpy as jnp
import numpy as np
from jax import lax

D = 1472
H = 6
DH = 64
FF = 3584
BUCKETS = 32
MAXLEN = 1024
TOK_DEV = 256
KEPT_DEV = 192
TOKENS = 4096
PACKED = 3072
SEQS = 8


def draw_keep_mask(key, part):
    key = jax.random.fold_in(key, 5)
    devices = TOKENS // TOK_DEV
    margin_rows = TOK_DEV // 8
    drift_key, special_key, order_key = jax.random.split(key, 3)
    drift = jax.random.randint(drift_key, (devices + 1,), -margin_rows, margin_rows + 1)
    places = jnp.arange(devices + 1)
    drift = jnp.where((places == 0) | (places == devices), 0, drift)
    special = jax.random.randint(special_key, (), 1, devices - 2)
    drift = jnp.where(places == special, margin_rows, drift)
    drift = jnp.where(places == special + 1, -margin_rows, drift)
    drift = jnp.where(places == special + 2, margin_rows, drift)
    counts = KEPT_DEV + drift[1:] - drift[:-1]
    order_keys = jax.random.split(order_key, devices)
    ranks = jax.vmap(lambda single: jax.random.permutation(single, TOK_DEV))(order_keys)
    return (ranks < counts[:, None]).astype(jnp.int32).reshape(TOKENS)


def shard_levels(key, shape, shards, low, largest):
    def one(position, blocks):
        heights = jax.random.uniform(jax.random.fold_in(jax.random.fold_in(key, 6), position), (blocks,), jnp.float32, low / len(shards), largest / len(shards))
        return jnp.repeat(jnp.exp(heights), shape[position] // blocks).reshape((-1,) + (1,) * (len(shape) - position - 1))

    level = one(*shards[0])
    for cut in shards[1:]:
        level = level * one(*cut)
    return level


def split_up(amount, total, most, lean):
    loads = [(1 << 20) // math.isqrt(standing ** lean) + 1 for standing in range(2, amount + 1)]
    rest, holding = total - most - (amount - 1), [1] * (amount - 1)
    while rest > 0:
        free = [i for i in range(amount - 1) if holding[i] < most]
        pool, remaining = sum([loads[i] for i in free]), rest
        for i in free:
            extra = min(most - holding[i], max(1, remaining * loads[i] // pool), rest)
            holding[i] = holding[i] + extra
            rest = rest - extra
    return np.array([most] + holding)


def ragged(own_key, number_of, total, bound, lean):
    if number_of == 2:
        one = jax.random.randint(own_key, (), max(1, total - bound), min(bound, total - 1) + 1)
        return jnp.stack([one, total - one])
    tallies = jnp.asarray(split_up(number_of, total, bound, lean), jnp.int32)
    twos = (number_of - 1) // 2
    source_of, taker = tallies[1:1 + 2 * twos:2], tallies[2:2 + 2 * twos:2]
    room = jnp.minimum(source_of - 1, bound - taker)
    shifted = jax.random.randint(jax.random.fold_in(own_key, 1), (twos,), 0, 1 << 20) % (room + 1)
    tallies = tallies.at[1:1 + 2 * twos:2].set(source_of - shifted).at[2:2 + 2 * twos:2].set(taker + shifted)
    return tallies[jax.random.permutation(jax.random.fold_in(own_key, 2), number_of)]


def scatter_about(stream_key, dims, scale, bound, pieces=(), held_as=jnp.bfloat16):
    array = scale * jax.random.normal(stream_key, dims, jnp.float32)
    if pieces:
        array = array * shard_levels(stream_key, dims, pieces, -0.22, 0.18)
    return jnp.clip(array, -bound, bound).astype(held_as)


def setup_inputs(seed: int = 0) -> dict:
    key_of = jax.random.split(jax.random.key(seed), 18)
    byte_rows = scatter_about(key_of[0], (TOKENS, D), 1.0, 6.0, ((0, 16),))
    lengths = ragged(key_of[1], SEQS, TOKENS, MAXLEN, 2).astype(jnp.int32)
    keep_mask = draw_keep_mask(jax.random.fold_in(key_of[17], 71), 0)
    w_delete = scatter_about(key_of[3], (D,), (9 * D) ** -0.5, 0.0546875, (), jnp.float32)
    g_delete = jnp.clip(1.0 + 0.1 * jax.random.normal(key_of[4], (D,), jnp.float32), 0.5, 1.5)
    g_attn = jnp.clip(1.0 + 0.1 * jax.random.normal(key_of[5], (D,), jnp.float32), 0.5, 1.5)
    w_query = scatter_about(key_of[6], (D, H * DH), (64 * D) ** -0.5, 0.01953125, ((1, 2),))
    w_key = scatter_about(key_of[7], (D, H * DH), D ** -0.5, 0.15625, ((1, 2),))
    w_value = scatter_about(key_of[8], (D, H * DH), D ** -0.5, 0.15625, ((1, 2),))
    w_out = scatter_about(key_of[9], (H * DH, D), (H * DH // 32) ** -0.5, 1.75, ((0, 2),))
    rel_bias = scatter_about(key_of[10], (BUCKETS, H), 1.0, 4.0, ((1, 2),), jnp.float32)
    g_ff = jnp.clip(1.0 + 0.1 * jax.random.normal(key_of[11], (D,), jnp.float32), 0.5, 1.5)
    w_gate = scatter_about(key_of[12], (D, FF), D ** -0.5, 0.15625, ((1, 32),))
    w_up = scatter_about(key_of[13], (D, FF), D ** -0.5, 0.15625, ((1, 32),))
    w_down = scatter_about(key_of[14], (FF, D), (FF // 4) ** -0.5, 0.1875, ((0, 32),))
    out_cot = scatter_about(key_of[15], (PACKED, D), 1.0, 6.0, ((0, 16),))
    gate_cot = scatter_about(key_of[16], (TOKENS,), 1.0, 6.0, ((0, 16),), jnp.float32)
    return dict(byte_rows=byte_rows, lengths=lengths, keep_mask=keep_mask, w_delete=w_delete, g_delete=g_delete, g_attn=g_attn, w_query=w_query, w_key=w_key, w_value=w_value, w_out=w_out, rel_bias=rel_bias, g_ff=g_ff, w_gate=w_gate, w_up=w_up, w_down=w_down, out_cot=out_cot, gate_cot=gate_cot)


@jax.custom_vjp
def low(v):
    return lax.optimization_barrier(v.astype(jnp.bfloat16)).astype(jnp.float32)

@jax.custom_vjp
def low_back(v):
    return v

def low_keep(v):
    return (low(v), None)

def low_pass(kept, grad):
    return (grad,)

def back_keep(v):
    return (v, None)

def back_low(kept, grad):
    return (low(grad),)
low.defvjp(low_keep, low_pass)
low_back.defvjp(back_keep, back_low)
EPS = 1e-06
DELETE_SCALE = -30.0
NEGATIVE = -1e+30
LIMITS = (1, 2, 3, 4, 5, 6, 7, 8, 12, 16, 23, 32, 46, 64, 91)
HIGH = lax.Precision.HIGHEST

def normalize(values, gain):
    return values * lax.rsqrt(lax.optimization_barrier(jnp.mean(values * values, axis=-1, keepdims=True)) + EPS) * gain

def delete_gate(rows_f, gain, weight):
    return DELETE_SCALE * jax.nn.sigmoid(jnp.dot(normalize(rows_f, gain), weight, precision=HIGH))

def bucket_of(query_place, key_place):
    offset = key_place[None, :] - query_place[:, None]
    distance = jnp.abs(offset)
    result = jnp.where(offset > 0, 16, 0).astype(jnp.int32)
    for limit in LIMITS:
        result = result + (distance >= limit).astype(jnp.int32)
    return result

def locate(lengths, raw_rows):
    ends = jnp.cumsum(lengths).astype(jnp.int32)
    starts = ends - lengths
    segment = lax.optimization_barrier(jnp.sum((ends[None, :] <= raw_rows[:, None]).astype(jnp.int32), axis=1)).astype(jnp.int32)
    segment = jnp.minimum(segment, lengths.shape[0] - 1)
    place = raw_rows - jnp.take(starts, segment)
    return (segment, place)

def reference(byte_rows, lengths, keep_mask, w_delete, g_delete, g_attn, w_query, w_key, w_value, w_out, rel_bias, g_ff, w_gate, w_up, w_down, out_cot, gate_cot):
    raw_rows = jnp.arange(TOKENS, dtype=jnp.int32)
    segment, place = locate(lengths, raw_rows)
    kept = jnp.nonzero(keep_mask > 0, size=PACKED)[0].astype(jnp.int32)
    query_segment = jnp.take(segment, kept)
    query_place = jnp.take(place, kept)
    margin = jnp.full((MAXLEN,), -1, jnp.int32)
    key_segment = jnp.concatenate([margin, query_segment, margin])
    key_place = jnp.concatenate([margin, query_place, margin])
    span = 2 * KEPT_DEV
    window = span + 2 * MAXLEN
    head_count = rel_bias.shape[1]
    head_size = w_query.shape[1] // head_count

    def forward(rows_f, delete_weight, delete_gain, attn_gain, query_weight, key_weight, value_weight, out_weight, bias_table, ff_gain, gate_weight, up_weight, down_weight):
        gate = delete_gate(rows_f, delete_gain, delete_weight)
        packed = jnp.take(rows_f, kept, axis=0)
        packed_gate = jnp.take(gate, kept)
        first = low(normalize(packed, attn_gain))
        queries = low_back(low(jnp.dot(first, query_weight, precision=HIGH)))
        keys = low_back(low(jnp.dot(first, key_weight, precision=HIGH)))
        values = low_back(low(jnp.dot(first, value_weight, precision=HIGH)))
        spaced = ((MAXLEN, MAXLEN), (0, 0), (0, 0))
        query_heads = queries.reshape(PACKED, head_count, head_size)
        key_heads = jnp.pad(keys.reshape(PACKED, head_count, head_size), spaced)
        value_heads = jnp.pad(values.reshape(PACKED, head_count, head_size), spaced)
        gate_padded = jnp.pad(packed_gate, (MAXLEN, MAXLEN))

        def block(start):
            query_block = lax.dynamic_slice_in_dim(query_heads, start, span, 0)
            key_block = lax.dynamic_slice_in_dim(key_heads, start, window, 0)
            value_block = lax.dynamic_slice_in_dim(value_heads, start, window, 0)
            gate_block = lax.dynamic_slice_in_dim(gate_padded, start, window, 0)
            segment_q = lax.dynamic_slice_in_dim(query_segment, start, span, 0)
            segment_k = lax.dynamic_slice_in_dim(key_segment, start, window, 0)
            place_q = lax.dynamic_slice_in_dim(query_place, start, span, 0)
            place_k = lax.dynamic_slice_in_dim(key_place, start, window, 0)
            product = low_back(jnp.einsum('qhd,khd->hqk', query_block, key_block, precision=HIGH))
            bias = jnp.moveaxis(jnp.take(bias_table, bucket_of(place_q, place_k), axis=0), 2, 0)
            allowed = (segment_q[:, None] == segment_k[None, :])[None]
            scores = jnp.where(allowed, product + bias + gate_block[None, None, :], NEGATIVE)
            top = lax.optimization_barrier(jnp.max(scores, axis=-1, keepdims=True))
            expo = jnp.exp(scores - top)
            probs = low(expo / lax.optimization_barrier(jnp.sum(expo, axis=-1, keepdims=True)))
            return jnp.einsum('hqk,khd->qhd', probs, value_block, precision=HIGH)
        starts = jnp.arange(PACKED // span, dtype=jnp.int32) * span
        attended = lax.map(jax.checkpoint(block), starts).reshape(PACKED, head_count * head_size)
        attended = low_back(low(attended))
        mixed = packed + low_back(jnp.dot(attended, out_weight, precision=HIGH))
        second = low(normalize(mixed, ff_gain))
        gated = low_back(jnp.dot(second, gate_weight, precision=HIGH))
        upper = low_back(jnp.dot(second, up_weight, precision=HIGH))
        middle = low(jax.nn.gelu(gated, approximate=True) * upper)
        return (mixed + low_back(jnp.dot(middle, down_weight, precision=HIGH)), gate)
    floats = (byte_rows.astype(jnp.float32), w_delete, g_delete, g_attn, w_query.astype(jnp.float32), w_key.astype(jnp.float32), w_value.astype(jnp.float32), w_out.astype(jnp.float32), rel_bias, g_ff, w_gate.astype(jnp.float32), w_up.astype(jnp.float32), w_down.astype(jnp.float32))
    outputs, pullback = jax.vjp(forward, *floats)
    grads = pullback((out_cot.astype(jnp.float32), gate_cot))
    return (outputs[0].astype(jnp.bfloat16), outputs[1], grads[0], grads[1], grads[2], grads[3], grads[4], grads[5], grads[6], grads[7], grads[8], grads[9], grads[10], grads[11], grads[12])
```

```python
import functools

import jax
import jax.numpy as jnp
from jax import lax
from jax.experimental import pallas as pl
from jax.experimental.pallas import tpu as pltpu
from jax.sharding import PartitionSpec as P

MAXLEN = 1024
MARGIN = 32
EPS = 1e-06
DELETE_SCALE = -30.0
NEGATIVE = -1e30
LIMITS = (1, 2, 3, 4, 5, 6, 7, 8, 12, 16, 23, 32, 46, 64, 91)
HALF = 16
HI = 4
MESH = pl.DeviceIdType.MESH
F32 = jnp.float32
BF16 = jnp.bfloat16
VMEM_LIMIT = 60 * 1024 * 1024


def nn(a, b):
    return lax.dot_general(a, b, (((1,), (0,)), ((), ())), preferred_element_type=F32)


def nt(a, b):
    return lax.dot_general(a, b, (((1,), (1,)), ((), ())), preferred_element_type=F32)


def tn(a, b):
    return lax.dot_general(a, b, (((0,), (0,)), ((), ())), preferred_element_type=F32)


def eye(count):
    return lax.broadcasted_iota(jnp.int32, (count, count), 0) == lax.broadcasted_iota(
        jnp.int32, (count, count), 1
    )


def to_row(column, diagonal):
    return jnp.sum(jnp.where(diagonal, column, 0.0), axis=0, keepdims=True)


def to_column(row, diagonal):
    return jnp.sum(jnp.where(diagonal, row, 0.0), axis=1, keepdims=True)


def row_scale(values):
    return lax.rsqrt(jnp.mean(values * values, axis=-1, keepdims=True) + EPS)


def gate_logit(values, scale, weight):
    return scale * jnp.sum(values * weight, axis=-1, keepdims=True)


def sigmoid(value):
    return 1.0 / (1.0 + jnp.exp(-value))


def norm_back(values, gain, grad):
    scale = row_scale(values)
    scaled = grad * gain
    inner = jnp.mean(scaled * values, axis=-1, keepdims=True)
    back = scale * scaled - values * (scale * scale * scale * inner)
    return back, jnp.sum(grad * values * scale, axis=0, keepdims=True)


def reach_of(raw_count, own_rows):
    span = (MAXLEN // raw_count - 1) * own_rows + 2 * MARGIN + raw_count
    return -(-(span - 1) // own_rows)


def slots_of(reach):
    far = list(range(2, reach + 1))
    return [-d for d in reversed(far)] + far + [-1, 0, 1]


def meet_rows(rows):
    me, core = lax.axis_index("rows"), lax.axis_index("tensor")
    barrier = pltpu.get_barrier_semaphore()

    def greet(step, carry):
        pl.semaphore_signal(
            barrier, inc=1, device_id=(lax.rem(me + step, rows), core), device_id_type=MESH
        )
        return carry

    lax.fori_loop(1, rows, greet, 0)
    pl.semaphore_signal(barrier, inc=1, device_id=(me, 1 - core), device_id_type=MESH)
    pl.semaphore_wait(barrier, rows)


def send(src, dst, send_sem, recv_sem, target):
    return pltpu.make_async_remote_copy(
        src_ref=src,
        dst_ref=dst,
        send_sem=send_sem,
        recv_sem=recv_sem,
        device_id=target,
        device_id_type=MESH,
    )


class Window:
    def __init__(self, rows, offsets):
        self.rows, self.offsets = rows, offsets
        self.me, self.core = lax.axis_index("rows"), lax.axis_index("tensor")
        self.slot = {offset: number for number, offset in enumerate(offsets)}
        self.own = self.slot[0]

    def inside(self, offset):
        if offset < 0:
            return self.me >= -offset
        return self.me < self.rows - offset

    def copy(self, ref, sems, offset):
        there = self.slot[-offset]
        return send(
            ref.at[self.own],
            ref.at[there],
            sems.at[0, self.slot[offset]],
            sems.at[1, there],
            (self.me + offset, self.core),
        )

    def start(self, pairs):
        for offset in sorted(self.offsets, key=abs, reverse=True):
            if offset:

                @pl.when(self.inside(offset))
                def _():
                    for ref, sems in pairs:
                        self.copy(ref, sems, offset).start()

    def finish(self, pairs):
        for offset in self.offsets:
            if offset:

                @pl.when(self.inside(offset))
                def _():
                    for ref, sems in pairs:
                        copy = self.copy(ref, sems, offset)
                        copy.wait_send()
                        arrival = send(
                            ref.at[self.own],
                            ref.at[self.slot[offset]],
                            sems.at[0, self.slot[offset]],
                            sems.at[1, self.slot[offset]],
                            (self.me + offset, self.core),
                        )
                        arrival.wait_recv()

    def clear(self, ref, value):
        for offset in self.offsets:
            if offset:

                @pl.when(jnp.logical_not(self.inside(offset)))
                def _():
                    ref[self.slot[offset]] = jnp.full(ref.shape[1:], value, ref.dtype)


def near_bias(gap, table_ref, head):
    bias = jnp.full(gap.shape, table_ref[0, head], F32)
    for number, limit in enumerate(LIMITS):
        bias = jnp.where(gap >= limit, table_ref[HALF + number + 1, head], bias)
        bias = jnp.where(gap <= -limit, table_ref[number + 1, head], bias)
    return bias


def joined_row(facts_ref, slots, line, width):
    return jnp.concatenate([facts_ref[slot, line : line + 1, :width] for slot in slots], axis=1)


def forward_kernel(
    rows,
    offsets,
    lengths_ref,
    table_ref,
    byte_ref,
    keep_ref,
    vec_ref,
    wq_ref,
    wk_ref,
    wv_ref,
    wo_ref,
    wg_ref,
    wu_ref,
    wd_ref,
    cot_ref,
    gate_ref,
    place_ref,
    packed_ref,
    first_ref,
    kv_ref,
    query_ref,
    facts_ref,
    att_ref,
    att_f_ref,
    lse_ref,
    mixed_ref,
    sec_ref,
    cots_ref,
    wall_ref,
    wout_ref,
    wqkv_ref,
    count_ref,
    ext_ref,
    extaux_ref,
    below_ref,
    above_ref,
    belowaux_ref,
    aboveaux_ref,
    packed_f,
    aux_f,
    count_sems,
    edge_sems,
    kv_sems,
    query_sems,
    facts_sems,
    wall_sems,
    pair_sems,
    cot_sems,
    cotf_sems,
    sec_sems,
    secf_sems,
):
    raw_count, width = byte_ref.shape
    own_rows = cot_ref.shape[0]
    inner = wq_ref.shape[1]
    heads = table_ref.shape[1]
    head_size = inner // heads
    share = wd_ref.shape[0]
    lows = rows // HI
    half = own_rows // 2
    me, core = lax.axis_index("rows"), lax.axis_index("tensor")
    high, low = lax.div(me, lows), lax.rem(me, lows)
    sibling = (me, 1 - core)
    mine = pl.ds(pl.multiple_of(core * half, half), half)
    window = Window(rows, offsets)
    own = window.own

    g_delete, w_delete = vec_ref[0:1, :], vec_ref[1:2, :]
    g_attn, g_ff = vec_ref[2:3, :], vec_ref[3:4, :]

    meet_rows(rows)

    keep = keep_ref[...].astype(F32)
    count_ref[me] = jnp.broadcast_to(jnp.sum(keep, axis=1, keepdims=True), (8, 128))

    def count_copy(step):
        return send(
            count_ref.at[me],
            count_ref.at[me],
            count_sems.at[0, step],
            count_sems.at[1, step],
            (lax.rem(me + step, rows), core),
        )

    def count_arrival(step):
        source = lax.rem(me + rows - step, rows)
        return send(
            count_ref.at[source],
            count_ref.at[source],
            count_sems.at[0, step],
            count_sems.at[1, step],
            (source, core),
        )

    def start_count(step, carry):
        count_copy(step).start()
        return carry

    lax.fori_loop(1, rows, start_count, 0)

    wout_ref[core] = wo_ref[...]
    for number, ref in enumerate((wq_ref, wk_ref, wv_ref)):
        wqkv_ref[core, number] = ref[...]
    wall_ref[2, low] = wd_ref[...]
    diagonal = jnp.where(eye(share), 1.0, 0.0).astype(BF16)
    wall_ref[0, low] = nt(diagonal, wg_ref[...]).astype(BF16)
    wall_ref[1, low] = nt(diagonal, wu_ref[...]).astype(BF16)
    wout_copy = send(
        wout_ref.at[core], wout_ref.at[core], pair_sems.at[0, 0], pair_sems.at[1, 0], sibling
    )
    wqkv_copy = send(
        wqkv_ref.at[core], wqkv_ref.at[core], pair_sems.at[0, 1], pair_sems.at[1, 1], sibling
    )

    def wall_copy(number, step):
        return send(
            wall_ref.at[number, low],
            wall_ref.at[number, low],
            wall_sems.at[0, number, step],
            wall_sems.at[1, number, step],
            (high * lows + lax.rem(low + step, lows), core),
        )

    def wall_arrival(number, step):
        source = lax.rem(low + lows - step, lows)
        return send(
            wall_ref.at[number, source],
            wall_ref.at[number, source],
            wall_sems.at[0, number, step],
            wall_sems.at[1, number, step],
            (high * lows + source, core),
        )

    def start_wall(step, carry):
        for number in range(3):
            wall_copy(number, step).start()
        return carry

    def hi_copy(ref, sems, step):
        return send(
            ref.at[high, mine],
            ref.at[high, mine],
            sems.at[0, step],
            sems.at[1, step],
            (lax.rem(high + step, HI) * lows + low, core),
        )

    def hi_arrival(ref, sems, step):
        source = lax.rem(high + HI - step, HI)
        return send(
            ref.at[source, mine],
            ref.at[source, mine],
            sems.at[0, step],
            sems.at[1, step],
            (source * lows + low, core),
        )

    def hi_forward(ref, sems, step):
        source = lax.rem(high + HI - step, HI)
        return send(
            ref.at[source, mine], ref.at[source, mine], sems.at[0, step], sems.at[1, step], sibling
        )

    def hi_forwarded(ref, sems, step):
        source = lax.rem(high + HI - step, HI)
        other = pl.ds(pl.multiple_of((1 - core) * half, half), half)
        return send(
            ref.at[source, other],
            ref.at[source, other],
            sems.at[0, step],
            sems.at[1, step],
            sibling,
        )

    rows_f = byte_ref[...].astype(F32)
    gate_weight = g_delete * w_delete
    raw_gate = DELETE_SCALE * sigmoid(gate_logit(rows_f, row_scale(rows_f), gate_weight))
    raw_eye = eye(raw_count)
    gate_ref[...] = jnp.broadcast_to(to_row(raw_gate, raw_eye), gate_ref.shape)
    upper = lax.broadcasted_iota(jnp.int32, (raw_count, raw_count), 0) <= lax.broadcasted_iota(
        jnp.int32, (raw_count, raw_count), 1
    )
    rank = nn(keep.astype(BF16), jnp.where(upper, 1.0, 0.0).astype(BF16)) - 1.0
    lane = lax.broadcasted_iota(jnp.int32, (raw_count, 128), 1)
    local = lax.broadcasted_iota(jnp.int32, (raw_count, 128), 0).astype(F32)
    aux = jnp.where(lane == 0, local, jnp.where(lane == 1, me.astype(F32), 0.0)).astype(BF16)
    window.clear(kv_ref, 0.0)
    window.clear(query_ref, 0.0)
    window.clear(facts_ref, -1.0)

    def finish_count(step, carry):
        count_copy(step).wait_send()
        count_arrival(step).wait_recv()
        return carry

    lax.fori_loop(1, rows, finish_count, 0)
    lower = lax.broadcasted_iota(jnp.int32, count_ref.shape, 0) < me
    before = jnp.sum(jnp.where(lower, count_ref[...], 0.0), axis=0)[0:1, 0:1]
    place = before + rank - (me * own_rows).astype(F32)
    place = jnp.where(keep > 0.0, place, -4096.0)
    place_ref[...] = jnp.broadcast_to(place, place_ref.shape)
    place_i = place.astype(jnp.int32)
    ext_rows = own_rows + 2 * MARGIN
    chosen = place_i + MARGIN == lax.broadcasted_iota(jnp.int32, (ext_rows, raw_count), 0)
    chosen = jnp.where(chosen, 1.0, 0.0).astype(BF16)
    ext_ref[...] = nn(chosen, byte_ref[...]).astype(BF16)
    extaux_ref[...] = nn(chosen, aux).astype(BF16)

    head_rows, tail_rows = pl.ds(0, MARGIN), pl.ds(own_rows + MARGIN, MARGIN)

    def edge_down(number, src, dst):
        return send(
            src.at[head_rows],
            dst,
            edge_sems.at[0, number],
            edge_sems.at[1, number],
            (me - 1, core),
        )

    def edge_up(number, src, dst):
        return send(
            src.at[tail_rows],
            dst,
            edge_sems.at[0, number],
            edge_sems.at[1, number],
            (me + 1, core),
        )

    @pl.when(me > 0)
    def _():
        edge_down(0, ext_ref, above_ref).start()
        edge_down(1, extaux_ref, aboveaux_ref).start()

    @pl.when(me < rows - 1)
    def _():
        edge_up(2, ext_ref, below_ref).start()
        edge_up(3, extaux_ref, belowaux_ref).start()

    @pl.when(me == 0)
    def _():
        below_ref[...] = jnp.zeros(below_ref.shape, BF16)
        belowaux_ref[...] = jnp.zeros(belowaux_ref.shape, BF16)

    @pl.when(me == rows - 1)
    def _():
        above_ref[...] = jnp.zeros(above_ref.shape, BF16)
        aboveaux_ref[...] = jnp.zeros(aboveaux_ref.shape, BF16)

    wout_copy.start()
    wqkv_copy.start()
    packed_f[...] = ext_ref[MARGIN : MARGIN + own_rows, :].astype(F32)
    aux_f[...] = extaux_ref[MARGIN : MARGIN + own_rows, :].astype(F32)

    @pl.when(me > 0)
    def _():
        edge_down(0, ext_ref, above_ref).wait_send()
        edge_down(1, extaux_ref, aboveaux_ref).wait_send()
        edge_up(2, ext_ref, below_ref).wait_recv()
        edge_up(3, extaux_ref, belowaux_ref).wait_recv()

    @pl.when(me < rows - 1)
    def _():
        edge_up(2, ext_ref, below_ref).wait_send()
        edge_up(3, extaux_ref, belowaux_ref).wait_send()
        edge_down(0, ext_ref, above_ref).wait_recv()
        edge_down(1, extaux_ref, aboveaux_ref).wait_recv()

    top = own_rows - MARGIN
    packed_f[0:MARGIN, :] = packed_f[0:MARGIN, :] + below_ref[...].astype(F32)
    packed_f[top:, :] = packed_f[top:, :] + above_ref[...].astype(F32)
    aux_f[0:MARGIN, :] = aux_f[0:MARGIN, :] + belowaux_ref[...].astype(F32)
    aux_f[top:, :] = aux_f[top:, :] + aboveaux_ref[...].astype(F32)

    packed = packed_f[...]
    packed_ref[...] = packed.astype(BF16)
    scale = row_scale(packed)
    first = (packed * scale * g_attn).astype(BF16)
    first_ref[...] = first
    kv_ref[own, :, 0:inner] = nn(first, wk_ref[...]).astype(BF16)
    kv_ref[own, :, inner : 2 * inner] = nn(first, wv_ref[...]).astype(BF16)

    gate = DELETE_SCALE * sigmoid(gate_logit(packed, scale, gate_weight))
    ids = aux_f[:, 0:1] + raw_count * aux_f[:, 1:2]
    ids_i = ids.astype(jnp.int32)
    starts = jnp.zeros_like(ids_i)
    end = jnp.int32(0)
    for number in range(lengths_ref.shape[0]):
        end = end + lengths_ref[number]
        starts = jnp.where(ids_i >= end, end, starts)
    starts = starts.astype(F32)
    own_eye = eye(own_rows)
    facts_ref[own] = jnp.zeros(facts_ref.shape[1:], F32)
    facts_ref[own, 0:1, 0:own_rows] = to_row(gate, own_eye)
    facts_ref[own, 1:2, 0:own_rows] = to_row(ids, own_eye)
    facts_ref[own, 2:3, 0:own_rows] = to_row(starts, own_eye)
    window.start([(kv_ref, kv_sems), (facts_ref, facts_sems)])
    query_ref[own] = nn(first, wq_ref[...]).astype(BF16)
    lax.fori_loop(1, lows, start_wall, 0)
    cots_ref[high] = cot_ref[...]
    for step in range(1, HI):
        hi_copy(cots_ref, cot_sems, step).start()

    window.finish([(kv_ref, kv_sems), (facts_ref, facts_sems)])
    window.start([(query_ref, query_sems)])

    far = (len(offsets) - 3) // 2
    segments = (range(0, far), range(far, 2 * far), range(2 * far, 2 * far + 3))
    fixed = (HALF - 1, 2 * HALF - 1, None)
    gaps = joined_row(facts_ref, segments[2], 1, own_rows) - ids
    lanes = lax.broadcasted_iota(jnp.int32, lse_ref.shape, 1)
    lse_all = jnp.zeros(lse_ref.shape, F32)
    for head in range(heads):
        cut = slice(head * head_size, (head + 1) * head_size)
        cut_v = slice(inner + head * head_size, inner + (head + 1) * head_size)
        query = query_ref[own, :, cut]
        parts = []
        for segment, bucket in zip(segments, fixed):
            span = slice(segment[0], segment[-1] + 1)
            keys = kv_ref[span, :, cut].reshape(-1, head_size)
            part = nt(query, keys) + joined_row(facts_ref, segment, 0, own_rows)
            if bucket is None:
                part = part + near_bias(gaps, table_ref, head)
            else:
                part = part + table_ref[bucket, head]
            allowed = joined_row(facts_ref, segment, 2, own_rows) == starts
            parts.append(jnp.where(allowed, part, NEGATIVE))
        most = jnp.max(parts[0], axis=1, keepdims=True)
        for part in parts[1:]:
            most = jnp.maximum(most, jnp.max(part, axis=1, keepdims=True))
        expos = [jnp.exp(part - most) for part in parts]
        total = sum(jnp.sum(expo, axis=1, keepdims=True) for expo in expos)
        lse_all = jnp.where(lanes == head, most + jnp.log(total), lse_all)
        attended = jnp.zeros((own_rows, head_size), F32)
        for segment, expo in zip(segments, expos):
            span = slice(segment[0], segment[-1] + 1)
            values = kv_ref[span, :, cut_v].reshape(-1, head_size)
            attended = attended + nn((expo / total).astype(BF16), values)
        att_f_ref[:, cut] = attended
        att_ref[core, :, cut] = attended.astype(BF16)
    lse_ref[...] = lse_all

    att_copy = send(
        att_ref.at[core], att_ref.at[core], pair_sems.at[0, 2], pair_sems.at[1, 2], sibling
    )
    att_copy.start()
    att_copy.wait()
    wout_copy.wait()
    wqkv_copy.wait()
    mixed = packed_f[...] + (nn(att_ref[0], wout_ref[0]) + nn(att_ref[1], wout_ref[1]))
    mixed_ref[...] = mixed
    sec_ref[high] = (mixed * row_scale(mixed) * g_ff).astype(BF16)
    for step in range(1, HI):
        hi_copy(sec_ref, sec_sems, step).start()
    for ref, sems, sems_f in ((cots_ref, cot_sems, cotf_sems), (sec_ref, sec_sems, secf_sems)):
        for step in range(1, HI):
            hi_arrival(ref, sems, step).wait_recv()
            hi_forward(ref, sems_f, step).start()
    for ref, sems, sems_f in ((cots_ref, cot_sems, cotf_sems), (sec_ref, sec_sems, secf_sems)):
        for step in range(1, HI):
            hi_copy(ref, sems, step).wait_send()
            hi_forward(ref, sems_f, step).wait_send()
            hi_forwarded(ref, sems_f, step).wait_recv()

    def finish_wall(step, carry):
        for number in range(3):
            wall_copy(number, step).wait_send()
            wall_arrival(number, step).wait_recv()
        return carry

    lax.fori_loop(1, lows, finish_wall, 0)
    window.finish([(query_ref, query_sems)])


def forward(rows, offsets, lengths, table, byte_rows, keep, vecs, wq, wk, wv, wo, wg, wu, wd, cot):
    raw_count, width = byte_rows.shape
    own_rows = cot.shape[0]
    inner = wq.shape[1]
    share = wd.shape[0]
    lows = rows // HI
    slots = len(offsets)
    vmem = pl.BlockSpec(memory_space=pltpu.VMEM)
    smem = pl.BlockSpec(memory_space=pltpu.SMEM)
    shape = jax.ShapeDtypeStruct
    outs = [
        shape((8, raw_count), F32),
        shape((8, raw_count), F32),
        shape((own_rows, width), BF16),
        shape((own_rows, width), BF16),
        shape((slots, own_rows, 2 * inner), BF16),
        shape((slots, own_rows, inner), BF16),
        shape((slots, 8, 256), F32),
        shape((2, own_rows, inner), BF16),
        shape((own_rows, inner), F32),
        shape((own_rows, 128), F32),
        shape((own_rows, width), F32),
        shape((HI, own_rows, width), BF16),
        shape((HI, own_rows, width), BF16),
        shape((3, lows, share, width), BF16),
        shape((2, inner, width), BF16),
        shape((2, 3, width, inner), BF16),
    ]
    dma = pltpu.SemaphoreType.DMA
    scratch = [
        pltpu.VMEM((rows, 8, 128), F32),
        pltpu.VMEM((own_rows + 2 * MARGIN, width), BF16),
        pltpu.VMEM((own_rows + 2 * MARGIN, 128), BF16),
        pltpu.VMEM((MARGIN, width), BF16),
        pltpu.VMEM((MARGIN, width), BF16),
        pltpu.VMEM((MARGIN, 128), BF16),
        pltpu.VMEM((MARGIN, 128), BF16),
        pltpu.VMEM((own_rows, width), F32),
        pltpu.VMEM((own_rows, 128), F32),
        dma((2, rows)),
        dma((2, 4)),
        dma((2, slots)),
        dma((2, slots)),
        dma((2, slots)),
        dma((2, 3, lows)),
        dma((2, 3)),
        dma((2, HI)),
        dma((2, HI)),
        dma((2, HI)),
        dma((2, HI)),
    ]
    return pl.pallas_call(
        functools.partial(forward_kernel, rows, offsets),
        name="forward",
        out_shape=outs,
        in_specs=[smem, smem] + [vmem] * 11,
        out_specs=[vmem] * len(outs),
        scratch_shapes=scratch,
        compiler_params=pltpu.CompilerParams(
            collective_id=0, has_side_effects=True, vmem_limit_bytes=VMEM_LIMIT
        ),
    )(lengths, table, byte_rows, keep, vecs, wq, wk, wv, wo, wg, wu, wd, cot)


def meet_few(targets):
    barrier = pltpu.get_barrier_semaphore()
    for target in targets:
        pl.semaphore_signal(barrier, inc=1, device_id=target, device_id_type=MESH)
    pl.semaphore_wait(barrier, len(targets))


GELU_A = 0.7978845608028654
GELU_B = 0.044715


def feed_kernel(
    rows,
    sec_ref,
    cot_ref,
    wall_ref,
    mixed_ref,
    block_ref,
    dsec_ref,
    grad_ref,
    mid_ref,
    dgate_ref,
    dup_ref,
    part_ref,
    keep_ref,
    out_ref,
    in_ref,
    hout_ref,
    hin_ref,
    sib_sems,
    hi_sems,
    half_sems,
):
    own_rows, width = mixed_ref.shape
    hidden = wall_ref.shape[1]
    lows = rows // HI
    half = own_rows // 2
    me, core = lax.axis_index("rows"), lax.axis_index("tensor")
    high, low = lax.div(me, lows), lax.rem(me, lows)
    sibling = (me, 1 - core)
    mine = pl.ds(pl.multiple_of(core * half, half), half)
    theirs = pl.ds(pl.multiple_of((1 - core) * half, half), half)

    def peer(step):
        return (lax.rem(high + step, HI) * lows + low, core)

    meet_few([peer(step) for step in range(1, HI)] + [sibling])

    def sib_copy(step):
        return send(
            out_ref.at[step], in_ref.at[step], sib_sems.at[0, step], sib_sems.at[1, step], sibling
        )

    def hi_copy(step):
        return send(
            hout_ref.at[step], hin_ref.at[step], hi_sems.at[0, step], hi_sems.at[1, step], peer(step)
        )

    def pass_on(step):
        sib_copy(step).wait()
        for number in range(2):
            both = keep_ref[step, number] + in_ref[step, number].astype(F32)
            hout_ref[step, number] = both.astype(BF16)
        hi_copy(step).start()

    order = list(range(1, HI)) + [0]
    for place, step in enumerate(order):
        chunk = lax.rem(high + step, HI)
        second, cotangent = sec_ref[chunk], cot_ref[chunk]
        gated = nt(second, wall_ref[0])
        upper = nt(second, wall_ref[1])
        d_middle = nt(cotangent, wall_ref[2])
        square = gated * gated
        bend = jnp.tanh(GELU_A * gated * (1.0 + GELU_B * square))
        lift = 0.5 * (1.0 + bend)
        slope = lift + 0.5 * gated * (1.0 - bend * bend) * (
            GELU_A * (1.0 + 3.0 * GELU_B * square)
        )
        gelu = gated * lift
        span = pl.ds(pl.multiple_of(chunk * own_rows, own_rows), own_rows)
        middle = (gelu * upper).astype(BF16)
        d_gated = (d_middle * upper * slope).astype(BF16)
        d_upper = (d_middle * gelu).astype(BF16)
        mid_ref[span, :] = middle
        dgate_ref[span, :] = d_gated
        dup_ref[span, :] = d_upper
        part_ref[0] = nn(middle, wall_ref[2])
        part_ref[1] = nn(d_gated, wall_ref[0]) + nn(d_upper, wall_ref[1])
        for number in range(2):
            out_ref[step, number] = part_ref[number, theirs, :].astype(BF16)
            keep_ref[step, number] = part_ref[number, mine, :]
        sib_copy(step).start()
        if place:
            pass_on(order[place - 1])

    everything = sec_ref[...].reshape(HI * own_rows, width)
    grad_ref[0] = tn(dgate_ref[...], everything).astype(BF16)
    grad_ref[1] = tn(dup_ref[...], everything).astype(BF16)
    grad_ref[2] = tn(mid_ref[...], cot_ref[...].reshape(HI * own_rows, width)).astype(BF16)

    sib_copy(0).wait()
    totals = [keep_ref[0, number] + in_ref[0, number].astype(F32) for number in range(2)]
    for step in range(1, HI):
        hi_copy(step).wait()
        for number in range(2):
            totals[number] = totals[number] + hin_ref[step, number].astype(F32)
    dsec_ref[mine, :] = totals[1]
    block_ref[mine, :] = (mixed_ref[mine, :] + totals[0]).astype(BF16)
    halves = [
        send(ref.at[mine], ref.at[mine], half_sems.at[0, i], half_sems.at[1, i], sibling)
        for i, ref in enumerate((dsec_ref, block_ref))
    ]
    for copy in halves:
        copy.start()
    for copy in halves:
        copy.wait()


def feed(rows, second, cotangent, wall, mixed):
    own_rows, width = mixed.shape
    hidden = wall.shape[1]
    half = own_rows // 2
    vmem = pl.BlockSpec(memory_space=pltpu.VMEM)
    shape = jax.ShapeDtypeStruct
    dma = pltpu.SemaphoreType.DMA
    outs = [
        shape((own_rows, width), BF16),
        shape((own_rows, width), F32),
        shape((3, hidden, width), BF16),
    ]
    scratch = [
        pltpu.VMEM((HI * own_rows, hidden), BF16),
        pltpu.VMEM((HI * own_rows, hidden), BF16),
        pltpu.VMEM((HI * own_rows, hidden), BF16),
        pltpu.VMEM((2, own_rows, width), F32),
        pltpu.VMEM((HI, 2, half, width), F32),
        pltpu.VMEM((HI, 2, half, width), BF16),
        pltpu.VMEM((HI, 2, half, width), BF16),
        pltpu.VMEM((HI, 2, half, width), BF16),
        pltpu.VMEM((HI, 2, half, width), BF16),
        dma((2, HI)),
        dma((2, HI)),
        dma((2, 2)),
    ]
    return pl.pallas_call(
        functools.partial(feed_kernel, rows),
        name="feed",
        out_shape=outs,
        in_specs=[vmem] * 4,
        out_specs=[vmem] * len(outs),
        scratch_shapes=scratch,
        compiler_params=pltpu.CompilerParams(
            collective_id=1, has_side_effects=True, vmem_limit_bytes=VMEM_LIMIT
        ),
    )(second, cotangent, wall, mixed)


def backward_kernel(
    rows,
    offsets,
    table_ref,
    byte_ref,
    vec_ref,
    cot_ref,
    gcot_ref,
    place_ref,
    packed_ref,
    first_ref,
    kv_ref,
    query_ref,
    facts_ref,
    att_ref,
    att_f_ref,
    lse_ref,
    mixed_ref,
    wout_ref,
    wqkv_ref,
    dsec_ref,
    ffg_ref,
    rows_ref,
    small_ref,
    attg_ref,
    ffo_ref,
    ffin_ref,
    dmix_ref,
    dout_ref,
    facts2_ref,
    heads_ref,
    dgate_ref,
    zout_ref,
    zin_ref,
    hout_ref,
    hin_ref,
    ext_ref,
    extaux_ref,
    slow_ref,
    shigh_ref,
    ff_sems,
    dout_sems,
    facts_sems,
    pair_sems,
    low_sems,
    high_sems,
    back_sems,
    last_sems,
    edge_sems,
    slow_sems,
    shigh_sems,
):
    raw_count, width = byte_ref.shape
    own_rows = cot_ref.shape[0]
    inner = wqkv_ref.shape[3]
    heads = table_ref.shape[1]
    head_size = inner // heads
    lows = rows // HI
    me, core = lax.axis_index("rows"), lax.axis_index("tensor")
    high, low = lax.div(me, lows), lax.rem(me, lows)
    sibling = (me, 1 - core)
    window = Window(rows, offsets)
    own = window.own
    g_delete, w_delete = vec_ref[0:1, :], vec_ref[1:2, :]
    g_attn, g_ff = vec_ref[2:3, :], vec_ref[3:4, :]
    own_eye = eye(own_rows)

    meet_rows(rows)

    def low_peer(step):
        return (high * lows + lax.rem(low + step, lows), core)

    def low_source(step):
        return lax.rem(low + lows - step, lows)

    def high_peer(step):
        return (lax.rem(high + step, HI) * lows + low, core)

    def high_source(step):
        return lax.rem(high + HI - step, HI)

    def ff_copy(number, step):
        return send(
            ffg_ref.at[number, lax.rem(low + step, lows)],
            ffin_ref.at[number, step],
            ff_sems.at[0, number, step],
            ff_sems.at[1, number, step],
            low_peer(step),
        )

    def start_ff(step, carry):
        for number in range(3):
            ff_copy(number, step).start()
        return carry

    lax.fori_loop(1, lows, start_ff, 0)

    mixed = mixed_ref[...]
    back, g_ff_grad = norm_back(mixed, g_ff, dsec_ref[...])
    d_mixed = cot_ref[...].astype(F32) + back
    dmix_ref[...] = d_mixed
    d_branch = d_mixed.astype(BF16)
    d_att = nt(d_branch, wout_ref[core]).astype(BF16)
    dout_ref[own] = d_att
    window.clear(dout_ref, 0.0)
    window.clear(facts2_ref, 0.0)
    facts2_ref[own] = jnp.zeros(facts2_ref.shape[1:], F32)
    deltas = []
    products = d_att.astype(F32) * att_f_ref[...]
    for head in range(heads):
        cut = slice(head * head_size, (head + 1) * head_size)
        delta = jnp.sum(products[:, cut], axis=1, keepdims=True)
        deltas.append(delta)
        facts2_ref[own, head : head + 1, 0:own_rows] = to_row(delta, own_eye)
        line = 4 + head
        facts2_ref[own, line : line + 1, 0:own_rows] = to_row(
            lse_ref[:, head : head + 1], own_eye
        )
    window.start([(dout_ref, dout_sems), (facts2_ref, facts_sems)])

    pieces = zout_ref.shape[0] // 4
    piece = zout_ref.shape[1]

    def keep_pieces(number, value):
        for part in range(pieces):
            zout_ref[number * pieces + part] = value[part * piece : (part + 1) * piece, :].astype(
                BF16
            )

    keep_pieces(3, tn(att_ref[core], d_branch))

    far = (len(offsets) - 3) // 2
    segments = (range(0, far), range(far, 2 * far), range(2 * far, 2 * far + 3))
    fixed = (HALF - 1, 2 * HALF - 1, None)
    ids = to_column(facts_ref[own, 1:2, 0:own_rows], own_eye)
    starts = to_column(facts_ref[own, 2:3, 0:own_rows], own_eye)
    gates = to_column(facts_ref[own, 0:1, 0:own_rows], own_eye)
    near_ids = joined_row(facts_ref, segments[2], 1, own_rows)
    gaps = near_ids - ids
    lane = lax.broadcasted_iota(jnp.int32, (1, width), 1)
    bias_grad = jnp.zeros((1, width), F32)

    def add_bias(bias_grad, head, bucket, value):
        return bias_grad + jnp.where(lane == head * 2 * HALF + bucket, value, 0.0)

    def total_of(value):
        return jnp.sum(jnp.sum(value, axis=0, keepdims=True), axis=1, keepdims=True)

    for head in range(heads):
        cut = slice(head * head_size, (head + 1) * head_size)
        cut_v = slice(inner + head * head_size, inner + (head + 1) * head_size)
        query, d_head = query_ref[own, :, cut], dout_ref[own, :, cut]
        lse = lse_ref[:, head : head + 1]
        d_query = jnp.zeros((own_rows, head_size), F32)
        for segment, bucket in zip(segments, fixed):
            span = slice(segment[0], segment[-1] + 1)
            keys = kv_ref[span, :, cut].reshape(-1, head_size)
            values = kv_ref[span, :, cut_v].reshape(-1, head_size)
            part = nt(query, keys) + joined_row(facts_ref, segment, 0, own_rows)
            if bucket is None:
                part = part + near_bias(gaps, table_ref, head)
            else:
                part = part + table_ref[bucket, head]
            allowed = joined_row(facts_ref, segment, 2, own_rows) == starts
            probs = jnp.exp(jnp.where(allowed, part, NEGATIVE) - lse)
            d_scores = probs * (nt(d_head, values) - deltas[head])
            d_query = d_query + nn(d_scores.astype(BF16), keys)
            if bucket is None:
                whole = total_of(d_scores)
                for sign in (1, -1):
                    base = HALF if sign > 0 else 0
                    sums = [
                        total_of(jnp.where(sign * gaps >= limit, d_scores, 0.0)) for limit in LIMITS
                    ]
                    whole = whole - sums[0]
                    for number in range(len(LIMITS)):
                        value = sums[number]
                        if number + 1 < len(LIMITS):
                            value = value - sums[number + 1]
                        bias_grad = add_bias(bias_grad, head, base + number + 1, value)
                bias_grad = add_bias(bias_grad, head, 0, whole)
            else:
                bias_grad = add_bias(bias_grad, head, bucket, total_of(d_scores))
        heads_ref[core, 0, :, cut] = d_query.astype(BF16)

    window.finish([(dout_ref, dout_sems), (facts2_ref, facts_sems)])
    d_gate = jnp.zeros((own_rows, 1), F32)
    gaps = ids - near_ids
    fixed = (2 * HALF - 1, HALF - 1, None)
    for head in range(heads):
        cut = slice(head * head_size, (head + 1) * head_size)
        cut_v = slice(inner + head * head_size, inner + (head + 1) * head_size)
        key, value = kv_ref[own, :, cut], kv_ref[own, :, cut_v]
        d_key = jnp.zeros((own_rows, head_size), F32)
        d_value = jnp.zeros((own_rows, head_size), F32)
        for segment, bucket in zip(segments, fixed):
            span = slice(segment[0], segment[-1] + 1)
            queries = query_ref[span, :, cut].reshape(-1, head_size)
            d_heads = dout_ref[span, :, cut].reshape(-1, head_size)
            part = nt(key, queries) + gates
            if bucket is None:
                part = part + near_bias(gaps, table_ref, head)
            else:
                part = part + table_ref[bucket, head]
            allowed = joined_row(facts_ref, segment, 2, own_rows) == starts
            lse = joined_row(facts2_ref, segment, 4 + head, own_rows)
            delta = joined_row(facts2_ref, segment, head, own_rows)
            probs = jnp.exp(jnp.where(allowed, part - lse, NEGATIVE))
            d_scores = probs * (nt(value, d_heads) - delta)
            d_value = d_value + nn(probs.astype(BF16), d_heads)
            d_key = d_key + nn(d_scores.astype(BF16), queries)
            d_gate = d_gate + jnp.sum(d_scores, axis=1, keepdims=True)
        heads_ref[core, 1, :, cut] = d_key.astype(BF16)
        heads_ref[core, 2, :, cut] = d_value.astype(BF16)
    dgate_ref[core] = jnp.broadcast_to(d_gate, dgate_ref.shape[1:])
    pair = [
        send(ref.at[core], ref.at[core], pair_sems.at[0, i], pair_sems.at[1, i], sibling)
        for i, ref in enumerate((heads_ref, dgate_ref))
    ]
    for copy in pair:
        copy.start()

    first = first_ref[...]
    for number in range(3):
        keep_pieces(number, tn(heads_ref[core, number], first))

    def low_copy(step):
        return send(
            zout_ref.at[lax.rem(low + step, lows)],
            zin_ref.at[low],
            low_sems.at[0, step],
            low_sems.at[1, step],
            low_peer(step),
        )

    def low_arrival(step):
        return send(
            zout_ref.at[low],
            zin_ref.at[low_source(step)],
            low_sems.at[0, step],
            low_sems.at[1, step],
            low_peer(step),
        )

    def start_low(step, carry):
        low_copy(step).start()
        return carry

    lax.fori_loop(1, lows, start_low, 0)
    zin_ref[low] = zout_ref[low]

    for copy in pair:
        copy.wait()
    d_first = jnp.zeros((own_rows, width), F32)
    for half in range(2):
        for number in range(3):
            d_first = d_first + nt(heads_ref[half, number], wqkv_ref[half, number])
    packed = packed_ref[...].astype(F32)
    back, g_attn_grad = norm_back(packed, g_attn, d_first)
    inside = slice(MARGIN, MARGIN + own_rows)
    ext_ref[inside, :] = (dmix_ref[...] + back).astype(BF16)
    d_gate = dgate_ref[0] + dgate_ref[1]
    lane_g = lax.broadcasted_iota(jnp.int32, d_gate.shape, 1)
    coarse = d_gate.astype(BF16)
    rest = d_gate - coarse.astype(F32)
    fine = rest.astype(BF16)
    finest = (rest - fine.astype(F32)).astype(BF16)
    extaux_ref[inside, :] = jnp.where(
        lane_g == 0,
        coarse.astype(F32),
        jnp.where(
            lane_g == 1, fine.astype(F32), jnp.where(lane_g == 2, finest.astype(F32), 0.0)
        ),
    ).astype(BF16)
    down_src, down_dst = pl.ds(MARGIN, MARGIN), pl.ds(own_rows + MARGIN, MARGIN)
    up_src, up_dst = pl.ds(own_rows, MARGIN), pl.ds(0, MARGIN)

    def edge(number, ref, src, dst, offset):
        return send(
            ref.at[src],
            ref.at[dst],
            edge_sems.at[0, number],
            edge_sems.at[1, number],
            (me + offset, core),
        )

    def downs():
        return [
            edge(0, ext_ref, down_src, down_dst, -1),
            edge(1, extaux_ref, down_src, down_dst, -1),
        ]

    def ups():
        return [edge(2, ext_ref, up_src, up_dst, 1), edge(3, extaux_ref, up_src, up_dst, 1)]

    @pl.when(me > 0)
    def _():
        for copy in downs():
            copy.start()

    @pl.when(me < rows - 1)
    def _():
        for copy in ups():
            copy.start()

    @pl.when(me == 0)
    def _():
        ext_ref[up_dst, :] = jnp.zeros((MARGIN, width), BF16)
        extaux_ref[up_dst, :] = jnp.zeros((MARGIN, 128), BF16)

    @pl.when(me == rows - 1)
    def _():
        ext_ref[down_dst, :] = jnp.zeros((MARGIN, width), BF16)
        extaux_ref[down_dst, :] = jnp.zeros((MARGIN, 128), BF16)

    rows_f = byte_ref[...].astype(F32)
    raw_scale = row_scale(rows_f)
    gate_weight = g_delete * w_delete
    logit = gate_logit(rows_f, raw_scale, gate_weight)
    raw_eye = eye(raw_count)
    place = to_column(place_ref[0:1, :], raw_eye).astype(jnp.int32)
    chosen = place + MARGIN == lax.broadcasted_iota(
        jnp.int32, (raw_count, own_rows + 2 * MARGIN), 1
    )
    chosen = jnp.where(chosen, 1.0, 0.0).astype(BF16)
    raw_cot = to_column(gcot_ref[...], raw_eye)
    gate_s = sigmoid(logit)

    @pl.when(me > 0)
    def _():
        for copy in downs():
            copy.wait_send()
        for copy in ups():
            copy.wait_recv()

    @pl.when(me < rows - 1)
    def _():
        for copy in ups():
            copy.wait_send()
        for copy in downs():
            copy.wait_recv()

    spread = nn(chosen, extaux_ref[...])
    raw_cot = raw_cot + (spread[:, 0:1] + spread[:, 1:2] + spread[:, 2:3])
    d_logit = raw_cot * (DELETE_SCALE * gate_s * (1.0 - gate_s))
    scaled = d_logit * raw_scale
    along = d_logit * logit * raw_scale * raw_scale * (1.0 / width)
    rows_ref[...] = nn(chosen, ext_ref[...]) + (scaled * gate_weight - along * rows_f)
    common = jnp.sum(scaled * rows_f, axis=0, keepdims=True)

    slow_ref[low, 0:1, :] = g_ff_grad
    slow_ref[low, 1:2, :] = g_attn_grad
    slow_ref[low, 2:3, :] = common * g_delete
    slow_ref[low, 3:4, :] = common * w_delete
    slow_ref[low, 4:5, :] = bias_grad
    slow_ref[low, 5:8, :] = jnp.zeros((3, width), F32)

    def slow_copy(step, target, source):
        return send(
            slow_ref.at[source],
            slow_ref.at[source],
            slow_sems.at[0, step],
            slow_sems.at[1, step],
            target,
        )

    def start_slow(step, carry):
        slow_copy(step, low_peer(step), low).start()
        return carry

    lax.fori_loop(1, lows, start_slow, 0)

    def finish_low(step, carry):
        low_copy(step).wait_send()
        low_arrival(step).wait_recv()
        return carry

    lax.fori_loop(1, lows, finish_low, 0)
    total = zin_ref[0].astype(F32)
    for number in range(1, lows):
        total = total + zin_ref[number].astype(F32)
    quarter = piece // HI
    for number in range(HI):
        hout_ref[number] = total[number * quarter : (number + 1) * quarter, :].astype(BF16)

    def high_copy(step):
        return send(
            hout_ref.at[lax.rem(high + step, HI)],
            hin_ref.at[high],
            high_sems.at[0, step],
            high_sems.at[1, step],
            high_peer(step),
        )

    def high_arrival(step):
        return send(
            hout_ref.at[high],
            hin_ref.at[high_source(step)],
            high_sems.at[0, step],
            high_sems.at[1, step],
            high_peer(step),
        )

    for step in range(1, HI):
        high_copy(step).start()
    hin_ref[high] = hout_ref[high]

    def finish_slow(step, carry):
        slow_copy(step, low_peer(step), low).wait_send()
        slow_copy(step, low_peer(step), low_source(step)).wait_recv()
        return carry

    lax.fori_loop(1, lows, finish_slow, 0)
    small = slow_ref[0]
    for number in range(1, lows):
        small = small + slow_ref[number]
    shigh_ref[high] = small

    def shigh_copy(step, source):
        return send(
            shigh_ref.at[source],
            shigh_ref.at[source],
            shigh_sems.at[0, step],
            shigh_sems.at[1, step],
            high_peer(step),
        )

    for step in range(1, HI):
        shigh_copy(step, high).start()

    for step in range(1, HI):
        high_copy(step).wait_send()
        high_arrival(step).wait_recv()
    total = hin_ref[0].astype(F32)
    for number in range(1, HI):
        total = total + hin_ref[number].astype(F32)
    attg_ref[low, high] = total.astype(BF16)

    def back_copy(step, source):
        return send(
            attg_ref.at[low, source],
            attg_ref.at[low, source],
            back_sems.at[0, step],
            back_sems.at[1, step],
            high_peer(step),
        )

    for step in range(1, HI):
        back_copy(step, high).start()
    for step in range(1, HI):
        shigh_copy(step, high).wait_send()
        shigh_copy(step, high_source(step)).wait_recv()
    small = shigh_ref[0]
    for number in range(1, HI):
        small = small + shigh_ref[number]
    small_ref[...] = small
    for step in range(1, HI):
        back_copy(step, high).wait_send()
        back_copy(step, high_source(step)).wait_recv()

    def last_copy(step, source):
        return send(
            attg_ref.at[source],
            attg_ref.at[source],
            last_sems.at[0, step],
            last_sems.at[1, step],
            low_peer(step),
        )

    def start_last(step, carry):
        last_copy(step, low).start()
        return carry

    lax.fori_loop(1, lows, start_last, 0)

    def finish_ff(step, carry):
        for number in range(3):
            ff_copy(number, step).wait()
        return carry

    lax.fori_loop(1, lows, finish_ff, 0)
    for number in range(3):
        total = ffg_ref[number, low].astype(F32)
        for step in range(1, lows):
            total = total + ffin_ref[number, step].astype(F32)
        ffo_ref[number] = total

    def finish_last(step, carry):
        last_copy(step, low).wait_send()
        last_copy(step, low_source(step)).wait_recv()
        return carry

    lax.fori_loop(1, lows, finish_last, 0)


def backward(rows, offsets, *operands):
    table, byte_rows, vecs, cot = operands[:4]
    ffg = operands[-1]
    raw_count, width = byte_rows.shape
    own_rows = cot.shape[0]
    inner = operands[16].shape[3]
    share = ffg.shape[2]
    lows = rows // HI
    slots = len(offsets)
    piece = 4 * inner // lows
    quarter = piece // HI
    vmem = pl.BlockSpec(memory_space=pltpu.VMEM)
    smem = pl.BlockSpec(memory_space=pltpu.SMEM)
    shape = jax.ShapeDtypeStruct
    dma = pltpu.SemaphoreType.DMA
    outs = [
        shape((raw_count, width), F32),
        shape((8, width), F32),
        shape((lows, HI, quarter, width), BF16),
        shape((3, share, width), F32),
    ]
    scratch = [
        pltpu.VMEM((3, lows, share, width), BF16),
        pltpu.VMEM((own_rows, width), F32),
        pltpu.VMEM((slots, own_rows, inner), BF16),
        pltpu.VMEM((slots, 8, 256), F32),
        pltpu.VMEM((2, 3, own_rows, inner), BF16),
        pltpu.VMEM((2, own_rows, 128), F32),
        pltpu.VMEM((lows, piece, width), BF16),
        pltpu.VMEM((lows, piece, width), BF16),
        pltpu.VMEM((HI, quarter, width), BF16),
        pltpu.VMEM((HI, quarter, width), BF16),
        pltpu.VMEM((own_rows + 2 * MARGIN, width), BF16),
        pltpu.VMEM((own_rows + 2 * MARGIN, 128), BF16),
        pltpu.VMEM((lows, 8, width), F32),
        pltpu.VMEM((HI, 8, width), F32),
        dma((2, 3, lows)),
        dma((2, slots)),
        dma((2, slots)),
        dma((2, 2)),
        dma((2, lows)),
        dma((2, HI)),
        dma((2, HI)),
        dma((2, lows)),
        dma((2, 4)),
        dma((2, lows)),
        dma((2, HI)),
    ]
    return pl.pallas_call(
        functools.partial(backward_kernel, rows, offsets),
        name="backward",
        out_shape=outs,
        in_specs=[smem] + [vmem] * (len(operands) - 1),
        out_specs=[vmem] * len(outs),
        scratch_shapes=scratch,
        compiler_params=pltpu.CompilerParams(
            collective_id=2, has_side_effects=True, vmem_limit_bytes=VMEM_LIMIT
        ),
    )(*operands)


def per_device(
    byte_rows,
    lengths,
    keep_mask,
    w_delete,
    g_delete,
    g_attn,
    w_query,
    w_key,
    w_value,
    w_out,
    rel_bias,
    g_ff,
    w_gate,
    w_up,
    w_down,
    out_cot,
    gate_cot,
):
    raw_count, width = byte_rows.shape
    own_rows = out_cot.shape[0]
    inner = w_query.shape[1]
    buckets, heads = rel_bias.shape
    rows = lax.axis_size("rows")
    lows = rows // HI
    share = w_down.shape[0]
    offsets = slots_of(reach_of(raw_count, own_rows))
    zero = jnp.zeros_like(g_ff)
    vecs = jnp.stack([g_delete, w_delete, g_attn, g_ff, zero, zero, zero, zero])
    (
        gate,
        place,
        packed,
        first,
        pairs,
        queries,
        facts,
        att,
        att_f,
        lse,
        mixed,
        second,
        cots,
        wall,
        wout,
        wqkv,
    ) = forward(
        rows,
        offsets,
        lengths,
        rel_bias,
        byte_rows,
        keep_mask.reshape(1, -1),
        vecs,
        w_query,
        w_key,
        w_value,
        w_out,
        w_gate,
        w_up,
        w_down,
        out_cot,
    )
    block_out, d_second, ff_grads = feed(
        rows, second, cots, wall.reshape(3, lows * share, width), mixed
    )
    grad_rows, small, att_grads, ff_sums = backward(
        rows,
        offsets,
        rel_bias,
        byte_rows,
        vecs,
        out_cot,
        gate_cot.reshape(1, -1),
        place,
        packed,
        first,
        pairs,
        queries,
        facts,
        att,
        att_f,
        lse,
        mixed,
        wout,
        wqkv,
        d_second,
        ff_grads.reshape(3, lows, share, width),
    )
    att_grads = att_grads.reshape(4, inner, width).astype(F32)
    grad_bias = small[4, : heads * buckets].reshape(heads, buckets).T
    return (
        block_out,
        gate[0],
        grad_rows,
        small[2],
        small[3],
        small[1],
        att_grads[0].T,
        att_grads[1].T,
        att_grads[2].T,
        att_grads[3],
        grad_bias,
        small[0],
        ff_sums[0].T,
        ff_sums[1].T,
        ff_sums[2],
    )


def solution(mesh):
    in_specs = (
        P("rows", None),
        P(),
        P("rows"),
        P(),
        P(),
        P(),
        P(None, "tensor"),
        P(None, "tensor"),
        P(None, "tensor"),
        P("tensor", None),
        P(None, "tensor"),
        P(),
        P(None, ("rows", "tensor")),
        P(None, ("rows", "tensor")),
        P(("rows", "tensor"), None),
        P("rows", None),
        P("rows"),
    )
    out_specs = (
        P("rows", None),
        P("rows"),
        P("rows", None),
        P(),
        P(),
        P(),
        P(None, "tensor"),
        P(None, "tensor"),
        P(None, "tensor"),
        P("tensor", None),
        P(None, "tensor"),
        P(),
        P(None, ("rows", "tensor")),
        P(None, ("rows", "tensor")),
        P(("rows", "tensor"), None),
    )
    return jax.shard_map(
        per_device, mesh=mesh, in_specs=in_specs, out_specs=out_specs, check_vma=False
    )
```

```python
import functools

import jax
import jax.numpy as jnp
from jax import lax
from jax.experimental import pallas as pl
from jax.experimental.pallas import tpu as pltpu
from jax.sharding import PartitionSpec as P

MAXLEN = 1024
MARGIN = 32
EPS = 1e-06
DELETE_SCALE = -30.0
NEGATIVE = -1e30
LIMITS = (1, 2, 3, 4, 5, 6, 7, 8, 12, 16, 23, 32, 46, 64, 91)
HALF = 16
HI = 4
MESH = pl.DeviceIdType.MESH
F32 = jnp.float32
BF16 = jnp.bfloat16
VMEM_LIMIT = 62 * 1024 * 1024


def nn(a, b):
    return lax.dot_general(a, b, (((1,), (0,)), ((), ())), preferred_element_type=F32)


def nt(a, b):
    return lax.dot_general(a, b, (((1,), (1,)), ((), ())), preferred_element_type=F32)


def tn(a, b):
    return lax.dot_general(a, b, (((0,), (0,)), ((), ())), preferred_element_type=F32)


def eye(count):
    return lax.broadcasted_iota(jnp.int32, (count, count), 0) == lax.broadcasted_iota(
        jnp.int32, (count, count), 1
    )


def to_row(column, diagonal):
    return jnp.sum(jnp.where(diagonal, column, 0.0), axis=0, keepdims=True)


def to_column(row, diagonal):
    return jnp.sum(jnp.where(diagonal, row, 0.0), axis=1, keepdims=True)


def row_scale(values):
    return lax.rsqrt(jnp.mean(values * values, axis=-1, keepdims=True) + EPS)


def gate_logit(values, scale, weight):
    return scale * jnp.sum(values * weight, axis=-1, keepdims=True)


def sigmoid(value):
    return 1.0 / (1.0 + jnp.exp(-value))


def norm_back(values, gain, grad):
    scale = row_scale(values)
    scaled = grad * gain
    inner = jnp.mean(scaled * values, axis=-1, keepdims=True)
    back = scale * scaled - values * (scale * scale * scale * inner)
    return back, jnp.sum(grad * values * scale, axis=0, keepdims=True)


def reach_of(raw_count, own_rows):
    span = (MAXLEN // raw_count - 1) * own_rows + 2 * MARGIN + raw_count
    return -(-(span - 1) // own_rows)


def slots_of(reach):
    far = list(range(2, reach + 1))
    return [-d for d in reversed(far)] + far + [-1, 0, 1]


def meet_rows(rows):
    me, core = lax.axis_index("rows"), lax.axis_index("tensor")
    barrier = pltpu.get_barrier_semaphore()

    def greet(step, carry):
        pl.semaphore_signal(
            barrier, inc=1, device_id=(lax.rem(me + step, rows), core), device_id_type=MESH
        )
        return carry

    lax.fori_loop(1, rows, greet, 0)
    pl.semaphore_signal(barrier, inc=1, device_id=(me, 1 - core), device_id_type=MESH)
    pl.semaphore_wait(barrier, rows)


def send(src, dst, send_sem, recv_sem, target):
    return pltpu.make_async_remote_copy(
        src_ref=src,
        dst_ref=dst,
        send_sem=send_sem,
        recv_sem=recv_sem,
        device_id=target,
        device_id_type=MESH,
    )


class Window:
    def __init__(self, rows, offsets):
        self.rows, self.offsets = rows, offsets
        self.me, self.core = lax.axis_index("rows"), lax.axis_index("tensor")
        self.slot = {offset: number for number, offset in enumerate(offsets)}
        self.own = self.slot[0]

    def inside(self, offset):
        if offset < 0:
            return self.me >= -offset
        return self.me < self.rows - offset

    def copy(self, ref, sems, offset):
        there = self.slot[-offset]
        return send(
            ref.at[self.own],
            ref.at[there],
            sems.at[0, self.slot[offset]],
            sems.at[1, there],
            (self.me + offset, self.core),
        )

    def start(self, pairs):
        for offset in sorted(self.offsets, key=abs, reverse=True):
            if offset:

                @pl.when(self.inside(offset))
                def _():
                    for ref, sems in pairs:
                        self.copy(ref, sems, offset).start()

    def finish(self, pairs):
        for offset in self.offsets:
            if offset:

                @pl.when(self.inside(offset))
                def _():
                    for ref, sems in pairs:
                        copy = self.copy(ref, sems, offset)
                        copy.wait_send()
                        arrival = send(
                            ref.at[self.own],
                            ref.at[self.slot[offset]],
                            sems.at[0, self.slot[offset]],
                            sems.at[1, self.slot[offset]],
                            (self.me + offset, self.core),
                        )
                        arrival.wait_recv()

    def clear(self, ref, value):
        for offset in self.offsets:
            if offset:

                @pl.when(jnp.logical_not(self.inside(offset)))
                def _():
                    ref[self.slot[offset]] = jnp.full(ref.shape[1:], value, ref.dtype)


def near_bias(gap, table_ref, head):
    bias = jnp.full(gap.shape, table_ref[0, head], F32)
    for number, limit in enumerate(LIMITS):
        bias = jnp.where(gap >= limit, table_ref[HALF + number + 1, head], bias)
        bias = jnp.where(gap <= -limit, table_ref[number + 1, head], bias)
    return bias


def joined_row(facts_ref, slots, line, width):
    return jnp.concatenate([facts_ref[slot, line : line + 1, :width] for slot in slots], axis=1)


GELU_A = 0.7978845608028654
GELU_B = 0.044715


def split3(value):
    one = value.astype(BF16).astype(F32)
    rest = value - one
    two = rest.astype(BF16).astype(F32)
    return one, two, (rest - two).astype(BF16).astype(F32)


def stacked_rows(rows, width):
    line = lax.broadcasted_iota(jnp.int32, (8, width), 0)
    result = jnp.zeros((8, width), F32)
    for number, row in enumerate(rows):
        result = jnp.where(line == number, row, result)
    return result.astype(BF16)


def layer_kernel(
    rows,
    offsets,
    lengths_ref,
    table_ref,
    byte_ref,
    keep_ref,
    vec_ref,
    gcot_ref,
    wq_ref,
    wk_ref,
    wv_ref,
    wo_ref,
    wg_ref,
    wu_ref,
    wd_ref,
    cot_ref,
    gate_ref,
    block_ref,
    rows_ref,
    small_ref,
    ffo_ref,
    attg_ref,
    ffin_ref,
    count_ref,
    chosen_ref,
    ext_ref,
    extaux_ref,
    below_ref,
    above_ref,
    belowaux_ref,
    aboveaux_ref,
    packed_ref,
    aux_ref,
    first_ref,
    kv_ref,
    query_ref,
    facts_ref,
    dout_ref,
    facts2_ref,
    biasq_ref,
    biask_ref,
    att_ref,
    attf_ref,
    lse_ref,
    mixed_ref,
    sec_ref,
    cots_ref,
    wall_ref,
    wout_ref,
    wqkv_ref,
    mid_ref,
    dgated_ref,
    dupper_ref,
    part_ref,
    kept_ref,
    sout_ref,
    sin_ref,
    hout_ref,
    hin_ref,
    dsec_ref,
    heads_ref,
    dgate_ref,
    zout_ref,
    zin_ref,
    yout_ref,
    yin_ref,
    slow_ref,
    shigh_ref,
    back_ref,
    backaux_ref,
    ffload_ref,
    count_sems,
    edge_sems,
    kv_sems,
    query_sems,
    facts_sems,
    dout_sems,
    facts2_sems,
    wall_sems,
    pair_sems,
    local_sems,
    cot_sems,
    cotf_sems,
    sec_sems,
    secf_sems,
    sib_sems,
    hi_sems,
    half_sems,
    ff_sems,
    low_sems,
    high_sems,
    back_sems,
    last_sems,
    edge2_sems,
    slow_sems,
    shigh_sems,
):
    width, raw_count = byte_ref.shape
    own_rows = cot_ref.shape[0]
    inner = wq_ref.shape[0]
    heads = table_ref.shape[1]
    head_size = inner // heads
    share = wd_ref.shape[0]
    lows = rows // HI
    half = own_rows // 2
    ext_rows = own_rows + 2 * MARGIN
    me, core = lax.axis_index("rows"), lax.axis_index("tensor")
    high, low = lax.div(me, lows), lax.rem(me, lows)
    sibling = (me, 1 - core)
    mine = pl.ds(pl.multiple_of(core * half, half), half)
    theirs = pl.ds(pl.multiple_of((1 - core) * half, half), half)
    window = Window(rows, offsets)
    own = window.own
    g_delete, w_delete = vec_ref[0:1, :], vec_ref[1:2, :]
    g_attn, g_ff = vec_ref[2:3, :], vec_ref[3:4, :]

    def low_peer(step):
        return (high * lows + lax.rem(low + step, lows), core)

    def low_source(step):
        return lax.rem(low + lows - step, lows)

    def high_other(step):
        if step == 0:
            return high
        if step == 1:
            return high + 1 - 2 * lax.rem(high, 2)
        if step == 2:
            return lax.rem(high + 2, HI)
        return HI - 1 - high

    def high_peer(step):
        return (high_other(step) * lows + low, core)

    middle_high = jnp.logical_and(high >= 1, high <= 2)
    end_high = jnp.logical_not(middle_high)

    meet_rows(rows)

    keep = keep_ref[...].astype(F32)
    count_ref[me] = jnp.broadcast_to(jnp.sum(keep, axis=1, keepdims=True), (8, 128))

    def count_copy(step):
        return send(
            count_ref.at[me],
            count_ref.at[me],
            count_sems.at[0, step],
            count_sems.at[1, step],
            (lax.rem(me + step, rows), core),
        )

    def count_arrival(step):
        source = lax.rem(me + rows - step, rows)
        return send(
            count_ref.at[source],
            count_ref.at[source],
            count_sems.at[0, step],
            count_sems.at[1, step],
            (source, core),
        )

    def start_count(step, carry):
        count_copy(step).start()
        return carry

    lax.fori_loop(1, rows, start_count, 0)

    weight_refs = (wg_ref, wu_ref, wd_ref)
    my_share = pl.ds(pl.multiple_of(low * share, share), share)
    locals_early = [
        pltpu.make_async_copy(ref, wqkv_ref.at[core, number], local_sems.at[number])
        for number, ref in enumerate((wq_ref, wk_ref, wv_ref))
    ]
    locals_late = [
        pltpu.make_async_copy(wo_ref, wout_ref.at[core], local_sems.at[3]),
        pltpu.make_async_copy(cot_ref, cots_ref.at[high], local_sems.at[4]),
    ] + [
        pltpu.make_async_copy(ref, wall_ref.at[number, my_share], local_sems.at[5 + number])
        for number, ref in enumerate(weight_refs)
    ]
    for copy in locals_early + locals_late:
        copy.start()

    def wall_copy(number, step):
        return send(
            weight_refs[number],
            wall_ref.at[number, my_share],
            wall_sems.at[0, number, step],
            wall_sems.at[1, number, step],
            low_peer(step),
        )

    def wall_arrival(number, step):
        source = low_source(step)
        return send(
            weight_refs[number],
            wall_ref.at[number, pl.ds(pl.multiple_of(source * share, share), share)],
            wall_sems.at[0, number, step],
            wall_sems.at[1, number, step],
            low_peer(step),
        )

    def start_wall(number):
        def one(step, carry):
            wall_copy(number, step).start()
            return carry

        lax.fori_loop(1, lows, one, 0)

    def finish_wall(number):
        def one(step, carry):
            wall_copy(number, step).wait_send()
            wall_arrival(number, step).wait_recv()
            return carry

        lax.fori_loop(1, lows, one, 0)

    class Gather:
        def __init__(self, ref, sems, sems_f, offset, count, source=None):
            self.ref, self.sems, self.sems_f = ref, sems, sems_f
            self.part = pl.ds(pl.multiple_of(core * half + offset, 16), count)
            self.other = pl.ds(pl.multiple_of((1 - core) * half + offset, 16), count)
            self.source = ref.at[high] if source is None else source

        def direct(self, step):
            return send(
                self.source.at[self.part],
                self.ref.at[high, self.part],
                self.sems.at[0, step],
                self.sems.at[1, step],
                high_peer(step),
            )

        def arrival(self, step):
            place = self.ref.at[high_other(step), self.part]
            return send(
                place, place, self.sems.at[0, step], self.sems.at[1, step], high_peer(step)
            )

        def relay(self):
            place = self.ref.at[high_other(2), self.part]
            return send(place, place, self.sems.at[0, 0], self.sems.at[1, 3], high_peer(1))

        def forward(self, step, part):
            place = self.ref.at[high_other(step), part]
            return send(
                place, place, self.sems_f.at[0, step], self.sems_f.at[1, step], sibling
            )

        def start(self):
            self.direct(1).start()
            self.direct(2).start()

            @pl.when(middle_high)
            def _():
                self.direct(3).start()

        def arrived(self, step):
            self.arrival(step).wait_recv()
            if step == 2:

                @pl.when(middle_high)
                def _():
                    self.relay().start()

            self.forward(step, self.part).start()

        def forwarded(self, step):
            self.forward(step, self.other).wait_recv()

        def close(self):
            self.direct(1).wait_send()
            self.direct(2).wait_send()

            @pl.when(middle_high)
            def _():
                self.direct(3).wait_send()
                self.relay().wait_send()

            for step in range(1, HI):
                self.forward(step, self.part).wait_send()

    quart = half // 2
    cot_gathers = [
        Gather(cots_ref, cot_sems.at[number], cotf_sems.at[number], number * quart, quart, cot_ref)
        for number in range(2)
    ]
    sec_gather = Gather(sec_ref, sec_sems, secf_sems, 0, half)

    start_wall(2)
    cot_gathers[0].start()
    pair_early = [
        send(wo_ref, wout_ref.at[core], pair_sems.at[0, 0], pair_sems.at[1, 0], sibling)
    ] + [
        send(
            ref,
            wqkv_ref.at[core, number],
            pair_sems.at[0, 1 + number],
            pair_sems.at[1, 1 + number],
            sibling,
        )
        for number, ref in enumerate((wq_ref, wk_ref, wv_ref))
    ]
    for copy in pair_early:
        copy.start()

    gate_weight = g_delete * w_delete
    raw = byte_ref[...]
    raw_f = raw.astype(F32)
    raw_scale = lax.rsqrt(jnp.mean(raw_f * raw_f, axis=0, keepdims=True) + EPS)
    raw_logit = raw_scale * jnp.sum(
        nn(stacked_rows(split3(gate_weight), width), raw), axis=0, keepdims=True
    )
    gate_ref[...] = DELETE_SCALE * sigmoid(raw_logit)
    upper = lax.broadcasted_iota(jnp.int32, (raw_count, raw_count), 0) <= lax.broadcasted_iota(
        jnp.int32, (raw_count, raw_count), 1
    )
    rank = nn(keep.astype(BF16), jnp.where(upper, 1.0, 0.0).astype(BF16)) - 1.0
    lane = lax.broadcasted_iota(jnp.int32, (raw_count, 128), 1)
    local = lax.broadcasted_iota(jnp.int32, (raw_count, 128), 0).astype(F32)
    aux = jnp.where(lane == 0, local, jnp.where(lane == 1, me.astype(F32), 0.0)).astype(BF16)
    window.clear(kv_ref, 0.0)
    window.clear(query_ref, 0.0)
    window.clear(facts_ref, -1.0)
    window.clear(dout_ref, 0.0)
    window.clear(facts2_ref, 0.0)

    def finish_count(step, carry):
        count_copy(step).wait_send()
        count_arrival(step).wait_recv()
        return carry

    lax.fori_loop(1, rows, finish_count, 0)
    lower = lax.broadcasted_iota(jnp.int32, count_ref.shape, 0) < me
    before = jnp.sum(jnp.where(lower, count_ref[...], 0.0), axis=0)[0:1, 0:1]
    place = before + rank - (me * own_rows).astype(F32)
    place = jnp.where(keep > 0.0, place, -4096.0).astype(jnp.int32)
    chosen = place + MARGIN == lax.broadcasted_iota(jnp.int32, (ext_rows, raw_count), 0)
    chosen = jnp.where(chosen, 1.0, 0.0).astype(BF16)
    chosen_ref[...] = chosen
    ext_ref[...] = nt(chosen, raw).astype(BF16)
    extaux_ref[...] = nn(chosen, aux).astype(BF16)

    def edges(sems, downs, ups):
        def copies(pairs, offset):
            return [
                send(src, dst, sems.at[0, number], sems.at[1, number], (me + offset, core))
                for number, src, dst in pairs
            ]

        def start():
            @pl.when(me > 0)
            def _():
                for copy in copies(downs, -1):
                    copy.start()

            @pl.when(me < rows - 1)
            def _():
                for copy in copies(ups, 1):
                    copy.start()

        def finish():
            @pl.when(me > 0)
            def _():
                for copy in copies(downs, -1):
                    copy.wait_send()
                for copy in copies(ups, 1):
                    copy.wait_recv()

            @pl.when(me < rows - 1)
            def _():
                for copy in copies(ups, 1):
                    copy.wait_send()
                for copy in copies(downs, -1):
                    copy.wait_recv()

        return start, finish

    first_rows, last_rows = pl.ds(0, MARGIN), pl.ds(own_rows + MARGIN, MARGIN)
    start_edges, finish_edges = edges(
        edge_sems,
        [
            (0, ext_ref.at[first_rows], above_ref),
            (1, extaux_ref.at[first_rows], aboveaux_ref),
        ],
        [
            (2, ext_ref.at[last_rows], below_ref),
            (3, extaux_ref.at[last_rows], belowaux_ref),
        ],
    )
    start_edges()

    @pl.when(me == 0)
    def _():
        below_ref[...] = jnp.zeros(below_ref.shape, BF16)
        belowaux_ref[...] = jnp.zeros(belowaux_ref.shape, BF16)

    @pl.when(me == rows - 1)
    def _():
        above_ref[...] = jnp.zeros(above_ref.shape, BF16)
        aboveaux_ref[...] = jnp.zeros(aboveaux_ref.shape, BF16)

    packed_ref[...] = ext_ref[MARGIN : MARGIN + own_rows, :]
    aux_ref[...] = extaux_ref[MARGIN : MARGIN + own_rows, :].astype(F32)
    for copy in locals_early:
        copy.wait()
    finish_edges()
    top = own_rows - MARGIN
    packed_ref[0:MARGIN, :] = packed_ref[0:MARGIN, :] + below_ref[...]
    packed_ref[top:, :] = packed_ref[top:, :] + above_ref[...]
    aux_ref[0:MARGIN, :] = aux_ref[0:MARGIN, :] + belowaux_ref[...].astype(F32)
    aux_ref[top:, :] = aux_ref[top:, :] + aboveaux_ref[...].astype(F32)

    packed = packed_ref[...].astype(F32)
    scale = row_scale(packed)
    first = (packed * scale * g_attn).astype(BF16)
    first_ref[...] = first
    kv_ref[own, :, 0:inner] = nt(first, wqkv_ref[core, 1]).astype(BF16)
    kv_ref[own, :, inner : 2 * inner] = nt(first, wqkv_ref[core, 2]).astype(BF16)

    gate = DELETE_SCALE * sigmoid(gate_logit(packed, scale, gate_weight))
    ids = aux_ref[:, 0:1] + raw_count * aux_ref[:, 1:2]
    ids_i = ids.astype(jnp.int32)
    starts = jnp.zeros_like(ids_i)
    end = jnp.int32(0)
    for number in range(lengths_ref.shape[0]):
        end = end + lengths_ref[number]
        starts = jnp.where(ids_i >= end, end, starts)
    starts = starts.astype(F32)
    own_eye = eye(own_rows)
    facts_ref[own] = jnp.zeros(facts_ref.shape[1:], F32)
    facts_ref[own, 0:1, 0:own_rows] = to_row(gate, own_eye)
    facts_ref[own, 1:2, 0:own_rows] = to_row(ids, own_eye)
    facts_ref[own, 2:3, 0:own_rows] = to_row(starts, own_eye)
    window.start([(facts_ref, facts_sems), (kv_ref, kv_sems)])
    query_ref[own] = nt(first, wqkv_ref[core, 0]).astype(BF16)

    far = (len(offsets) - 3) // 2
    segments = (range(0, far), range(far, 2 * far), range(2 * far, 2 * far + 3))
    window.finish([(facts_ref, facts_sems)])
    near_ids = joined_row(facts_ref, segments[2], 1, own_rows)
    near_gates = joined_row(facts_ref, segments[2], 0, own_rows)
    near_allowed = joined_row(facts_ref, segments[2], 2, own_rows) == starts
    gaps = near_ids - ids
    for head in range(heads):
        bias = near_bias(gaps, table_ref, head)
        biasq_ref[head] = jnp.where(near_allowed, bias + near_gates, NEGATIVE)
    for head in range(heads):
        bias = near_bias(-gaps, table_ref, head)
        biask_ref[head] = jnp.where(near_allowed, bias + gate, NEGATIVE)

    window.finish([(kv_ref, kv_sems)])
    start_wall(0)
    start_wall(1)
    for step in range(1, HI):
        cot_gathers[0].arrived(step)
    cot_gathers[1].start()

    def spans(segment):
        return slice(segment[0], segment[-1] + 1)

    def far_added(segment, column):
        allowed = joined_row(facts_ref, segment, 2, own_rows) == starts
        return jnp.where(allowed, column, NEGATIVE)

    added = [
        far_added(segment, joined_row(facts_ref, segment, 0, own_rows)) for segment in segments[:2]
    ]
    fixed = (HALF - 1, 2 * HALF - 1)
    lanes = lax.broadcasted_iota(jnp.int32, lse_ref.shape, 1)
    lse_all = jnp.zeros(lse_ref.shape, F32)
    for head in range(heads):
        cut = slice(head * head_size, (head + 1) * head_size)
        cut_v = slice(inner + head * head_size, inner + (head + 1) * head_size)
        query = query_ref[own, :, cut]
        parts = []
        for number, segment in enumerate(segments):
            keys = kv_ref[spans(segment), :, cut].reshape(-1, head_size)
            if number < 2:
                extra = added[number] + table_ref[fixed[number], head]
            else:
                extra = biasq_ref[head]
            parts.append(nt(query, keys) + extra)
        most = jnp.max(parts[0], axis=1, keepdims=True)
        for part in parts[1:]:
            most = jnp.maximum(most, jnp.max(part, axis=1, keepdims=True))
        expos = [jnp.exp(part - most) for part in parts]
        total = sum(jnp.sum(expo, axis=1, keepdims=True) for expo in expos)
        lse_all = jnp.where(lanes == head, most + jnp.log(total), lse_all)
        attended = jnp.zeros((own_rows, head_size), F32)
        for segment, expo in zip(segments, expos):
            values = kv_ref[spans(segment), :, cut_v].reshape(-1, head_size)
            attended = attended + nn((expo / total).astype(BF16), values)
        attf_ref[:, cut] = attended
        att_ref[core, :, cut] = attended.astype(BF16)
    lse_ref[...] = lse_all

    att_copy = send(
        att_ref.at[core], att_ref.at[core], pair_sems.at[0, 4], pair_sems.at[1, 4], sibling
    )
    att_copy.start()
    for copy in locals_late:
        copy.wait()
    for copy in pair_early:
        copy.wait()
    att_copy.wait()
    mixed = packed_ref[...].astype(F32) + (nn(att_ref[0], wout_ref[0]) + nn(att_ref[1], wout_ref[1]))
    mixed_ref[...] = mixed
    sec_ref[high] = (mixed * row_scale(mixed) * g_ff).astype(BF16)
    sec_gather.start()

    for step in range(1, HI):
        cot_gathers[1].arrived(step)
    for number in (2, 0, 1):
        finish_wall(number)

    def sib_copy(kind, step):
        return send(
            sout_ref.at[step],
            sin_ref.at[kind, step],
            sib_sems.at[0, kind, step],
            sib_sems.at[1, kind, step],
            sibling,
        )

    def hi_copy(kind, step):
        return send(
            hout_ref.at[step - 1],
            hin_ref.at[kind, step - 1],
            hi_sems.at[0, kind, step],
            hi_sems.at[1, kind, step],
            high_peer(step),
        )

    def hand_over(kind, step, value):
        part_ref[...] = value
        sout_ref[step] = part_ref[theirs, :].astype(BF16)
        kept_ref[kind if step == 0 else 2 + step % 2] = part_ref[mine, :]
        sib_copy(kind, step).start()

    def pass_on(kind, step):
        sib_copy(kind, step).wait()
        both = kept_ref[2 + step % 2] + sin_ref[kind, step].astype(F32)
        hout_ref[step - 1] = both.astype(BF16)

    def chunk_rows(step):
        return pl.ds(pl.multiple_of(high_other(step) * own_rows, own_rows), own_rows)

    for step in range(HI):
        if step:
            if step == 1:
                for earlier in range(1, HI):
                    for gather in cot_gathers:
                        gather.forwarded(earlier)
                sec_gather.arrived(1)
                sec_gather.arrived(2)
                sec_gather.arrived(3)
            sec_gather.forwarded(step)
        chunk = high_other(step)
        second = sec_ref[chunk]
        gated = nt(second, wall_ref[0])
        upper = nt(second, wall_ref[1])
        d_middle = nt(cots_ref[chunk], wall_ref[2])
        square = gated * gated
        bend = jnp.tanh(GELU_A * gated * (1.0 + GELU_B * square))
        lift = 0.5 * (1.0 + bend)
        slope = lift + 0.5 * gated * (1.0 - bend * bend) * (
            GELU_A * (1.0 + 3.0 * GELU_B * square)
        )
        gelu = gated * lift
        d_gated = (d_middle * upper * slope).astype(BF16)
        d_upper = (d_middle * gelu).astype(BF16)
        mid_ref[chunk_rows(step), :] = (gelu * upper).astype(BF16)
        dgated_ref[chunk_rows(step), :] = d_gated
        dupper_ref[chunk_rows(step), :] = d_upper
        hand_over(1, step, nn(d_gated, wall_ref[0]) + nn(d_upper, wall_ref[1]))
        if step > 1:
            pass_on(1, step - 1)
            hi_copy(1, step - 1).start()
    pass_on(1, HI - 1)
    hi_copy(1, HI - 1).start()
    for gather in cot_gathers + [sec_gather]:
        gather.close()

    def ff_copy(number, step):
        peer = lax.rem(low + step, lows)
        return send(
            wall_ref.at[number, pl.ds(pl.multiple_of(peer * share, share), share)],
            ffin_ref.at[number, step],
            ff_sems.at[0, number, step],
            ff_sems.at[1, number, step],
            low_peer(step),
        )

    def start_ff(number):
        def one(step, carry):
            ff_copy(number, step).start()
            return carry

        lax.fori_loop(1, lows, one, 0)

    hidden = wall_ref.shape[1]

    def weight_grad(number, left_ref, right_ref):
        for begin in range(0, hidden, 256):
            units = slice(begin, min(begin + 256, hidden))
            right = right_ref[...].reshape(HI * own_rows, width)
            wall_ref[number, units, :] = tn(left_ref[:, units], right).astype(BF16)
        start_ff(number)

    weight_grad(0, dgated_ref, sec_ref)
    weight_grad(1, dupper_ref, sec_ref)
    sib_copy(1, 0).wait()
    for step in range(1, HI):
        hi_copy(1, step).wait_send()
    for place, step in enumerate((3, 2, 1, 0)):
        hand_over(0, step, nn(mid_ref[chunk_rows(step), :], wall_ref[2]))
        if place:
            pass_on(0, step + 1)
    weight_grad(2, mid_ref, cots_ref)

    window.start([(query_ref, query_sems)])
    total = kept_ref[1] + sin_ref[1, 0].astype(F32)
    for step in range(1, HI):
        hi_copy(1, step).wait_recv()
        total = total + hin_ref[1, step - 1].astype(F32)
    dsec_ref[mine, :] = total
    dsec_copy = send(
        dsec_ref.at[mine], dsec_ref.at[mine], half_sems.at[0, 0], half_sems.at[1, 0], sibling
    )
    dsec_copy.start()
    dsec_copy.wait()

    back, g_ff_grad = norm_back(mixed_ref[...], g_ff, dsec_ref[...])
    d_mixed = cots_ref[high].astype(F32) + back
    part_ref[...] = d_mixed
    d_branch = d_mixed.astype(BF16)
    d_att = nt(d_branch, wout_ref[core]).astype(BF16)
    dout_ref[own] = d_att
    facts2_ref[own] = jnp.zeros(facts2_ref.shape[1:], F32)
    deltas = []
    products = d_att.astype(F32) * attf_ref[...]
    for head in range(heads):
        cut = slice(head * head_size, (head + 1) * head_size)
        delta = jnp.sum(products[:, cut], axis=1, keepdims=True)
        deltas.append(delta)
        facts2_ref[own, head : head + 1, 0:own_rows] = to_row(delta, own_eye)
        line = 4 + head
        facts2_ref[own, line : line + 1, 0:own_rows] = to_row(
            lse_ref[:, head : head + 1], own_eye
        )
    window.start([(facts2_ref, facts2_sems), (dout_ref, dout_sems)])

    pieces = zout_ref.shape[0] // 4
    piece = zout_ref.shape[1]

    def keep_pieces(number, value):
        for part in range(pieces):
            zout_ref[number * pieces + part] = value[part * piece : (part + 1) * piece, :].astype(
                BF16
            )

    keep_pieces(3, tn(att_ref[core], d_branch))

    lane = lax.broadcasted_iota(jnp.int32, (1, width), 1)
    bias_grad = jnp.zeros((1, width), F32)

    def add_bias(bias_grad, head, bucket, value):
        return bias_grad + jnp.where(lane == head * 2 * HALF + bucket, value, 0.0)

    def total_of(value):
        return jnp.sum(jnp.sum(value, axis=0, keepdims=True), axis=1, keepdims=True)

    for head in range(heads):
        cut = slice(head * head_size, (head + 1) * head_size)
        cut_v = slice(inner + head * head_size, inner + (head + 1) * head_size)
        query, d_head = query_ref[own, :, cut], dout_ref[own, :, cut]
        lse = lse_ref[:, head : head + 1]
        d_query = jnp.zeros((own_rows, head_size), F32)
        for number, segment in enumerate(segments):
            keys = kv_ref[spans(segment), :, cut].reshape(-1, head_size)
            values = kv_ref[spans(segment), :, cut_v].reshape(-1, head_size)
            if number < 2:
                extra = added[number] + table_ref[fixed[number], head]
            else:
                extra = biasq_ref[head]
            probs = jnp.exp(nt(query, keys) + extra - lse)
            d_scores = probs * (nt(d_head, values) - deltas[head])
            d_query = d_query + nn(d_scores.astype(BF16), keys)
            if number < 2:
                bias_grad = add_bias(bias_grad, head, fixed[number], total_of(d_scores))
                continue
            whole = total_of(d_scores)
            for sign in (1, -1):
                base = HALF if sign > 0 else 0
                sums = [
                    total_of(jnp.where(sign * gaps >= limit, d_scores, 0.0)) for limit in LIMITS
                ]
                whole = whole - sums[0]
                for place in range(len(LIMITS)):
                    value = sums[place]
                    if place + 1 < len(LIMITS):
                        value = value - sums[place + 1]
                    bias_grad = add_bias(bias_grad, head, base + place + 1, value)
            bias_grad = add_bias(bias_grad, head, 0, whole)
        heads_ref[core, 0, :, cut] = d_query.astype(BF16)

    window.finish([(query_ref, query_sems), (facts2_ref, facts2_sems), (dout_ref, dout_sems)])
    for step in (3, 2, 1):
        hi_copy(0, step).start()
    d_gate = jnp.zeros((own_rows, 1), F32)
    added = [far_added(segment, gate) for segment in segments[:2]]
    fixed = (2 * HALF - 1, HALF - 1)
    for head in range(heads):
        cut = slice(head * head_size, (head + 1) * head_size)
        cut_v = slice(inner + head * head_size, inner + (head + 1) * head_size)
        key, value = kv_ref[own, :, cut], kv_ref[own, :, cut_v]
        d_key = jnp.zeros((own_rows, head_size), F32)
        d_value = jnp.zeros((own_rows, head_size), F32)
        for number, segment in enumerate(segments):
            queries = query_ref[spans(segment), :, cut].reshape(-1, head_size)
            d_heads = dout_ref[spans(segment), :, cut].reshape(-1, head_size)
            if number < 2:
                extra = added[number] + table_ref[fixed[number], head]
            else:
                extra = biask_ref[head]
            lse = joined_row(facts2_ref, segment, 4 + head, own_rows)
            delta = joined_row(facts2_ref, segment, head, own_rows)
            probs = jnp.exp(nt(key, queries) + extra - lse)
            d_scores = probs * (nt(value, d_heads) - delta)
            d_value = d_value + nn(probs.astype(BF16), d_heads)
            d_key = d_key + nn(d_scores.astype(BF16), queries)
            d_gate = d_gate + jnp.sum(d_scores, axis=1, keepdims=True)
        heads_ref[core, 1, :, cut] = d_key.astype(BF16)
        heads_ref[core, 2, :, cut] = d_value.astype(BF16)
    dgate_ref[core] = jnp.broadcast_to(d_gate, dgate_ref.shape[1:])
    pair_late = [
        send(ref.at[core], ref.at[core], pair_sems.at[0, 5 + i], pair_sems.at[1, 5 + i], sibling)
        for i, ref in enumerate((heads_ref, dgate_ref))
    ]
    for copy in pair_late:
        copy.start()
    for number in range(3):
        keep_pieces(number, tn(heads_ref[core, number], first_ref[...]))

    def low_copy(step):
        return send(
            zout_ref.at[lax.rem(low + step, lows)],
            zin_ref.at[low],
            low_sems.at[0, step],
            low_sems.at[1, step],
            low_peer(step),
        )

    def low_arrival(step):
        return send(
            zout_ref.at[low],
            zin_ref.at[low_source(step)],
            low_sems.at[0, step],
            low_sems.at[1, step],
            low_peer(step),
        )

    def start_low(step, carry):
        low_copy(step).start()
        return carry

    lax.fori_loop(1, lows, start_low, 0)
    zin_ref[low] = zout_ref[low]

    for copy in pair_late:
        copy.wait()
    d_first = jnp.zeros((own_rows, width), F32)
    for side in range(2):
        for number in range(3):
            d_first = d_first + nn(heads_ref[side, number], wqkv_ref[side, number])
    back, g_attn_grad = norm_back(packed_ref[...].astype(F32), g_attn, d_first)
    inside = slice(MARGIN, MARGIN + own_rows)
    back_ref[inside, :] = (part_ref[...] + back).astype(BF16)
    d_gate = dgate_ref[0] + dgate_ref[1]
    lane_g = lax.broadcasted_iota(jnp.int32, d_gate.shape, 1)
    terms = jnp.zeros(d_gate.shape, F32)
    for number, term in enumerate(split3(d_gate)):
        terms = jnp.where(lane_g == number, term, terms)
    backaux_ref[inside, :] = terms.astype(BF16)
    down_src, down_dst = pl.ds(MARGIN, MARGIN), pl.ds(own_rows + MARGIN, MARGIN)
    up_src, up_dst = pl.ds(own_rows, MARGIN), pl.ds(0, MARGIN)
    start_edges, finish_edges = edges(
        edge2_sems,
        [
            (0, back_ref.at[down_src], back_ref.at[down_dst]),
            (1, backaux_ref.at[down_src], backaux_ref.at[down_dst]),
        ],
        [
            (2, back_ref.at[up_src], back_ref.at[up_dst]),
            (3, backaux_ref.at[up_src], backaux_ref.at[up_dst]),
        ],
    )
    start_edges()

    @pl.when(me == 0)
    def _():
        back_ref[up_dst, :] = jnp.zeros((MARGIN, width), BF16)
        backaux_ref[up_dst, :] = jnp.zeros((MARGIN, 128), BF16)

    @pl.when(me == rows - 1)
    def _():
        back_ref[down_dst, :] = jnp.zeros((MARGIN, width), BF16)
        backaux_ref[down_dst, :] = jnp.zeros((MARGIN, 128), BF16)

    finish_edges()

    spread = tn(backaux_ref[...], chosen_ref[...])
    raw_cot = gcot_ref[...] + (spread[0:1, :] + spread[1:2, :] + spread[2:3, :])
    gate_s = sigmoid(raw_logit)
    d_logit = raw_cot * (DELETE_SCALE * gate_s * (1.0 - gate_s))
    scaled = d_logit * raw_scale
    along = d_logit * raw_logit * raw_scale * raw_scale * (1.0 / width)
    s1, s2, s3 = split3(scaled)
    w1, w2, w3 = split3(gate_weight)
    outer = tn(
        stacked_rows((w1, w1, w2, w2, w1, w3), width),
        stacked_rows((s1, s2, s1, s2, s3, s1), raw_count),
    )
    rows_ref[...] = outer - along * byte_ref[...].astype(F32)
    rows_ref[...] = rows_ref[...] + tn(back_ref[...], chosen_ref[...])
    common = jnp.sum(
        nt(stacked_rows((s1, s2, s3), raw_count), byte_ref[...]), axis=0, keepdims=True
    )

    slow_ref[low, 0:1, :] = g_ff_grad
    slow_ref[low, 1:2, :] = g_attn_grad
    slow_ref[low, 2:3, :] = common * g_delete
    slow_ref[low, 3:4, :] = common * w_delete
    slow_ref[low, 4:5, :] = bias_grad
    slow_ref[low, 5:8, :] = jnp.zeros((3, width), F32)

    def slow_copy(step, target, source):
        return send(
            slow_ref.at[source],
            slow_ref.at[source],
            slow_sems.at[0, step],
            slow_sems.at[1, step],
            target,
        )

    def start_slow(step, carry):
        slow_copy(step, low_peer(step), low).start()
        return carry

    lax.fori_loop(1, lows, start_slow, 0)

    def finish_low(step, carry):
        low_copy(step).wait_send()
        low_arrival(step).wait_recv()
        return carry

    lax.fori_loop(1, lows, finish_low, 0)
    total = zin_ref[0].astype(F32)
    for number in range(1, lows):
        total = total + zin_ref[number].astype(F32)
    quarter = piece // HI
    for number in range(HI):
        yout_ref[number] = total[number * quarter : (number + 1) * quarter, :].astype(BF16)

    def high_copy(step):
        return send(
            yout_ref.at[high_other(step)],
            yin_ref.at[high],
            high_sems.at[0, step],
            high_sems.at[1, step],
            high_peer(step),
        )

    def high_arrival(step):
        return send(
            yout_ref.at[high],
            yin_ref.at[high_other(step)],
            high_sems.at[0, step],
            high_sems.at[1, step],
            high_peer(step),
        )

    for step in range(1, HI):
        high_copy(step).start()
    yin_ref[high] = yout_ref[high]

    def finish_slow(step, carry):
        slow_copy(step, low_peer(step), low).wait_send()
        slow_copy(step, low_peer(step), low_source(step)).wait_recv()
        return carry

    lax.fori_loop(1, lows, finish_slow, 0)
    small = slow_ref[0]
    for number in range(1, lows):
        small = small + slow_ref[number]
    shigh_ref[high] = small

    def shigh_copy(step, source):
        return send(
            shigh_ref.at[source],
            shigh_ref.at[source],
            shigh_sems.at[0, step],
            shigh_sems.at[1, step],
            high_peer(step),
        )

    for step in range(1, HI):
        shigh_copy(step, high).start()

    for step in range(1, HI):
        high_copy(step).wait_send()
        high_arrival(step).wait_recv()
    total = yin_ref[0].astype(F32)
    for number in range(1, HI):
        total = total + yin_ref[number].astype(F32)
    yout_ref[high] = total.astype(BF16)
    keep_share = pltpu.make_async_copy(
        yout_ref.at[high], attg_ref.at[low, high], local_sems.at[1]
    )
    keep_share.start()

    def back_copy(step, source):
        return send(
            yout_ref.at[high],
            attg_ref.at[low, source],
            back_sems.at[0, step],
            back_sems.at[1, step],
            high_peer(step),
        )

    for step in range(1, HI):
        back_copy(step, high).start()
    for step in range(1, HI):
        shigh_copy(step, high).wait_send()
        shigh_copy(step, high_other(step)).wait_recv()
    small = shigh_ref[0]
    for number in range(1, HI):
        small = small + shigh_ref[number]
    small_ref[...] = small
    for step in range(1, HI):
        back_copy(step, high).wait_send()
        back_copy(step, high_other(step)).wait_recv()
    keep_share.wait()

    def last_copy(step, source):
        return send(
            attg_ref.at[source],
            attg_ref.at[source],
            last_sems.at[0, step],
            last_sems.at[1, step],
            low_peer(step),
        )

    def start_last(step, carry):
        last_copy(step, low).start()
        return carry

    lax.fori_loop(1, lows, start_last, 0)

    sib_copy(0, 0).wait()
    total = mixed_ref[mine, :] + (kept_ref[0] + sin_ref[0, 0].astype(F32))
    for step in range(1, HI):
        hi_copy(0, step).wait()
        total = total + hin_ref[0, step - 1].astype(F32)
    block_ref[mine, :] = total.astype(BF16)
    block_copy = send(
        block_ref.at[mine], block_ref.at[mine], half_sems.at[0, 1], half_sems.at[1, 1], sibling
    )
    block_copy.start()

    def finish_ff(step, carry):
        for number in range(3):
            ff_copy(number, step).wait()
        return carry

    lax.fori_loop(1, lows, finish_ff, 0)
    for number in range(3):
        load = pltpu.make_async_copy(ffin_ref.at[number], ffload_ref, local_sems.at[0])
        load.start()
        load.wait()
        total = wall_ref[number, my_share, :].astype(F32)
        for step in range(1, lows):
            total = total + ffload_ref[step].astype(F32)
        ffo_ref[number] = total
    block_copy.wait()

    def finish_last(step, carry):
        last_copy(step, low).wait_send()
        last_copy(step, low_source(step)).wait_recv()
        return carry

    lax.fori_loop(1, lows, finish_last, 0)


def layer(rows, offsets, *operands):
    lengths, table, byte_t, keep, vecs, gcot, wq, wk, wv, wo, wg, wu, wd, cot = operands
    width, raw_count = byte_t.shape
    own_rows = cot.shape[0]
    inner = wq.shape[0]
    heads = table.shape[1]
    share = wd.shape[0]
    lows = rows // HI
    hidden = lows * share
    slots = len(offsets)
    half = own_rows // 2
    piece = 4 * inner // lows
    quarter = piece // HI
    ext_rows = own_rows + 2 * MARGIN
    vmem = pl.BlockSpec(memory_space=pltpu.VMEM)
    smem = pl.BlockSpec(memory_space=pltpu.SMEM)
    anywhere = pl.BlockSpec(memory_space=pl.ANY)
    shape = jax.ShapeDtypeStruct
    dma = pltpu.SemaphoreType.DMA
    outs = [
        shape((1, raw_count), F32),
        shape((own_rows, width), BF16),
        shape((width, raw_count), F32),
        shape((8, width), F32),
        shape((3, share, width), F32),
        shape((lows, HI, quarter, width), BF16),
        shape((3, lows, share, width), BF16),
    ]
    out_specs = [vmem] * 5 + [anywhere] * 2
    scratch = [
        pltpu.VMEM((rows, 8, 128), F32),
        pltpu.VMEM((ext_rows, raw_count), BF16),
        pltpu.VMEM((ext_rows, width), BF16),
        pltpu.VMEM((ext_rows, 128), BF16),
        pltpu.VMEM((MARGIN, width), BF16),
        pltpu.VMEM((MARGIN, width), BF16),
        pltpu.VMEM((MARGIN, 128), BF16),
        pltpu.VMEM((MARGIN, 128), BF16),
        pltpu.VMEM((own_rows, width), BF16),
        pltpu.VMEM((own_rows, 128), F32),
        pltpu.VMEM((own_rows, width), BF16),
        pltpu.VMEM((slots, own_rows, 2 * inner), BF16),
        pltpu.VMEM((slots, own_rows, inner), BF16),
        pltpu.VMEM((slots, 8, 256), F32),
        pltpu.VMEM((slots, own_rows, inner), BF16),
        pltpu.VMEM((slots, 8, 256), F32),
        pltpu.VMEM((heads, own_rows, 3 * own_rows), F32),
        pltpu.VMEM((heads, own_rows, 3 * own_rows), F32),
        pltpu.VMEM((2, own_rows, inner), BF16),
        pltpu.VMEM((own_rows, inner), F32),
        pltpu.VMEM((own_rows, 128), F32),
        pltpu.VMEM((own_rows, width), F32),
        pltpu.VMEM((HI, own_rows, width), BF16),
        pltpu.VMEM((HI, own_rows, width), BF16),
        pltpu.VMEM((3, hidden, width), BF16),
        pltpu.VMEM((2, inner, width), BF16),
        pltpu.VMEM((2, 3, inner, width), BF16),
        pltpu.VMEM((HI * own_rows, hidden), BF16),
        pltpu.VMEM((HI * own_rows, hidden), BF16),
        pltpu.VMEM((HI * own_rows, hidden), BF16),
        pltpu.VMEM((own_rows, width), F32),
        pltpu.VMEM((4, half, width), F32),
        pltpu.VMEM((HI, half, width), BF16),
        pltpu.VMEM((2, HI, half, width), BF16),
        pltpu.VMEM((HI - 1, half, width), BF16),
        pltpu.VMEM((2, HI - 1, half, width), BF16),
        pltpu.VMEM((own_rows, width), F32),
        pltpu.VMEM((2, 3, own_rows, inner), BF16),
        pltpu.VMEM((2, own_rows, 128), F32),
        pltpu.VMEM((lows, piece, width), BF16),
        pltpu.VMEM((lows, piece, width), BF16),
        pltpu.VMEM((HI, quarter, width), BF16),
        pltpu.VMEM((HI, quarter, width), BF16),
        pltpu.VMEM((lows, 8, width), F32),
        pltpu.VMEM((HI, 8, width), F32),
        pltpu.VMEM((ext_rows, width), BF16),
        pltpu.VMEM((ext_rows, 128), BF16),
        pltpu.VMEM((lows, share, width), BF16),
        dma((2, rows)),
        dma((2, 4)),
        dma((2, slots)),
        dma((2, slots)),
        dma((2, slots)),
        dma((2, slots)),
        dma((2, slots)),
        dma((2, 3, lows)),
        dma((2, 7)),
        dma((8,)),
        dma((2, 2, HI)),
        dma((2, 2, HI)),
        dma((2, HI)),
        dma((2, HI)),
        dma((2, 2, HI)),
        dma((2, 2, HI)),
        dma((2, 2)),
        dma((2, 3, lows)),
        dma((2, lows)),
        dma((2, HI)),
        dma((2, HI)),
        dma((2, lows)),
        dma((2, 4)),
        dma((2, lows)),
        dma((2, HI)),
    ]
    return pl.pallas_call(
        functools.partial(layer_kernel, rows, offsets),
        name="layer",
        out_shape=outs,
        in_specs=[smem, smem] + [vmem] * 4 + [anywhere] * 8,
        out_specs=out_specs,
        scratch_shapes=scratch,
        compiler_params=pltpu.CompilerParams(
            collective_id=0, has_side_effects=True, vmem_limit_bytes=VMEM_LIMIT
        ),
    )(*operands)


def per_device(
    byte_rows,
    lengths,
    keep_mask,
    w_delete,
    g_delete,
    g_attn,
    w_query,
    w_key,
    w_value,
    w_out,
    rel_bias,
    g_ff,
    w_gate,
    w_up,
    w_down,
    out_cot,
    gate_cot,
):
    raw_count, width = byte_rows.shape
    own_rows = out_cot.shape[0]
    inner = w_query.shape[1]
    buckets, heads = rel_bias.shape
    rows = lax.axis_size("rows")
    share = w_down.shape[0]
    offsets = slots_of(reach_of(raw_count, own_rows))
    line = lax.broadcasted_iota(jnp.int32, (8, width), 0)
    vecs = jnp.zeros((8, width), F32)
    for number, vector in enumerate((g_delete, w_delete, g_attn, g_ff)):
        vecs = jnp.where(line == number, vector[None, :], vecs)
    spare = -share % 16
    weights = [jnp.pad(w, ((0, spare), (0, 0))) for w in (w_gate.T, w_up.T, w_down)]
    gate, block_out, grad_rows, small, ff_sums, att_grads, _ = layer(
        rows,
        offsets,
        lengths,
        rel_bias,
        byte_rows.T,
        keep_mask.reshape(1, -1),
        vecs,
        gate_cot.reshape(1, -1),
        w_query.T,
        w_key.T,
        w_value.T,
        w_out,
        *weights,
        out_cot,
    )
    att_grads = att_grads.reshape(4, inner, width).astype(F32)
    ff_sums = ff_sums[:, :share]
    grad_bias = small[4, : heads * buckets].reshape(heads, buckets).T
    return (
        block_out,
        gate[0],
        grad_rows.T,
        small[2],
        small[3],
        small[1],
        att_grads[0].T,
        att_grads[1].T,
        att_grads[2].T,
        att_grads[3],
        grad_bias,
        small[0],
        ff_sums[0].T,
        ff_sums[1].T,
        ff_sums[2],
    )


def solution(mesh):
    in_specs = (
        P("rows", None),
        P(),
        P("rows"),
        P(),
        P(),
        P(),
        P(None, "tensor"),
        P(None, "tensor"),
        P(None, "tensor"),
        P("tensor", None),
        P(None, "tensor"),
        P(),
        P(None, ("rows", "tensor")),
        P(None, ("rows", "tensor")),
        P(("rows", "tensor"), None),
        P("rows", None),
        P("rows"),
    )
    out_specs = (
        P("rows", None),
        P("rows"),
        P("rows", None),
        P(),
        P(),
        P(),
        P(None, "tensor"),
        P(None, "tensor"),
        P(None, "tensor"),
        P("tensor", None),
        P(None, "tensor"),
        P(),
        P(None, ("rows", "tensor")),
        P(None, ("rows", "tensor")),
        P(("rows", "tensor"), None),
    )
    return jax.shard_map(
        per_device, mesh=mesh, in_specs=in_specs, out_specs=out_specs, check_vma=False
    )
```

```python
import functools

import jax
import jax.numpy as jnp
from jax import lax
from jax.experimental import pallas as pl
from jax.experimental.pallas import tpu as pltpu
from jax.sharding import PartitionSpec as P

MAXLEN = 1024
MARGIN = 32
EPS = 1e-06
DELETE_SCALE = -30.0
NEGATIVE = -1e30
LIMITS = (1, 2, 3, 4, 5, 6, 7, 8, 12, 16, 23, 32, 46, 64, 91)
HALF = 16
HI = 4
MESH = pl.DeviceIdType.MESH
F32 = jnp.float32
BF16 = jnp.bfloat16
VMEM_LIMIT = 63 * 1024 * 1024


def nn(a, b):
    return lax.dot_general(a, b, (((1,), (0,)), ((), ())), preferred_element_type=F32)


def nt(a, b):
    return lax.dot_general(a, b, (((1,), (1,)), ((), ())), preferred_element_type=F32)


def tn(a, b):
    return lax.dot_general(a, b, (((0,), (0,)), ((), ())), preferred_element_type=F32)


def eye(count):
    return lax.broadcasted_iota(jnp.int32, (count, count), 0) == lax.broadcasted_iota(
        jnp.int32, (count, count), 1
    )


def to_row(column, diagonal):
    return jnp.sum(jnp.where(diagonal, column, 0.0), axis=0, keepdims=True)


def to_column(row, diagonal):
    return jnp.sum(jnp.where(diagonal, row, 0.0), axis=1, keepdims=True)


def row_scale(values):
    return lax.rsqrt(jnp.mean(values * values, axis=-1, keepdims=True) + EPS)


def gate_logit(values, scale, weight):
    return scale * jnp.sum(values * weight, axis=-1, keepdims=True)


def sigmoid(value):
    return 1.0 / (1.0 + jnp.exp(-value))


def norm_back(values, gain, grad):
    scale = row_scale(values)
    scaled = grad * gain
    inner = jnp.mean(scaled * values, axis=-1, keepdims=True)
    back = scale * scaled - values * (scale * scale * scale * inner)
    return back, jnp.sum(grad * values * scale, axis=0, keepdims=True)


def reach_of(raw_count, own_rows):
    span = (MAXLEN // raw_count - 1) * own_rows + 2 * MARGIN + raw_count
    return -(-(span - 1) // own_rows)


def slots_of(reach):
    far = list(range(2, reach + 1))
    return [-d for d in reversed(far)] + far + [-1, 0, 1]


def meet_rows(rows):
    me, core = lax.axis_index("rows"), lax.axis_index("tensor")
    barrier = pltpu.get_barrier_semaphore()

    def greet(step, carry):
        pl.semaphore_signal(
            barrier, inc=1, device_id=(lax.rem(me + step, rows), core), device_id_type=MESH
        )
        return carry

    lax.fori_loop(1, rows, greet, 0)
    pl.semaphore_signal(barrier, inc=1, device_id=(me, 1 - core), device_id_type=MESH)
    pl.semaphore_wait(barrier, rows)


def send(src, dst, send_sem, recv_sem, target):
    return pltpu.make_async_remote_copy(
        src_ref=src,
        dst_ref=dst,
        send_sem=send_sem,
        recv_sem=recv_sem,
        device_id=target,
        device_id_type=MESH,
    )


class Window:
    def __init__(self, rows, offsets):
        self.rows, self.offsets = rows, offsets
        self.me, self.core = lax.axis_index("rows"), lax.axis_index("tensor")
        self.slot = {offset: number for number, offset in enumerate(offsets)}
        self.own = self.slot[0]

    def inside(self, offset):
        if offset < 0:
            return self.me >= -offset
        return self.me < self.rows - offset

    def copy(self, ref, sems, offset):
        there = self.slot[-offset]
        return send(
            ref.at[self.own],
            ref.at[there],
            sems.at[0, self.slot[offset]],
            sems.at[1, there],
            (self.me + offset, self.core),
        )

    def start(self, pairs):
        for offset in sorted(self.offsets, key=abs, reverse=True):
            if offset:

                @pl.when(self.inside(offset))
                def _():
                    for ref, sems in pairs:
                        self.copy(ref, sems, offset).start()

    def finish(self, pairs, offsets=None):
        for offset in self.offsets if offsets is None else offsets:
            if offset:

                @pl.when(self.inside(offset))
                def _():
                    for ref, sems in pairs:
                        copy = self.copy(ref, sems, offset)
                        copy.wait_send()
                        arrival = send(
                            ref.at[self.own],
                            ref.at[self.slot[offset]],
                            sems.at[0, self.slot[offset]],
                            sems.at[1, self.slot[offset]],
                            (self.me + offset, self.core),
                        )
                        arrival.wait_recv()

    def clear(self, ref, value):
        for offset in self.offsets:
            if offset:

                @pl.when(jnp.logical_not(self.inside(offset)))
                def _():
                    ref[self.slot[offset]] = jnp.full(ref.shape[1:], value, ref.dtype)


EDGE = -(-LIMITS[-1] // 16) * 16


def near_bias(gap, table_ref, head, above, below):
    if above and below:
        bias = jnp.full(gap.shape, table_ref[head, 0], F32)
    else:
        bias = jnp.full(gap.shape, table_ref[head, HALF if above else 0], F32)
    for number, limit in enumerate(LIMITS):
        if above:
            bias = jnp.where(gap >= limit, table_ref[head, HALF + number + 1], bias)
        if below:
            bias = jnp.where(gap <= -limit, table_ref[head, number + 1], bias)
    return bias


def joined_row(facts_ref, slots, line, width):
    return jnp.concatenate([facts_ref[slot, line : line + 1, :width] for slot in slots], axis=1)


GELU_A = 0.7978845608028654
GELU_B = 0.044715


def split3(value):
    one = value.astype(BF16).astype(F32)
    rest = value - one
    two = rest.astype(BF16).astype(F32)
    return one, two, (rest - two).astype(BF16).astype(F32)


def stacked_rows(rows, width):
    line = lax.broadcasted_iota(jnp.int32, (8, width), 0)
    result = jnp.zeros((8, width), F32)
    for number, row in enumerate(rows):
        result = jnp.where(line == number, row, result)
    return result.astype(BF16)


def layer_kernel(
    rows,
    offsets,
    lengths_ref,
    table_ref,
    byte_ref,
    keep_ref,
    vec_ref,
    gcot_ref,
    wq_ref,
    wk_ref,
    wv_ref,
    wo_ref,
    wg_ref,
    wu_ref,
    wd_ref,
    cot_ref,
    gate_ref,
    block_ref,
    rows_ref,
    small_ref,
    ffo_ref,
    attg_ref,
    ffin_ref,
    count_ref,
    chosen_ref,
    ext_ref,
    extaux_ref,
    below_ref,
    above_ref,
    belowaux_ref,
    aboveaux_ref,
    packed_ref,
    aux_ref,
    first_ref,
    kv_ref,
    query_ref,
    facts_ref,
    dout_ref,
    facts2_ref,
    biasq_ref,
    biask_ref,
    att_ref,
    attf_ref,
    lse_ref,
    mixed_ref,
    sec_ref,
    cots_ref,
    wall_ref,
    wout_ref,
    wqkv_ref,
    mid_ref,
    dgated_ref,
    dupper_ref,
    part_ref,
    kept_ref,
    sout_ref,
    sin_ref,
    hout_ref,
    hin_ref,
    dsec_ref,
    heads_ref,
    dgate_ref,
    zout_ref,
    zin_ref,
    yin_ref,
    fin_ref,
    slow_ref,
    shigh_ref,
    back_ref,
    backaux_ref,
    ffa_ref,
    ffb_ref,
    za_ref,
    zb_ref,
    count_sems,
    edge_sems,
    kv_sems,
    query_sems,
    facts_sems,
    dout_sems,
    facts2_sems,
    wall_sems,
    pair_sems,
    local_sems,
    cot_sems,
    cotf_sems,
    sec_sems,
    secf_sems,
    sib_sems,
    hi_sems,
    half_sems,
    ff_sems,
    low_sems,
    high_sems,
    back_sems,
    last_sems,
    edge2_sems,
    slow_sems,
    shigh_sems,
):
    width, raw_count = byte_ref.shape
    own_rows = cot_ref.shape[0]
    inner = wq_ref.shape[0]
    heads = table_ref.shape[0]
    head_size = inner // heads
    share = wd_ref.shape[0]
    lows = rows // HI
    half = own_rows // 2
    ext_rows = own_rows + 2 * MARGIN
    me, core = lax.axis_index("rows"), lax.axis_index("tensor")
    high, low = lax.div(me, lows), lax.rem(me, lows)
    sibling = (me, 1 - core)
    mine = pl.ds(pl.multiple_of(core * half, half), half)
    theirs = pl.ds(pl.multiple_of((1 - core) * half, half), half)
    window = Window(rows, offsets)
    own = window.own
    g_delete, w_delete = vec_ref[0:1, :], vec_ref[1:2, :]
    g_attn, g_ff = vec_ref[2:3, :], vec_ref[3:4, :]

    is_square = lows == 4

    def low_other(step):
        if step == 1:
            return low + 1 - 2 * lax.rem(low, 2)
        if step == 2:
            return lax.rem(low + 2, lows)
        return lows - 1 - low

    def low_pair(step):
        return (high * lows + low_other(step), core)

    def low_peer(step):
        return (high * lows + lax.rem(low + step, lows), core)

    def low_source(step):
        return lax.rem(low + lows - step, lows)

    def high_other(step):
        if step == 0:
            return high
        if step == 1:
            return high + 1 - 2 * lax.rem(high, 2)
        if step == 2:
            return lax.rem(high + 2, HI)
        return HI - 1 - high

    def high_peer(step):
        return (high_other(step) * lows + low, core)

    middle_high = jnp.logical_and(high >= 1, high <= 2)

    def first_half(count):
        return count // 2 // 16 * 16

    class LowGather:
        def __init__(self, source, block, count, sems):
            self.source, self.block, self.count, self.sems = source, block, count, sems
            cut = first_half(count)
            self.halves = ((0, cut), (cut, count - cut))

        def copy(self, src, dst, number, target):
            return send(src, dst, self.sems.at[0, number], self.sems.at[1, number], target)

        def direct(self, step):
            if is_square:
                target = low_pair(step)
            else:
                target = low_peer(step)
            return self.copy(self.source, self.block(low, 0, self.count), step, target)

        def arrival(self, step):
            place = self.block(low_other(step) if is_square else low_source(step), 0, self.count)
            return self.copy(place, place, step, sibling)

        def passed(self, side):
            place = self.block(low_other(2 - side), *self.halves[side])
            return self.copy(place, place, 3 + side, low_pair(1 + side))

        def start(self):
            if is_square:
                self.direct(1).start()
                self.direct(2).start()
                return

            def one(step, carry):
                self.direct(step).start()
                return carry

            lax.fori_loop(1, lows, one, 0)

        def relay(self):
            if is_square:
                for side in (1, 0):
                    self.arrival(2 - side).wait_recv()
                    self.passed(side).start()

        def finish(self):
            if is_square:
                for step in (1, 2):
                    self.direct(step).wait_send()
                for side in range(2):
                    self.passed(side).wait_send()
                    place = self.block(low_other(3), *self.halves[side])
                    self.copy(place, place, 3 + side, sibling).wait_recv()
                return

            def one(step, carry):
                self.direct(step).wait_send()
                self.arrival(step).wait_recv()
                return carry

            lax.fori_loop(1, lows, one, 0)

    class LowReduce:
        def __init__(self, part, count, relays, arrivals, sems):
            self.part, self.count, self.sems = part, count, sems
            self.relays, self.arrivals = relays, arrivals
            cut = first_half(count)
            self.halves = ((0, cut), (cut, count - cut))

        def copy(self, src, dst, number, target):
            return send(src, dst, self.sems.at[0, number], self.sems.at[1, number], target)

        def half(self, side):
            return self.copy(
                self.part(low_other(3), *self.halves[side]),
                self.relays[side],
                side,
                low_pair(2 - side),
            )

        def summed(self, side):
            return self.copy(
                self.part(low_other(1 + side), 0, self.count),
                self.arrivals.at[side],
                2 + side,
                low_pair(1 + side),
            )

        def direct(self, step):
            return self.copy(
                self.part(lax.rem(low + step, lows), 0, self.count),
                self.arrivals.at[step],
                step,
                low_peer(step),
            )

        def start(self):
            if is_square:
                for side in range(2):
                    self.half(side).start()
                return

            def one(step, carry):
                self.direct(step).start()
                return carry

            lax.fori_loop(1, lows, one, 0)

        def relay(self):
            if is_square:
                for side in range(2):
                    self.half(side).wait()
                    mine_too = self.part(low_other(1 + side), *self.halves[side])
                    both = mine_too[...].astype(F32) + self.relays[side][...].astype(F32)
                    mine_too[...] = both.astype(BF16)
                    self.summed(side).start()

        def finish(self):
            if is_square:
                for side in range(2):
                    self.summed(side).wait()
                return

            def one(step, carry):
                self.direct(step).wait()
                return carry

            lax.fori_loop(1, lows, one, 0)

    arrived = range(2) if is_square else range(1, lows)

    meet_rows(rows)

    keep = keep_ref[...].astype(F32)
    count_ref[me] = jnp.broadcast_to(jnp.sum(keep, axis=1, keepdims=True), (8, 128))

    def count_copy(step):
        return send(
            count_ref.at[me],
            count_ref.at[me],
            count_sems.at[0, step],
            count_sems.at[1, step],
            (lax.rem(me + step, rows), core),
        )

    def count_arrival(step):
        source = lax.rem(me + rows - step, rows)
        return send(
            count_ref.at[source],
            count_ref.at[source],
            count_sems.at[0, step],
            count_sems.at[1, step],
            (source, core),
        )

    def start_count(step, carry):
        count_copy(step).start()
        return carry

    lax.fori_loop(1, rows, start_count, 0)

    weight_refs = (wg_ref, wu_ref, wd_ref)
    my_share = pl.ds(pl.multiple_of(low * share, share), share)
    locals_early = [
        pltpu.make_async_copy(ref, wqkv_ref.at[core, number], local_sems.at[number])
        for number, ref in enumerate((wq_ref, wk_ref, wv_ref))
    ]
    locals_late = [
        pltpu.make_async_copy(wo_ref, wout_ref.at[core], local_sems.at[3]),
        pltpu.make_async_copy(cot_ref, cots_ref.at[high], local_sems.at[4]),
    ] + [
        pltpu.make_async_copy(ref, wall_ref.at[number, my_share], local_sems.at[5 + number])
        for number, ref in enumerate(weight_refs)
    ]
    for copy in locals_early + locals_late:
        copy.start()

    def wall_gather(number):
        def block(place, begin, count):
            inside = pl.ds(pl.multiple_of(place * share + begin, 16), count)
            return wall_ref.at[number, inside]

        return LowGather(weight_refs[number], block, share, wall_sems.at[number])

    walls = [wall_gather(number) for number in range(3)]

    class Gather:
        def __init__(self, ref, sems, sems_f, offset, count, source=None):
            self.ref, self.sems, self.sems_f = ref, sems, sems_f
            self.part = pl.ds(pl.multiple_of(core * half + offset, 16), count)
            self.other = pl.ds(pl.multiple_of((1 - core) * half + offset, 16), count)
            self.source = ref.at[high] if source is None else source

        def direct(self, step):
            return send(
                self.source.at[self.part],
                self.ref.at[high, self.part],
                self.sems.at[0, step],
                self.sems.at[1, step],
                high_peer(step),
            )

        def arrival(self, step):
            place = self.ref.at[high_other(step), self.part]
            return send(
                place, place, self.sems.at[0, step], self.sems.at[1, step], high_peer(step)
            )

        def relay(self):
            place = self.ref.at[high_other(2), self.part]
            return send(place, place, self.sems.at[0, 0], self.sems.at[1, 3], high_peer(1))

        def forward(self, step, part):
            place = self.ref.at[high_other(step), part]
            return send(
                place, place, self.sems_f.at[0, step], self.sems_f.at[1, step], sibling
            )

        def start(self):
            self.direct(1).start()
            self.direct(2).start()

            @pl.when(middle_high)
            def _():
                self.direct(3).start()

        def arrived(self, step):
            self.arrival(step).wait_recv()
            if step == 2:

                @pl.when(middle_high)
                def _():
                    self.relay().start()

            self.forward(step, self.part).start()

        def forwarded(self, step):
            self.forward(step, self.other).wait_recv()

        def close(self):
            self.direct(1).wait_send()
            self.direct(2).wait_send()

            @pl.when(middle_high)
            def _():
                self.direct(3).wait_send()
                self.relay().wait_send()

            for step in range(1, HI):
                self.forward(step, self.part).wait_send()

    third = half // 3 // 16 * 16
    cot_gathers = [
        Gather(cots_ref, cot_sems.at[number], cotf_sems.at[number], begin, count, cot_ref)
        for number, (begin, count) in enumerate(((0, third), (third, half - third)))
    ]
    sec_gather = Gather(sec_ref, sec_sems, secf_sems, 0, half)

    pair_early = [
        send(wo_ref, wout_ref.at[core], pair_sems.at[0, 0], pair_sems.at[1, 0], sibling)
    ] + [
        send(
            ref,
            wqkv_ref.at[core, number],
            pair_sems.at[0, 1 + number],
            pair_sems.at[1, 1 + number],
            sibling,
        )
        for number, ref in enumerate((wq_ref, wk_ref, wv_ref))
    ]
    for copy in pair_early:
        copy.start()

    gate_weight = g_delete * w_delete
    raw = byte_ref[...]
    raw_f = raw.astype(F32)
    raw_scale = lax.rsqrt(jnp.mean(raw_f * raw_f, axis=0, keepdims=True) + EPS)
    raw_logit = raw_scale * jnp.sum(
        nn(stacked_rows(split3(gate_weight), width), raw), axis=0, keepdims=True
    )
    gate_ref[...] = DELETE_SCALE * sigmoid(raw_logit)
    upper = lax.broadcasted_iota(jnp.int32, (raw_count, raw_count), 0) <= lax.broadcasted_iota(
        jnp.int32, (raw_count, raw_count), 1
    )
    rank = nn(keep.astype(BF16), jnp.where(upper, 1.0, 0.0).astype(BF16)) - 1.0
    lane = lax.broadcasted_iota(jnp.int32, (raw_count, 128), 1)
    local = lax.broadcasted_iota(jnp.int32, (raw_count, 128), 0).astype(F32)
    aux = jnp.where(lane == 0, local, jnp.where(lane == 1, me.astype(F32), 0.0)).astype(BF16)
    window.clear(kv_ref, 0.0)
    window.clear(query_ref, 0.0)
    window.clear(facts_ref, -1.0)
    window.clear(dout_ref, 0.0)
    window.clear(facts2_ref, 0.0)

    def finish_count(step, carry):
        count_copy(step).wait_send()
        count_arrival(step).wait_recv()
        return carry

    lax.fori_loop(1, rows, finish_count, 0)
    lower = lax.broadcasted_iota(jnp.int32, count_ref.shape, 0) < me
    before = jnp.sum(jnp.where(lower, count_ref[...], 0.0), axis=0)[0:1, 0:1]
    place = before + rank - (me * own_rows).astype(F32)
    place = jnp.where(keep > 0.0, place, -4096.0).astype(jnp.int32)
    chosen = place + MARGIN == lax.broadcasted_iota(jnp.int32, (ext_rows, raw_count), 0)
    chosen = jnp.where(chosen, 1.0, 0.0).astype(BF16)
    chosen_ref[...] = chosen
    ext_ref[...] = nt(chosen, raw).astype(BF16)
    extaux_ref[...] = nn(chosen, aux).astype(BF16)

    def edges(sems, downs, ups):
        def copies(pairs, offset):
            return [
                send(src, dst, sems.at[0, number], sems.at[1, number], (me + offset, core))
                for number, src, dst in pairs
            ]

        def start():
            @pl.when(me > 0)
            def _():
                for copy in copies(downs, -1):
                    copy.start()

            @pl.when(me < rows - 1)
            def _():
                for copy in copies(ups, 1):
                    copy.start()

        def finish():
            @pl.when(me > 0)
            def _():
                for copy in copies(downs, -1):
                    copy.wait_send()
                for copy in copies(ups, 1):
                    copy.wait_recv()

            @pl.when(me < rows - 1)
            def _():
                for copy in copies(ups, 1):
                    copy.wait_send()
                for copy in copies(downs, -1):
                    copy.wait_recv()

        return start, finish

    first_rows, last_rows = pl.ds(0, MARGIN), pl.ds(own_rows + MARGIN, MARGIN)
    start_edges, finish_edges = edges(
        edge_sems,
        [
            (0, ext_ref.at[first_rows], above_ref),
            (1, extaux_ref.at[first_rows], aboveaux_ref),
        ],
        [
            (2, ext_ref.at[last_rows], below_ref),
            (3, extaux_ref.at[last_rows], belowaux_ref),
        ],
    )
    start_edges()
    walls[2].start()
    cot_gathers[0].start()

    @pl.when(me == 0)
    def _():
        below_ref[...] = jnp.zeros(below_ref.shape, BF16)
        belowaux_ref[...] = jnp.zeros(belowaux_ref.shape, BF16)

    @pl.when(me == rows - 1)
    def _():
        above_ref[...] = jnp.zeros(above_ref.shape, BF16)
        aboveaux_ref[...] = jnp.zeros(aboveaux_ref.shape, BF16)

    packed_ref[...] = ext_ref[MARGIN : MARGIN + own_rows, :]
    aux_ref[...] = extaux_ref[MARGIN : MARGIN + own_rows, :].astype(F32)
    for copy in locals_early:
        copy.wait()
    finish_edges()
    top = own_rows - MARGIN
    packed_ref[0:MARGIN, :] = packed_ref[0:MARGIN, :] + below_ref[...]
    packed_ref[top:, :] = packed_ref[top:, :] + above_ref[...]
    aux_ref[0:MARGIN, :] = aux_ref[0:MARGIN, :] + belowaux_ref[...].astype(F32)
    aux_ref[top:, :] = aux_ref[top:, :] + aboveaux_ref[...].astype(F32)

    packed = packed_ref[...].astype(F32)
    scale = row_scale(packed)
    first = (packed * scale * g_attn).astype(BF16)
    first_ref[...] = first
    kv_ref[own, :, 0:inner] = nt(first, wqkv_ref[core, 1]).astype(BF16)
    kv_ref[own, :, inner : 2 * inner] = nt(first, wqkv_ref[core, 2]).astype(BF16)

    gate = DELETE_SCALE * sigmoid(gate_logit(packed, scale, gate_weight))
    ids = aux_ref[:, 0:1] + raw_count * aux_ref[:, 1:2]
    ids_i = ids.astype(jnp.int32)
    starts = jnp.zeros_like(ids_i)
    end = jnp.int32(0)
    for number in range(lengths_ref.shape[0]):
        end = end + lengths_ref[number]
        starts = jnp.where(ids_i >= end, end, starts)
    starts = starts.astype(F32)
    own_eye = eye(own_rows)
    facts_ref[own] = jnp.zeros(facts_ref.shape[1:], F32)
    facts_ref[own, 0:1, 0:own_rows] = to_row(gate, own_eye)
    facts_ref[own, 1:2, 0:own_rows] = to_row(ids, own_eye)
    facts_ref[own, 2:3, 0:own_rows] = to_row(starts, own_eye)
    window.start([(facts_ref, facts_sems), (kv_ref, kv_sems)])
    query_ref[own] = nt(first, wqkv_ref[core, 0]).astype(BF16)

    far = (len(offsets) - 3) // 2
    segments = (range(0, far), range(far, 2 * far), range(2 * far, 2 * far + 3))
    def add_near(added_ref, slot, rows_at, gap, extra, allowed, above, below):
        place = 1 + slot
        lanes_at = slice(place * own_rows, (place + 1) * own_rows)
        for head in range(heads):
            if rows_at is not None:
                rest = table_ref[head, 2 * HALF - 1 if above else HALF - 1]
                added_ref[head, :, lanes_at] = jnp.where(allowed, rest + extra, NEGATIVE)
            cut = slice(0, own_rows) if rows_at is None else rows_at
            bias = near_bias(gap[cut], table_ref, head, above, below)
            more = extra if extra.shape[0] == 1 else extra[cut]
            added_ref[head, cut, lanes_at] = jnp.where(allowed[cut], bias + more, NEGATIVE)

    def fact(slot, line):
        at = window.slot[slot]
        return facts_ref[at, line : line + 1, :own_rows]

    border = {-1: slice(0, EDGE), 0: None, 1: slice(own_rows - EDGE, own_rows)}

    def near_queries(slot):
        gap, allowed = fact(slot, 1) - ids, fact(slot, 2) == starts
        add_near(
            biasq_ref, slot, border[slot], gap, fact(slot, 0), allowed, slot >= 0, slot <= 0
        )

    def near_keys(slot):
        gap, allowed = ids - fact(slot, 1), fact(slot, 2) == starts
        add_near(biask_ref, slot, border[slot], gap, gate, allowed, slot <= 0, slot >= 0)

    near_queries(0)
    window.finish([(facts_ref, facts_sems)], (-1, 1))
    near_queries(-1)
    near_queries(1)
    window.finish([(facts_ref, facts_sems)], [d for d in offsets if abs(d) > 1])
    window.finish([(kv_ref, kv_sems)])
    walls[2].relay()
    walls[0].start()
    walls[1].start()
    cot_gathers[1].start()

    def spans(segment):
        return slice(segment[0], segment[-1] + 1)

    def far_added(segment, column):
        allowed = joined_row(facts_ref, segment, 2, own_rows) == starts
        return jnp.where(allowed, column, NEGATIVE)

    added = [
        far_added(segment, joined_row(facts_ref, segment, 0, own_rows)) for segment in segments[:2]
    ]
    fixed = (HALF - 1, 2 * HALF - 1)
    lanes = lax.broadcasted_iota(jnp.int32, lse_ref.shape, 1)
    lse_all = jnp.zeros(lse_ref.shape, F32)
    for head in range(heads):
        cut = slice(head * head_size, (head + 1) * head_size)
        cut_v = slice(inner + head * head_size, inner + (head + 1) * head_size)
        query = query_ref[own, :, cut]
        parts = []
        for number, segment in enumerate(segments):
            keys = kv_ref[spans(segment), :, cut].reshape(-1, head_size)
            if number < 2:
                extra = added[number] + table_ref[head, fixed[number]]
            else:
                extra = biasq_ref[head]
            parts.append(nt(query, keys) + extra)
        most = jnp.max(parts[0], axis=1, keepdims=True)
        for part in parts[1:]:
            most = jnp.maximum(most, jnp.max(part, axis=1, keepdims=True))
        expos = [jnp.exp(part - most) for part in parts]
        total = sum(jnp.sum(expo, axis=1, keepdims=True) for expo in expos)
        lse_all = jnp.where(lanes == head, most + jnp.log(total), lse_all)
        attended = jnp.zeros((own_rows, head_size), F32)
        for segment, expo in zip(segments, expos):
            values = kv_ref[spans(segment), :, cut_v].reshape(-1, head_size)
            attended = attended + nn((expo / total).astype(BF16), values)
        attf_ref[:, cut] = attended
        att_ref[core, :, cut] = attended.astype(BF16)
    lse_ref[...] = lse_all

    att_copy = send(
        att_ref.at[core], att_ref.at[core], pair_sems.at[0, 4], pair_sems.at[1, 4], sibling
    )
    att_copy.start()
    for copy in locals_late:
        copy.wait()
    for copy in pair_early:
        copy.wait()
    att_copy.wait()
    mixed = packed_ref[...].astype(F32) + (nn(att_ref[0], wout_ref[0]) + nn(att_ref[1], wout_ref[1]))
    mixed_ref[...] = mixed
    sec_ref[high] = (mixed * row_scale(mixed) * g_ff).astype(BF16)
    sec_gather.start()

    walls[0].relay()
    for gather in cot_gathers:
        for step in range(1, HI):
            gather.arrived(step)
    walls[1].relay()
    sec_gather.arrived(1)
    sec_gather.arrived(2)
    for number in (2, 0, 1):
        walls[number].finish()
    window.start([(query_ref, query_sems)])

    def sib_copy(kind, step):
        return send(
            sout_ref.at[step],
            sin_ref.at[kind, step],
            sib_sems.at[0, kind, step],
            sib_sems.at[1, kind, step],
            sibling,
        )

    def hi_copy(kind, step):
        return send(
            hout_ref.at[kind, step - 1],
            hin_ref.at[kind, step - 1],
            hi_sems.at[0, kind, step],
            hi_sems.at[1, kind, step],
            high_peer(step),
        )

    def hand_over(kind, step, value):
        part_ref[...] = value
        sout_ref[step] = part_ref[theirs, :].astype(BF16)
        kept_ref[kind if step == 0 else 2 + step % 2] = part_ref[mine, :]
        sib_copy(kind, step).start()

    def pass_on(kind, step):
        sib_copy(kind, step).wait()
        both = kept_ref[2 + step % 2] + sin_ref[kind, step].astype(F32)
        hout_ref[kind, step - 1] = both.astype(BF16)

    def chunk_rows(step):
        return pl.ds(pl.multiple_of(high_other(step) * own_rows, own_rows), own_rows)

    for step in range(HI):
        if step:
            if step == 1:
                for earlier in range(1, HI):
                    for gather in cot_gathers:
                        gather.forwarded(earlier)
            if step == HI - 1:
                sec_gather.arrived(step)
            sec_gather.forwarded(step)
        chunk = high_other(step)
        second = sec_ref[chunk]
        gated = nt(second, wall_ref[0])
        upper = nt(second, wall_ref[1])
        d_middle = nt(cots_ref[chunk], wall_ref[2])
        square = gated * gated
        bend = jnp.tanh(GELU_A * gated * (1.0 + GELU_B * square))
        lift = 0.5 * (1.0 + bend)
        slope = lift + 0.5 * gated * (1.0 - bend * bend) * (
            GELU_A * (1.0 + 3.0 * GELU_B * square)
        )
        gelu = gated * lift
        d_gated = (d_middle * upper * slope).astype(BF16)
        d_upper = (d_middle * gelu).astype(BF16)
        mid_ref[chunk_rows(step), :] = (gelu * upper).astype(BF16)
        dgated_ref[chunk_rows(step), :] = d_gated
        dupper_ref[chunk_rows(step), :] = d_upper
        hand_over(1, step, nn(d_gated, wall_ref[0]) + nn(d_upper, wall_ref[1]))
        if step > 1:
            pass_on(1, step - 1)
            hi_copy(1, step - 1).start()
    pass_on(1, HI - 1)
    hi_copy(1, HI - 1).start()
    for gather in cot_gathers + [sec_gather]:
        gather.close()

    def ff_reduce(number):
        def part(place, begin, count):
            inside = pl.ds(pl.multiple_of(place * share + begin, 16), count)
            return wall_ref.at[number, inside]

        relays = (ffa_ref.at[number], ffb_ref.at[number])
        return LowReduce(part, share, relays, ffin_ref.at[number], ff_sems.at[number])

    reduces = [ff_reduce(number) for number in range(3)]
    hidden = wall_ref.shape[1]

    def weight_grad(number, left_ref, right_ref):
        for begin in range(0, hidden, 256):
            units = slice(begin, min(begin + 256, hidden))
            right = right_ref[...].reshape(HI * own_rows, width)
            wall_ref[number, units, :] = tn(left_ref[:, units], right).astype(BF16)

    weight_grad(0, dgated_ref, sec_ref)
    reduces[0].start()
    weight_grad(1, dupper_ref, sec_ref)
    reduces[1].start()
    sib_copy(1, 0).wait()
    for place, step in enumerate((3, 2, 1, 0)):
        hand_over(0, step, nn(mid_ref[chunk_rows(step), :], wall_ref[2]))
        if place:
            pass_on(0, step + 1)
    weight_grad(2, mid_ref, cots_ref)
    reduces[2].start()

    for slot in (-1, 0, 1):
        near_keys(slot)
    reduces[0].relay()
    reduces[1].relay()
    total = kept_ref[1] + sin_ref[1, 0].astype(F32)
    for step in range(1, HI):
        hi_copy(1, step).wait()
        total = total + hin_ref[1, step - 1].astype(F32)
    dsec_ref[mine, :] = total
    dsec_copy = send(
        dsec_ref.at[mine], dsec_ref.at[mine], half_sems.at[0, 0], half_sems.at[1, 0], sibling
    )
    dsec_copy.start()
    dsec_copy.wait()

    back, g_ff_grad = norm_back(mixed_ref[...], g_ff, dsec_ref[...])
    d_mixed = cots_ref[high].astype(F32) + back
    part_ref[...] = d_mixed
    d_branch = d_mixed.astype(BF16)
    d_att = nt(d_branch, wout_ref[core]).astype(BF16)
    dout_ref[own] = d_att
    facts2_ref[own] = jnp.zeros(facts2_ref.shape[1:], F32)
    deltas = []
    products = d_att.astype(F32) * attf_ref[...]
    for head in range(heads):
        cut = slice(head * head_size, (head + 1) * head_size)
        delta = jnp.sum(products[:, cut], axis=1, keepdims=True)
        deltas.append(delta)
        facts2_ref[own, head : head + 1, 0:own_rows] = to_row(delta, own_eye)
        line = 4 + head
        facts2_ref[own, line : line + 1, 0:own_rows] = to_row(
            lse_ref[:, head : head + 1], own_eye
        )
    window.start([(facts2_ref, facts2_sems), (dout_ref, dout_sems)])
    hi_copy(0, 1).start()
    hi_copy(0, 3).start()
    reduces[2].relay()

    piece = zout_ref.shape[2]
    pieces = lows // 2
    lanes_all = zout_ref.shape[3]
    quarter = lanes_all // HI

    def keep_pieces(group, number, value):
        for part in range(pieces):
            block = value[part * piece : (part + 1) * piece, :]
            zout_ref[group, number * pieces + part, :, 0:width] = block.astype(BF16)

    def quarter_of(place):
        return pl.ds(pl.multiple_of(place * quarter, 128), quarter)

    def low_sum(group):
        def part(place, begin, count):
            return zout_ref.at[group, place, pl.ds(begin, count)]

        relays = (za_ref.at[group], zb_ref.at[group])
        return LowReduce(part, piece, relays, zin_ref.at[group], low_sems.at[group])

    lows_sum = [low_sum(group) for group in range(2)]

    def high_copy(group, step, place):
        return send(
            zout_ref.at[group, low, :, quarter_of(high_other(step))],
            yin_ref.at[group, place],
            high_sems.at[0, group, step],
            high_sems.at[1, group, step],
            high_peer(step),
        )

    def share_low(group):
        lows_sum[group].finish()
        total = zout_ref[group, low].astype(F32)
        for number in arrived:
            total = total + zin_ref[group, number].astype(F32)
        zout_ref[group, low] = total.astype(BF16)
        for step in range(1, HI):
            high_copy(group, step, high).start()

    def back_copy(group, step, place):
        lanes_at = (group, slice(None), quarter_of(place))
        return send(
            fin_ref.at[lanes_at],
            fin_ref.at[lanes_at],
            back_sems.at[0, group, step],
            back_sems.at[1, group, step],
            high_peer(step),
        )

    def share_high(group):
        for step in range(1, HI):
            high_copy(group, step, high).wait_send()
            high_copy(group, step, high_other(step)).wait_recv()
        yin_ref[group, high] = zout_ref[group, low, :, quarter_of(high)]
        total = yin_ref[group, 0].astype(F32)
        for number in range(1, HI):
            total = total + yin_ref[group, number].astype(F32)
        fin_ref[group, :, quarter_of(high)] = total.astype(BF16)
        for step in range(1, HI):
            back_copy(group, step, high).start()

    def last_gather(group):
        def block(place, begin, count):
            return attg_ref.at[group, place, pl.ds(begin, count)]

        return LowGather(fin_ref.at[group], block, piece, last_sems.at[group])

    lasts = [last_gather(group) for group in range(2)]
    own_lasts = [
        pltpu.make_async_copy(
            fin_ref.at[group], attg_ref.at[group, low], local_sems.at[1 + group]
        )
        for group in range(2)
    ]

    def spread_low(group):
        for step in range(1, HI):
            back_copy(group, step, high).wait_send()
            back_copy(group, step, high_other(step)).wait_recv()
        lasts[group].start()
        own_lasts[group].start()

    if lanes_all > width:
        zout_ref[:, :, :, width:] = jnp.zeros(zout_ref.shape[:3] + (lanes_all - width,), BF16)
    keep_pieces(0, 0, tn(att_ref[core], d_branch))

    lane = lax.broadcasted_iota(jnp.int32, (1, width), 1)
    bias_grad = jnp.zeros((1, width), F32)

    def add_bias(bias_grad, head, bucket, value):
        return bias_grad + jnp.where(lane == head * 2 * HALF + bucket, value, 0.0)

    def total_of(value):
        return jnp.sum(jnp.sum(value, axis=0, keepdims=True), axis=1, keepdims=True)

    for head in range(heads):
        cut = slice(head * head_size, (head + 1) * head_size)
        cut_v = slice(inner + head * head_size, inner + (head + 1) * head_size)
        query, d_head = query_ref[own, :, cut], dout_ref[own, :, cut]
        lse = lse_ref[:, head : head + 1]
        d_query = jnp.zeros((own_rows, head_size), F32)
        for number, segment in enumerate(segments):
            keys = kv_ref[spans(segment), :, cut].reshape(-1, head_size)
            values = kv_ref[spans(segment), :, cut_v].reshape(-1, head_size)
            if number < 2:
                extra = added[number] + table_ref[head, fixed[number]]
            else:
                extra = biasq_ref[head]
            probs = jnp.exp(nt(query, keys) + extra - lse)
            d_scores = probs * (nt(d_head, values) - deltas[head])
            d_query = d_query + nn(d_scores.astype(BF16), keys)
            if number < 2:
                bias_grad = add_bias(bias_grad, head, fixed[number], total_of(d_scores))
                continue
            for slot in (-1, 0, 1):
                lanes_at = slice((1 + slot) * own_rows, (2 + slot) * own_rows)
                block = d_scores[:, lanes_at]
                gap = fact(slot, 1) - ids
                whole = total_of(block)
                rows_at = border[slot]
                if rows_at is not None:
                    block, gap = block[rows_at], gap[rows_at]
                for sign in (1, -1):
                    if sign * slot < 0:
                        continue
                    base = HALF if sign > 0 else 0
                    sums = [
                        total_of(jnp.where(sign * gap >= limit, block, 0.0)) for limit in LIMITS
                    ]
                    if slot:
                        sums = [whole] + [value + (whole - total_of(block)) for value in sums[1:]]
                    whole = whole - sums[0]
                    for place in range(len(LIMITS)):
                        value = sums[place]
                        if place + 1 < len(LIMITS):
                            value = value - sums[place + 1]
                        bias_grad = add_bias(bias_grad, head, base + place + 1, value)
                if not slot:
                    bias_grad = add_bias(bias_grad, head, 0, whole)
        heads_ref[core, 0, :, cut] = d_query.astype(BF16)

    keep_pieces(0, 1, tn(heads_ref[core, 0], first_ref[...]))
    lows_sum[0].start()

    window.finish([(query_ref, query_sems), (facts2_ref, facts2_sems), (dout_ref, dout_sems)])
    lows_sum[0].relay()
    d_gate = jnp.zeros((own_rows, 1), F32)
    added = [far_added(segment, gate) for segment in segments[:2]]
    fixed = (2 * HALF - 1, HALF - 1)
    for head in range(heads):
        cut = slice(head * head_size, (head + 1) * head_size)
        cut_v = slice(inner + head * head_size, inner + (head + 1) * head_size)
        key, value = kv_ref[own, :, cut], kv_ref[own, :, cut_v]
        d_key = jnp.zeros((own_rows, head_size), F32)
        d_value = jnp.zeros((own_rows, head_size), F32)
        for number, segment in enumerate(segments):
            queries = query_ref[spans(segment), :, cut].reshape(-1, head_size)
            d_heads = dout_ref[spans(segment), :, cut].reshape(-1, head_size)
            if number < 2:
                extra = added[number] + table_ref[head, fixed[number]]
            else:
                extra = biask_ref[head]
            lse = joined_row(facts2_ref, segment, 4 + head, own_rows)
            delta = joined_row(facts2_ref, segment, head, own_rows)
            probs = jnp.exp(nt(key, queries) + extra - lse)
            d_scores = probs * (nt(value, d_heads) - delta)
            d_value = d_value + nn(probs.astype(BF16), d_heads)
            d_key = d_key + nn(d_scores.astype(BF16), queries)
            d_gate = d_gate + jnp.sum(d_scores, axis=1, keepdims=True)
        heads_ref[core, 1, :, cut] = d_key.astype(BF16)
        heads_ref[core, 2, :, cut] = d_value.astype(BF16)
    dgate_ref[core] = jnp.broadcast_to(d_gate, dgate_ref.shape[1:])
    pair_late = [
        send(ref.at[core], ref.at[core], pair_sems.at[0, 5 + i], pair_sems.at[1, 5 + i], sibling)
        for i, ref in enumerate((heads_ref, dgate_ref))
    ]
    for copy in pair_late:
        copy.start()
    for number in range(2):
        keep_pieces(1, number, tn(heads_ref[core, 1 + number], first_ref[...]))
    lows_sum[1].start()
    share_low(0)

    for copy in pair_late:
        copy.wait()
    d_first = jnp.zeros((own_rows, width), F32)
    for side in range(2):
        for number in range(3):
            d_first = d_first + nn(heads_ref[side, number], wqkv_ref[side, number])
    back, g_attn_grad = norm_back(packed_ref[...].astype(F32), g_attn, d_first)
    inside = slice(MARGIN, MARGIN + own_rows)
    back_ref[inside, :] = (part_ref[...] + back).astype(BF16)
    d_gate = dgate_ref[0] + dgate_ref[1]
    lane_g = lax.broadcasted_iota(jnp.int32, d_gate.shape, 1)
    terms = jnp.zeros(d_gate.shape, F32)
    for number, term in enumerate(split3(d_gate)):
        terms = jnp.where(lane_g == number, term, terms)
    backaux_ref[inside, :] = terms.astype(BF16)
    down_src, down_dst = pl.ds(MARGIN, MARGIN), pl.ds(own_rows + MARGIN, MARGIN)
    up_src, up_dst = pl.ds(own_rows, MARGIN), pl.ds(0, MARGIN)
    start_edges, finish_edges = edges(
        edge2_sems,
        [
            (0, back_ref.at[down_src], back_ref.at[down_dst]),
            (1, backaux_ref.at[down_src], backaux_ref.at[down_dst]),
        ],
        [
            (2, back_ref.at[up_src], back_ref.at[up_dst]),
            (3, backaux_ref.at[up_src], backaux_ref.at[up_dst]),
        ],
    )
    start_edges()

    @pl.when(me == 0)
    def _():
        back_ref[up_dst, :] = jnp.zeros((MARGIN, width), BF16)
        backaux_ref[up_dst, :] = jnp.zeros((MARGIN, 128), BF16)

    @pl.when(me == rows - 1)
    def _():
        back_ref[down_dst, :] = jnp.zeros((MARGIN, width), BF16)
        backaux_ref[down_dst, :] = jnp.zeros((MARGIN, 128), BF16)

    gate_s = sigmoid(raw_logit)
    gate_slope = DELETE_SCALE * gate_s * (1.0 - gate_s)
    raw_scaled = gcot_ref[...] * gate_slope * raw_scale
    common = jnp.sum(
        nt(stacked_rows(split3(raw_scaled), raw_count), byte_ref[...]), axis=0, keepdims=True
    )
    packed = packed_ref[...].astype(F32)
    scale = row_scale(packed)
    own_s = sigmoid(gate_logit(packed, scale, gate_weight))
    own_scaled = d_gate[:, 0:1] * (DELETE_SCALE * own_s * (1.0 - own_s)) * scale
    common = common + jnp.sum(own_scaled * packed, axis=0, keepdims=True)
    slow_ref[low, 0:1, :] = g_ff_grad
    slow_ref[low, 1:2, :] = g_attn_grad
    slow_ref[low, 2:3, :] = common * g_delete
    slow_ref[low, 3:4, :] = common * w_delete
    slow_ref[low, 4:5, :] = bias_grad
    slow_ref[low, 5:8, :] = jnp.zeros((3, width), F32)

    def slow_copy(step, source):
        return send(
            slow_ref.at[source],
            slow_ref.at[source],
            slow_sems.at[0, step],
            slow_sems.at[1, step],
            low_peer(step),
        )

    def start_slow(step, carry):
        slow_copy(step, low).start()
        return carry

    def finish_slow(step, carry):
        slow_copy(step, low).wait_send()
        slow_copy(step, low_source(step)).wait_recv()
        return carry

    def shigh_copy(step, source):
        return send(
            shigh_ref.at[source],
            shigh_ref.at[source],
            shigh_sems.at[0, step],
            shigh_sems.at[1, step],
            high_peer(step),
        )

    lax.fori_loop(1, lows, start_slow, 0)
    lows_sum[1].relay()
    share_high(0)
    share_low(1)
    spread_low(0)
    lax.fori_loop(1, lows, finish_slow, 0)
    small = slow_ref[0]
    for number in range(1, lows):
        small = small + slow_ref[number]
    shigh_ref[high] = small
    for step in range(1, HI):
        shigh_copy(step, high).start()
    share_high(1)
    hi_copy(0, 2).start()
    lasts[0].relay()
    spread_low(1)

    finish_edges()
    spread = tn(backaux_ref[...], chosen_ref[...])
    raw_cot = gcot_ref[...] + (spread[0:1, :] + spread[1:2, :] + spread[2:3, :])
    d_logit = raw_cot * gate_slope
    scaled = d_logit * raw_scale
    along = d_logit * raw_logit * raw_scale * raw_scale * (1.0 / width)
    s1, s2, s3 = split3(scaled)
    w1, w2, w3 = split3(gate_weight)
    outer = tn(
        stacked_rows((w1, w1, w2, w2, w1, w3), width),
        stacked_rows((s1, s2, s1, s2, s3, s1), raw_count),
    )
    rows_ref[...] = outer - along * byte_ref[...].astype(F32)
    rows_ref[...] = rows_ref[...] + tn(back_ref[...], chosen_ref[...])
    for step in range(1, HI):
        shigh_copy(step, high).wait_send()
        shigh_copy(step, high_other(step)).wait_recv()
    small = shigh_ref[0]
    for number in range(1, HI):
        small = small + shigh_ref[number]
    small_ref[...] = small

    sib_copy(0, 0).wait()
    total = mixed_ref[mine, :] + (kept_ref[0] + sin_ref[0, 0].astype(F32))
    for step in range(1, HI):
        hi_copy(0, step).wait()
        total = total + hin_ref[0, step - 1].astype(F32)
    block_ref[mine, :] = total.astype(BF16)
    block_copy = send(
        block_ref.at[mine], block_ref.at[mine], half_sems.at[0, 1], half_sems.at[1, 1], sibling
    )
    block_copy.start()

    def finish_reduce(number):
        reduces[number].finish()
        total = wall_ref[number, my_share, :].astype(F32)
        for begin in range(0, len(arrived), HI):
            loads = [
                pltpu.make_async_copy(
                    ffin_ref.at[number, slot],
                    sec_ref.at[place, pl.ds(0, share)],
                    local_sems.at[3 + place],
                )
                for place, slot in enumerate(arrived[begin : begin + HI])
            ]
            for load in loads:
                load.start()
            for load in loads:
                load.wait()
            for place in range(len(loads)):
                total = total + sec_ref[place, 0:share, :].astype(F32)
        ffo_ref[number] = total

    finish_reduce(0)
    finish_reduce(1)
    lasts[1].relay()
    finish_reduce(2)
    block_copy.wait()
    for group in range(2):
        lasts[group].finish()
        own_lasts[group].wait()


def layer(rows, offsets, *operands):
    lengths, table, byte_t, keep, vecs, gcot, wq, wk, wv, wo, wg, wu, wd, cot = operands
    width, raw_count = byte_t.shape
    own_rows = cot.shape[0]
    inner = wq.shape[0]
    heads = table.shape[0]
    share = wd.shape[0]
    lows = rows // HI
    hidden = lows * share
    slots = len(offsets)
    half = own_rows // 2
    piece = 2 * inner // lows
    lanes = -(-width // (128 * HI)) * 128 * HI
    slots_in = 2 if lows == 4 else lows
    ff_cut, z_cut = share // 2 // 16 * 16, piece // 2 // 16 * 16
    ext_rows = own_rows + 2 * MARGIN
    vmem = pl.BlockSpec(memory_space=pltpu.VMEM)
    smem = pl.BlockSpec(memory_space=pltpu.SMEM)
    anywhere = pl.BlockSpec(memory_space=pl.ANY)
    shape = jax.ShapeDtypeStruct
    dma = pltpu.SemaphoreType.DMA
    outs = [
        shape((1, raw_count), F32),
        shape((own_rows, width), BF16),
        shape((width, raw_count), F32),
        shape((8, width), F32),
        shape((3, share, width), F32),
        shape((2, lows, piece, lanes), BF16),
        shape((3, slots_in, share, width), BF16),
    ]
    out_specs = [vmem] * 5 + [anywhere] * 2
    scratch = [
        pltpu.VMEM((rows, 8, 128), F32),
        pltpu.VMEM((ext_rows, raw_count), BF16),
        pltpu.VMEM((ext_rows, width), BF16),
        pltpu.VMEM((ext_rows, 128), BF16),
        pltpu.VMEM((MARGIN, width), BF16),
        pltpu.VMEM((MARGIN, width), BF16),
        pltpu.VMEM((MARGIN, 128), BF16),
        pltpu.VMEM((MARGIN, 128), BF16),
        pltpu.VMEM((own_rows, width), BF16),
        pltpu.VMEM((own_rows, 128), F32),
        pltpu.VMEM((own_rows, width), BF16),
        pltpu.VMEM((slots, own_rows, 2 * inner), BF16),
        pltpu.VMEM((slots, own_rows, inner), BF16),
        pltpu.VMEM((slots, 8, 256), F32),
        pltpu.VMEM((slots, own_rows, inner), BF16),
        pltpu.VMEM((slots, 8, 256), F32),
        pltpu.VMEM((heads, own_rows, 3 * own_rows), F32),
        pltpu.VMEM((heads, own_rows, 3 * own_rows), F32),
        pltpu.VMEM((2, own_rows, inner), BF16),
        pltpu.VMEM((own_rows, inner), F32),
        pltpu.VMEM((own_rows, 128), F32),
        pltpu.VMEM((own_rows, width), F32),
        pltpu.VMEM((HI, own_rows, width), BF16),
        pltpu.VMEM((HI, own_rows, width), BF16),
        pltpu.VMEM((3, hidden, width), BF16),
        pltpu.VMEM((2, inner, width), BF16),
        pltpu.VMEM((2, 3, inner, width), BF16),
        pltpu.VMEM((HI * own_rows, hidden), BF16),
        pltpu.VMEM((HI * own_rows, hidden), BF16),
        pltpu.VMEM((HI * own_rows, hidden), BF16),
        pltpu.VMEM((own_rows, width), F32),
        pltpu.VMEM((4, half, width), F32),
        pltpu.VMEM((HI, half, width), BF16),
        pltpu.VMEM((2, HI, half, width), BF16),
        pltpu.VMEM((2, HI - 1, half, width), BF16),
        pltpu.VMEM((2, HI - 1, half, width), BF16),
        pltpu.VMEM((own_rows, width), F32),
        pltpu.VMEM((2, 3, own_rows, inner), BF16),
        pltpu.VMEM((2, own_rows, 128), F32),
        pltpu.VMEM((2, lows, piece, lanes), BF16),
        pltpu.VMEM((2, slots_in, piece, lanes), BF16),
        pltpu.VMEM((2, HI, piece, lanes // HI), BF16),
        pltpu.VMEM((2, piece, lanes), BF16),
        pltpu.VMEM((lows, 8, width), F32),
        pltpu.VMEM((HI, 8, width), F32),
        pltpu.VMEM((ext_rows, width), BF16),
        pltpu.VMEM((ext_rows, 128), BF16),
        pltpu.VMEM((3, max(ff_cut, 16), width), BF16),
        pltpu.VMEM((3, share - ff_cut, width), BF16),
        pltpu.VMEM((2, max(z_cut, 16), lanes), BF16),
        pltpu.VMEM((2, piece - z_cut, lanes), BF16),
        dma((2, rows)),
        dma((2, 4)),
        dma((2, slots)),
        dma((2, slots)),
        dma((2, slots)),
        dma((2, slots)),
        dma((2, slots)),
        dma((3, 2, max(5, lows))),
        dma((2, 7)),
        dma((8,)),
        dma((2, 2, HI)),
        dma((2, 2, HI)),
        dma((2, HI)),
        dma((2, HI)),
        dma((2, 2, HI)),
        dma((2, 2, HI)),
        dma((2, 2)),
        dma((3, 2, max(5, lows))),
        dma((2, 2, max(5, lows))),
        dma((2, 2, HI)),
        dma((2, 2, HI)),
        dma((2, 2, max(5, lows))),
        dma((2, 4)),
        dma((2, lows)),
        dma((2, HI)),
    ]
    return pl.pallas_call(
        functools.partial(layer_kernel, rows, offsets),
        name="layer",
        out_shape=outs,
        in_specs=[smem, smem] + [vmem] * 4 + [anywhere] * 8,
        out_specs=out_specs,
        scratch_shapes=scratch,
        compiler_params=pltpu.CompilerParams(
            collective_id=0, has_side_effects=True, vmem_limit_bytes=VMEM_LIMIT
        ),
    )(*operands)


def per_device(
    byte_rows,
    lengths,
    keep_mask,
    w_delete,
    g_delete,
    g_attn,
    w_query,
    w_key,
    w_value,
    w_out,
    rel_bias,
    g_ff,
    w_gate,
    w_up,
    w_down,
    out_cot,
    gate_cot,
):
    raw_count, width = byte_rows.shape
    own_rows = out_cot.shape[0]
    inner = w_query.shape[1]
    buckets, heads = rel_bias.shape
    rows = lax.axis_size("rows")
    share = w_down.shape[0]
    offsets = slots_of(reach_of(raw_count, own_rows))
    line = lax.broadcasted_iota(jnp.int32, (8, width), 0)
    vecs = jnp.zeros((8, width), F32)
    for number, vector in enumerate((g_delete, w_delete, g_attn, g_ff)):
        vecs = jnp.where(line == number, vector[None, :], vecs)
    spare = -share % 16
    weights = [jnp.pad(w, ((0, spare), (0, 0))) for w in (w_gate.T, w_up.T, w_down)]
    gate, block_out, grad_rows, small, ff_sums, att_grads, _ = layer(
        rows,
        offsets,
        lengths,
        rel_bias.T,
        byte_rows.T,
        keep_mask.reshape(1, -1),
        vecs,
        gate_cot.reshape(1, -1),
        w_query.T,
        w_key.T,
        w_value.T,
        w_out,
        *weights,
        out_cot,
    )
    att_grads = att_grads.reshape(4, inner, -1)[:, :, :width].astype(F32)
    ff_sums = ff_sums[:, :share]
    grad_bias = small[4, : heads * buckets].reshape(heads, buckets).T
    return (
        block_out,
        gate[0],
        grad_rows.T,
        small[2],
        small[3],
        small[1],
        att_grads[1].T,
        att_grads[2].T,
        att_grads[3].T,
        att_grads[0],
        grad_bias,
        small[0],
        ff_sums[0].T,
        ff_sums[1].T,
        ff_sums[2],
    )


def solution(mesh):
    in_specs = (
        P("rows", None),
        P(),
        P("rows"),
        P(),
        P(),
        P(),
        P(None, "tensor"),
        P(None, "tensor"),
        P(None, "tensor"),
        P("tensor", None),
        P(None, "tensor"),
        P(),
        P(None, ("rows", "tensor")),
        P(None, ("rows", "tensor")),
        P(("rows", "tensor"), None),
        P("rows", None),
        P("rows"),
    )
    out_specs = (
        P("rows", None),
        P("rows"),
        P("rows", None),
        P(),
        P(),
        P(),
        P(None, "tensor"),
        P(None, "tensor"),
        P(None, "tensor"),
        P("tensor", None),
        P(None, "tensor"),
        P(),
        P(None, ("rows", "tensor")),
        P(None, ("rows", "tensor")),
        P(("rows", "tensor"), None),
    )
    return jax.shard_map(
        per_device, mesh=mesh, in_specs=in_specs, out_specs=out_specs, check_vma=False
    )
```

```python
import functools

import jax
import jax.numpy as jnp
from jax import lax
from jax.experimental import pallas as pl
from jax.experimental.pallas import tpu as pltpu
from jax.sharding import PartitionSpec as P

MAXLEN = 1024
MARGIN = 32
EPS = 1e-06
DELETE_SCALE = -30.0
NEGATIVE = -1e30
LIMITS = (1, 2, 3, 4, 5, 6, 7, 8, 12, 16, 23, 32, 46, 64, 91)
HALF = 16
HI = 4
MESH = pl.DeviceIdType.MESH
F32 = jnp.float32
BF16 = jnp.bfloat16
VMEM_LIMIT = 63 * 1024 * 1024


def nn(a, b):
    return lax.dot_general(a, b, (((1,), (0,)), ((), ())), preferred_element_type=F32)


def nt(a, b):
    return lax.dot_general(a, b, (((1,), (1,)), ((), ())), preferred_element_type=F32)


def tn(a, b):
    return lax.dot_general(a, b, (((0,), (0,)), ((), ())), preferred_element_type=F32)


def eye(count):
    return lax.broadcasted_iota(jnp.int32, (count, count), 0) == lax.broadcasted_iota(
        jnp.int32, (count, count), 1
    )


def to_row(column, diagonal):
    return jnp.sum(jnp.where(diagonal, column, 0.0), axis=0, keepdims=True)


def to_column(row, diagonal):
    return jnp.sum(jnp.where(diagonal, row, 0.0), axis=1, keepdims=True)


def row_scale(values):
    return lax.rsqrt(jnp.mean(values * values, axis=-1, keepdims=True) + EPS)


def gate_logit(values, scale, weight):
    return scale * jnp.sum(values * weight, axis=-1, keepdims=True)


def sigmoid(value):
    return 1.0 / (1.0 + jnp.exp(-value))


def norm_back(values, gain, grad):
    scale = row_scale(values)
    scaled = grad * gain
    inner = jnp.mean(scaled * values, axis=-1, keepdims=True)
    back = scale * scaled - values * (scale * scale * scale * inner)
    return back, jnp.sum(grad * values * scale, axis=0, keepdims=True)


def reach_of(raw_count, own_rows):
    span = (MAXLEN // raw_count - 1) * own_rows + 2 * MARGIN + raw_count
    return -(-(span - 1) // own_rows)


def slots_of(reach):
    far = list(range(2, reach + 1))
    return [-d for d in reversed(far)] + far + [-1, 0, 1]


def meet_rows(rows):
    me, core = lax.axis_index("rows"), lax.axis_index("tensor")
    barrier = pltpu.get_barrier_semaphore()

    def greet(step, carry):
        pl.semaphore_signal(
            barrier, inc=1, device_id=(lax.rem(me + step, rows), core), device_id_type=MESH
        )
        return carry

    lax.fori_loop(1, rows, greet, 0)
    pl.semaphore_signal(barrier, inc=1, device_id=(me, 1 - core), device_id_type=MESH)
    pl.semaphore_wait(barrier, rows)


def send(src, dst, send_sem, recv_sem, target):
    return pltpu.make_async_remote_copy(
        src_ref=src,
        dst_ref=dst,
        send_sem=send_sem,
        recv_sem=recv_sem,
        device_id=target,
        device_id_type=MESH,
    )


class Window:
    def __init__(self, rows, offsets):
        self.rows, self.offsets = rows, offsets
        self.me, self.core = lax.axis_index("rows"), lax.axis_index("tensor")
        self.slot = {offset: number for number, offset in enumerate(offsets)}
        self.own = self.slot[0]
        self.lows = rows // HI
        self.planes = self.lows == 4
        self.low = lax.rem(self.me, self.lows)
        self.passes = []
        if self.planes:
            for side in (self.lows, -self.lows):
                for step in range(1 - self.lows, self.lows):
                    if step and side - step in self.slot:
                        self.passes.append((side, step))

    def inside(self, offset):
        if offset < 0:
            return self.me >= -offset
        return self.me < self.rows - offset

    def in_plane(self, step):
        place = self.low + step
        return jnp.logical_and(place >= 0, place < self.lows)

    def direct(self, offset):
        if not self.planes or abs(offset) == self.lows:
            return self.inside(offset)
        place = self.low + offset
        beyond = jnp.logical_or(place >= 2 * self.lows, place < -self.lows)
        return jnp.logical_and(self.inside(offset), jnp.logical_or(self.in_plane(offset), beyond))

    def copy(self, ref, sems, offset):
        there = self.slot[-offset]
        return send(
            ref.at[self.own],
            ref.at[there],
            sems.at[0, self.slot[offset]],
            sems.at[1, there],
            (self.me + offset, self.core),
        )

    def arrival(self, ref, sems, offset):
        place = ref.at[self.slot[offset]]
        return send(
            place,
            place,
            sems.at[0, self.slot[offset]],
            sems.at[1, self.slot[offset]],
            (self.me + offset, self.core),
        )

    def passed(self, ref, sems, number):
        side, step = self.passes[number]
        there = self.slot[side - step]
        return send(
            ref.at[self.slot[side]],
            ref.at[there],
            sems.at[0, len(self.offsets) + number],
            sems.at[1, there],
            (self.me + step, self.core),
        )

    def start(self, pairs):
        far_first = sorted(self.offsets, key=lambda d: (abs(d) != self.lows, -abs(d)))
        for offset in far_first:
            if offset:

                @pl.when(self.direct(offset))
                def _():
                    for ref, sems in pairs:
                        self.copy(ref, sems, offset).start()

    def relay(self, pairs):
        for side in (self.lows, -self.lows):
            numbers = [n for n, (beside, _) in enumerate(self.passes) if beside == side]
            if not numbers:
                continue

            @pl.when(self.inside(side))
            def _():
                for ref, sems in pairs:
                    self.arrival(ref, sems, side).wait_recv()
                    for number in numbers:

                        @pl.when(self.in_plane(self.passes[number][1]))
                        def _():
                            self.passed(ref, sems, number).start()

    def finish(self, pairs, offsets=None):
        for offset in self.offsets if offsets is None else offsets:
            if offset:

                @pl.when(self.direct(offset))
                def _():
                    for ref, sems in pairs:
                        self.copy(ref, sems, offset).wait_send()

                if self.planes and abs(offset) == self.lows:
                    continue

                @pl.when(self.inside(offset))
                def _():
                    for ref, sems in pairs:
                        self.arrival(ref, sems, offset).wait_recv()

    def close(self, pairs):
        for number, (side, step) in enumerate(self.passes):

            @pl.when(jnp.logical_and(self.inside(side), self.in_plane(step)))
            def _():
                for ref, sems in pairs:
                    self.passed(ref, sems, number).wait_send()

    def clear(self, ref, value):
        for offset in self.offsets:
            if offset:

                @pl.when(jnp.logical_not(self.inside(offset)))
                def _():
                    ref[self.slot[offset]] = jnp.full(ref.shape[1:], value, ref.dtype)


EDGE = -(-LIMITS[-1] // 16) * 16


def near_bias(gap, table_ref, head, above, below):
    if above and below:
        bias = jnp.full(gap.shape, table_ref[head, 0], F32)
    else:
        bias = jnp.full(gap.shape, table_ref[head, HALF if above else 0], F32)
    for number, limit in enumerate(LIMITS):
        if above:
            bias = jnp.where(gap >= limit, table_ref[head, HALF + number + 1], bias)
        if below:
            bias = jnp.where(gap <= -limit, table_ref[head, number + 1], bias)
    return bias


def joined_row(facts_ref, slots, line, width):
    return jnp.concatenate([facts_ref[slot, line : line + 1, :width] for slot in slots], axis=1)


GELU_A = 0.7978845608028654
GELU_B = 0.044715


def split3(value):
    one = value.astype(BF16).astype(F32)
    rest = value - one
    two = rest.astype(BF16).astype(F32)
    return one, two, (rest - two).astype(BF16).astype(F32)


def stacked_rows(rows, width):
    line = lax.broadcasted_iota(jnp.int32, (8, width), 0)
    result = jnp.zeros((8, width), F32)
    for number, row in enumerate(rows):
        result = jnp.where(line == number, row, result)
    return result.astype(BF16)


def layer_kernel(
    rows,
    offsets,
    lengths_ref,
    table_ref,
    byte_ref,
    keep_ref,
    vec_ref,
    gcot_ref,
    wq_ref,
    wk_ref,
    wv_ref,
    wo_ref,
    wg_ref,
    wu_ref,
    wd_ref,
    cot_ref,
    gate_ref,
    block_ref,
    rows_ref,
    small_ref,
    ffo_ref,
    attg_ref,
    ffin_ref,
    count_ref,
    chosen_ref,
    ext_ref,
    extaux_ref,
    below_ref,
    above_ref,
    belowaux_ref,
    aboveaux_ref,
    packed_ref,
    aux_ref,
    first_ref,
    kv_ref,
    query_ref,
    facts_ref,
    dout_ref,
    facts2_ref,
    biasq_ref,
    biask_ref,
    att_ref,
    attf_ref,
    lse_ref,
    mixed_ref,
    sec_ref,
    cots_ref,
    wall_ref,
    wout_ref,
    wqkv_ref,
    mid_ref,
    dgated_ref,
    dupper_ref,
    part_ref,
    kept_ref,
    sout_ref,
    sin_ref,
    hout_ref,
    hin_ref,
    dsec_ref,
    heads_ref,
    dgate_ref,
    zout_ref,
    zin_ref,
    yin_ref,
    fin_ref,
    slow_ref,
    shigh_ref,
    back_ref,
    backaux_ref,
    ffa_ref,
    ffb_ref,
    za_ref,
    zb_ref,
    count_sems,
    edge_sems,
    kv_sems,
    query_sems,
    facts_sems,
    dout_sems,
    facts2_sems,
    wall_sems,
    pair_sems,
    local_sems,
    cot_sems,
    cotf_sems,
    sec_sems,
    secf_sems,
    sib_sems,
    hi_sems,
    half_sems,
    ff_sems,
    low_sems,
    high_sems,
    back_sems,
    last_sems,
    edge2_sems,
    slow_sems,
    shigh_sems,
):
    width, raw_count = byte_ref.shape
    own_rows = cot_ref.shape[0]
    inner = wq_ref.shape[0]
    heads = table_ref.shape[0]
    head_size = inner // heads
    share = wd_ref.shape[0]
    lows = rows // HI
    half = own_rows // 2
    ext_rows = own_rows + 2 * MARGIN
    me, core = lax.axis_index("rows"), lax.axis_index("tensor")
    high, low = lax.div(me, lows), lax.rem(me, lows)
    sibling = (me, 1 - core)
    mine = pl.ds(pl.multiple_of(core * half, half), half)
    theirs = pl.ds(pl.multiple_of((1 - core) * half, half), half)
    window = Window(rows, offsets)
    own = window.own
    g_delete, w_delete = vec_ref[0:1, :], vec_ref[1:2, :]
    g_attn, g_ff = vec_ref[2:3, :], vec_ref[3:4, :]

    is_square = lows == 4

    def low_other(step):
        if step == 1:
            return low + 1 - 2 * lax.rem(low, 2)
        if step == 2:
            return lax.rem(low + 2, lows)
        return lows - 1 - low

    def low_pair(step):
        return (high * lows + low_other(step), core)

    def low_peer(step):
        return (high * lows + lax.rem(low + step, lows), core)

    def low_source(step):
        return lax.rem(low + lows - step, lows)

    def high_other(step):
        if step == 0:
            return high
        if step == 1:
            return high + 1 - 2 * lax.rem(high, 2)
        if step == 2:
            return lax.rem(high + 2, HI)
        return HI - 1 - high

    def high_peer(step):
        return (high_other(step) * lows + low, core)

    middle_high = jnp.logical_and(high >= 1, high <= 2)

    def first_half(count):
        return count // 2 // 16 * 16

    class LowGather:
        def __init__(self, source, block, count, sems):
            self.source, self.block, self.count, self.sems = source, block, count, sems
            cut = first_half(count)
            self.halves = ((0, cut), (cut, count - cut))

        def copy(self, src, dst, number, target):
            return send(src, dst, self.sems.at[0, number], self.sems.at[1, number], target)

        def direct(self, step):
            if is_square:
                target = low_pair(step)
            else:
                target = low_peer(step)
            return self.copy(self.source, self.block(low, 0, self.count), step, target)

        def arrival(self, step):
            place = self.block(low_other(step) if is_square else low_source(step), 0, self.count)
            return self.copy(place, place, step, sibling)

        def passed(self, side):
            place = self.block(low_other(2 - side), *self.halves[side])
            return self.copy(place, place, 3 + side, low_pair(1 + side))

        def start(self):
            if is_square:
                self.direct(1).start()
                self.direct(2).start()
                return

            def one(step, carry):
                self.direct(step).start()
                return carry

            lax.fori_loop(1, lows, one, 0)

        def relay(self):
            if is_square:
                for side in (1, 0):
                    self.arrival(2 - side).wait_recv()
                    self.passed(side).start()

        def finish(self):
            if is_square:
                for step in (1, 2):
                    self.direct(step).wait_send()
                for side in range(2):
                    self.passed(side).wait_send()
                    place = self.block(low_other(3), *self.halves[side])
                    self.copy(place, place, 3 + side, sibling).wait_recv()
                return

            def one(step, carry):
                self.direct(step).wait_send()
                self.arrival(step).wait_recv()
                return carry

            lax.fori_loop(1, lows, one, 0)

    class LowReduce:
        def __init__(self, part, count, relays, arrivals, sems):
            self.part, self.count, self.sems = part, count, sems
            self.relays, self.arrivals = relays, arrivals
            cut = first_half(count)
            self.halves = ((0, cut), (cut, count - cut))

        def copy(self, src, dst, number, target):
            return send(src, dst, self.sems.at[0, number], self.sems.at[1, number], target)

        def half(self, side):
            return self.copy(
                self.part(low_other(3), *self.halves[side]),
                self.relays[side],
                side,
                low_pair(2 - side),
            )

        def summed(self, side):
            return self.copy(
                self.part(low_other(1 + side), 0, self.count),
                self.arrivals.at[side],
                2 + side,
                low_pair(1 + side),
            )

        def direct(self, step):
            return self.copy(
                self.part(lax.rem(low + step, lows), 0, self.count),
                self.arrivals.at[step],
                step,
                low_peer(step),
            )

        def start(self):
            if is_square:
                for side in range(2):
                    self.half(side).start()
                return

            def one(step, carry):
                self.direct(step).start()
                return carry

            lax.fori_loop(1, lows, one, 0)

        def relay(self):
            if is_square:
                for side in range(2):
                    self.half(side).wait()
                    mine_too = self.part(low_other(1 + side), *self.halves[side])
                    both = mine_too[...].astype(F32) + self.relays[side][...].astype(F32)
                    mine_too[...] = both.astype(BF16)
                    self.summed(side).start()

        def finish(self):
            if is_square:
                for side in range(2):
                    self.summed(side).wait()
                return

            def one(step, carry):
                self.direct(step).wait()
                return carry

            lax.fori_loop(1, lows, one, 0)

    arrived = range(2) if is_square else range(1, lows)

    meet_rows(rows)

    keep = keep_ref[...].astype(F32)
    count_ref[me] = jnp.broadcast_to(jnp.sum(keep, axis=1, keepdims=True), (8, 128))

    def count_copy(step):
        return send(
            count_ref.at[me],
            count_ref.at[me],
            count_sems.at[0, step],
            count_sems.at[1, step],
            (lax.rem(me + step, rows), core),
        )

    def count_arrival(step):
        source = lax.rem(me + rows - step, rows)
        return send(
            count_ref.at[source],
            count_ref.at[source],
            count_sems.at[0, step],
            count_sems.at[1, step],
            (source, core),
        )

    def start_count(step, carry):
        count_copy(step).start()
        return carry

    lax.fori_loop(1, rows, start_count, 0)

    weight_refs = (wg_ref, wu_ref, wd_ref)
    my_share = pl.ds(pl.multiple_of(low * share, share), share)
    locals_early = [
        pltpu.make_async_copy(ref, wqkv_ref.at[core, number], local_sems.at[number])
        for number, ref in enumerate((wq_ref, wk_ref, wv_ref))
    ]
    locals_late = [
        pltpu.make_async_copy(wo_ref, wout_ref.at[core], local_sems.at[3]),
        pltpu.make_async_copy(cot_ref, cots_ref.at[high], local_sems.at[4]),
    ] + [
        pltpu.make_async_copy(ref, wall_ref.at[number, my_share], local_sems.at[5 + number])
        for number, ref in enumerate(weight_refs)
    ]
    for copy in locals_early + locals_late:
        copy.start()

    def wall_gather(place, number, start, size):
        def block(place, begin, count):
            inside = pl.ds(pl.multiple_of(place * share + start + begin, 16), count)
            return wall_ref.at[number, inside]

        source = weight_refs[number].at[pl.ds(start, size)]
        return LowGather(source, block, size, wall_sems.at[place])

    early = share * 3 // 7 // 16 * 16
    wall_cuts = [(2, 0, early), (2, early, share - early), (0, 0, share), (1, 0, share)]
    walls = [
        wall_gather(place, *cut) if cut[2] else None for place, cut in enumerate(wall_cuts)
    ]

    class Gather:
        def __init__(self, ref, sems, sems_f, offset, count, source=None):
            self.ref, self.sems, self.sems_f = ref, sems, sems_f
            self.part = pl.ds(pl.multiple_of(core * half + offset, 16), count)
            self.other = pl.ds(pl.multiple_of((1 - core) * half + offset, 16), count)
            self.source = ref.at[high] if source is None else source

        def direct(self, step):
            return send(
                self.source.at[self.part],
                self.ref.at[high, self.part],
                self.sems.at[0, step],
                self.sems.at[1, step],
                high_peer(step),
            )

        def arrival(self, step):
            place = self.ref.at[high_other(step), self.part]
            return send(
                place, place, self.sems.at[0, step], self.sems.at[1, step], high_peer(step)
            )

        def relay(self):
            place = self.ref.at[high_other(2), self.part]
            return send(place, place, self.sems.at[0, 0], self.sems.at[1, 3], high_peer(1))

        def forward(self, step, part):
            place = self.ref.at[high_other(step), part]
            return send(
                place, place, self.sems_f.at[0, step], self.sems_f.at[1, step], sibling
            )

        def start(self):
            self.direct(1).start()
            self.direct(2).start()

            @pl.when(middle_high)
            def _():
                self.direct(3).start()

        def arrived(self, step):
            self.arrival(step).wait_recv()
            if step == 2:

                @pl.when(middle_high)
                def _():
                    self.relay().start()

            self.forward(step, self.part).start()

        def forwarded(self, step):
            self.forward(step, self.other).wait_recv()

        def close(self):
            self.direct(1).wait_send()
            self.direct(2).wait_send()

            @pl.when(middle_high)
            def _():
                self.direct(3).wait_send()
                self.relay().wait_send()

            for step in range(1, HI):
                self.forward(step, self.part).wait_send()

    third = half // 3 // 16 * 16
    cot_gathers = [
        Gather(cots_ref, cot_sems.at[number], cotf_sems.at[number], begin, count, cot_ref)
        for number, (begin, count) in enumerate(((0, third), (third, half - third)))
    ]
    sec_gather = Gather(sec_ref, sec_sems, secf_sems, 0, half)

    if early:
        walls[0].start()
    cot_gathers[0].start()
    pair_early = [
        send(wo_ref, wout_ref.at[core], pair_sems.at[0, 0], pair_sems.at[1, 0], sibling)
    ] + [
        send(
            ref,
            wqkv_ref.at[core, number],
            pair_sems.at[0, 1 + number],
            pair_sems.at[1, 1 + number],
            sibling,
        )
        for number, ref in enumerate((wq_ref, wk_ref, wv_ref))
    ]
    for copy in pair_early:
        copy.start()

    gate_weight = g_delete * w_delete
    raw = byte_ref[...]
    raw_f = raw.astype(F32)
    raw_scale = lax.rsqrt(jnp.mean(raw_f * raw_f, axis=0, keepdims=True) + EPS)
    raw_logit = raw_scale * jnp.sum(
        nn(stacked_rows(split3(gate_weight), width), raw), axis=0, keepdims=True
    )
    gate_ref[...] = DELETE_SCALE * sigmoid(raw_logit)
    upper = lax.broadcasted_iota(jnp.int32, (raw_count, raw_count), 0) <= lax.broadcasted_iota(
        jnp.int32, (raw_count, raw_count), 1
    )
    rank = nn(keep.astype(BF16), jnp.where(upper, 1.0, 0.0).astype(BF16)) - 1.0
    lane = lax.broadcasted_iota(jnp.int32, (raw_count, 128), 1)
    local = lax.broadcasted_iota(jnp.int32, (raw_count, 128), 0).astype(F32)
    aux = jnp.where(lane == 0, local, jnp.where(lane == 1, me.astype(F32), 0.0)).astype(BF16)
    window.clear(kv_ref, 0.0)
    window.clear(query_ref, 0.0)
    window.clear(facts_ref, -1.0)
    window.clear(dout_ref, 0.0)
    window.clear(facts2_ref, 0.0)

    def finish_count(step, carry):
        count_copy(step).wait_send()
        count_arrival(step).wait_recv()
        return carry

    lax.fori_loop(1, rows, finish_count, 0)
    lower = lax.broadcasted_iota(jnp.int32, count_ref.shape, 0) < me
    before = jnp.sum(jnp.where(lower, count_ref[...], 0.0), axis=0)[0:1, 0:1]
    place = before + rank - (me * own_rows).astype(F32)
    place = jnp.where(keep > 0.0, place, -4096.0).astype(jnp.int32)
    chosen = place + MARGIN == lax.broadcasted_iota(jnp.int32, (ext_rows, raw_count), 0)
    chosen = jnp.where(chosen, 1.0, 0.0).astype(BF16)
    chosen_ref[...] = chosen
    ext_ref[...] = nt(chosen, raw).astype(BF16)
    extaux_ref[...] = nn(chosen, aux).astype(BF16)

    def edges(sems, downs, ups):
        def copies(pairs, offset):
            return [
                send(src, dst, sems.at[0, number], sems.at[1, number], (me + offset, core))
                for number, src, dst in pairs
            ]

        def start():
            @pl.when(me > 0)
            def _():
                for copy in copies(downs, -1):
                    copy.start()

            @pl.when(me < rows - 1)
            def _():
                for copy in copies(ups, 1):
                    copy.start()

        def finish():
            @pl.when(me > 0)
            def _():
                for copy in copies(downs, -1):
                    copy.wait_send()
                for copy in copies(ups, 1):
                    copy.wait_recv()

            @pl.when(me < rows - 1)
            def _():
                for copy in copies(ups, 1):
                    copy.wait_send()
                for copy in copies(downs, -1):
                    copy.wait_recv()

        return start, finish

    first_rows, last_rows = pl.ds(0, MARGIN), pl.ds(own_rows + MARGIN, MARGIN)
    start_edges, finish_edges = edges(
        edge_sems,
        [
            (0, ext_ref.at[first_rows], above_ref),
            (1, extaux_ref.at[first_rows], aboveaux_ref),
        ],
        [
            (2, ext_ref.at[last_rows], below_ref),
            (3, extaux_ref.at[last_rows], belowaux_ref),
        ],
    )
    start_edges()

    @pl.when(me == 0)
    def _():
        below_ref[...] = jnp.zeros(below_ref.shape, BF16)
        belowaux_ref[...] = jnp.zeros(belowaux_ref.shape, BF16)

    @pl.when(me == rows - 1)
    def _():
        above_ref[...] = jnp.zeros(above_ref.shape, BF16)
        aboveaux_ref[...] = jnp.zeros(aboveaux_ref.shape, BF16)

    packed_ref[...] = ext_ref[MARGIN : MARGIN + own_rows, :]
    aux_ref[...] = extaux_ref[MARGIN : MARGIN + own_rows, :].astype(F32)
    for copy in locals_early:
        copy.wait()
    finish_edges()
    top = own_rows - MARGIN
    packed_ref[0:MARGIN, :] = packed_ref[0:MARGIN, :] + below_ref[...]
    packed_ref[top:, :] = packed_ref[top:, :] + above_ref[...]
    aux_ref[0:MARGIN, :] = aux_ref[0:MARGIN, :] + belowaux_ref[...].astype(F32)
    aux_ref[top:, :] = aux_ref[top:, :] + aboveaux_ref[...].astype(F32)

    packed = packed_ref[...].astype(F32)
    scale = row_scale(packed)
    first = (packed * scale * g_attn).astype(BF16)
    first_ref[...] = first
    kv_ref[own, :, 0:inner] = nt(first, wqkv_ref[core, 1]).astype(BF16)
    kv_ref[own, :, inner : 2 * inner] = nt(first, wqkv_ref[core, 2]).astype(BF16)

    gate = DELETE_SCALE * sigmoid(gate_logit(packed, scale, gate_weight))
    ids = aux_ref[:, 0:1] + raw_count * aux_ref[:, 1:2]
    ids_i = ids.astype(jnp.int32)
    starts = jnp.zeros_like(ids_i)
    end = jnp.int32(0)
    for number in range(lengths_ref.shape[0]):
        end = end + lengths_ref[number]
        starts = jnp.where(ids_i >= end, end, starts)
    starts = starts.astype(F32)
    own_eye = eye(own_rows)
    facts_ref[own] = jnp.zeros(facts_ref.shape[1:], F32)
    facts_ref[own, 0:1, 0:own_rows] = to_row(gate, own_eye)
    facts_ref[own, 1:2, 0:own_rows] = to_row(ids, own_eye)
    facts_ref[own, 2:3, 0:own_rows] = to_row(starts, own_eye)
    window.start([(facts_ref, facts_sems), (kv_ref, kv_sems)])
    cot_gathers[1].start()
    query_ref[own] = nt(first, wqkv_ref[core, 0]).astype(BF16)

    far = (len(offsets) - 3) // 2
    segments = (range(0, far), range(far, 2 * far), range(2 * far, 2 * far + 3))
    def add_near(added_ref, slot, rows_at, gap, extra, allowed, above, below):
        place = 1 + slot
        lanes_at = slice(place * own_rows, (place + 1) * own_rows)
        for head in range(heads):
            if rows_at is not None:
                rest = table_ref[head, 2 * HALF - 1 if above else HALF - 1]
                added_ref[head, :, lanes_at] = jnp.where(allowed, rest + extra, NEGATIVE)
            cut = slice(0, own_rows) if rows_at is None else rows_at
            bias = near_bias(gap[cut], table_ref, head, above, below)
            more = extra if extra.shape[0] == 1 else extra[cut]
            added_ref[head, cut, lanes_at] = jnp.where(allowed[cut], bias + more, NEGATIVE)

    def fact(slot, line):
        at = window.slot[slot]
        return facts_ref[at, line : line + 1, :own_rows]

    border = {-1: slice(0, EDGE), 0: None, 1: slice(own_rows - EDGE, own_rows)}

    def near_queries(slot):
        gap, allowed = fact(slot, 1) - ids, fact(slot, 2) == starts
        add_near(
            biasq_ref, slot, border[slot], gap, fact(slot, 0), allowed, slot >= 0, slot <= 0
        )

    def near_keys(slot):
        gap, allowed = ids - fact(slot, 1), fact(slot, 2) == starts
        add_near(biask_ref, slot, border[slot], gap, gate, allowed, slot <= 0, slot >= 0)

    near_queries(0)
    window.relay([(facts_ref, facts_sems), (kv_ref, kv_sems)])
    walls[1].start()
    walls[2].start()
    window.finish([(facts_ref, facts_sems)], (-1, 1))
    near_queries(-1)
    near_queries(1)
    window.finish([(facts_ref, facts_sems)], [d for d in offsets if abs(d) > 1])
    window.finish([(kv_ref, kv_sems)])
    window.close([(facts_ref, facts_sems), (kv_ref, kv_sems)])
    walls[3].start()
    if early:
        walls[0].relay()

    def spans(segment):
        return slice(segment[0], segment[-1] + 1)

    def far_added(segment, column):
        allowed = joined_row(facts_ref, segment, 2, own_rows) == starts
        return jnp.where(allowed, column, NEGATIVE)

    added = [
        far_added(segment, joined_row(facts_ref, segment, 0, own_rows)) for segment in segments[:2]
    ]
    fixed = (HALF - 1, 2 * HALF - 1)
    lanes = lax.broadcasted_iota(jnp.int32, lse_ref.shape, 1)
    lse_all = jnp.zeros(lse_ref.shape, F32)
    for head in range(heads):
        cut = slice(head * head_size, (head + 1) * head_size)
        cut_v = slice(inner + head * head_size, inner + (head + 1) * head_size)
        query = query_ref[own, :, cut]
        parts = []
        for number, segment in enumerate(segments):
            keys = kv_ref[spans(segment), :, cut].reshape(-1, head_size)
            if number < 2:
                extra = added[number] + table_ref[head, fixed[number]]
            else:
                extra = biasq_ref[head]
            parts.append(nt(query, keys) + extra)
        most = jnp.max(parts[0], axis=1, keepdims=True)
        for part in parts[1:]:
            most = jnp.maximum(most, jnp.max(part, axis=1, keepdims=True))
        expos = [jnp.exp(part - most) for part in parts]
        total = sum(jnp.sum(expo, axis=1, keepdims=True) for expo in expos)
        lse_all = jnp.where(lanes == head, most + jnp.log(total), lse_all)
        attended = jnp.zeros((own_rows, head_size), F32)
        for segment, expo in zip(segments, expos):
            values = kv_ref[spans(segment), :, cut_v].reshape(-1, head_size)
            attended = attended + nn((expo / total).astype(BF16), values)
        attf_ref[:, cut] = attended
        att_ref[core, :, cut] = attended.astype(BF16)
    lse_ref[...] = lse_all

    att_copy = send(
        att_ref.at[core], att_ref.at[core], pair_sems.at[0, 4], pair_sems.at[1, 4], sibling
    )
    att_copy.start()
    for copy in locals_late:
        copy.wait()
    for copy in pair_early:
        copy.wait()
    att_copy.wait()
    mixed = packed_ref[...].astype(F32) + (nn(att_ref[0], wout_ref[0]) + nn(att_ref[1], wout_ref[1]))
    mixed_ref[...] = mixed
    sec_ref[high] = (mixed * row_scale(mixed) * g_ff).astype(BF16)
    sec_gather.start()

    walls[1].relay()
    walls[2].relay()
    for gather in cot_gathers:
        gather.arrived(1)
        gather.arrived(2)
    walls[3].relay()
    sec_gather.arrived(1)
    sec_gather.arrived(2)
    for wall in walls[0 if early else 1 :]:
        wall.finish()

    def sib_copy(kind, step):
        return send(
            sout_ref.at[step],
            sin_ref.at[kind, step],
            sib_sems.at[0, kind, step],
            sib_sems.at[1, kind, step],
            sibling,
        )

    def hi_copy(kind, step):
        return send(
            hout_ref.at[kind, step - 1],
            hin_ref.at[kind, step - 1],
            hi_sems.at[0, kind, step],
            hi_sems.at[1, kind, step],
            high_peer(step),
        )

    def hand_over(kind, step, value):
        part_ref[...] = value
        sout_ref[step] = part_ref[theirs, :].astype(BF16)
        kept_ref[kind if step == 0 else 2 + step % 2] = part_ref[mine, :]
        sib_copy(kind, step).start()

    def pass_on(kind, step):
        sib_copy(kind, step).wait()
        both = kept_ref[2 + step % 2] + sin_ref[kind, step].astype(F32)
        hout_ref[kind, step - 1] = both.astype(BF16)

    def chunk_rows(step):
        return pl.ds(pl.multiple_of(high_other(step) * own_rows, own_rows), own_rows)

    for step in range(HI):
        if step:
            for gather in cot_gathers + [sec_gather]:
                if step == HI - 1:
                    gather.arrived(step)
                gather.forwarded(step)
        chunk = high_other(step)
        second = sec_ref[chunk]
        gated = nt(second, wall_ref[0])
        upper = nt(second, wall_ref[1])
        d_middle = nt(cots_ref[chunk], wall_ref[2])
        square = gated * gated
        bend = jnp.tanh(GELU_A * gated * (1.0 + GELU_B * square))
        lift = 0.5 * (1.0 + bend)
        slope = lift + 0.5 * gated * (1.0 - bend * bend) * (
            GELU_A * (1.0 + 3.0 * GELU_B * square)
        )
        gelu = gated * lift
        d_gated = (d_middle * upper * slope).astype(BF16)
        d_upper = (d_middle * gelu).astype(BF16)
        mid_ref[chunk_rows(step), :] = (gelu * upper).astype(BF16)
        dgated_ref[chunk_rows(step), :] = d_gated
        dupper_ref[chunk_rows(step), :] = d_upper
        hand_over(1, step, nn(d_gated, wall_ref[0]) + nn(d_upper, wall_ref[1]))
        if step == 0:
            window.start([(query_ref, query_sems)])
        if step == HI - 1:
            window.relay([(query_ref, query_sems)])
        if step > 1:
            pass_on(1, step - 1)
            hi_copy(1, step - 1).start()
    pass_on(1, HI - 1)
    hi_copy(1, HI - 1).start()
    for gather in cot_gathers + [sec_gather]:
        gather.close()

    def ff_reduce(number):
        def part(place, begin, count):
            inside = pl.ds(pl.multiple_of(place * share + begin, 16), count)
            return wall_ref.at[number, inside]

        relays = (ffa_ref.at[number], ffb_ref.at[number])
        return LowReduce(part, share, relays, ffin_ref.at[number], ff_sems.at[number])

    reduces = [ff_reduce(number) for number in range(3)]
    hidden = wall_ref.shape[1]

    def weight_grad(number, left_ref, right_ref):
        for begin in range(0, hidden, 256):
            units = slice(begin, min(begin + 256, hidden))
            right = right_ref[...].reshape(HI * own_rows, width)
            wall_ref[number, units, :] = tn(left_ref[:, units], right).astype(BF16)

    weight_grad(0, dgated_ref, sec_ref)
    reduces[0].start()
    weight_grad(1, dupper_ref, sec_ref)
    reduces[1].start()
    sib_copy(1, 0).wait()
    for place, step in enumerate((3, 2, 1, 0)):
        hand_over(0, step, nn(mid_ref[chunk_rows(step), :], wall_ref[2]))
        if place:
            pass_on(0, step + 1)
    reduces[0].relay()
    weight_grad(2, mid_ref, cots_ref)
    reduces[1].relay()

    for slot in (-1, 0, 1):
        near_keys(slot)
    total = kept_ref[1] + sin_ref[1, 0].astype(F32)
    for step in range(1, HI):
        hi_copy(1, step).wait()
        total = total + hin_ref[1, step - 1].astype(F32)
    dsec_ref[mine, :] = total
    dsec_copy = send(
        dsec_ref.at[mine], dsec_ref.at[mine], half_sems.at[0, 0], half_sems.at[1, 0], sibling
    )
    dsec_copy.start()
    dsec_copy.wait()

    back, g_ff_grad = norm_back(mixed_ref[...], g_ff, dsec_ref[...])
    d_mixed = cots_ref[high].astype(F32) + back
    part_ref[...] = d_mixed
    d_branch = d_mixed.astype(BF16)
    d_att = nt(d_branch, wout_ref[core]).astype(BF16)
    dout_ref[own] = d_att
    facts2_ref[own] = jnp.zeros(facts2_ref.shape[1:], F32)
    deltas = []
    products = d_att.astype(F32) * attf_ref[...]
    for head in range(heads):
        cut = slice(head * head_size, (head + 1) * head_size)
        delta = jnp.sum(products[:, cut], axis=1, keepdims=True)
        deltas.append(delta)
        facts2_ref[own, head : head + 1, 0:own_rows] = to_row(delta, own_eye)
        line = 4 + head
        facts2_ref[own, line : line + 1, 0:own_rows] = to_row(
            lse_ref[:, head : head + 1], own_eye
        )
    window.start([(facts2_ref, facts2_sems), (dout_ref, dout_sems)])

    piece = zout_ref.shape[2]
    pieces = lows // 2
    lanes_all = zout_ref.shape[3]
    quarter = lanes_all // HI

    def keep_pieces(group, number, value):
        for part in range(pieces):
            block = value[part * piece : (part + 1) * piece, :]
            zout_ref[group, number * pieces + part, :, 0:width] = block.astype(BF16)

    def quarter_of(place):
        return pl.ds(pl.multiple_of(place * quarter, 128), quarter)

    def low_sum(group):
        def part(place, begin, count):
            return zout_ref.at[group, place, pl.ds(begin, count)]

        relays = (za_ref.at[group], zb_ref.at[group])
        return LowReduce(part, piece, relays, zin_ref.at[group], low_sems.at[group])

    lows_sum = [low_sum(group) for group in range(2)]

    def high_copy(group, step, place):
        return send(
            zout_ref.at[group, low, :, quarter_of(high_other(step))],
            yin_ref.at[group, place],
            high_sems.at[0, group, step],
            high_sems.at[1, group, step],
            high_peer(step),
        )

    def share_low(group):
        lows_sum[group].finish()
        total = zout_ref[group, low].astype(F32)
        for number in arrived:
            total = total + zin_ref[group, number].astype(F32)
        zout_ref[group, low] = total.astype(BF16)
        for step in range(1, HI):
            high_copy(group, step, high).start()

    def back_copy(group, step, place):
        lanes_at = (group, slice(None), quarter_of(place))
        return send(
            fin_ref.at[lanes_at],
            fin_ref.at[lanes_at],
            back_sems.at[0, group, step],
            back_sems.at[1, group, step],
            high_peer(step),
        )

    def share_high(group):
        for step in range(1, HI):
            high_copy(group, step, high).wait_send()
            high_copy(group, step, high_other(step)).wait_recv()
        yin_ref[group, high] = zout_ref[group, low, :, quarter_of(high)]
        total = yin_ref[group, 0].astype(F32)
        for number in range(1, HI):
            total = total + yin_ref[group, number].astype(F32)
        fin_ref[group, :, quarter_of(high)] = total.astype(BF16)
        for step in range(1, HI):
            back_copy(group, step, high).start()

    def last_gather(group):
        def block(place, begin, count):
            return attg_ref.at[group, place, pl.ds(begin, count)]

        return LowGather(fin_ref.at[group], block, piece, last_sems.at[group])

    lasts = [last_gather(group) for group in range(2)]
    own_lasts = [
        pltpu.make_async_copy(
            fin_ref.at[group], attg_ref.at[group, low], local_sems.at[1 + group]
        )
        for group in range(2)
    ]

    def spread_low(group):
        for step in range(1, HI):
            back_copy(group, step, high).wait_send()
            back_copy(group, step, high_other(step)).wait_recv()
        lasts[group].start()
        own_lasts[group].start()

    if lanes_all > width:
        zout_ref[:, :, :, width:] = jnp.zeros(zout_ref.shape[:3] + (lanes_all - width,), BF16)
    keep_pieces(0, 0, tn(att_ref[core], d_branch))

    lane = lax.broadcasted_iota(jnp.int32, (1, width), 1)
    bias_grad = jnp.zeros((1, width), F32)

    def add_bias(bias_grad, head, bucket, value):
        return bias_grad + jnp.where(lane == head * 2 * HALF + bucket, value, 0.0)

    def total_of(value):
        return jnp.sum(jnp.sum(value, axis=0, keepdims=True), axis=1, keepdims=True)

    for head in range(heads):
        cut = slice(head * head_size, (head + 1) * head_size)
        cut_v = slice(inner + head * head_size, inner + (head + 1) * head_size)
        query, d_head = query_ref[own, :, cut], dout_ref[own, :, cut]
        lse = lse_ref[:, head : head + 1]
        d_query = jnp.zeros((own_rows, head_size), F32)
        for number, segment in enumerate(segments):
            keys = kv_ref[spans(segment), :, cut].reshape(-1, head_size)
            values = kv_ref[spans(segment), :, cut_v].reshape(-1, head_size)
            if number < 2:
                extra = added[number] + table_ref[head, fixed[number]]
            else:
                extra = biasq_ref[head]
            probs = jnp.exp(nt(query, keys) + extra - lse)
            d_scores = probs * (nt(d_head, values) - deltas[head])
            d_query = d_query + nn(d_scores.astype(BF16), keys)
            if number < 2:
                bias_grad = add_bias(bias_grad, head, fixed[number], total_of(d_scores))
                continue
            for slot in (-1, 0, 1):
                lanes_at = slice((1 + slot) * own_rows, (2 + slot) * own_rows)
                block = d_scores[:, lanes_at]
                gap = fact(slot, 1) - ids
                whole = total_of(block)
                rows_at = border[slot]
                if rows_at is not None:
                    block, gap = block[rows_at], gap[rows_at]
                for sign in (1, -1):
                    if sign * slot < 0:
                        continue
                    base = HALF if sign > 0 else 0
                    sums = [
                        total_of(jnp.where(sign * gap >= limit, block, 0.0)) for limit in LIMITS
                    ]
                    if slot:
                        sums = [whole] + [value + (whole - total_of(block)) for value in sums[1:]]
                    whole = whole - sums[0]
                    for place in range(len(LIMITS)):
                        value = sums[place]
                        if place + 1 < len(LIMITS):
                            value = value - sums[place + 1]
                        bias_grad = add_bias(bias_grad, head, base + place + 1, value)
                if not slot:
                    bias_grad = add_bias(bias_grad, head, 0, whole)
        heads_ref[core, 0, :, cut] = d_query.astype(BF16)
        if head == 1:
            window.relay([(facts2_ref, facts2_sems), (dout_ref, dout_sems)])
            for step in (3, 2, 1):
                hi_copy(0, step).start()

    keep_pieces(0, 1, tn(heads_ref[core, 0], first_ref[...]))
    lows_sum[0].start()

    window_late = [(query_ref, query_sems), (facts2_ref, facts2_sems), (dout_ref, dout_sems)]
    window.finish(window_late)
    window.close(window_late)
    lows_sum[0].relay()
    d_gate = jnp.zeros((own_rows, 1), F32)
    added = [far_added(segment, gate) for segment in segments[:2]]
    fixed = (2 * HALF - 1, HALF - 1)
    for head in range(heads):
        cut = slice(head * head_size, (head + 1) * head_size)
        cut_v = slice(inner + head * head_size, inner + (head + 1) * head_size)
        key, value = kv_ref[own, :, cut], kv_ref[own, :, cut_v]
        d_key = jnp.zeros((own_rows, head_size), F32)
        d_value = jnp.zeros((own_rows, head_size), F32)
        for number, segment in enumerate(segments):
            queries = query_ref[spans(segment), :, cut].reshape(-1, head_size)
            d_heads = dout_ref[spans(segment), :, cut].reshape(-1, head_size)
            if number < 2:
                extra = added[number] + table_ref[head, fixed[number]]
            else:
                extra = biask_ref[head]
            lse = joined_row(facts2_ref, segment, 4 + head, own_rows)
            delta = joined_row(facts2_ref, segment, head, own_rows)
            probs = jnp.exp(nt(key, queries) + extra - lse)
            d_scores = probs * (nt(value, d_heads) - delta)
            d_value = d_value + nn(probs.astype(BF16), d_heads)
            d_key = d_key + nn(d_scores.astype(BF16), queries)
            d_gate = d_gate + jnp.sum(d_scores, axis=1, keepdims=True)
        heads_ref[core, 1, :, cut] = d_key.astype(BF16)
        heads_ref[core, 2, :, cut] = d_value.astype(BF16)
    dgate_ref[core] = jnp.broadcast_to(d_gate, dgate_ref.shape[1:])
    pair_late = [
        send(ref.at[core], ref.at[core], pair_sems.at[0, 5 + i], pair_sems.at[1, 5 + i], sibling)
        for i, ref in enumerate((heads_ref, dgate_ref))
    ]
    for copy in pair_late:
        copy.start()
    for number in range(2):
        keep_pieces(1, number, tn(heads_ref[core, 1 + number], first_ref[...]))
    lows_sum[1].start()

    for copy in pair_late:
        copy.wait()
    d_first = jnp.zeros((own_rows, width), F32)
    for side in range(2):
        for number in range(3):
            d_first = d_first + nn(heads_ref[side, number], wqkv_ref[side, number])
    back, g_attn_grad = norm_back(packed_ref[...].astype(F32), g_attn, d_first)
    inside = slice(MARGIN, MARGIN + own_rows)
    back_ref[inside, :] = (part_ref[...] + back).astype(BF16)
    d_gate = dgate_ref[0] + dgate_ref[1]
    lane_g = lax.broadcasted_iota(jnp.int32, d_gate.shape, 1)
    terms = jnp.zeros(d_gate.shape, F32)
    for number, term in enumerate(split3(d_gate)):
        terms = jnp.where(lane_g == number, term, terms)
    backaux_ref[inside, :] = terms.astype(BF16)
    down_src, down_dst = pl.ds(MARGIN, MARGIN), pl.ds(own_rows + MARGIN, MARGIN)
    up_src, up_dst = pl.ds(own_rows, MARGIN), pl.ds(0, MARGIN)
    start_edges, finish_edges = edges(
        edge2_sems,
        [
            (0, back_ref.at[down_src], back_ref.at[down_dst]),
            (1, backaux_ref.at[down_src], backaux_ref.at[down_dst]),
        ],
        [
            (2, back_ref.at[up_src], back_ref.at[up_dst]),
            (3, backaux_ref.at[up_src], backaux_ref.at[up_dst]),
        ],
    )
    start_edges()

    @pl.when(me == 0)
    def _():
        back_ref[up_dst, :] = jnp.zeros((MARGIN, width), BF16)
        backaux_ref[up_dst, :] = jnp.zeros((MARGIN, 128), BF16)

    @pl.when(me == rows - 1)
    def _():
        back_ref[down_dst, :] = jnp.zeros((MARGIN, width), BF16)
        backaux_ref[down_dst, :] = jnp.zeros((MARGIN, 128), BF16)

    gate_s = sigmoid(raw_logit)
    gate_slope = DELETE_SCALE * gate_s * (1.0 - gate_s)
    raw_scaled = gcot_ref[...] * gate_slope * raw_scale
    common = jnp.sum(
        nt(stacked_rows(split3(raw_scaled), raw_count), byte_ref[...]), axis=0, keepdims=True
    )
    packed = packed_ref[...].astype(F32)
    scale = row_scale(packed)
    own_s = sigmoid(gate_logit(packed, scale, gate_weight))
    own_scaled = d_gate[:, 0:1] * (DELETE_SCALE * own_s * (1.0 - own_s)) * scale
    common = common + jnp.sum(own_scaled * packed, axis=0, keepdims=True)
    slow_ref[low, 0:1, :] = g_ff_grad
    slow_ref[low, 1:2, :] = g_attn_grad
    slow_ref[low, 2:3, :] = common * g_delete
    slow_ref[low, 3:4, :] = common * w_delete
    slow_ref[low, 4:5, :] = bias_grad
    slow_ref[low, 5:8, :] = jnp.zeros((3, width), F32)

    def slow_copy(step, source):
        return send(
            slow_ref.at[source],
            slow_ref.at[source],
            slow_sems.at[0, step],
            slow_sems.at[1, step],
            low_peer(step),
        )

    def start_slow(step, carry):
        slow_copy(step, low).start()
        return carry

    def finish_slow(step, carry):
        slow_copy(step, low).wait_send()
        slow_copy(step, low_source(step)).wait_recv()
        return carry

    def shigh_copy(step, source):
        return send(
            shigh_ref.at[source],
            shigh_ref.at[source],
            shigh_sems.at[0, step],
            shigh_sems.at[1, step],
            high_peer(step),
        )

    lax.fori_loop(1, lows, start_slow, 0)
    lows_sum[1].relay()
    reduces[2].start()
    share_low(0)
    share_low(1)
    share_high(0)
    lax.fori_loop(1, lows, finish_slow, 0)
    small = slow_ref[0]
    for number in range(1, lows):
        small = small + slow_ref[number]
    shigh_ref[high] = small
    for step in range(1, HI):
        shigh_copy(step, high).start()
    reduces[2].relay()
    share_high(1)
    spread_low(0)
    spread_low(1)

    finish_edges()
    spread = tn(backaux_ref[...], chosen_ref[...])
    raw_cot = gcot_ref[...] + (spread[0:1, :] + spread[1:2, :] + spread[2:3, :])
    d_logit = raw_cot * gate_slope
    scaled = d_logit * raw_scale
    along = d_logit * raw_logit * raw_scale * raw_scale * (1.0 / width)
    s1, s2, s3 = split3(scaled)
    w1, w2, w3 = split3(gate_weight)
    outer = tn(
        stacked_rows((w1, w1, w2, w2, w1, w3), width),
        stacked_rows((s1, s2, s1, s2, s3, s1), raw_count),
    )
    rows_ref[...] = outer - along * byte_ref[...].astype(F32)
    rows_ref[...] = rows_ref[...] + tn(back_ref[...], chosen_ref[...])
    for step in range(1, HI):
        shigh_copy(step, high).wait_send()
        shigh_copy(step, high_other(step)).wait_recv()
    small = shigh_ref[0]
    for number in range(1, HI):
        small = small + shigh_ref[number]
    small_ref[...] = small

    sib_copy(0, 0).wait()
    total = mixed_ref[mine, :] + (kept_ref[0] + sin_ref[0, 0].astype(F32))
    for step in range(1, HI):
        hi_copy(0, step).wait()
        total = total + hin_ref[0, step - 1].astype(F32)
    block_ref[mine, :] = total.astype(BF16)
    block_copy = send(
        block_ref.at[mine], block_ref.at[mine], half_sems.at[0, 1], half_sems.at[1, 1], sibling
    )
    block_copy.start()

    def finish_reduce(number):
        reduces[number].finish()
        total = wall_ref[number, my_share, :].astype(F32)
        for begin in range(0, len(arrived), HI):
            loads = [
                pltpu.make_async_copy(
                    ffin_ref.at[number, slot],
                    sec_ref.at[place, pl.ds(0, share)],
                    local_sems.at[3 + place],
                )
                for place, slot in enumerate(arrived[begin : begin + HI])
            ]
            for load in loads:
                load.start()
            for load in loads:
                load.wait()
            for place in range(len(loads)):
                total = total + sec_ref[place, 0:share, :].astype(F32)
        ffo_ref[number] = total

    lasts[0].relay()
    finish_reduce(0)
    finish_reduce(1)
    lasts[1].relay()
    finish_reduce(2)
    block_copy.wait()
    for group in range(2):
        lasts[group].finish()
        own_lasts[group].wait()


def layer(rows, offsets, *operands):
    lengths, table, byte_t, keep, vecs, gcot, wq, wk, wv, wo, wg, wu, wd, cot = operands
    width, raw_count = byte_t.shape
    own_rows = cot.shape[0]
    inner = wq.shape[0]
    heads = table.shape[0]
    share = wd.shape[0]
    lows = rows // HI
    hidden = lows * share
    slots = len(offsets)
    half = own_rows // 2
    piece = 2 * inner // lows
    lanes = -(-width // (128 * HI)) * 128 * HI
    slots_in = 2 if lows == 4 else lows
    window_sems = 3 * slots
    ff_cut, z_cut = share // 2 // 16 * 16, piece // 2 // 16 * 16
    ext_rows = own_rows + 2 * MARGIN
    vmem = pl.BlockSpec(memory_space=pltpu.VMEM)
    smem = pl.BlockSpec(memory_space=pltpu.SMEM)
    anywhere = pl.BlockSpec(memory_space=pl.ANY)
    shape = jax.ShapeDtypeStruct
    dma = pltpu.SemaphoreType.DMA
    outs = [
        shape((1, raw_count), F32),
        shape((own_rows, width), BF16),
        shape((width, raw_count), F32),
        shape((8, width), F32),
        shape((3, share, width), F32),
        shape((2, lows, piece, lanes), BF16),
        shape((3, slots_in, share, width), BF16),
    ]
    out_specs = [vmem] * 5 + [anywhere] * 2
    scratch = [
        pltpu.VMEM((rows, 8, 128), F32),
        pltpu.VMEM((ext_rows, raw_count), BF16),
        pltpu.VMEM((ext_rows, width), BF16),
        pltpu.VMEM((ext_rows, 128), BF16),
        pltpu.VMEM((MARGIN, width), BF16),
        pltpu.VMEM((MARGIN, width), BF16),
        pltpu.VMEM((MARGIN, 128), BF16),
        pltpu.VMEM((MARGIN, 128), BF16),
        pltpu.VMEM((own_rows, width), BF16),
        pltpu.VMEM((own_rows, 128), F32),
        pltpu.VMEM((own_rows, width), BF16),
        pltpu.VMEM((slots, own_rows, 2 * inner), BF16),
        pltpu.VMEM((slots, own_rows, inner), BF16),
        pltpu.VMEM((slots, 8, 256), F32),
        pltpu.VMEM((slots, own_rows, inner), BF16),
        pltpu.VMEM((slots, 8, 256), F32),
        pltpu.VMEM((heads, own_rows, 3 * own_rows), F32),
        pltpu.VMEM((heads, own_rows, 3 * own_rows), F32),
        pltpu.VMEM((2, own_rows, inner), BF16),
        pltpu.VMEM((own_rows, inner), F32),
        pltpu.VMEM((own_rows, 128), F32),
        pltpu.VMEM((own_rows, width), F32),
        pltpu.VMEM((HI, own_rows, width), BF16),
        pltpu.VMEM((HI, own_rows, width), BF16),
        pltpu.VMEM((3, hidden, width), BF16),
        pltpu.VMEM((2, inner, width), BF16),
        pltpu.VMEM((2, 3, inner, width), BF16),
        pltpu.VMEM((HI * own_rows, hidden), BF16),
        pltpu.VMEM((HI * own_rows, hidden), BF16),
        pltpu.VMEM((HI * own_rows, hidden), BF16),
        pltpu.VMEM((own_rows, width), F32),
        pltpu.VMEM((4, half, width), F32),
        pltpu.VMEM((HI, half, width), BF16),
        pltpu.VMEM((2, HI, half, width), BF16),
        pltpu.VMEM((2, HI - 1, half, width), BF16),
        pltpu.VMEM((2, HI - 1, half, width), BF16),
        pltpu.VMEM((own_rows, width), F32),
        pltpu.VMEM((2, 3, own_rows, inner), BF16),
        pltpu.VMEM((2, own_rows, 128), F32),
        pltpu.VMEM((2, lows, piece, lanes), BF16),
        pltpu.VMEM((2, slots_in, piece, lanes), BF16),
        pltpu.VMEM((2, HI, piece, lanes // HI), BF16),
        pltpu.VMEM((2, piece, lanes), BF16),
        pltpu.VMEM((lows, 8, width), F32),
        pltpu.VMEM((HI, 8, width), F32),
        pltpu.VMEM((ext_rows, width), BF16),
        pltpu.VMEM((ext_rows, 128), BF16),
        pltpu.VMEM((3, max(ff_cut, 16), width), BF16),
        pltpu.VMEM((3, share - ff_cut, width), BF16),
        pltpu.VMEM((2, max(z_cut, 16), lanes), BF16),
        pltpu.VMEM((2, piece - z_cut, lanes), BF16),
        dma((2, rows)),
        dma((2, 4)),
        dma((2, window_sems)),
        dma((2, window_sems)),
        dma((2, window_sems)),
        dma((2, window_sems)),
        dma((2, window_sems)),
        dma((4, 2, max(5, lows))),
        dma((2, 7)),
        dma((8,)),
        dma((2, 2, HI)),
        dma((2, 2, HI)),
        dma((2, HI)),
        dma((2, HI)),
        dma((2, 2, HI)),
        dma((2, 2, HI)),
        dma((2, 2)),
        dma((3, 2, max(5, lows))),
        dma((2, 2, max(5, lows))),
        dma((2, 2, HI)),
        dma((2, 2, HI)),
        dma((2, 2, max(5, lows))),
        dma((2, 4)),
        dma((2, lows)),
        dma((2, HI)),
    ]
    return pl.pallas_call(
        functools.partial(layer_kernel, rows, offsets),
        name="layer",
        out_shape=outs,
        in_specs=[smem, smem] + [vmem] * 4 + [anywhere] * 8,
        out_specs=out_specs,
        scratch_shapes=scratch,
        compiler_params=pltpu.CompilerParams(
            collective_id=0, has_side_effects=True, vmem_limit_bytes=VMEM_LIMIT
        ),
    )(*operands)


def per_device(
    byte_rows,
    lengths,
    keep_mask,
    w_delete,
    g_delete,
    g_attn,
    w_query,
    w_key,
    w_value,
    w_out,
    rel_bias,
    g_ff,
    w_gate,
    w_up,
    w_down,
    out_cot,
    gate_cot,
):
    raw_count, width = byte_rows.shape
    own_rows = out_cot.shape[0]
    inner = w_query.shape[1]
    buckets, heads = rel_bias.shape
    rows = lax.axis_size("rows")
    share = w_down.shape[0]
    offsets = slots_of(reach_of(raw_count, own_rows))
    line = lax.broadcasted_iota(jnp.int32, (8, width), 0)
    vecs = jnp.zeros((8, width), F32)
    for number, vector in enumerate((g_delete, w_delete, g_attn, g_ff)):
        vecs = jnp.where(line == number, vector[None, :], vecs)
    spare = -share % 16
    weights = [jnp.pad(w, ((0, spare), (0, 0))) for w in (w_gate.T, w_up.T, w_down)]
    gate, block_out, grad_rows, small, ff_sums, att_grads, _ = layer(
        rows,
        offsets,
        lengths,
        rel_bias.T,
        byte_rows.T,
        keep_mask.reshape(1, -1),
        vecs,
        gate_cot.reshape(1, -1),
        w_query.T,
        w_key.T,
        w_value.T,
        w_out,
        *weights,
        out_cot,
    )
    att_grads = att_grads.reshape(4, inner, -1)[:, :, :width].astype(F32)
    ff_sums = ff_sums[:, :share]
    grad_bias = small[4, : heads * buckets].reshape(heads, buckets).T
    return (
        block_out,
        gate[0],
        grad_rows.T,
        small[2],
        small[3],
        small[1],
        att_grads[1].T,
        att_grads[2].T,
        att_grads[3].T,
        att_grads[0],
        grad_bias,
        small[0],
        ff_sums[0].T,
        ff_sums[1].T,
        ff_sums[2],
    )


def solution(mesh):
    in_specs = (
        P("rows", None),
        P(),
        P("rows"),
        P(),
        P(),
        P(),
        P(None, "tensor"),
        P(None, "tensor"),
        P(None, "tensor"),
        P("tensor", None),
        P(None, "tensor"),
        P(),
        P(None, ("rows", "tensor")),
        P(None, ("rows", "tensor")),
        P(("rows", "tensor"), None),
        P("rows", None),
        P("rows"),
    )
    out_specs = (
        P("rows", None),
        P("rows"),
        P("rows", None),
        P(),
        P(),
        P(),
        P(None, "tensor"),
        P(None, "tensor"),
        P(None, "tensor"),
        P("tensor", None),
        P(None, "tensor"),
        P(),
        P(None, ("rows", "tensor")),
        P(None, ("rows", "tensor")),
        P(("rows", "tensor"), None),
    )
    return jax.shard_map(
        per_device, mesh=mesh, in_specs=in_specs, out_specs=out_specs, check_vma=False
    )
```

```python
import functools

import jax
import jax.numpy as jnp
from jax import lax
from jax.experimental import pallas as pl
from jax.experimental.pallas import tpu as pltpu
from jax.sharding import PartitionSpec as P

MAXLEN = 1024
MARGIN = 32
EPS = 1e-06
DELETE_SCALE = -30.0
NEGATIVE = -1e30
LIMITS = (1, 2, 3, 4, 5, 6, 7, 8, 12, 16, 23, 32, 46, 64, 91)
HALF = 16
HI = 4
MESH = pl.DeviceIdType.MESH
F32 = jnp.float32
BF16 = jnp.bfloat16
VMEM_LIMIT = 63 * 1024 * 1024


def nn(a, b):
    return lax.dot_general(a, b, (((1,), (0,)), ((), ())), preferred_element_type=F32)


def nt(a, b):
    return lax.dot_general(a, b, (((1,), (1,)), ((), ())), preferred_element_type=F32)


def tn(a, b):
    return lax.dot_general(a, b, (((0,), (0,)), ((), ())), preferred_element_type=F32)


def eye(count):
    return lax.broadcasted_iota(jnp.int32, (count, count), 0) == lax.broadcasted_iota(
        jnp.int32, (count, count), 1
    )


def to_row(column, diagonal):
    return jnp.sum(jnp.where(diagonal, column, 0.0), axis=0, keepdims=True)


def to_column(row, diagonal):
    return jnp.sum(jnp.where(diagonal, row, 0.0), axis=1, keepdims=True)


def row_scale(values):
    return lax.rsqrt(jnp.mean(values * values, axis=-1, keepdims=True) + EPS)


def gate_logit(values, scale, weight):
    return scale * jnp.sum(values * weight, axis=-1, keepdims=True)


def sigmoid(value):
    return 1.0 / (1.0 + jnp.exp(-value))


def norm_back(values, gain, grad):
    scale = row_scale(values)
    scaled = grad * gain
    inner = jnp.mean(scaled * values, axis=-1, keepdims=True)
    back = scale * scaled - values * (scale * scale * scale * inner)
    return back, jnp.sum(grad * values * scale, axis=0, keepdims=True)


def reach_of(raw_count, own_rows):
    span = (MAXLEN // raw_count - 1) * own_rows + 2 * MARGIN + raw_count
    return -(-(span - 1) // own_rows)


def slots_of(reach):
    far = list(range(2, reach + 1))
    return [-d for d in reversed(far)] + far + [-1, 0, 1]


def meet_rows(rows):
    me, core = lax.axis_index("rows"), lax.axis_index("tensor")
    barrier = pltpu.get_barrier_semaphore()

    def greet(step, carry):
        pl.semaphore_signal(
            barrier, inc=1, device_id=(lax.rem(me + step, rows), core), device_id_type=MESH
        )
        return carry

    lax.fori_loop(1, rows, greet, 0)
    pl.semaphore_signal(barrier, inc=1, device_id=(me, 1 - core), device_id_type=MESH)
    pl.semaphore_wait(barrier, rows)


def send(src, dst, send_sem, recv_sem, target):
    return pltpu.make_async_remote_copy(
        src_ref=src,
        dst_ref=dst,
        send_sem=send_sem,
        recv_sem=recv_sem,
        device_id=target,
        device_id_type=MESH,
    )


class Window:
    def __init__(self, rows, offsets):
        self.rows, self.offsets = rows, offsets
        self.me, self.core = lax.axis_index("rows"), lax.axis_index("tensor")
        self.slot = {offset: number for number, offset in enumerate(offsets)}
        self.own = self.slot[0]
        side = rows // HI
        self.low = lax.rem(self.me, side)
        self.first, self.second, self.third = [], {}, []
        self.awaited = {}
        if side != 4:
            self.first = [(self.inside(d), self.own, d, self.slot[-d]) for d in offsets if d]
            self.number_all()
            return
        both = jnp.logical_and
        along_x = {1: lax.rem(self.low, 2) == 0, -1: lax.rem(self.low, 2) == 1}
        along_y = {2: self.low < 2, -2: self.low >= 2}
        beside = [*along_x.items(), *along_y.items()]
        for d in (side, -side):
            self.first.append((self.inside(d), self.own, d, self.slot[-d]))
        for step, when in beside:
            self.first.append((when, self.own, step, self.slot[-step]))
        for d in offsets:
            if abs(d) > side:
                when = self.low + d >= 2 * side if d > 0 else self.low + d < -side
                self.first.append((both(when, self.inside(d)), self.own, d, self.slot[-d]))
        for d in (side, -side):
            self.awaited[d] = [self.inside(d)]
            self.second[d] = [
                (when, self.slot[d], step, self.slot[d - step])
                for step, when in beside
                if d - step in self.slot
            ]
        for step_x, when_x in along_x.items():
            for step_y, when_y in along_y.items():
                when = both(when_x, when_y)
                entry = (when, self.slot[step_y], step_x, self.slot[step_y - step_x])
                self.third.append((step_y, entry))
                for d in (side, -side):
                    came = d + step_x
                    if came - step_y in self.slot:
                        there = both(when, self.inside(d))
                        entry = (there, self.slot[came], step_y, self.slot[came - step_y])
                        self.third.append((came, entry))
        for came, entry in self.third:
            self.awaited.setdefault(came, []).append(entry[0])
        self.number_all()

    def number_all(self):
        entries = list(self.first)
        for later in self.second.values():
            entries += later
        entries += [entry for _, entry in self.third]
        self.entries = entries

    def inside(self, offset):
        if offset < 0:
            return self.me >= -offset
        return self.me < self.rows - offset

    def copy(self, ref, sems, entry):
        _, here, step, there = entry
        number = [other is entry for other in self.entries].index(True)
        target = (self.me + step, self.core)
        return send(
            ref.at[here], ref.at[there], sems.at[0, number], sems.at[1, there], target
        )

    def arrival(self, ref, sems, offset):
        place = ref.at[self.slot[offset]]
        other = (self.me, 1 - self.core)
        return send(place, place, sems.at[0, 0], sems.at[1, self.slot[offset]], other)

    def start(self, pairs):
        for entry in self.first:

            @pl.when(entry[0])
            def _():
                for ref, sems in pairs:
                    self.copy(ref, sems, entry).start()

    def relay(self, pairs):
        for offset, entries in self.second.items():

            @pl.when(self.inside(offset))
            def _():
                for ref, sems in pairs:
                    self.arrival(ref, sems, offset).wait_recv()

                for entry in entries:

                    @pl.when(entry[0])
                    def _():
                        for ref, sems in pairs:
                            self.copy(ref, sems, entry).start()

    def relay_diagonal(self, pairs):
        for offset, entry in self.third:

            @pl.when(entry[0])
            def _():
                for ref, sems in pairs:
                    self.arrival(ref, sems, offset).wait_recv()
                    self.copy(ref, sems, entry).start()

    def finish(self, pairs):
        for offset in self.offsets:
            if offset:
                waiting = self.inside(offset)
                for when in self.awaited.get(offset, ()):
                    waiting = jnp.logical_and(waiting, jnp.logical_not(when))

                @pl.when(waiting)
                def _():
                    for ref, sems in pairs:
                        self.arrival(ref, sems, offset).wait_recv()

        for entry in self.entries:
            when = entry[0]
            for offset, entries in self.second.items():
                if any(entry is other for other in entries):
                    when = jnp.logical_and(when, self.inside(offset))

            @pl.when(when)
            def _():
                for ref, sems in pairs:
                    self.copy(ref, sems, entry).wait_send()

    def clear(self, ref, value):
        for offset in self.offsets:
            if offset:

                @pl.when(jnp.logical_not(self.inside(offset)))
                def _():
                    ref[self.slot[offset]] = jnp.full(ref.shape[1:], value, ref.dtype)


EDGE = -(-LIMITS[-1] // 16) * 16


def near_bias(gap, table_ref, head, above, below):
    if above and below:
        bias = jnp.full(gap.shape, table_ref[head, 0], F32)
    else:
        bias = jnp.full(gap.shape, table_ref[head, HALF if above else 0], F32)
    for number, limit in enumerate(LIMITS):
        if above:
            bias = jnp.where(gap >= limit, table_ref[head, HALF + number + 1], bias)
        if below:
            bias = jnp.where(gap <= -limit, table_ref[head, number + 1], bias)
    return bias


def joined_row(facts_ref, slots, line, width):
    return jnp.concatenate([facts_ref[slot, line : line + 1, :width] for slot in slots], axis=1)


GELU_A = 0.7978845608028654
GELU_B = 0.044715


def split3(value):
    one = value.astype(BF16).astype(F32)
    rest = value - one
    two = rest.astype(BF16).astype(F32)
    return one, two, (rest - two).astype(BF16).astype(F32)


def stacked_rows(rows, width):
    line = lax.broadcasted_iota(jnp.int32, (8, width), 0)
    result = jnp.zeros((8, width), F32)
    for number, row in enumerate(rows):
        result = jnp.where(line == number, row, result)
    return result.astype(BF16)


def layer_kernel(
    rows,
    offsets,
    lengths_ref,
    table_ref,
    byte_ref,
    keep_ref,
    vec_ref,
    gcot_ref,
    wq_ref,
    wk_ref,
    wv_ref,
    wo_ref,
    wg_ref,
    wu_ref,
    wd_ref,
    cot_ref,
    gate_ref,
    block_ref,
    rows_ref,
    small_ref,
    ffo_ref,
    attg_ref,
    ffin_ref,
    count_ref,
    chosen_ref,
    ext_ref,
    extaux_ref,
    below_ref,
    above_ref,
    belowaux_ref,
    aboveaux_ref,
    packed_ref,
    aux_ref,
    first_ref,
    kv_ref,
    query_ref,
    facts_ref,
    dout_ref,
    facts2_ref,
    biasq_ref,
    biask_ref,
    att_ref,
    attf_ref,
    lse_ref,
    mixed_ref,
    sec_ref,
    cots_ref,
    wall_ref,
    wout_ref,
    wqkv_ref,
    mid_ref,
    dgated_ref,
    dupper_ref,
    part_ref,
    kept_ref,
    sout_ref,
    sin_ref,
    hout_ref,
    hin_ref,
    line_ref,
    dsec_ref,
    heads_ref,
    dgate_ref,
    zout_ref,
    zin_ref,
    yin_ref,
    fin_ref,
    slow_ref,
    shigh_ref,
    back_ref,
    backaux_ref,
    ffa_ref,
    ffb_ref,
    za_ref,
    zb_ref,
    count_sems,
    edge_sems,
    kv_sems,
    query_sems,
    facts_sems,
    dout_sems,
    facts2_sems,
    wall_sems,
    pair_sems,
    local_sems,
    cot_sems,
    cotf_sems,
    sec_sems,
    secf_sems,
    sib_sems,
    hi_sems,
    line_sems,
    half_sems,
    ff_sems,
    low_sems,
    high_sems,
    back_sems,
    last_sems,
    edge2_sems,
    slow_sems,
    shigh_sems,
):
    width, raw_count = byte_ref.shape
    own_rows = cot_ref.shape[0]
    inner = wq_ref.shape[0]
    heads = table_ref.shape[0]
    head_size = inner // heads
    share = wd_ref.shape[0]
    lows = rows // HI
    half = own_rows // 2
    ext_rows = own_rows + 2 * MARGIN
    me, core = lax.axis_index("rows"), lax.axis_index("tensor")
    high, low = lax.div(me, lows), lax.rem(me, lows)
    sibling = (me, 1 - core)
    mine = pl.ds(pl.multiple_of(core * half, half), half)
    theirs = pl.ds(pl.multiple_of((1 - core) * half, half), half)
    window = Window(rows, offsets)
    own = window.own
    g_delete, w_delete = vec_ref[0:1, :], vec_ref[1:2, :]
    g_attn, g_ff = vec_ref[2:3, :], vec_ref[3:4, :]

    is_square = lows == 4

    def low_other(step):
        if step == 1:
            return low + 1 - 2 * lax.rem(low, 2)
        if step == 2:
            return lax.rem(low + 2, lows)
        return lows - 1 - low

    def low_pair(step):
        return (high * lows + low_other(step), core)

    def low_peer(step):
        return (high * lows + lax.rem(low + step, lows), core)

    def low_source(step):
        return lax.rem(low + lows - step, lows)

    def high_other(step):
        if step == 0:
            return high
        if step == 1:
            return high + 1 - 2 * lax.rem(high, 2)
        if step == 2:
            return lax.rem(high + 2, HI)
        return HI - 1 - high

    def high_peer(step):
        return (high_other(step) * lows + low, core)

    middle_high = jnp.logical_and(high >= 1, high <= 2)
    end_high = jnp.logical_not(middle_high)
    upper_high = lax.div(high, 2)
    inner_high = high + 1 - 2 * upper_high
    outer_high = high - 1 + 2 * upper_high

    def line_chunk(turn):
        if turn == 0:
            return high
        if turn == 1:
            return 3 - 3 * upper_high
        if turn == 2:
            return 2 - upper_high
        return 1 - high + 4 * upper_high

    def first_half(count):
        return count // 2 // 16 * 16

    class LowGather:
        def __init__(self, source, block, count, sems):
            self.source, self.block, self.count, self.sems = source, block, count, sems
            cut = first_half(count)
            self.halves = ((0, cut), (cut, count - cut))

        def copy(self, src, dst, number, target):
            return send(src, dst, self.sems.at[0, number], self.sems.at[1, number], target)

        def direct(self, step):
            if is_square:
                target = low_pair(step)
            else:
                target = low_peer(step)
            return self.copy(self.source, self.block(low, 0, self.count), step, target)

        def arrival(self, step):
            place = self.block(low_other(step) if is_square else low_source(step), 0, self.count)
            return self.copy(place, place, step, sibling)

        def passed(self, side):
            place = self.block(low_other(2 - side), *self.halves[side])
            return self.copy(place, place, 3 + side, low_pair(1 + side))

        def start(self):
            if is_square:
                self.direct(1).start()
                self.direct(2).start()
                return

            def one(step, carry):
                self.direct(step).start()
                return carry

            lax.fori_loop(1, lows, one, 0)

        def relay(self):
            if is_square:
                for side in (1, 0):
                    self.arrival(2 - side).wait_recv()
                    self.passed(side).start()

        def finish(self):
            if is_square:
                for step in (1, 2):
                    self.direct(step).wait_send()
                for side in range(2):
                    self.passed(side).wait_send()
                    place = self.block(low_other(3), *self.halves[side])
                    self.copy(place, place, 3 + side, sibling).wait_recv()
                return

            def one(step, carry):
                self.direct(step).wait_send()
                self.arrival(step).wait_recv()
                return carry

            lax.fori_loop(1, lows, one, 0)

    class LowReduce:
        def __init__(self, part, count, relays, arrivals, sems):
            self.part, self.count, self.sems = part, count, sems
            self.relays, self.arrivals = relays, arrivals
            cut = first_half(count)
            self.halves = ((0, cut), (cut, count - cut))

        def copy(self, src, dst, number, target):
            return send(src, dst, self.sems.at[0, number], self.sems.at[1, number], target)

        def half(self, side):
            return self.copy(
                self.part(low_other(3), *self.halves[side]),
                self.relays[side],
                side,
                low_pair(2 - side),
            )

        def summed(self, side):
            return self.copy(
                self.part(low_other(1 + side), 0, self.count),
                self.arrivals.at[side],
                2 + side,
                low_pair(1 + side),
            )

        def direct(self, step):
            return self.copy(
                self.part(lax.rem(low + step, lows), 0, self.count),
                self.arrivals.at[step],
                step,
                low_peer(step),
            )

        def start(self):
            if is_square:
                for side in range(2):
                    self.half(side).start()
                return

            def one(step, carry):
                self.direct(step).start()
                return carry

            lax.fori_loop(1, lows, one, 0)

        def relay(self):
            if is_square:
                for side in range(2):
                    self.half(side).wait()
                    mine_too = self.part(low_other(1 + side), *self.halves[side])
                    both = mine_too[...].astype(F32) + self.relays[side][...].astype(F32)
                    mine_too[...] = both.astype(BF16)
                    self.summed(side).start()

        def finish(self):
            if is_square:
                for side in range(2):
                    self.summed(side).wait()
                return

            def one(step, carry):
                self.direct(step).wait()
                return carry

            lax.fori_loop(1, lows, one, 0)

    arrived = range(2) if is_square else range(1, lows)

    meet_rows(rows)

    keep = keep_ref[...].astype(F32)
    count_ref[me] = jnp.broadcast_to(jnp.sum(keep, axis=1, keepdims=True), (8, 128))

    def count_copy(step):
        return send(
            count_ref.at[me],
            count_ref.at[me],
            count_sems.at[0, step],
            count_sems.at[1, step],
            (lax.rem(me + step, rows), core),
        )

    def count_arrival(step):
        source = lax.rem(me + rows - step, rows)
        return send(
            count_ref.at[source],
            count_ref.at[source],
            count_sems.at[0, step],
            count_sems.at[1, step],
            (source, core),
        )

    def start_count(step, carry):
        count_copy(step).start()
        return carry

    lax.fori_loop(1, rows, start_count, 0)

    weight_refs = (wg_ref, wu_ref, wd_ref)
    my_share = pl.ds(pl.multiple_of(low * share, share), share)
    locals_early = [
        pltpu.make_async_copy(ref, wqkv_ref.at[core, number], local_sems.at[number])
        for number, ref in enumerate((wq_ref, wk_ref, wv_ref))
    ]
    locals_late = [
        pltpu.make_async_copy(wo_ref, wout_ref.at[core], local_sems.at[3]),
        pltpu.make_async_copy(cot_ref, cots_ref.at[high], local_sems.at[4]),
    ] + [
        pltpu.make_async_copy(ref, wall_ref.at[number, my_share], local_sems.at[5 + number])
        for number, ref in enumerate(weight_refs)
    ]
    for copy in locals_early + locals_late:
        copy.start()

    def wall_gather(place, number, start, size):
        def block(place, begin, count):
            inside = pl.ds(pl.multiple_of(place * share + start + begin, 16), count)
            return wall_ref.at[number, inside]

        source = weight_refs[number].at[pl.ds(start, size)]
        return LowGather(source, block, size, wall_sems.at[place])

    early = share * 3 // 7 // 16 * 16
    wall_cuts = [(2, 0, early), (2, early, share - early), (0, 0, share), (1, 0, share)]
    walls = [
        wall_gather(place, *cut) if cut[2] else None for place, cut in enumerate(wall_cuts)
    ]

    class Gather:
        def __init__(self, ref, sems, sems_f, offset, count, source=None):
            self.ref, self.sems, self.sems_f = ref, sems, sems_f
            self.part = pl.ds(pl.multiple_of(core * half + offset, 16), count)
            self.other = pl.ds(pl.multiple_of((1 - core) * half + offset, 16), count)
            self.source = ref.at[high] if source is None else source

        def direct(self, step):
            return send(
                self.source.at[self.part],
                self.ref.at[high, self.part],
                self.sems.at[0, step],
                self.sems.at[1, step],
                high_peer(step),
            )

        def arrival(self, step):
            place = self.ref.at[high_other(step), self.part]
            return send(
                place, place, self.sems.at[0, step], self.sems.at[1, step], high_peer(step)
            )

        def relay(self):
            place = self.ref.at[high_other(2), self.part]
            return send(place, place, self.sems.at[0, 0], self.sems.at[1, 3], high_peer(1))

        def forward(self, step, part):
            place = self.ref.at[high_other(step), part]
            return send(
                place, place, self.sems_f.at[0, step], self.sems_f.at[1, step], sibling
            )

        def start(self):
            self.direct(1).start()
            self.direct(2).start()

            @pl.when(middle_high)
            def _():
                self.direct(3).start()

        def arrived(self, step):
            self.arrival(step).wait_recv()
            if step == 2:

                @pl.when(middle_high)
                def _():
                    self.relay().start()

            self.forward(step, self.part).start()

        def forwarded(self, step):
            self.forward(step, self.other).wait_recv()

        def close(self):
            self.direct(1).wait_send()
            self.direct(2).wait_send()

            @pl.when(middle_high)
            def _():
                self.direct(3).wait_send()
                self.relay().wait_send()

            for step in range(1, HI):
                self.forward(step, self.part).wait_send()

    third = half // 3 // 16 * 16
    cot_gathers = [
        Gather(cots_ref, cot_sems.at[number], cotf_sems.at[number], begin, count, cot_ref)
        for number, (begin, count) in enumerate(((0, third), (third, half - third)))
    ]
    sec_gather = Gather(sec_ref, sec_sems, secf_sems, 0, half)

    if early:
        walls[0].start()
    cot_gathers[0].start()
    pair_early = [
        send(wo_ref, wout_ref.at[core], pair_sems.at[0, 0], pair_sems.at[1, 0], sibling)
    ] + [
        send(
            ref,
            wqkv_ref.at[core, number],
            pair_sems.at[0, 1 + number],
            pair_sems.at[1, 1 + number],
            sibling,
        )
        for number, ref in enumerate((wq_ref, wk_ref, wv_ref))
    ]
    for copy in pair_early:
        copy.start()

    gate_weight = g_delete * w_delete
    raw = byte_ref[...]
    raw_f = raw.astype(F32)
    raw_scale = lax.rsqrt(jnp.mean(raw_f * raw_f, axis=0, keepdims=True) + EPS)
    raw_logit = raw_scale * jnp.sum(
        nn(stacked_rows(split3(gate_weight), width), raw), axis=0, keepdims=True
    )
    gate_ref[...] = DELETE_SCALE * sigmoid(raw_logit)
    upper = lax.broadcasted_iota(jnp.int32, (raw_count, raw_count), 0) <= lax.broadcasted_iota(
        jnp.int32, (raw_count, raw_count), 1
    )
    rank = nn(keep.astype(BF16), jnp.where(upper, 1.0, 0.0).astype(BF16)) - 1.0
    lane = lax.broadcasted_iota(jnp.int32, (raw_count, 128), 1)
    local = lax.broadcasted_iota(jnp.int32, (raw_count, 128), 0).astype(F32)
    aux = jnp.where(lane == 0, local, jnp.where(lane == 1, me.astype(F32), 0.0)).astype(BF16)
    window.clear(kv_ref, 0.0)
    window.clear(query_ref, 0.0)
    window.clear(facts_ref, -1.0)
    window.clear(dout_ref, 0.0)
    window.clear(facts2_ref, 0.0)

    def finish_count(step, carry):
        count_copy(step).wait_send()
        count_arrival(step).wait_recv()
        return carry

    lax.fori_loop(1, rows, finish_count, 0)
    lower = lax.broadcasted_iota(jnp.int32, count_ref.shape, 0) < me
    before = jnp.sum(jnp.where(lower, count_ref[...], 0.0), axis=0)[0:1, 0:1]
    place = before + rank - (me * own_rows).astype(F32)
    place = jnp.where(keep > 0.0, place, -4096.0).astype(jnp.int32)
    chosen = place + MARGIN == lax.broadcasted_iota(jnp.int32, (ext_rows, raw_count), 0)
    chosen = jnp.where(chosen, 1.0, 0.0).astype(BF16)
    chosen_ref[...] = chosen
    ext_ref[...] = nt(chosen, raw).astype(BF16)
    extaux_ref[...] = nn(chosen, aux).astype(BF16)

    def edges(sems, downs, ups):
        def copies(pairs, offset):
            return [
                send(src, dst, sems.at[0, number], sems.at[1, number], (me + offset, core))
                for number, src, dst in pairs
            ]

        def start():
            @pl.when(me > 0)
            def _():
                for copy in copies(downs, -1):
                    copy.start()

            @pl.when(me < rows - 1)
            def _():
                for copy in copies(ups, 1):
                    copy.start()

        def finish():
            @pl.when(me > 0)
            def _():
                for copy in copies(downs, -1):
                    copy.wait_send()
                for copy in copies(ups, 1):
                    copy.wait_recv()

            @pl.when(me < rows - 1)
            def _():
                for copy in copies(ups, 1):
                    copy.wait_send()
                for copy in copies(downs, -1):
                    copy.wait_recv()

        return start, finish

    first_rows, last_rows = pl.ds(0, MARGIN), pl.ds(own_rows + MARGIN, MARGIN)
    start_edges, finish_edges = edges(
        edge_sems,
        [
            (0, ext_ref.at[first_rows], above_ref),
            (1, extaux_ref.at[first_rows], aboveaux_ref),
        ],
        [
            (2, ext_ref.at[last_rows], below_ref),
            (3, extaux_ref.at[last_rows], belowaux_ref),
        ],
    )
    start_edges()

    @pl.when(me == 0)
    def _():
        below_ref[...] = jnp.zeros(below_ref.shape, BF16)
        belowaux_ref[...] = jnp.zeros(belowaux_ref.shape, BF16)

    @pl.when(me == rows - 1)
    def _():
        above_ref[...] = jnp.zeros(above_ref.shape, BF16)
        aboveaux_ref[...] = jnp.zeros(aboveaux_ref.shape, BF16)

    packed_ref[...] = ext_ref[MARGIN : MARGIN + own_rows, :]
    aux_ref[...] = extaux_ref[MARGIN : MARGIN + own_rows, :].astype(F32)
    for copy in locals_early:
        copy.wait()
    finish_edges()
    top = own_rows - MARGIN
    packed_ref[0:MARGIN, :] = packed_ref[0:MARGIN, :] + below_ref[...]
    packed_ref[top:, :] = packed_ref[top:, :] + above_ref[...]
    aux_ref[0:MARGIN, :] = aux_ref[0:MARGIN, :] + belowaux_ref[...].astype(F32)
    aux_ref[top:, :] = aux_ref[top:, :] + aboveaux_ref[...].astype(F32)

    packed = packed_ref[...].astype(F32)
    scale = row_scale(packed)
    first = (packed * scale * g_attn).astype(BF16)
    first_ref[...] = first
    kv_ref[own, :, 0:inner] = nt(first, wqkv_ref[core, 1]).astype(BF16)
    kv_ref[own, :, inner : 2 * inner] = nt(first, wqkv_ref[core, 2]).astype(BF16)

    gate = DELETE_SCALE * sigmoid(gate_logit(packed, scale, gate_weight))
    ids = aux_ref[:, 0:1] + raw_count * aux_ref[:, 1:2]
    ids_i = ids.astype(jnp.int32)
    starts = jnp.zeros_like(ids_i)
    end = jnp.int32(0)
    for number in range(lengths_ref.shape[0]):
        end = end + lengths_ref[number]
        starts = jnp.where(ids_i >= end, end, starts)
    starts = starts.astype(F32)
    own_eye = eye(own_rows)
    facts_ref[own] = jnp.zeros(facts_ref.shape[1:], F32)
    facts_ref[own, 0:1, 0:own_rows] = to_row(gate, own_eye)
    facts_ref[own, 1:2, 0:own_rows] = to_row(ids, own_eye)
    facts_ref[own, 2:3, 0:own_rows] = to_row(starts, own_eye)
    window.start([(facts_ref, facts_sems), (kv_ref, kv_sems)])
    cot_gathers[1].start()
    query_ref[own] = nt(first, wqkv_ref[core, 0]).astype(BF16)

    far = (len(offsets) - 3) // 2
    segments = (range(0, far), range(far, 2 * far), range(2 * far, 2 * far + 3))
    def add_near(added_ref, slot, rows_at, gap, extra, allowed, above, below):
        place = 1 + slot
        lanes_at = slice(place * own_rows, (place + 1) * own_rows)
        for head in range(heads):
            if rows_at is not None:
                rest = table_ref[head, 2 * HALF - 1 if above else HALF - 1]
                added_ref[head, :, lanes_at] = jnp.where(allowed, rest + extra, NEGATIVE)
            cut = slice(0, own_rows) if rows_at is None else rows_at
            bias = near_bias(gap[cut], table_ref, head, above, below)
            more = extra if extra.shape[0] == 1 else extra[cut]
            added_ref[head, cut, lanes_at] = jnp.where(allowed[cut], bias + more, NEGATIVE)

    def fact(slot, line):
        at = window.slot[slot]
        return facts_ref[at, line : line + 1, :own_rows]

    border = {-1: slice(0, EDGE), 0: None, 1: slice(own_rows - EDGE, own_rows)}

    def near_queries(slot):
        gap, allowed = fact(slot, 1) - ids, fact(slot, 2) == starts
        add_near(
            biasq_ref, slot, border[slot], gap, fact(slot, 0), allowed, slot >= 0, slot <= 0
        )

    def near_keys(slot):
        gap, allowed = ids - fact(slot, 1), fact(slot, 2) == starts
        add_near(biask_ref, slot, border[slot], gap, gate, allowed, slot <= 0, slot >= 0)

    near_queries(0)
    window_early = [(facts_ref, facts_sems), (kv_ref, kv_sems)]
    window.relay(window_early)
    window.relay_diagonal(window_early)
    walls[1].start()
    walls[2].start()
    window.finish(window_early)
    near_queries(-1)
    near_queries(1)
    walls[3].start()
    if early:
        walls[0].relay()

    def spans(segment):
        return slice(segment[0], segment[-1] + 1)

    def far_added(segment, column):
        allowed = joined_row(facts_ref, segment, 2, own_rows) == starts
        return jnp.where(allowed, column, NEGATIVE)

    added = [
        far_added(segment, joined_row(facts_ref, segment, 0, own_rows)) for segment in segments[:2]
    ]
    fixed = (HALF - 1, 2 * HALF - 1)
    lanes = lax.broadcasted_iota(jnp.int32, lse_ref.shape, 1)
    lse_all = jnp.zeros(lse_ref.shape, F32)
    for head in range(heads):
        cut = slice(head * head_size, (head + 1) * head_size)
        cut_v = slice(inner + head * head_size, inner + (head + 1) * head_size)
        query = query_ref[own, :, cut]
        parts = []
        for number, segment in enumerate(segments):
            keys = kv_ref[spans(segment), :, cut].reshape(-1, head_size)
            if number < 2:
                extra = added[number] + table_ref[head, fixed[number]]
            else:
                extra = biasq_ref[head]
            parts.append(nt(query, keys) + extra)
        most = jnp.max(parts[0], axis=1, keepdims=True)
        for part in parts[1:]:
            most = jnp.maximum(most, jnp.max(part, axis=1, keepdims=True))
        expos = [jnp.exp(part - most) for part in parts]
        total = sum(jnp.sum(expo, axis=1, keepdims=True) for expo in expos)
        lse_all = jnp.where(lanes == head, most + jnp.log(total), lse_all)
        attended = jnp.zeros((own_rows, head_size), F32)
        for segment, expo in zip(segments, expos):
            values = kv_ref[spans(segment), :, cut_v].reshape(-1, head_size)
            attended = attended + nn((expo / total).astype(BF16), values)
        attf_ref[:, cut] = attended
        att_ref[core, :, cut] = attended.astype(BF16)
    lse_ref[...] = lse_all

    att_copy = send(
        att_ref.at[core], att_ref.at[core], pair_sems.at[0, 4], pair_sems.at[1, 4], sibling
    )
    att_copy.start()
    for copy in locals_late:
        copy.wait()
    for copy in pair_early:
        copy.wait()
    att_copy.wait()
    mixed = packed_ref[...].astype(F32) + (nn(att_ref[0], wout_ref[0]) + nn(att_ref[1], wout_ref[1]))
    mixed_ref[...] = mixed
    sec_ref[high] = (mixed * row_scale(mixed) * g_ff).astype(BF16)
    sec_gather.start()

    walls[1].relay()
    walls[2].relay()
    for gather in cot_gathers:
        gather.arrived(1)
        gather.arrived(2)
    walls[3].relay()
    sec_gather.arrived(1)
    sec_gather.arrived(2)
    for wall in walls[0 if early else 1 :]:
        wall.finish()

    def sib_copy(kind, step):
        return send(
            sout_ref.at[step],
            sin_ref.at[kind, step],
            sib_sems.at[0, kind, step],
            sib_sems.at[1, kind, step],
            sibling,
        )

    def hi_copy(kind, step):
        return send(
            hout_ref.at[kind, step - 1],
            hin_ref.at[step - 1],
            hi_sems.at[0, step],
            hi_sems.at[1, step],
            high_peer(step),
        )

    def hand_over(kind, step, value):
        part_ref[...] = value
        sout_ref[step] = part_ref[theirs, :].astype(BF16)
        kept_ref[kind if step == 0 else 2 + step % 2] = part_ref[mine, :]
        sib_copy(kind, step).start()

    def pass_on(kind, step):
        sib_copy(kind, step).wait()
        both = kept_ref[2 + step % 2] + sin_ref[kind, step].astype(F32)
        hout_ref[kind, step - 1] = both.astype(BF16)

    def chunk_rows(chunk):
        return pl.ds(pl.multiple_of(chunk * own_rows, own_rows), own_rows)

    def line_copy(turn, middle):
        slot, target = turn - 1, inner_high
        if middle:
            slot = (3, 4, 0)[turn - 1]
            target = outer_high if turn == 3 else inner_high
        return send(
            hout_ref.at[0, turn - 1],
            line_ref.at[slot],
            line_sems.at[0, turn],
            line_sems.at[1, slot],
            (target * lows + low, core),
        )

    def line_arrived(slot):
        place = line_ref.at[slot]
        send(place, place, line_sems.at[0, 0], line_sems.at[1, slot], sibling).wait_recv()

    def ship_end(turn):
        @pl.when(end_high)
        def _():
            hout_ref[0, turn - 1] = kept_ref[1 + turn].astype(BF16)
            line_copy(turn, False).start()

    def ship_middle(turn):
        @pl.when(middle_high)
        def _():
            slot = (0, 1, 3)[turn - 1]
            line_arrived(slot)
            total = kept_ref[1 + turn] + line_ref[slot].astype(F32)
            hout_ref[0, turn - 1] = total.astype(BF16)
            line_copy(turn, True).start()

    for step in range(HI):
        if step:
            for gather in cot_gathers + [sec_gather]:
                if step == HI - 1:
                    gather.arrived(step)
                gather.forwarded(step)
        chunk = high_other(step)
        second = sec_ref[chunk]
        gated = nt(second, wall_ref[0])
        upper = nt(second, wall_ref[1])
        d_middle = nt(cots_ref[chunk], wall_ref[2])
        square = gated * gated
        bend = jnp.tanh(GELU_A * gated * (1.0 + GELU_B * square))
        lift = 0.5 * (1.0 + bend)
        slope = lift + 0.5 * gated * (1.0 - bend * bend) * (
            GELU_A * (1.0 + 3.0 * GELU_B * square)
        )
        gelu = gated * lift
        d_gated = (d_middle * upper * slope).astype(BF16)
        d_upper = (d_middle * gelu).astype(BF16)
        mid_ref[chunk_rows(chunk), :] = (gelu * upper).astype(BF16)
        dgated_ref[chunk_rows(chunk), :] = d_gated
        dupper_ref[chunk_rows(chunk), :] = d_upper
        hand_over(1, step, nn(d_gated, wall_ref[0]) + nn(d_upper, wall_ref[1]))
        if step == 0:
            window.start([(query_ref, query_sems)])
        if step == 2:
            window.relay([(query_ref, query_sems)])
        if step > 1:
            pass_on(1, step - 1)
            hi_copy(1, step - 1).start()
    pass_on(1, HI - 1)
    hi_copy(1, HI - 1).start()
    for gather in cot_gathers + [sec_gather]:
        gather.close()

    def ff_reduce(number):
        def part(place, begin, count):
            inside = pl.ds(pl.multiple_of(place * share + begin, 16), count)
            return wall_ref.at[number, inside]

        relays = (ffa_ref.at[number], ffb_ref.at[number])
        return LowReduce(part, share, relays, ffin_ref.at[number], ff_sems.at[number])

    reduces = [ff_reduce(number) for number in range(3)]
    hidden = wall_ref.shape[1]

    def weight_grad(number, left_ref, right_ref):
        for begin in range(0, hidden, 256):
            units = slice(begin, min(begin + 256, hidden))
            right = right_ref[...].reshape(HI * own_rows, width)
            wall_ref[number, units, :] = tn(left_ref[:, units], right).astype(BF16)

    weight_grad(0, dgated_ref, sec_ref)
    reduces[0].start()
    weight_grad(1, dupper_ref, sec_ref)
    reduces[1].start()
    window.relay_diagonal([(query_ref, query_sems)])
    sib_copy(1, 0).wait()
    for turn in (1, 2, 3, 0):
        part_ref[...] = nn(mid_ref[chunk_rows(line_chunk(turn)), :], wall_ref[2])
        sout_ref[turn] = part_ref[theirs, :].astype(BF16)
        kept_ref[1 + turn if turn else 0] = part_ref[mine, :]
        sib_copy(0, turn).start()
        if turn != 1:
            before = turn - 1 if turn else HI - 1
            sib_copy(0, before).wait()
            kept_ref[1 + before] = kept_ref[1 + before] + sin_ref[0, before].astype(F32)
    reduces[0].relay()
    weight_grad(2, mid_ref, cots_ref)
    reduces[1].relay()

    for slot in (-1, 0, 1):
        near_keys(slot)
    total = kept_ref[1] + sin_ref[1, 0].astype(F32)
    for step in range(1, HI):
        hi_copy(1, step).wait()
        total = total + hin_ref[step - 1].astype(F32)
    dsec_ref[mine, :] = total
    dsec_copy = send(
        dsec_ref.at[mine], dsec_ref.at[mine], half_sems.at[0, 0], half_sems.at[1, 0], sibling
    )
    dsec_copy.start()
    dsec_copy.wait()

    back, g_ff_grad = norm_back(mixed_ref[...], g_ff, dsec_ref[...])
    d_mixed = cots_ref[high].astype(F32) + back
    part_ref[...] = d_mixed
    d_branch = d_mixed.astype(BF16)
    d_att = nt(d_branch, wout_ref[core]).astype(BF16)
    dout_ref[own] = d_att
    facts2_ref[own] = jnp.zeros(facts2_ref.shape[1:], F32)
    deltas = []
    products = d_att.astype(F32) * attf_ref[...]
    for head in range(heads):
        cut = slice(head * head_size, (head + 1) * head_size)
        delta = jnp.sum(products[:, cut], axis=1, keepdims=True)
        deltas.append(delta)
        facts2_ref[own, head : head + 1, 0:own_rows] = to_row(delta, own_eye)
        line = 4 + head
        facts2_ref[own, line : line + 1, 0:own_rows] = to_row(
            lse_ref[:, head : head + 1], own_eye
        )
    window.start([(facts2_ref, facts2_sems), (dout_ref, dout_sems)])
    for turn in range(1, HI):
        ship_end(turn)

    groups = zout_ref.shape[0]
    piece = zout_ref.shape[2]
    lanes_all = zout_ref.shape[3]
    quarter = lanes_all // HI

    def keep_pieces(number, value):
        for begin in range(0, inner, piece):
            group, place = divmod((number * inner + begin) // piece, lows)
            block = value[begin : begin + piece, :]
            zout_ref[group, place, :, 0:width] = block.astype(BF16)

    def quarter_of(place):
        return pl.ds(pl.multiple_of(place * quarter, 128), quarter)

    def low_sum(group):
        def part(place, begin, count):
            return zout_ref.at[group, place, pl.ds(begin, count)]

        relays = (za_ref.at[group], zb_ref.at[group])
        return LowReduce(part, piece, relays, zin_ref.at[group], low_sems.at[group])

    lows_sum = [low_sum(group) for group in range(groups)]
    early_groups, late_groups = range(groups // 2), range(groups // 2, groups)

    def high_copy(group, step, place):
        return send(
            zout_ref.at[group, low, :, quarter_of(high_other(step))],
            yin_ref.at[group, place],
            high_sems.at[0, group, step],
            high_sems.at[1, group, step],
            high_peer(step),
        )

    def share_low(group):
        lows_sum[group].finish()
        total = zout_ref[group, low].astype(F32)
        for number in arrived:
            total = total + zin_ref[group, number].astype(F32)
        zout_ref[group, low] = total.astype(BF16)
        for step in range(1, HI):
            high_copy(group, step, high).start()

    def back_copy(group, step, place):
        lanes_at = (group, slice(None), quarter_of(place))
        return send(
            fin_ref.at[lanes_at],
            fin_ref.at[lanes_at],
            back_sems.at[0, group, step],
            back_sems.at[1, group, step],
            high_peer(step),
        )

    def share_high(group):
        for step in range(1, HI):
            high_copy(group, step, high).wait_send()
            high_copy(group, step, high_other(step)).wait_recv()
        yin_ref[group, high] = zout_ref[group, low, :, quarter_of(high)]
        total = yin_ref[group, 0].astype(F32)
        for number in range(1, HI):
            total = total + yin_ref[group, number].astype(F32)
        fin_ref[group, :, quarter_of(high)] = total.astype(BF16)
        for step in range(1, HI):
            back_copy(group, step, high).start()

    def last_gather(group):
        def block(place, begin, count):
            return attg_ref.at[group, place, pl.ds(begin, count)]

        return LowGather(fin_ref.at[group], block, piece, last_sems.at[group])

    lasts = [last_gather(group) for group in range(groups)]
    own_lasts = [
        pltpu.make_async_copy(
            fin_ref.at[group], attg_ref.at[group, low], local_sems.at[8 + group]
        )
        for group in range(groups)
    ]

    def spread_low(group):
        for step in range(1, HI):
            back_copy(group, step, high).wait_send()
            back_copy(group, step, high_other(step)).wait_recv()
        lasts[group].start()
        own_lasts[group].start()

    if lanes_all > width:
        zout_ref[:, :, :, width:] = jnp.zeros(zout_ref.shape[:3] + (lanes_all - width,), BF16)
    keep_pieces(0, tn(att_ref[core], d_branch))

    lane = lax.broadcasted_iota(jnp.int32, (1, width), 1)
    bias_grad = jnp.zeros((1, width), F32)

    def add_bias(bias_grad, head, bucket, value):
        return bias_grad + jnp.where(lane == head * 2 * HALF + bucket, value, 0.0)

    def total_of(value):
        return jnp.sum(jnp.sum(value, axis=0, keepdims=True), axis=1, keepdims=True)

    for head in range(heads):
        cut = slice(head * head_size, (head + 1) * head_size)
        cut_v = slice(inner + head * head_size, inner + (head + 1) * head_size)
        query, d_head = query_ref[own, :, cut], dout_ref[own, :, cut]
        lse = lse_ref[:, head : head + 1]
        d_query = jnp.zeros((own_rows, head_size), F32)
        for number, segment in enumerate(segments):
            keys = kv_ref[spans(segment), :, cut].reshape(-1, head_size)
            values = kv_ref[spans(segment), :, cut_v].reshape(-1, head_size)
            if number < 2:
                extra = added[number] + table_ref[head, fixed[number]]
            else:
                extra = biasq_ref[head]
            probs = jnp.exp(nt(query, keys) + extra - lse)
            d_scores = probs * (nt(d_head, values) - deltas[head])
            d_query = d_query + nn(d_scores.astype(BF16), keys)
            if number < 2:
                bias_grad = add_bias(bias_grad, head, fixed[number], total_of(d_scores))
                continue
            for slot in (-1, 0, 1):
                lanes_at = slice((1 + slot) * own_rows, (2 + slot) * own_rows)
                block = d_scores[:, lanes_at]
                gap = fact(slot, 1) - ids
                whole = total_of(block)
                rows_at = border[slot]
                if rows_at is not None:
                    block, gap = block[rows_at], gap[rows_at]
                for sign in (1, -1):
                    if sign * slot < 0:
                        continue
                    base = HALF if sign > 0 else 0
                    sums = [
                        total_of(jnp.where(sign * gap >= limit, block, 0.0)) for limit in LIMITS
                    ]
                    if slot:
                        sums = [whole] + [value + (whole - total_of(block)) for value in sums[1:]]
                    whole = whole - sums[0]
                    for place in range(len(LIMITS)):
                        value = sums[place]
                        if place + 1 < len(LIMITS):
                            value = value - sums[place + 1]
                        bias_grad = add_bias(bias_grad, head, base + place + 1, value)
                if not slot:
                    bias_grad = add_bias(bias_grad, head, 0, whole)
        heads_ref[core, 0, :, cut] = d_query.astype(BF16)
        if head == 1:
            window.relay([(facts2_ref, facts2_sems), (dout_ref, dout_sems)])
            ship_middle(1)

    window.relay_diagonal([(facts2_ref, facts2_sems), (dout_ref, dout_sems)])
    ship_middle(2)
    keep_pieces(1, tn(heads_ref[core, 0], first_ref[...]))
    for group in early_groups:
        lows_sum[group].start()
    reduces[2].start()

    window_late = [(query_ref, query_sems), (facts2_ref, facts2_sems), (dout_ref, dout_sems)]
    window.finish(window_late)
    for group in early_groups:
        lows_sum[group].relay()
    ship_middle(3)
    d_gate = jnp.zeros((own_rows, 1), F32)
    added = [far_added(segment, gate) for segment in segments[:2]]
    fixed = (2 * HALF - 1, HALF - 1)
    for head in range(heads):
        cut = slice(head * head_size, (head + 1) * head_size)
        cut_v = slice(inner + head * head_size, inner + (head + 1) * head_size)
        key, value = kv_ref[own, :, cut], kv_ref[own, :, cut_v]
        d_key = jnp.zeros((own_rows, head_size), F32)
        d_value = jnp.zeros((own_rows, head_size), F32)
        for number, segment in enumerate(segments):
            queries = query_ref[spans(segment), :, cut].reshape(-1, head_size)
            d_heads = dout_ref[spans(segment), :, cut].reshape(-1, head_size)
            if number < 2:
                extra = added[number] + table_ref[head, fixed[number]]
            else:
                extra = biask_ref[head]
            lse = joined_row(facts2_ref, segment, 4 + head, own_rows)
            delta = joined_row(facts2_ref, segment, head, own_rows)
            probs = jnp.exp(nt(key, queries) + extra - lse)
            d_scores = probs * (nt(value, d_heads) - delta)
            d_value = d_value + nn(probs.astype(BF16), d_heads)
            d_key = d_key + nn(d_scores.astype(BF16), queries)
            d_gate = d_gate + jnp.sum(d_scores, axis=1, keepdims=True)
        heads_ref[core, 1, :, cut] = d_key.astype(BF16)
        heads_ref[core, 2, :, cut] = d_value.astype(BF16)
    dgate_ref[core] = jnp.broadcast_to(d_gate, dgate_ref.shape[1:])
    pair_late = [
        send(ref.at[core], ref.at[core], pair_sems.at[0, 5 + i], pair_sems.at[1, 5 + i], sibling)
        for i, ref in enumerate((heads_ref, dgate_ref))
    ]
    for copy in pair_late:
        copy.start()
    for number in range(2):
        keep_pieces(2 + number, tn(heads_ref[core, 1 + number], first_ref[...]))
    for group in late_groups:
        lows_sum[group].start()

    for copy in pair_late:
        copy.wait()
    d_first = jnp.zeros((own_rows, width), F32)
    for side in range(2):
        for number in range(3):
            d_first = d_first + nn(heads_ref[side, number], wqkv_ref[side, number])
    back, g_attn_grad = norm_back(packed_ref[...].astype(F32), g_attn, d_first)
    inside = slice(MARGIN, MARGIN + own_rows)
    back_ref[inside, :] = (part_ref[...] + back).astype(BF16)
    d_gate = dgate_ref[0] + dgate_ref[1]
    lane_g = lax.broadcasted_iota(jnp.int32, d_gate.shape, 1)
    terms = jnp.zeros(d_gate.shape, F32)
    for number, term in enumerate(split3(d_gate)):
        terms = jnp.where(lane_g == number, term, terms)
    backaux_ref[inside, :] = terms.astype(BF16)
    down_src, down_dst = pl.ds(MARGIN, MARGIN), pl.ds(own_rows + MARGIN, MARGIN)
    up_src, up_dst = pl.ds(own_rows, MARGIN), pl.ds(0, MARGIN)
    start_edges, finish_edges = edges(
        edge2_sems,
        [
            (0, back_ref.at[down_src], back_ref.at[down_dst]),
            (1, backaux_ref.at[down_src], backaux_ref.at[down_dst]),
        ],
        [
            (2, back_ref.at[up_src], back_ref.at[up_dst]),
            (3, backaux_ref.at[up_src], backaux_ref.at[up_dst]),
        ],
    )
    start_edges()

    @pl.when(me == 0)
    def _():
        back_ref[up_dst, :] = jnp.zeros((MARGIN, width), BF16)
        backaux_ref[up_dst, :] = jnp.zeros((MARGIN, 128), BF16)

    @pl.when(me == rows - 1)
    def _():
        back_ref[down_dst, :] = jnp.zeros((MARGIN, width), BF16)
        backaux_ref[down_dst, :] = jnp.zeros((MARGIN, 128), BF16)

    gate_s = sigmoid(raw_logit)
    gate_slope = DELETE_SCALE * gate_s * (1.0 - gate_s)
    raw_scaled = gcot_ref[...] * gate_slope * raw_scale
    common = jnp.sum(
        nt(stacked_rows(split3(raw_scaled), raw_count), byte_ref[...]), axis=0, keepdims=True
    )
    packed = packed_ref[...].astype(F32)
    scale = row_scale(packed)
    own_s = sigmoid(gate_logit(packed, scale, gate_weight))
    own_scaled = d_gate[:, 0:1] * (DELETE_SCALE * own_s * (1.0 - own_s)) * scale
    common = common + jnp.sum(own_scaled * packed, axis=0, keepdims=True)
    slow_ref[low, 0:1, :] = g_ff_grad
    slow_ref[low, 1:2, :] = g_attn_grad
    slow_ref[low, 2:3, :] = common * g_delete
    slow_ref[low, 3:4, :] = common * w_delete
    slow_ref[low, 4:5, :] = bias_grad
    slow_ref[low, 5:8, :] = jnp.zeros((3, width), F32)

    def slow_copy(step, source):
        return send(
            slow_ref.at[source],
            slow_ref.at[source],
            slow_sems.at[0, step],
            slow_sems.at[1, step],
            low_peer(step),
        )

    def start_slow(step, carry):
        slow_copy(step, low).start()
        return carry

    def finish_slow(step, carry):
        slow_copy(step, low).wait_send()
        slow_copy(step, low_source(step)).wait_recv()
        return carry

    def shigh_copy(step, source):
        return send(
            shigh_ref.at[source],
            shigh_ref.at[source],
            shigh_sems.at[0, step],
            shigh_sems.at[1, step],
            high_peer(step),
        )

    lax.fori_loop(1, lows, start_slow, 0)
    for group in early_groups:
        share_low(group)
    for group in late_groups:
        lows_sum[group].relay()
    reduces[2].relay()
    for group in early_groups:
        share_high(group)
    for group in late_groups:
        share_low(group)
    lax.fori_loop(1, lows, finish_slow, 0)
    small = slow_ref[0]
    for number in range(1, lows):
        small = small + slow_ref[number]
    shigh_ref[high] = small
    for step in range(1, HI):
        shigh_copy(step, high).start()
    for group in early_groups:
        spread_low(group)
    for group in late_groups:
        share_high(group)
    for group in early_groups:
        lasts[group].relay()
    for group in late_groups:
        spread_low(group)

    finish_edges()
    spread = tn(backaux_ref[...], chosen_ref[...])
    raw_cot = gcot_ref[...] + (spread[0:1, :] + spread[1:2, :] + spread[2:3, :])
    d_logit = raw_cot * gate_slope
    scaled = d_logit * raw_scale
    along = d_logit * raw_logit * raw_scale * raw_scale * (1.0 / width)
    s1, s2, s3 = split3(scaled)
    w1, w2, w3 = split3(gate_weight)
    outer = tn(
        stacked_rows((w1, w1, w2, w2, w1, w3), width),
        stacked_rows((s1, s2, s1, s2, s3, s1), raw_count),
    )
    rows_ref[...] = outer - along * byte_ref[...].astype(F32)
    rows_ref[...] = rows_ref[...] + tn(back_ref[...], chosen_ref[...])
    for step in range(1, HI):
        shigh_copy(step, high).wait_send()
        shigh_copy(step, high_other(step)).wait_recv()
    small = shigh_ref[0]
    for number in range(1, HI):
        small = small + shigh_ref[number]
    small_ref[...] = small

    sib_copy(0, 0).wait()
    part_ref[mine, :] = mixed_ref[mine, :] + (kept_ref[0] + sin_ref[0, 0].astype(F32))

    def add_line(middle):
        for slot in (2, 4) if middle else (0,):
            line_arrived(slot)
            part_ref[mine, :] = part_ref[mine, :] + line_ref[slot].astype(F32)
        for turn in range(1, HI):
            line_copy(turn, middle).wait_send()

    @pl.when(end_high)
    def _():
        add_line(False)

    @pl.when(middle_high)
    def _():
        add_line(True)

    block_ref[mine, :] = part_ref[mine, :].astype(BF16)
    block_copy = send(
        block_ref.at[mine], block_ref.at[mine], half_sems.at[0, 1], half_sems.at[1, 1], sibling
    )
    block_copy.start()

    def finish_reduce(number):
        reduces[number].finish()
        total = wall_ref[number, my_share, :].astype(F32)
        for begin in range(0, len(arrived), HI):
            loads = [
                pltpu.make_async_copy(
                    ffin_ref.at[number, slot],
                    sec_ref.at[place, pl.ds(0, share)],
                    local_sems.at[3 + place],
                )
                for place, slot in enumerate(arrived[begin : begin + HI])
            ]
            for load in loads:
                load.start()
            for load in loads:
                load.wait()
            for place in range(len(loads)):
                total = total + sec_ref[place, 0:share, :].astype(F32)
        ffo_ref[number] = total

    finish_reduce(0)
    finish_reduce(1)
    for group in late_groups:
        lasts[group].relay()
    finish_reduce(2)
    block_copy.wait()
    for group in range(groups):
        lasts[group].finish()
        own_lasts[group].wait()


def layer(rows, offsets, *operands):
    lengths, table, byte_t, keep, vecs, gcot, wq, wk, wv, wo, wg, wu, wd, cot = operands
    width, raw_count = byte_t.shape
    own_rows = cot.shape[0]
    inner = wq.shape[0]
    heads = table.shape[0]
    share = wd.shape[0]
    lows = rows // HI
    hidden = lows * share
    slots = len(offsets)
    half = own_rows // 2
    groups = 4 * inner // 128
    piece = 128 // lows
    lanes = -(-width // (128 * HI)) * 128 * HI
    slots_in = 2 if lows == 4 else lows
    window_sems = 3 * slots
    ff_cut, z_cut = share // 2 // 16 * 16, piece // 2 // 16 * 16
    ext_rows = own_rows + 2 * MARGIN
    vmem = pl.BlockSpec(memory_space=pltpu.VMEM)
    smem = pl.BlockSpec(memory_space=pltpu.SMEM)
    anywhere = pl.BlockSpec(memory_space=pl.ANY)
    shape = jax.ShapeDtypeStruct
    dma = pltpu.SemaphoreType.DMA
    outs = [
        shape((1, raw_count), F32),
        shape((own_rows, width), BF16),
        shape((width, raw_count), F32),
        shape((8, width), F32),
        shape((3, share, width), F32),
        shape((groups, lows, piece, lanes), BF16),
        shape((3, slots_in, share, width), BF16),
    ]
    out_specs = [vmem] * 5 + [anywhere] * 2
    scratch = [
        pltpu.VMEM((rows, 8, 128), F32),
        pltpu.VMEM((ext_rows, raw_count), BF16),
        pltpu.VMEM((ext_rows, width), BF16),
        pltpu.VMEM((ext_rows, 128), BF16),
        pltpu.VMEM((MARGIN, width), BF16),
        pltpu.VMEM((MARGIN, width), BF16),
        pltpu.VMEM((MARGIN, 128), BF16),
        pltpu.VMEM((MARGIN, 128), BF16),
        pltpu.VMEM((own_rows, width), BF16),
        pltpu.VMEM((own_rows, 128), F32),
        pltpu.VMEM((own_rows, width), BF16),
        pltpu.VMEM((slots, own_rows, 2 * inner), BF16),
        pltpu.VMEM((slots, own_rows, inner), BF16),
        pltpu.VMEM((slots, 8, 256), F32),
        pltpu.VMEM((slots, own_rows, inner), BF16),
        pltpu.VMEM((slots, 8, 256), F32),
        pltpu.VMEM((heads, own_rows, 3 * own_rows), F32),
        pltpu.VMEM((heads, own_rows, 3 * own_rows), F32),
        pltpu.VMEM((2, own_rows, inner), BF16),
        pltpu.VMEM((own_rows, inner), F32),
        pltpu.VMEM((own_rows, 128), F32),
        pltpu.VMEM((own_rows, width), F32),
        pltpu.VMEM((HI, own_rows, width), BF16),
        pltpu.VMEM((HI, own_rows, width), BF16),
        pltpu.VMEM((3, hidden, width), BF16),
        pltpu.VMEM((2, inner, width), BF16),
        pltpu.VMEM((2, 3, inner, width), BF16),
        pltpu.VMEM((HI * own_rows, hidden), BF16),
        pltpu.VMEM((HI * own_rows, hidden), BF16),
        pltpu.VMEM((HI * own_rows, hidden), BF16),
        pltpu.VMEM((own_rows, width), F32),
        pltpu.VMEM((5, half, width), F32),
        pltpu.VMEM((HI, half, width), BF16),
        pltpu.VMEM((2, HI, half, width), BF16),
        pltpu.VMEM((2, HI - 1, half, width), BF16),
        pltpu.VMEM((HI - 1, half, width), BF16),
        pltpu.VMEM((5, half, width), BF16),
        pltpu.VMEM((own_rows, width), F32),
        pltpu.VMEM((2, 3, own_rows, inner), BF16),
        pltpu.VMEM((2, own_rows, 128), F32),
        pltpu.VMEM((groups, lows, piece, lanes), BF16),
        pltpu.VMEM((groups, slots_in, piece, lanes), BF16),
        pltpu.VMEM((groups, HI, piece, lanes // HI), BF16),
        pltpu.VMEM((groups, piece, lanes), BF16),
        pltpu.VMEM((lows, 8, width), F32),
        pltpu.VMEM((HI, 8, width), F32),
        pltpu.VMEM((ext_rows, width), BF16),
        pltpu.VMEM((ext_rows, 128), BF16),
        pltpu.VMEM((3, max(ff_cut, 16), width), BF16),
        pltpu.VMEM((3, share - ff_cut, width), BF16),
        pltpu.VMEM((groups, max(z_cut, 16), lanes), BF16),
        pltpu.VMEM((groups, piece - z_cut, lanes), BF16),
        dma((2, rows)),
        dma((2, 4)),
        dma((2, window_sems)),
        dma((2, window_sems)),
        dma((2, window_sems)),
        dma((2, window_sems)),
        dma((2, window_sems)),
        dma((4, 2, max(5, lows))),
        dma((2, 7)),
        dma((8 + groups,)),
        dma((2, 2, HI)),
        dma((2, 2, HI)),
        dma((2, HI)),
        dma((2, HI)),
        dma((2, 2, HI)),
        dma((2, HI)),
        dma((2, 5)),
        dma((2, 2)),
        dma((3, 2, max(5, lows))),
        dma((groups, 2, max(5, lows))),
        dma((2, groups, HI)),
        dma((2, groups, HI)),
        dma((groups, 2, max(5, lows))),
        dma((2, 4)),
        dma((2, lows)),
        dma((2, HI)),
    ]
    return pl.pallas_call(
        functools.partial(layer_kernel, rows, offsets),
        name="layer",
        out_shape=outs,
        in_specs=[smem, smem] + [vmem] * 4 + [anywhere] * 8,
        out_specs=out_specs,
        scratch_shapes=scratch,
        compiler_params=pltpu.CompilerParams(
            collective_id=0, has_side_effects=True, vmem_limit_bytes=VMEM_LIMIT
        ),
    )(*operands)


def per_device(
    byte_rows,
    lengths,
    keep_mask,
    w_delete,
    g_delete,
    g_attn,
    w_query,
    w_key,
    w_value,
    w_out,
    rel_bias,
    g_ff,
    w_gate,
    w_up,
    w_down,
    out_cot,
    gate_cot,
):
    raw_count, width = byte_rows.shape
    own_rows = out_cot.shape[0]
    inner = w_query.shape[1]
    buckets, heads = rel_bias.shape
    rows = lax.axis_size("rows")
    share = w_down.shape[0]
    offsets = slots_of(reach_of(raw_count, own_rows))
    line = lax.broadcasted_iota(jnp.int32, (8, width), 0)
    vecs = jnp.zeros((8, width), F32)
    for number, vector in enumerate((g_delete, w_delete, g_attn, g_ff)):
        vecs = jnp.where(line == number, vector[None, :], vecs)
    spare = -share % 16
    weights = [jnp.pad(w, ((0, spare), (0, 0))) for w in (w_gate.T, w_up.T, w_down)]
    gate, block_out, grad_rows, small, ff_sums, att_grads, _ = layer(
        rows,
        offsets,
        lengths,
        rel_bias.T,
        byte_rows.T,
        keep_mask.reshape(1, -1),
        vecs,
        gate_cot.reshape(1, -1),
        w_query.T,
        w_key.T,
        w_value.T,
        w_out,
        *weights,
        out_cot,
    )
    att_grads = att_grads.reshape(4, inner, -1)[:, :, :width].astype(F32)
    ff_sums = ff_sums[:, :share]
    grad_bias = small[4, : heads * buckets].reshape(heads, buckets).T
    return (
        block_out,
        gate[0],
        grad_rows.T,
        small[2],
        small[3],
        small[1],
        att_grads[1].T,
        att_grads[2].T,
        att_grads[3].T,
        att_grads[0],
        grad_bias,
        small[0],
        ff_sums[0].T,
        ff_sums[1].T,
        ff_sums[2],
    )


def solution(mesh):
    in_specs = (
        P("rows", None),
        P(),
        P("rows"),
        P(),
        P(),
        P(),
        P(None, "tensor"),
        P(None, "tensor"),
        P(None, "tensor"),
        P("tensor", None),
        P(None, "tensor"),
        P(),
        P(None, ("rows", "tensor")),
        P(None, ("rows", "tensor")),
        P(("rows", "tensor"), None),
        P("rows", None),
        P("rows"),
    )
    out_specs = (
        P("rows", None),
        P("rows"),
        P("rows", None),
        P(),
        P(),
        P(),
        P(None, "tensor"),
        P(None, "tensor"),
        P(None, "tensor"),
        P("tensor", None),
        P(None, "tensor"),
        P(),
        P(None, ("rows", "tensor")),
        P(None, ("rows", "tensor")),
        P(("rows", "tensor"), None),
    )
    return jax.shard_map(
        per_device, mesh=mesh, in_specs=in_specs, out_specs=out_specs, check_vma=False
    )
```

```python
import functools

import jax
import jax.numpy as jnp
from jax import lax
from jax.experimental import pallas as pl
from jax.experimental.pallas import tpu as pltpu
from jax.sharding import PartitionSpec as P

MAXLEN = 1024
MARGIN = 32
EPS = 1e-06
DELETE_SCALE = -30.0
NEGATIVE = -1e30
LIMITS = (1, 2, 3, 4, 5, 6, 7, 8, 12, 16, 23, 32, 46, 64, 91)
HALF = 16
HI = 4
MESH = pl.DeviceIdType.MESH
F32 = jnp.float32
BF16 = jnp.bfloat16
VMEM_LIMIT = 63 * 1024 * 1024


def nn(a, b):
    return lax.dot_general(a, b, (((1,), (0,)), ((), ())), preferred_element_type=F32)


def nt(a, b):
    return lax.dot_general(a, b, (((1,), (1,)), ((), ())), preferred_element_type=F32)


def tn(a, b):
    return lax.dot_general(a, b, (((0,), (0,)), ((), ())), preferred_element_type=F32)


def eye(count):
    return lax.broadcasted_iota(jnp.int32, (count, count), 0) == lax.broadcasted_iota(
        jnp.int32, (count, count), 1
    )


def to_row(column, diagonal):
    return jnp.sum(jnp.where(diagonal, column, 0.0), axis=0, keepdims=True)


def to_column(row, diagonal):
    return jnp.sum(jnp.where(diagonal, row, 0.0), axis=1, keepdims=True)


def row_scale(values):
    return lax.rsqrt(jnp.mean(values * values, axis=-1, keepdims=True) + EPS)


def gate_logit(values, scale, weight):
    return scale * jnp.sum(values * weight, axis=-1, keepdims=True)


def sigmoid(value):
    return 1.0 / (1.0 + jnp.exp(-value))


def norm_back(values, gain, grad):
    scale = row_scale(values)
    scaled = grad * gain
    inner = jnp.mean(scaled * values, axis=-1, keepdims=True)
    back = scale * scaled - values * (scale * scale * scale * inner)
    return back, jnp.sum(grad * values * scale, axis=0, keepdims=True)


def reach_of(raw_count, own_rows):
    span = (MAXLEN // raw_count - 1) * own_rows + 2 * MARGIN + raw_count
    return -(-(span - 1) // own_rows)


def slots_of(reach):
    far = list(range(2, reach + 1))
    return [-d for d in reversed(far)] + far + [-1, 0, 1]


def meet_rows(rows):
    me, core = lax.axis_index("rows"), lax.axis_index("tensor")
    barrier = pltpu.get_barrier_semaphore()

    def greet(step, carry):
        pl.semaphore_signal(
            barrier, inc=1, device_id=(lax.rem(me + step, rows), core), device_id_type=MESH
        )
        return carry

    lax.fori_loop(1, rows, greet, 0)
    pl.semaphore_signal(barrier, inc=1, device_id=(me, 1 - core), device_id_type=MESH)
    pl.semaphore_wait(barrier, rows)


def send(src, dst, send_sem, recv_sem, target):
    return pltpu.make_async_remote_copy(
        src_ref=src,
        dst_ref=dst,
        send_sem=send_sem,
        recv_sem=recv_sem,
        device_id=target,
        device_id_type=MESH,
    )


class Window:
    def __init__(self, rows, offsets):
        self.rows, self.offsets = rows, offsets
        self.me, self.core = lax.axis_index("rows"), lax.axis_index("tensor")
        self.slot = {offset: number for number, offset in enumerate(offsets)}
        self.own = self.slot[0]
        side = rows // HI
        self.low = lax.rem(self.me, side)
        self.first, self.second, self.third = [], {}, []
        self.awaited = {}
        if side != 4:
            self.first = [(self.inside(d), self.own, d, self.slot[-d]) for d in offsets if d]
            self.number_all()
            return
        both = jnp.logical_and
        along_x = {1: lax.rem(self.low, 2) == 0, -1: lax.rem(self.low, 2) == 1}
        along_y = {2: self.low < 2, -2: self.low >= 2}
        beside = [*along_x.items(), *along_y.items()]
        for d in (side, -side):
            self.first.append((self.inside(d), self.own, d, self.slot[-d]))
        for step, when in beside:
            self.first.append((when, self.own, step, self.slot[-step]))
        for d in offsets:
            if abs(d) > side:
                when = self.low + d >= 2 * side if d > 0 else self.low + d < -side
                self.first.append((both(when, self.inside(d)), self.own, d, self.slot[-d]))
        for d in (side, -side):
            self.awaited[d] = [self.inside(d)]
            self.second[d] = [
                (when, self.slot[d], step, self.slot[d - step])
                for step, when in beside
                if d - step in self.slot
            ]
        for step_x, when_x in along_x.items():
            for step_y, when_y in along_y.items():
                when = both(when_x, when_y)
                entry = (when, self.slot[step_y], step_x, self.slot[step_y - step_x])
                self.third.append((step_y, entry))
                for d in (side, -side):
                    came = d + step_x
                    if came - step_y in self.slot:
                        there = both(when, self.inside(d))
                        entry = (there, self.slot[came], step_y, self.slot[came - step_y])
                        self.third.append((came, entry))
        for came, entry in self.third:
            self.awaited.setdefault(came, []).append(entry[0])
        self.number_all()

    def number_all(self):
        entries = list(self.first)
        for later in self.second.values():
            entries += later
        entries += [entry for _, entry in self.third]
        self.entries = entries

    def inside(self, offset):
        if offset < 0:
            return self.me >= -offset
        return self.me < self.rows - offset

    def copy(self, ref, sems, entry):
        _, here, step, there = entry
        number = [other is entry for other in self.entries].index(True)
        target = (self.me + step, self.core)
        return send(
            ref.at[here], ref.at[there], sems.at[0, number], sems.at[1, there], target
        )

    def arrival(self, ref, sems, offset):
        place = ref.at[self.slot[offset]]
        other = (self.me, 1 - self.core)
        return send(place, place, sems.at[0, 0], sems.at[1, self.slot[offset]], other)

    def start(self, pairs):
        for entry in self.first:

            @pl.when(entry[0])
            def _():
                for ref, sems in pairs:
                    self.copy(ref, sems, entry).start()

    def relay(self, pairs):
        for offset, entries in self.second.items():

            @pl.when(self.inside(offset))
            def _():
                for ref, sems in pairs:
                    self.arrival(ref, sems, offset).wait_recv()

                for entry in entries:

                    @pl.when(entry[0])
                    def _():
                        for ref, sems in pairs:
                            self.copy(ref, sems, entry).start()

    def relay_diagonal(self, pairs):
        for offset, entry in self.third:

            @pl.when(entry[0])
            def _():
                for ref, sems in pairs:
                    self.arrival(ref, sems, offset).wait_recv()
                    self.copy(ref, sems, entry).start()

    def finish(self, pairs):
        for offset in self.offsets:
            if offset:
                waiting = self.inside(offset)
                for when in self.awaited.get(offset, ()):
                    waiting = jnp.logical_and(waiting, jnp.logical_not(when))

                @pl.when(waiting)
                def _():
                    for ref, sems in pairs:
                        self.arrival(ref, sems, offset).wait_recv()

        for entry in self.entries:
            when = entry[0]
            for offset, entries in self.second.items():
                if any(entry is other for other in entries):
                    when = jnp.logical_and(when, self.inside(offset))

            @pl.when(when)
            def _():
                for ref, sems in pairs:
                    self.copy(ref, sems, entry).wait_send()

    def clear(self, ref, value):
        for offset in self.offsets:
            if offset:

                @pl.when(jnp.logical_not(self.inside(offset)))
                def _():
                    ref[self.slot[offset]] = jnp.full(ref.shape[1:], value, ref.dtype)


EDGE = -(-LIMITS[-1] // 16) * 16


def near_bias(gap, table_ref, head, above, below):
    if above and below:
        bias = jnp.full(gap.shape, table_ref[head, 0], F32)
    else:
        bias = jnp.full(gap.shape, table_ref[head, HALF if above else 0], F32)
    for number, limit in enumerate(LIMITS):
        if above:
            bias = jnp.where(gap >= limit, table_ref[head, HALF + number + 1], bias)
        if below:
            bias = jnp.where(gap <= -limit, table_ref[head, number + 1], bias)
    return bias


def joined_row(facts_ref, slots, line, width):
    return jnp.concatenate([facts_ref[slot, line : line + 1, :width] for slot in slots], axis=1)


GELU_A = 0.7978845608028654
GELU_B = 0.044715


def folded_row(facts_ref, slots, line, width):
    half = width // 2
    return jnp.concatenate(
        [
            facts_ref[slot, line : line + 1, begin : begin + half]
            for begin in (0, half)
            for slot in slots
        ],
        axis=1,
    )


def split3(value):
    one = value.astype(BF16).astype(F32)
    rest = value - one
    two = rest.astype(BF16).astype(F32)
    return one, two, (rest - two).astype(BF16).astype(F32)


def stacked_rows(rows, width):
    line = lax.broadcasted_iota(jnp.int32, (8, width), 0)
    result = jnp.zeros((8, width), F32)
    for number, row in enumerate(rows):
        result = jnp.where(line == number, row, result)
    return result.astype(BF16)


def layer_kernel(
    rows,
    offsets,
    lengths_ref,
    table_ref,
    byte_ref,
    keep_ref,
    vec_ref,
    gcot_ref,
    wq_ref,
    wk_ref,
    wv_ref,
    wo_ref,
    wg_ref,
    wu_ref,
    wd_ref,
    cot_ref,
    gate_ref,
    block_ref,
    rows_ref,
    small_ref,
    ffo_ref,
    attg_ref,
    ffin_ref,
    count_ref,
    chosen_ref,
    ext_ref,
    extaux_ref,
    below_ref,
    above_ref,
    belowaux_ref,
    aboveaux_ref,
    packed_ref,
    aux_ref,
    first_ref,
    kv_ref,
    query_ref,
    facts_ref,
    dout_ref,
    facts2_ref,
    biasq_ref,
    biask_ref,
    att_ref,
    attf_ref,
    lse_ref,
    mixed_ref,
    sec_ref,
    cots_ref,
    wall_ref,
    wout_ref,
    wqkv_ref,
    mid_ref,
    dgated_ref,
    dupper_ref,
    part_ref,
    kept_ref,
    sout_ref,
    sin_ref,
    hout_ref,
    hin_ref,
    line_ref,
    dsec_ref,
    heads_ref,
    dgate_ref,
    zout_ref,
    zin_ref,
    yin_ref,
    fin_ref,
    slow_ref,
    shigh_ref,
    back_ref,
    backaux_ref,
    ffa_ref,
    ffb_ref,
    za_ref,
    zb_ref,
    count_sems,
    edge_sems,
    kv_sems,
    query_sems,
    facts_sems,
    dout_sems,
    facts2_sems,
    wall_sems,
    pair_sems,
    local_sems,
    cot_sems,
    cotf_sems,
    sec_sems,
    secf_sems,
    sib_sems,
    hi_sems,
    line_sems,
    half_sems,
    ff_sems,
    low_sems,
    high_sems,
    back_sems,
    last_sems,
    edge2_sems,
    slow_sems,
    shigh_sems,
):
    width, raw_count = byte_ref.shape
    own_rows = cot_ref.shape[0]
    inner = wq_ref.shape[0]
    heads = table_ref.shape[0]
    head_size = inner // heads
    share = wd_ref.shape[0]
    lows = rows // HI
    half = own_rows // 2
    ext_rows = own_rows + 2 * MARGIN
    me, core = lax.axis_index("rows"), lax.axis_index("tensor")
    high, low = lax.div(me, lows), lax.rem(me, lows)
    sibling = (me, 1 - core)
    mine = pl.ds(pl.multiple_of(core * half, half), half)
    theirs = pl.ds(pl.multiple_of((1 - core) * half, half), half)
    window = Window(rows, offsets)
    own = window.own
    g_delete, w_delete = vec_ref[0:1, :], vec_ref[1:2, :]
    g_attn, g_ff = vec_ref[2:3, :], vec_ref[3:4, :]

    is_square = lows == 4

    def low_other(step):
        if step == 1:
            return low + 1 - 2 * lax.rem(low, 2)
        if step == 2:
            return lax.rem(low + 2, lows)
        return lows - 1 - low

    def low_pair(step):
        return (high * lows + low_other(step), core)

    def low_peer(step):
        return (high * lows + lax.rem(low + step, lows), core)

    def low_source(step):
        return lax.rem(low + lows - step, lows)

    def high_other(step):
        if step == 0:
            return high
        if step == 1:
            return high + 1 - 2 * lax.rem(high, 2)
        if step == 2:
            return lax.rem(high + 2, HI)
        return HI - 1 - high

    def high_peer(step):
        return (high_other(step) * lows + low, core)

    middle_high = jnp.logical_and(high >= 1, high <= 2)
    end_high = jnp.logical_not(middle_high)
    upper_high = lax.div(high, 2)
    inner_high = high + 1 - 2 * upper_high
    outer_high = high - 1 + 2 * upper_high

    def line_chunk(turn):
        if turn == 0:
            return high
        if turn == 1:
            return 3 - 3 * upper_high
        if turn == 2:
            return 2 - upper_high
        return 1 - high + 4 * upper_high

    def first_half(count):
        return count // 2 // 16 * 16

    class LowGather:
        def __init__(self, source, block, count, sems):
            self.source, self.block, self.count, self.sems = source, block, count, sems
            cut = first_half(count)
            self.halves = ((0, cut), (cut, count - cut))

        def copy(self, src, dst, number, target):
            return send(src, dst, self.sems.at[0, number], self.sems.at[1, number], target)

        def direct(self, step):
            if is_square:
                target = low_pair(step)
            else:
                target = low_peer(step)
            return self.copy(self.source, self.block(low, 0, self.count), step, target)

        def arrival(self, step):
            place = self.block(low_other(step) if is_square else low_source(step), 0, self.count)
            return self.copy(place, place, step, sibling)

        def passed(self, side):
            place = self.block(low_other(2 - side), *self.halves[side])
            return self.copy(place, place, 3 + side, low_pair(1 + side))

        def start(self):
            if is_square:
                self.direct(1).start()
                self.direct(2).start()
                return

            def one(step, carry):
                self.direct(step).start()
                return carry

            lax.fori_loop(1, lows, one, 0)

        def relay(self):
            if is_square:
                for side in (1, 0):
                    self.arrival(2 - side).wait_recv()
                    self.passed(side).start()

        def finish(self):
            if is_square:
                for step in (1, 2):
                    self.direct(step).wait_send()
                for side in range(2):
                    self.passed(side).wait_send()
                    place = self.block(low_other(3), *self.halves[side])
                    self.copy(place, place, 3 + side, sibling).wait_recv()
                return

            def one(step, carry):
                self.direct(step).wait_send()
                self.arrival(step).wait_recv()
                return carry

            lax.fori_loop(1, lows, one, 0)

    class LowReduce:
        def __init__(self, part, count, relays, arrivals, sems):
            self.part, self.count, self.sems = part, count, sems
            self.relays, self.arrivals = relays, arrivals
            cut = first_half(count)
            self.halves = ((0, cut), (cut, count - cut))

        def copy(self, src, dst, number, target):
            return send(src, dst, self.sems.at[0, number], self.sems.at[1, number], target)

        def half(self, side):
            return self.copy(
                self.part(low_other(3), *self.halves[side]),
                self.relays[side],
                side,
                low_pair(2 - side),
            )

        def summed(self, side):
            return self.copy(
                self.part(low_other(1 + side), 0, self.count),
                self.arrivals.at[side],
                2 + side,
                low_pair(1 + side),
            )

        def direct(self, step):
            return self.copy(
                self.part(lax.rem(low + step, lows), 0, self.count),
                self.arrivals.at[step],
                step,
                low_peer(step),
            )

        def start(self):
            if is_square:
                for side in range(2):
                    self.half(side).start()
                return

            def one(step, carry):
                self.direct(step).start()
                return carry

            lax.fori_loop(1, lows, one, 0)

        def relay(self):
            if is_square:
                for side in range(2):
                    self.half(side).wait()
                    mine_too = self.part(low_other(1 + side), *self.halves[side])
                    both = mine_too[...].astype(F32) + self.relays[side][...].astype(F32)
                    mine_too[...] = both.astype(BF16)
                    self.summed(side).start()

        def finish(self):
            if is_square:
                for side in range(2):
                    self.summed(side).wait()
                return

            def one(step, carry):
                self.direct(step).wait()
                return carry

            lax.fori_loop(1, lows, one, 0)

    arrived = range(2) if is_square else range(1, lows)

    meet_rows(rows)

    keep = keep_ref[...].astype(F32)
    count_ref[me] = jnp.broadcast_to(jnp.sum(keep, axis=1, keepdims=True), (8, 128))

    def count_copy(step):
        return send(
            count_ref.at[me],
            count_ref.at[me],
            count_sems.at[0, step],
            count_sems.at[1, step],
            (lax.rem(me + step, rows), core),
        )

    def count_arrival(step):
        source = lax.rem(me + rows - step, rows)
        return send(
            count_ref.at[source],
            count_ref.at[source],
            count_sems.at[0, step],
            count_sems.at[1, step],
            (source, core),
        )

    def start_count(step, carry):
        count_copy(step).start()
        return carry

    lax.fori_loop(1, rows, start_count, 0)

    weight_refs = (wg_ref, wu_ref, wd_ref)
    my_share = pl.ds(pl.multiple_of(low * share, share), share)
    locals_early = [
        pltpu.make_async_copy(ref, wqkv_ref.at[core, number], local_sems.at[number])
        for number, ref in enumerate((wq_ref, wk_ref, wv_ref))
    ]
    locals_late = [
        pltpu.make_async_copy(wo_ref, wout_ref.at[core], local_sems.at[3]),
        pltpu.make_async_copy(cot_ref, cots_ref.at[high], local_sems.at[4]),
    ] + [
        pltpu.make_async_copy(ref, wall_ref.at[number, my_share], local_sems.at[5 + number])
        for number, ref in enumerate(weight_refs)
    ]
    for copy in locals_early + locals_late:
        copy.start()

    def wall_gather(place, number, start, size):
        def block(place, begin, count):
            inside = pl.ds(pl.multiple_of(place * share + start + begin, 16), count)
            return wall_ref.at[number, inside]

        source = weight_refs[number].at[pl.ds(start, size)]
        return LowGather(source, block, size, wall_sems.at[place])

    early = share * 3 // 7 // 16 * 16
    wall_cuts = [(2, 0, early), (2, early, share - early), (0, 0, share), (1, 0, share)]
    walls = [
        wall_gather(place, *cut) if cut[2] else None for place, cut in enumerate(wall_cuts)
    ]

    class Gather:
        def __init__(self, ref, sems, sems_f, offset, count, source=None):
            self.ref, self.sems, self.sems_f = ref, sems, sems_f
            self.part = pl.ds(pl.multiple_of(core * half + offset, 16), count)
            self.other = pl.ds(pl.multiple_of((1 - core) * half + offset, 16), count)
            self.source = ref.at[high] if source is None else source

        def direct(self, step):
            return send(
                self.source.at[self.part],
                self.ref.at[high, self.part],
                self.sems.at[0, step],
                self.sems.at[1, step],
                high_peer(step),
            )

        def arrival(self, step):
            place = self.ref.at[high_other(step), self.part]
            return send(
                place, place, self.sems.at[0, step], self.sems.at[1, step], high_peer(step)
            )

        def relay(self):
            place = self.ref.at[high_other(2), self.part]
            return send(place, place, self.sems.at[0, 0], self.sems.at[1, 3], high_peer(1))

        def forward(self, step, part):
            place = self.ref.at[high_other(step), part]
            return send(
                place, place, self.sems_f.at[0, step], self.sems_f.at[1, step], sibling
            )

        def start(self):
            self.direct(1).start()
            self.direct(2).start()

            @pl.when(middle_high)
            def _():
                self.direct(3).start()

        def arrived(self, step):
            self.arrival(step).wait_recv()
            if step == 2:

                @pl.when(middle_high)
                def _():
                    self.relay().start()

            self.forward(step, self.part).start()

        def forwarded(self, step):
            self.forward(step, self.other).wait_recv()

        def close(self):
            self.direct(1).wait_send()
            self.direct(2).wait_send()

            @pl.when(middle_high)
            def _():
                self.direct(3).wait_send()
                self.relay().wait_send()

            for step in range(1, HI):
                self.forward(step, self.part).wait_send()

    third = half // 3 // 16 * 16
    cot_gathers = [
        Gather(cots_ref, cot_sems.at[number], cotf_sems.at[number], begin, count, cot_ref)
        for number, (begin, count) in enumerate(((0, third), (third, half - third)))
    ]
    sec_gather = Gather(sec_ref, sec_sems, secf_sems, 0, half)

    if early:
        walls[0].start()
    cot_gathers[0].start()
    pair_early = [
        send(wo_ref, wout_ref.at[core], pair_sems.at[0, 0], pair_sems.at[1, 0], sibling)
    ] + [
        send(
            ref,
            wqkv_ref.at[core, number],
            pair_sems.at[0, 1 + number],
            pair_sems.at[1, 1 + number],
            sibling,
        )
        for number, ref in enumerate((wq_ref, wk_ref, wv_ref))
    ]
    for copy in pair_early:
        copy.start()

    gate_weight = g_delete * w_delete
    raw = byte_ref[...]
    raw_f = raw.astype(F32)
    raw_scale = lax.rsqrt(jnp.mean(raw_f * raw_f, axis=0, keepdims=True) + EPS)
    raw_logit = raw_scale * jnp.sum(
        nn(stacked_rows(split3(gate_weight), width), raw), axis=0, keepdims=True
    )
    gate_ref[...] = DELETE_SCALE * sigmoid(raw_logit)
    upper = lax.broadcasted_iota(jnp.int32, (raw_count, raw_count), 0) <= lax.broadcasted_iota(
        jnp.int32, (raw_count, raw_count), 1
    )
    rank = nn(keep.astype(BF16), jnp.where(upper, 1.0, 0.0).astype(BF16)) - 1.0
    lane = lax.broadcasted_iota(jnp.int32, (raw_count, 128), 1)
    local = lax.broadcasted_iota(jnp.int32, (raw_count, 128), 0).astype(F32)
    aux = jnp.where(lane == 0, local, jnp.where(lane == 1, me.astype(F32), 0.0)).astype(BF16)
    window.clear(kv_ref, 0.0)
    window.clear(query_ref, 0.0)
    window.clear(facts_ref, -1.0)
    window.clear(dout_ref, 0.0)
    window.clear(facts2_ref, 0.0)

    def finish_count(step, carry):
        count_copy(step).wait_send()
        count_arrival(step).wait_recv()
        return carry

    lax.fori_loop(1, rows, finish_count, 0)
    lower = lax.broadcasted_iota(jnp.int32, count_ref.shape, 0) < me
    before = jnp.sum(jnp.where(lower, count_ref[...], 0.0), axis=0)[0:1, 0:1]
    place = before + rank - (me * own_rows).astype(F32)
    place = jnp.where(keep > 0.0, place, -4096.0).astype(jnp.int32)
    chosen = place + MARGIN == lax.broadcasted_iota(jnp.int32, (ext_rows, raw_count), 0)
    chosen = jnp.where(chosen, 1.0, 0.0).astype(BF16)
    chosen_ref[...] = chosen
    ext_ref[...] = nt(chosen, raw).astype(BF16)
    extaux_ref[...] = nn(chosen, aux).astype(BF16)

    def edges(sems, downs, ups):
        def copies(pairs, offset):
            return [
                send(src, dst, sems.at[0, number], sems.at[1, number], (me + offset, core))
                for number, src, dst in pairs
            ]

        def start():
            @pl.when(me > 0)
            def _():
                for copy in copies(downs, -1):
                    copy.start()

            @pl.when(me < rows - 1)
            def _():
                for copy in copies(ups, 1):
                    copy.start()

        def finish():
            @pl.when(me > 0)
            def _():
                for copy in copies(downs, -1):
                    copy.wait_send()
                for copy in copies(ups, 1):
                    copy.wait_recv()

            @pl.when(me < rows - 1)
            def _():
                for copy in copies(ups, 1):
                    copy.wait_send()
                for copy in copies(downs, -1):
                    copy.wait_recv()

        return start, finish

    first_rows, last_rows = pl.ds(0, MARGIN), pl.ds(own_rows + MARGIN, MARGIN)
    start_edges, finish_edges = edges(
        edge_sems,
        [
            (0, ext_ref.at[first_rows], above_ref),
            (1, extaux_ref.at[first_rows], aboveaux_ref),
        ],
        [
            (2, ext_ref.at[last_rows], below_ref),
            (3, extaux_ref.at[last_rows], belowaux_ref),
        ],
    )
    start_edges()

    @pl.when(me == 0)
    def _():
        below_ref[...] = jnp.zeros(below_ref.shape, BF16)
        belowaux_ref[...] = jnp.zeros(belowaux_ref.shape, BF16)

    @pl.when(me == rows - 1)
    def _():
        above_ref[...] = jnp.zeros(above_ref.shape, BF16)
        aboveaux_ref[...] = jnp.zeros(aboveaux_ref.shape, BF16)

    packed_ref[...] = ext_ref[MARGIN : MARGIN + own_rows, :]
    aux_ref[...] = extaux_ref[MARGIN : MARGIN + own_rows, :].astype(F32)
    for copy in locals_early:
        copy.wait()
    finish_edges()
    top = own_rows - MARGIN
    packed_ref[0:MARGIN, :] = packed_ref[0:MARGIN, :] + below_ref[...]
    packed_ref[top:, :] = packed_ref[top:, :] + above_ref[...]
    aux_ref[0:MARGIN, :] = aux_ref[0:MARGIN, :] + belowaux_ref[...].astype(F32)
    aux_ref[top:, :] = aux_ref[top:, :] + aboveaux_ref[...].astype(F32)

    packed = packed_ref[...].astype(F32)
    scale = row_scale(packed)
    first = (packed * scale * g_attn).astype(BF16)
    first_ref[...] = first
    kv_ref[own, :, 0:inner] = nt(first, wqkv_ref[core, 1]).astype(BF16)
    kv_ref[own, :, inner : 2 * inner] = nt(first, wqkv_ref[core, 2]).astype(BF16)

    gate = DELETE_SCALE * sigmoid(gate_logit(packed, scale, gate_weight))
    ids = aux_ref[:, 0:1] + raw_count * aux_ref[:, 1:2]
    ids_i = ids.astype(jnp.int32)
    starts = jnp.zeros_like(ids_i)
    end = jnp.int32(0)
    for number in range(lengths_ref.shape[0]):
        end = end + lengths_ref[number]
        starts = jnp.where(ids_i >= end, end, starts)
    starts = starts.astype(F32)
    own_eye = eye(own_rows)
    facts_ref[own] = jnp.zeros(facts_ref.shape[1:], F32)
    facts_ref[own, 0:1, 0:own_rows] = to_row(gate, own_eye)
    facts_ref[own, 1:2, 0:own_rows] = to_row(ids, own_eye)
    facts_ref[own, 2:3, 0:own_rows] = to_row(starts, own_eye)
    window.start([(facts_ref, facts_sems), (kv_ref, kv_sems)])
    cot_gathers[1].start()
    def fold(ref, value):
        ref[own, :, 0:inner] = value[0:half, :]
        ref[own, :, inner : 2 * inner] = value[half:, :]

    def unfold(ref, head):
        parts = []
        for begin in (0, inner):
            cut = slice(begin + head * head_size, begin + (head + 1) * head_size)
            parts.append(ref[own, :, cut])
        return jnp.concatenate(parts, axis=0)

    def folded(ref, span, head):
        parts = []
        for begin in (0, inner):
            cut = slice(begin + head * head_size, begin + (head + 1) * head_size)
            parts.append(ref[span, :, cut].reshape(-1, head_size))
        return jnp.concatenate(parts, axis=0)

    fold(query_ref, nt(first, wqkv_ref[core, 0]).astype(BF16))

    far = (len(offsets) - 3) // 2
    segments = (range(0, far), range(far, 2 * far), range(2 * far, 2 * far + 3))
    def add_near(added_ref, pieces, rows_at, gap, extra, allowed, above, below):
        def keep(head, cut, value):
            for begin, there, count in pieces:
                added_ref[head, cut, there : there + count] = value[:, begin : begin + count]

        for head in range(heads):
            if rows_at is not None:
                rest = table_ref[head, 2 * HALF - 1 if above else HALF - 1]
                keep(head, slice(0, own_rows), jnp.where(allowed, rest + extra, NEGATIVE))
            cut = slice(0, own_rows) if rows_at is None else rows_at
            bias = near_bias(gap[cut], table_ref, head, above, below)
            more = extra if extra.shape[0] == 1 else extra[cut]
            keep(head, cut, jnp.where(allowed[cut], bias + more, NEGATIVE))

    def fact(slot, line):
        at = window.slot[slot]
        return facts_ref[at, line : line + 1, :own_rows]

    border = {-1: slice(0, EDGE), 0: None, 1: slice(own_rows - EDGE, own_rows)}

    def near_queries(slot):
        gap, allowed = fact(slot, 1) - ids, fact(slot, 2) == starts
        pieces = [(0, (1 + slot) * own_rows, own_rows)]
        add_near(
            biasq_ref, pieces, border[slot], gap, fact(slot, 0), allowed, slot >= 0, slot <= 0
        )

    def near_keys(slot):
        gap, allowed = ids - fact(slot, 1), fact(slot, 2) == starts
        pieces = [(side * half, (3 * side + 1 + slot) * half, half) for side in range(2)]
        add_near(biask_ref, pieces, border[slot], gap, gate, allowed, slot <= 0, slot >= 0)

    near_queries(0)
    window_early = [(facts_ref, facts_sems), (kv_ref, kv_sems)]
    window.relay(window_early)
    window.relay_diagonal(window_early)
    walls[1].start()
    walls[2].start()
    window.finish(window_early)
    near_queries(-1)
    near_queries(1)
    walls[3].start()
    if early:
        walls[0].relay()

    def spans(segment):
        return slice(segment[0], segment[-1] + 1)

    def far_added(segment, column, row_of=joined_row):
        allowed = row_of(facts_ref, segment, 2, own_rows) == starts
        return jnp.where(allowed, column, NEGATIVE)

    added = [
        far_added(segment, joined_row(facts_ref, segment, 0, own_rows)) for segment in segments[:2]
    ]
    fixed = (HALF - 1, 2 * HALF - 1)
    lanes = lax.broadcasted_iota(jnp.int32, lse_ref.shape, 1)
    lse_all = jnp.zeros(lse_ref.shape, F32)
    for head in range(heads):
        cut = slice(head * head_size, (head + 1) * head_size)
        cut_v = slice(inner + head * head_size, inner + (head + 1) * head_size)
        query = unfold(query_ref, head)
        parts = []
        for number, segment in enumerate(segments):
            keys = kv_ref[spans(segment), :, cut].reshape(-1, head_size)
            if number < 2:
                extra = added[number] + table_ref[head, fixed[number]]
            else:
                extra = biasq_ref[head]
            parts.append(nt(query, keys) + extra)
        most = jnp.max(parts[0], axis=1, keepdims=True)
        for part in parts[1:]:
            most = jnp.maximum(most, jnp.max(part, axis=1, keepdims=True))
        expos = [jnp.exp(part - most) for part in parts]
        total = sum(jnp.sum(expo, axis=1, keepdims=True) for expo in expos)
        lse_all = jnp.where(lanes == head, most + jnp.log(total), lse_all)
        attended = jnp.zeros((own_rows, head_size), F32)
        for segment, expo in zip(segments, expos):
            values = kv_ref[spans(segment), :, cut_v].reshape(-1, head_size)
            attended = attended + nn((expo / total).astype(BF16), values)
        attf_ref[:, cut] = attended
        att_ref[core, :, cut] = attended.astype(BF16)
    lse_ref[...] = lse_all

    att_copy = send(
        att_ref.at[core], att_ref.at[core], pair_sems.at[0, 4], pair_sems.at[1, 4], sibling
    )
    att_copy.start()
    for copy in locals_late:
        copy.wait()
    for copy in pair_early:
        copy.wait()
    att_copy.wait()
    mixed = packed_ref[...].astype(F32) + (nn(att_ref[0], wout_ref[0]) + nn(att_ref[1], wout_ref[1]))
    mixed_ref[...] = mixed
    sec_ref[high] = (mixed * row_scale(mixed) * g_ff).astype(BF16)
    sec_gather.start()

    walls[1].relay()
    walls[2].relay()
    for gather in cot_gathers:
        gather.arrived(1)
        gather.arrived(2)
    walls[3].relay()
    sec_gather.arrived(1)
    sec_gather.arrived(2)
    for wall in walls[0 if early else 1 :]:
        wall.finish()

    def sib_copy(kind, step):
        return send(
            sout_ref.at[step],
            sin_ref.at[kind, step],
            sib_sems.at[0, kind, step],
            sib_sems.at[1, kind, step],
            sibling,
        )

    def hi_copy(kind, step):
        return send(
            hout_ref.at[kind, step - 1],
            hin_ref.at[step - 1],
            hi_sems.at[0, step],
            hi_sems.at[1, step],
            high_peer(step),
        )

    def hand_over(kind, step, value):
        part_ref[...] = value
        sout_ref[step] = part_ref[theirs, :].astype(BF16)
        kept_ref[kind if step == 0 else 2 + step % 2] = part_ref[mine, :]
        sib_copy(kind, step).start()

    def pass_on(kind, step):
        sib_copy(kind, step).wait()
        both = kept_ref[2 + step % 2] + sin_ref[kind, step].astype(F32)
        hout_ref[kind, step - 1] = both.astype(BF16)

    def chunk_rows(chunk):
        return pl.ds(pl.multiple_of(chunk * own_rows, own_rows), own_rows)

    def line_copy(turn, middle):
        slot, target = turn - 1, inner_high
        if middle:
            slot = (3, 4, 0)[turn - 1]
            target = outer_high if turn == 3 else inner_high
        return send(
            hout_ref.at[0, turn - 1],
            line_ref.at[slot],
            line_sems.at[0, turn],
            line_sems.at[1, slot],
            (target * lows + low, core),
        )

    def line_arrived(slot):
        place = line_ref.at[slot]
        send(place, place, line_sems.at[0, 0], line_sems.at[1, slot], sibling).wait_recv()

    def ship_end(turn):
        @pl.when(end_high)
        def _():
            hout_ref[0, turn - 1] = kept_ref[1 + turn].astype(BF16)
            line_copy(turn, False).start()

    def ship_middle(turn):
        @pl.when(middle_high)
        def _():
            slot = (0, 1, 3)[turn - 1]
            line_arrived(slot)
            total = kept_ref[1 + turn] + line_ref[slot].astype(F32)
            hout_ref[0, turn - 1] = total.astype(BF16)
            line_copy(turn, True).start()

    for step in range(HI):
        if step:
            for gather in cot_gathers + [sec_gather]:
                if step == HI - 1:
                    gather.arrived(step)
                gather.forwarded(step)
        chunk = high_other(step)
        second = sec_ref[chunk]
        gated = nt(second, wall_ref[0])
        upper = nt(second, wall_ref[1])
        d_middle = nt(cots_ref[chunk], wall_ref[2])
        square = gated * gated
        bend = jnp.tanh(GELU_A * gated * (1.0 + GELU_B * square))
        lift = 0.5 * (1.0 + bend)
        slope = lift + 0.5 * gated * (1.0 - bend * bend) * (
            GELU_A * (1.0 + 3.0 * GELU_B * square)
        )
        gelu = gated * lift
        d_gated = (d_middle * upper * slope).astype(BF16)
        d_upper = (d_middle * gelu).astype(BF16)
        mid_ref[chunk_rows(chunk), :] = (gelu * upper).astype(BF16)
        dgated_ref[chunk_rows(chunk), :] = d_gated
        dupper_ref[chunk_rows(chunk), :] = d_upper
        hand_over(1, step, nn(d_gated, wall_ref[0]) + nn(d_upper, wall_ref[1]))
        if step == 0:
            window.start([(query_ref, query_sems)])
        if step == 2:
            window.relay([(query_ref, query_sems)])
        if step > 1:
            pass_on(1, step - 1)
            hi_copy(1, step - 1).start()
    pass_on(1, HI - 1)
    hi_copy(1, HI - 1).start()
    for gather in cot_gathers + [sec_gather]:
        gather.close()

    def ff_reduce(number):
        def part(place, begin, count):
            inside = pl.ds(pl.multiple_of(place * share + begin, 16), count)
            return wall_ref.at[number, inside]

        relays = (ffa_ref.at[number], ffb_ref.at[number])
        return LowReduce(part, share, relays, ffin_ref.at[number], ff_sems.at[number])

    reduces = [ff_reduce(number) for number in range(3)]
    hidden = wall_ref.shape[1]

    def weight_grad(number, left_ref, right_ref):
        for begin in range(0, hidden, 256):
            units = slice(begin, min(begin + 256, hidden))
            right = right_ref[...].reshape(HI * own_rows, width)
            wall_ref[number, units, :] = tn(left_ref[:, units], right).astype(BF16)

    weight_grad(0, dgated_ref, sec_ref)
    reduces[0].start()
    weight_grad(1, dupper_ref, sec_ref)
    reduces[1].start()
    window.relay_diagonal([(query_ref, query_sems)])
    sib_copy(1, 0).wait()
    for turn in (1, 2, 3, 0):
        part_ref[...] = nn(mid_ref[chunk_rows(line_chunk(turn)), :], wall_ref[2])
        sout_ref[turn] = part_ref[theirs, :].astype(BF16)
        kept_ref[1 + turn if turn else 0] = part_ref[mine, :]
        sib_copy(0, turn).start()
        if turn != 1:
            before = turn - 1 if turn else HI - 1
            sib_copy(0, before).wait()
            kept_ref[1 + before] = kept_ref[1 + before] + sin_ref[0, before].astype(F32)
    reduces[0].relay()
    weight_grad(2, mid_ref, cots_ref)
    reduces[1].relay()

    for slot in (-1, 0, 1):
        near_keys(slot)
    total = kept_ref[1] + sin_ref[1, 0].astype(F32)
    for step in range(1, HI):
        hi_copy(1, step).wait()
        total = total + hin_ref[step - 1].astype(F32)
    dsec_ref[mine, :] = total
    dsec_copy = send(
        dsec_ref.at[mine], dsec_ref.at[mine], half_sems.at[0, 0], half_sems.at[1, 0], sibling
    )
    dsec_copy.start()
    dsec_copy.wait()

    back, g_ff_grad = norm_back(mixed_ref[...], g_ff, dsec_ref[...])
    d_mixed = cots_ref[high].astype(F32) + back
    part_ref[...] = d_mixed
    d_branch = d_mixed.astype(BF16)
    d_att = nt(d_branch, wout_ref[core]).astype(BF16)
    fold(dout_ref, d_att)
    facts2_ref[own] = jnp.zeros(facts2_ref.shape[1:], F32)
    deltas = []
    products = d_att.astype(F32) * attf_ref[...]
    for head in range(heads):
        cut = slice(head * head_size, (head + 1) * head_size)
        delta = jnp.sum(products[:, cut], axis=1, keepdims=True)
        deltas.append(delta)
        facts2_ref[own, head : head + 1, 0:own_rows] = to_row(delta, own_eye)
        line = 4 + head
        facts2_ref[own, line : line + 1, 0:own_rows] = to_row(
            lse_ref[:, head : head + 1], own_eye
        )
    window.start([(facts2_ref, facts2_sems), (dout_ref, dout_sems)])
    for turn in range(1, HI):
        ship_end(turn)

    groups = zout_ref.shape[0]
    piece = zout_ref.shape[2]
    lanes_all = zout_ref.shape[3]
    quarter = lanes_all // HI

    def keep_pieces(number, value):
        for begin in range(0, inner, piece):
            group, place = divmod((number * inner + begin) // piece, lows)
            block = value[begin : begin + piece, :]
            zout_ref[group, place, :, 0:width] = block.astype(BF16)

    def quarter_of(place):
        return pl.ds(pl.multiple_of(place * quarter, 128), quarter)

    def low_sum(group):
        def part(place, begin, count):
            return zout_ref.at[group, place, pl.ds(begin, count)]

        relays = (za_ref.at[group], zb_ref.at[group])
        return LowReduce(part, piece, relays, zin_ref.at[group], low_sems.at[group])

    lows_sum = [low_sum(group) for group in range(groups)]
    early_groups, late_groups = range(groups // 2), range(groups // 2, groups)

    def high_copy(group, step, place):
        return send(
            zout_ref.at[group, low, :, quarter_of(high_other(step))],
            yin_ref.at[group, place],
            high_sems.at[0, group, step],
            high_sems.at[1, group, step],
            high_peer(step),
        )

    def share_low(group):
        lows_sum[group].finish()
        total = zout_ref[group, low].astype(F32)
        for number in arrived:
            total = total + zin_ref[group, number].astype(F32)
        zout_ref[group, low] = total.astype(BF16)
        for step in range(1, HI):
            high_copy(group, step, high).start()

    def back_copy(group, step, place):
        lanes_at = (group, slice(None), quarter_of(place))
        return send(
            fin_ref.at[lanes_at],
            fin_ref.at[lanes_at],
            back_sems.at[0, group, step],
            back_sems.at[1, group, step],
            high_peer(step),
        )

    def share_high(group):
        for step in range(1, HI):
            high_copy(group, step, high).wait_send()
            high_copy(group, step, high_other(step)).wait_recv()
        yin_ref[group, high] = zout_ref[group, low, :, quarter_of(high)]
        total = yin_ref[group, 0].astype(F32)
        for number in range(1, HI):
            total = total + yin_ref[group, number].astype(F32)
        fin_ref[group, :, quarter_of(high)] = total.astype(BF16)
        for step in range(1, HI):
            back_copy(group, step, high).start()

    def last_gather(group):
        def block(place, begin, count):
            return attg_ref.at[group, place, pl.ds(begin, count)]

        return LowGather(fin_ref.at[group], block, piece, last_sems.at[group])

    lasts = [last_gather(group) for group in range(groups)]
    own_lasts = [
        pltpu.make_async_copy(
            fin_ref.at[group], attg_ref.at[group, low], local_sems.at[8 + group]
        )
        for group in range(groups)
    ]

    def spread_low(group):
        for step in range(1, HI):
            back_copy(group, step, high).wait_send()
            back_copy(group, step, high_other(step)).wait_recv()
        lasts[group].start()
        own_lasts[group].start()

    if lanes_all > width:
        zout_ref[:, :, :, width:] = jnp.zeros(zout_ref.shape[:3] + (lanes_all - width,), BF16)
    keep_pieces(0, tn(att_ref[core], d_branch))

    lane = lax.broadcasted_iota(jnp.int32, (1, width), 1)
    bias_grad = jnp.zeros((1, width), F32)

    def add_bias(bias_grad, head, bucket, value):
        return bias_grad + jnp.where(lane == head * 2 * HALF + bucket, value, 0.0)

    def total_of(value):
        return jnp.sum(jnp.sum(value, axis=0, keepdims=True), axis=1, keepdims=True)

    for head in range(heads):
        cut = slice(head * head_size, (head + 1) * head_size)
        cut_v = slice(inner + head * head_size, inner + (head + 1) * head_size)
        query, d_head = unfold(query_ref, head), unfold(dout_ref, head)
        lse = lse_ref[:, head : head + 1]
        d_query = jnp.zeros((own_rows, head_size), F32)
        for number, segment in enumerate(segments):
            keys = kv_ref[spans(segment), :, cut].reshape(-1, head_size)
            values = kv_ref[spans(segment), :, cut_v].reshape(-1, head_size)
            if number < 2:
                extra = added[number] + table_ref[head, fixed[number]]
            else:
                extra = biasq_ref[head]
            probs = jnp.exp(nt(query, keys) + extra - lse)
            d_scores = probs * (nt(d_head, values) - deltas[head])
            d_query = d_query + nn(d_scores.astype(BF16), keys)
            if number < 2:
                bias_grad = add_bias(bias_grad, head, fixed[number], total_of(d_scores))
                continue
            for slot in (-1, 0, 1):
                lanes_at = slice((1 + slot) * own_rows, (2 + slot) * own_rows)
                block = d_scores[:, lanes_at]
                gap = fact(slot, 1) - ids
                whole = total_of(block)
                rows_at = border[slot]
                if rows_at is not None:
                    block, gap = block[rows_at], gap[rows_at]
                for sign in (1, -1):
                    if sign * slot < 0:
                        continue
                    base = HALF if sign > 0 else 0
                    sums = [
                        total_of(jnp.where(sign * gap >= limit, block, 0.0)) for limit in LIMITS
                    ]
                    if slot:
                        sums = [whole] + [value + (whole - total_of(block)) for value in sums[1:]]
                    whole = whole - sums[0]
                    for place in range(len(LIMITS)):
                        value = sums[place]
                        if place + 1 < len(LIMITS):
                            value = value - sums[place + 1]
                        bias_grad = add_bias(bias_grad, head, base + place + 1, value)
                if not slot:
                    bias_grad = add_bias(bias_grad, head, 0, whole)
        heads_ref[core, 0, :, cut] = d_query.astype(BF16)
        if head == 1:
            window.relay([(facts2_ref, facts2_sems), (dout_ref, dout_sems)])
            ship_middle(1)

    window.relay_diagonal([(facts2_ref, facts2_sems), (dout_ref, dout_sems)])
    ship_middle(2)
    keep_pieces(1, tn(heads_ref[core, 0], first_ref[...]))
    for group in early_groups:
        lows_sum[group].start()
    reduces[2].start()

    window_late = [(query_ref, query_sems), (facts2_ref, facts2_sems), (dout_ref, dout_sems)]
    window.finish(window_late)
    for group in early_groups:
        lows_sum[group].relay()
    ship_middle(3)
    d_gate = jnp.zeros((own_rows, 1), F32)
    added = [far_added(segment, gate, folded_row) for segment in segments[:2]]
    fixed = (2 * HALF - 1, HALF - 1)
    for head in range(heads):
        cut = slice(head * head_size, (head + 1) * head_size)
        cut_v = slice(inner + head * head_size, inner + (head + 1) * head_size)
        key, value = kv_ref[own, :, cut], kv_ref[own, :, cut_v]
        d_key = jnp.zeros((own_rows, head_size), F32)
        d_value = jnp.zeros((own_rows, head_size), F32)
        for number, segment in enumerate(segments):
            queries = folded(query_ref, spans(segment), head)
            d_heads = folded(dout_ref, spans(segment), head)
            if number < 2:
                extra = added[number] + table_ref[head, fixed[number]]
            else:
                extra = biask_ref[head]
            lse = folded_row(facts2_ref, segment, 4 + head, own_rows)
            delta = folded_row(facts2_ref, segment, head, own_rows)
            probs = jnp.exp(nt(key, queries) + extra - lse)
            d_scores = probs * (nt(value, d_heads) - delta)
            d_value = d_value + nn(probs.astype(BF16), d_heads)
            d_key = d_key + nn(d_scores.astype(BF16), queries)
            d_gate = d_gate + jnp.sum(d_scores, axis=1, keepdims=True)
        heads_ref[core, 1, :, cut] = d_key.astype(BF16)
        heads_ref[core, 2, :, cut] = d_value.astype(BF16)
    dgate_ref[core] = jnp.broadcast_to(d_gate, dgate_ref.shape[1:])
    pair_late = [
        send(ref.at[core], ref.at[core], pair_sems.at[0, 5 + i], pair_sems.at[1, 5 + i], sibling)
        for i, ref in enumerate((heads_ref, dgate_ref))
    ]
    for copy in pair_late:
        copy.start()
    for number in range(2):
        keep_pieces(2 + number, tn(heads_ref[core, 1 + number], first_ref[...]))
    for group in late_groups:
        lows_sum[group].start()

    for copy in pair_late:
        copy.wait()
    d_first = jnp.zeros((own_rows, width), F32)
    for side in range(2):
        for number in range(3):
            d_first = d_first + nn(heads_ref[side, number], wqkv_ref[side, number])
    back, g_attn_grad = norm_back(packed_ref[...].astype(F32), g_attn, d_first)
    inside = slice(MARGIN, MARGIN + own_rows)
    back_ref[inside, :] = (part_ref[...] + back).astype(BF16)
    d_gate = dgate_ref[0] + dgate_ref[1]
    lane_g = lax.broadcasted_iota(jnp.int32, d_gate.shape, 1)
    terms = jnp.zeros(d_gate.shape, F32)
    for number, term in enumerate(split3(d_gate)):
        terms = jnp.where(lane_g == number, term, terms)
    backaux_ref[inside, :] = terms.astype(BF16)
    down_src, down_dst = pl.ds(MARGIN, MARGIN), pl.ds(own_rows + MARGIN, MARGIN)
    up_src, up_dst = pl.ds(own_rows, MARGIN), pl.ds(0, MARGIN)
    start_edges, finish_edges = edges(
        edge2_sems,
        [
            (0, back_ref.at[down_src], back_ref.at[down_dst]),
            (1, backaux_ref.at[down_src], backaux_ref.at[down_dst]),
        ],
        [
            (2, back_ref.at[up_src], back_ref.at[up_dst]),
            (3, backaux_ref.at[up_src], backaux_ref.at[up_dst]),
        ],
    )
    start_edges()

    @pl.when(me == 0)
    def _():
        back_ref[up_dst, :] = jnp.zeros((MARGIN, width), BF16)
        backaux_ref[up_dst, :] = jnp.zeros((MARGIN, 128), BF16)

    @pl.when(me == rows - 1)
    def _():
        back_ref[down_dst, :] = jnp.zeros((MARGIN, width), BF16)
        backaux_ref[down_dst, :] = jnp.zeros((MARGIN, 128), BF16)

    gate_s = sigmoid(raw_logit)
    gate_slope = DELETE_SCALE * gate_s * (1.0 - gate_s)
    raw_scaled = gcot_ref[...] * gate_slope * raw_scale
    common = jnp.sum(
        nt(stacked_rows(split3(raw_scaled), raw_count), byte_ref[...]), axis=0, keepdims=True
    )
    packed = packed_ref[...].astype(F32)
    scale = row_scale(packed)
    own_s = sigmoid(gate_logit(packed, scale, gate_weight))
    own_scaled = d_gate[:, 0:1] * (DELETE_SCALE * own_s * (1.0 - own_s)) * scale
    common = common + jnp.sum(own_scaled * packed, axis=0, keepdims=True)
    slow_ref[low, 0:1, :] = g_ff_grad
    slow_ref[low, 1:2, :] = g_attn_grad
    slow_ref[low, 2:3, :] = common * g_delete
    slow_ref[low, 3:4, :] = common * w_delete
    slow_ref[low, 4:5, :] = bias_grad
    slow_ref[low, 5:8, :] = jnp.zeros((3, width), F32)

    def slow_copy(step, source):
        return send(
            slow_ref.at[source],
            slow_ref.at[source],
            slow_sems.at[0, step],
            slow_sems.at[1, step],
            low_peer(step),
        )

    def start_slow(step, carry):
        slow_copy(step, low).start()
        return carry

    def finish_slow(step, carry):
        slow_copy(step, low).wait_send()
        slow_copy(step, low_source(step)).wait_recv()
        return carry

    def shigh_copy(step, source):
        return send(
            shigh_ref.at[source],
            shigh_ref.at[source],
            shigh_sems.at[0, step],
            shigh_sems.at[1, step],
            high_peer(step),
        )

    lax.fori_loop(1, lows, start_slow, 0)
    for group in early_groups:
        share_low(group)
    for group in late_groups:
        lows_sum[group].relay()
    reduces[2].relay()
    for group in early_groups:
        share_high(group)
    for group in late_groups:
        share_low(group)
    lax.fori_loop(1, lows, finish_slow, 0)
    small = slow_ref[0]
    for number in range(1, lows):
        small = small + slow_ref[number]
    shigh_ref[high] = small
    for step in range(1, HI):
        shigh_copy(step, high).start()
    for group in early_groups:
        spread_low(group)
    for group in late_groups:
        share_high(group)
    for group in early_groups:
        lasts[group].relay()
    for group in late_groups:
        spread_low(group)

    finish_edges()
    spread = tn(backaux_ref[...], chosen_ref[...])
    raw_cot = gcot_ref[...] + (spread[0:1, :] + spread[1:2, :] + spread[2:3, :])
    d_logit = raw_cot * gate_slope
    scaled = d_logit * raw_scale
    along = d_logit * raw_logit * raw_scale * raw_scale * (1.0 / width)
    s1, s2, s3 = split3(scaled)
    w1, w2, w3 = split3(gate_weight)
    outer = tn(
        stacked_rows((w1, w1, w2, w2, w1, w3), width),
        stacked_rows((s1, s2, s1, s2, s3, s1), raw_count),
    )
    rows_ref[...] = outer - along * byte_ref[...].astype(F32)
    rows_ref[...] = rows_ref[...] + tn(back_ref[...], chosen_ref[...])
    for step in range(1, HI):
        shigh_copy(step, high).wait_send()
        shigh_copy(step, high_other(step)).wait_recv()
    small = shigh_ref[0]
    for number in range(1, HI):
        small = small + shigh_ref[number]
    small_ref[...] = small

    sib_copy(0, 0).wait()
    part_ref[mine, :] = mixed_ref[mine, :] + (kept_ref[0] + sin_ref[0, 0].astype(F32))

    def add_line(middle):
        for slot in (2, 4) if middle else (0,):
            line_arrived(slot)
            part_ref[mine, :] = part_ref[mine, :] + line_ref[slot].astype(F32)
        for turn in range(1, HI):
            line_copy(turn, middle).wait_send()

    @pl.when(end_high)
    def _():
        add_line(False)

    @pl.when(middle_high)
    def _():
        add_line(True)

    block_ref[mine, :] = part_ref[mine, :].astype(BF16)
    block_copy = send(
        block_ref.at[mine], block_ref.at[mine], half_sems.at[0, 1], half_sems.at[1, 1], sibling
    )
    block_copy.start()

    def finish_reduce(number):
        reduces[number].finish()
        total = wall_ref[number, my_share, :].astype(F32)
        for begin in range(0, len(arrived), HI):
            loads = [
                pltpu.make_async_copy(
                    ffin_ref.at[number, slot],
                    sec_ref.at[place, pl.ds(0, share)],
                    local_sems.at[3 + place],
                )
                for place, slot in enumerate(arrived[begin : begin + HI])
            ]
            for load in loads:
                load.start()
            for load in loads:
                load.wait()
            for place in range(len(loads)):
                total = total + sec_ref[place, 0:share, :].astype(F32)
        ffo_ref[number] = total

    finish_reduce(0)
    finish_reduce(1)
    for group in late_groups:
        lasts[group].relay()
    finish_reduce(2)
    block_copy.wait()
    for group in range(groups):
        lasts[group].finish()
        own_lasts[group].wait()


def layer(rows, offsets, *operands):
    lengths, table, byte_t, keep, vecs, gcot, wq, wk, wv, wo, wg, wu, wd, cot = operands
    width, raw_count = byte_t.shape
    own_rows = cot.shape[0]
    inner = wq.shape[0]
    heads = table.shape[0]
    share = wd.shape[0]
    lows = rows // HI
    hidden = lows * share
    slots = len(offsets)
    half = own_rows // 2
    groups = 4 * inner // 128
    piece = 128 // lows
    lanes = -(-width // (128 * HI)) * 128 * HI
    slots_in = 2 if lows == 4 else lows
    window_sems = 3 * slots
    ff_cut, z_cut = share // 2 // 16 * 16, piece // 2 // 16 * 16
    ext_rows = own_rows + 2 * MARGIN
    vmem = pl.BlockSpec(memory_space=pltpu.VMEM)
    smem = pl.BlockSpec(memory_space=pltpu.SMEM)
    anywhere = pl.BlockSpec(memory_space=pl.ANY)
    shape = jax.ShapeDtypeStruct
    dma = pltpu.SemaphoreType.DMA
    outs = [
        shape((1, raw_count), F32),
        shape((own_rows, width), BF16),
        shape((width, raw_count), F32),
        shape((8, width), F32),
        shape((3, share, width), F32),
        shape((groups, lows, piece, lanes), BF16),
        shape((3, slots_in, share, width), BF16),
    ]
    out_specs = [vmem] * 5 + [anywhere] * 2
    scratch = [
        pltpu.VMEM((rows, 8, 128), F32),
        pltpu.VMEM((ext_rows, raw_count), BF16),
        pltpu.VMEM((ext_rows, width), BF16),
        pltpu.VMEM((ext_rows, 128), BF16),
        pltpu.VMEM((MARGIN, width), BF16),
        pltpu.VMEM((MARGIN, width), BF16),
        pltpu.VMEM((MARGIN, 128), BF16),
        pltpu.VMEM((MARGIN, 128), BF16),
        pltpu.VMEM((own_rows, width), BF16),
        pltpu.VMEM((own_rows, 128), F32),
        pltpu.VMEM((own_rows, width), BF16),
        pltpu.VMEM((slots, own_rows, 2 * inner), BF16),
        pltpu.VMEM((slots, half, 2 * inner), BF16),
        pltpu.VMEM((slots, 8, 256), F32),
        pltpu.VMEM((slots, half, 2 * inner), BF16),
        pltpu.VMEM((slots, 8, 256), F32),
        pltpu.VMEM((heads, own_rows, 3 * own_rows), F32),
        pltpu.VMEM((heads, own_rows, 3 * own_rows), F32),
        pltpu.VMEM((2, own_rows, inner), BF16),
        pltpu.VMEM((own_rows, inner), F32),
        pltpu.VMEM((own_rows, 128), F32),
        pltpu.VMEM((own_rows, width), F32),
        pltpu.VMEM((HI, own_rows, width), BF16),
        pltpu.VMEM((HI, own_rows, width), BF16),
        pltpu.VMEM((3, hidden, width), BF16),
        pltpu.VMEM((2, inner, width), BF16),
        pltpu.VMEM((2, 3, inner, width), BF16),
        pltpu.VMEM((HI * own_rows, hidden), BF16),
        pltpu.VMEM((HI * own_rows, hidden), BF16),
        pltpu.VMEM((HI * own_rows, hidden), BF16),
        pltpu.VMEM((own_rows, width), F32),
        pltpu.VMEM((5, half, width), F32),
        pltpu.VMEM((HI, half, width), BF16),
        pltpu.VMEM((2, HI, half, width), BF16),
        pltpu.VMEM((2, HI - 1, half, width), BF16),
        pltpu.VMEM((HI - 1, half, width), BF16),
        pltpu.VMEM((5, half, width), BF16),
        pltpu.VMEM((own_rows, width), F32),
        pltpu.VMEM((2, 3, own_rows, inner), BF16),
        pltpu.VMEM((2, own_rows, 128), F32),
        pltpu.VMEM((groups, lows, piece, lanes), BF16),
        pltpu.VMEM((groups, slots_in, piece, lanes), BF16),
        pltpu.VMEM((groups, HI, piece, lanes // HI), BF16),
        pltpu.VMEM((groups, piece, lanes), BF16),
        pltpu.VMEM((lows, 8, width), F32),
        pltpu.VMEM((HI, 8, width), F32),
        pltpu.VMEM((ext_rows, width), BF16),
        pltpu.VMEM((ext_rows, 128), BF16),
        pltpu.VMEM((3, max(ff_cut, 16), width), BF16),
        pltpu.VMEM((3, share - ff_cut, width), BF16),
        pltpu.VMEM((groups, max(z_cut, 16), lanes), BF16),
        pltpu.VMEM((groups, piece - z_cut, lanes), BF16),
        dma((2, rows)),
        dma((2, 4)),
        dma((2, window_sems)),
        dma((2, window_sems)),
        dma((2, window_sems)),
        dma((2, window_sems)),
        dma((2, window_sems)),
        dma((4, 2, max(5, lows))),
        dma((2, 7)),
        dma((8 + groups,)),
        dma((2, 2, HI)),
        dma((2, 2, HI)),
        dma((2, HI)),
        dma((2, HI)),
        dma((2, 2, HI)),
        dma((2, HI)),
        dma((2, 5)),
        dma((2, 2)),
        dma((3, 2, max(5, lows))),
        dma((groups, 2, max(5, lows))),
        dma((2, groups, HI)),
        dma((2, groups, HI)),
        dma((groups, 2, max(5, lows))),
        dma((2, 4)),
        dma((2, lows)),
        dma((2, HI)),
    ]
    return pl.pallas_call(
        functools.partial(layer_kernel, rows, offsets),
        name="layer",
        out_shape=outs,
        in_specs=[smem, smem] + [vmem] * 4 + [anywhere] * 8,
        out_specs=out_specs,
        scratch_shapes=scratch,
        compiler_params=pltpu.CompilerParams(
            collective_id=0, has_side_effects=True, vmem_limit_bytes=VMEM_LIMIT
        ),
    )(*operands)


def finish_kernel(
    att_ref,
    ff_ref,
    block_ref,
    rows_ref,
    gate_ref,
    small_ref,
    out_ref,
    query_ref,
    key_ref,
    value_ref,
    ffg_ref,
    ffu_ref,
    ffd_ref,
    block_out_ref,
    rows_out_ref,
    gate_out_ref,
    bias_ref,
    load_ref,
    wide_ref,
    ff_hold_ref,
    rows_hold_ref,
    block_hold_ref,
    gate_hold_ref,
    load_sems,
    store_sems,
    pass_sems,
):
    width = out_ref.shape[1]
    heads, buckets = bias_ref.shape
    results = (out_ref, query_ref, key_ref, value_ref)
    loads = [
        pltpu.make_async_copy(att_ref.at[number], load_ref.at[number], load_sems.at[number])
        for number in range(4)
    ]
    for load in loads:
        load.start()
    holds = [
        (rows_ref, rows_hold_ref, rows_out_ref),
        (ff_ref.at[0], ff_hold_ref.at[0], ffg_ref),
        (ff_ref.at[1], ff_hold_ref.at[1], ffu_ref),
        (ff_ref.at[2], ff_hold_ref.at[2], ffd_ref),
        (block_ref, block_hold_ref, block_out_ref),
        (gate_ref, gate_hold_ref, gate_out_ref),
    ]
    fetches = [
        pltpu.make_async_copy(src, hold, pass_sems.at[0, number])
        for number, (src, hold, _) in enumerate(holds)
    ]
    for copy in fetches:
        copy.start()
    for head in range(heads):
        bias_ref[head : head + 1, :] = small_ref[4:5, head * buckets : (head + 1) * buckets]
    stores = []
    for number, (_, hold, result) in enumerate(holds):
        fetches[number].wait()
        store = pltpu.make_async_copy(hold, result, pass_sems.at[1, number])
        store.start()
        stores.append(store)
    for number, load in enumerate(loads):
        load.wait()
        wide_ref[number] = load_ref[number, :, 0:width].astype(F32)
        store = pltpu.make_async_copy(
            wide_ref.at[number], results[number], store_sems.at[number]
        )
        store.start()
        stores.append(store)
    for copy in stores:
        copy.wait()


def finish(att_grads, ff_sums, block, grad_rows, gate, small, heads, buckets):
    _, inner, lanes = att_grads.shape
    _, share, width = ff_sums.shape
    vmem = pl.BlockSpec(memory_space=pltpu.VMEM)
    anywhere = pl.BlockSpec(memory_space=pl.ANY)
    shape = jax.ShapeDtypeStruct
    dma = pltpu.SemaphoreType.DMA
    outs = [shape((inner, width), F32)] * 4 + [shape((share, width), F32)] * 3
    outs += [shape(array.shape, array.dtype) for array in (block, grad_rows, gate)]
    outs += [shape((heads, buckets), F32)]
    return pl.pallas_call(
        finish_kernel,
        name="finish",
        out_shape=outs,
        in_specs=[anywhere] * 5 + [vmem],
        out_specs=[anywhere] * 10 + [vmem],
        scratch_shapes=[
            pltpu.VMEM((4, inner, lanes), BF16),
            pltpu.VMEM((4, inner, width), F32),
            pltpu.VMEM((3, share, width), F32),
            pltpu.VMEM(grad_rows.shape, F32),
            pltpu.VMEM(block.shape, BF16),
            pltpu.VMEM(gate.shape, F32),
            dma((4,)),
            dma((4,)),
            dma((2, 6)),
        ],
        compiler_params=pltpu.CompilerParams(vmem_limit_bytes=VMEM_LIMIT),
    )(att_grads, ff_sums, block, grad_rows, gate, small)


def per_device(
    byte_rows,
    lengths,
    keep_mask,
    w_delete,
    g_delete,
    g_attn,
    w_query,
    w_key,
    w_value,
    w_out,
    rel_bias,
    g_ff,
    w_gate,
    w_up,
    w_down,
    out_cot,
    gate_cot,
):
    raw_count, width = byte_rows.shape
    own_rows = out_cot.shape[0]
    inner = w_query.shape[1]
    buckets, heads = rel_bias.shape
    rows = lax.axis_size("rows")
    share = w_down.shape[0]
    offsets = slots_of(reach_of(raw_count, own_rows))
    line = lax.broadcasted_iota(jnp.int32, (8, width), 0)
    vecs = jnp.zeros((8, width), F32)
    for number, vector in enumerate((g_delete, w_delete, g_attn, g_ff)):
        vecs = jnp.where(line == number, vector[None, :], vecs)
    spare = -share % 16
    weights = [jnp.pad(w, ((0, spare), (0, 0))) for w in (w_gate.T, w_up.T, w_down)]
    gate, block_out, grad_rows, small, ff_sums, att_grads, _ = layer(
        rows,
        offsets,
        lengths,
        rel_bias.T,
        byte_rows.T,
        keep_mask.reshape(1, -1),
        vecs,
        gate_cot.reshape(1, -1),
        w_query.T,
        w_key.T,
        w_value.T,
        w_out,
        *weights,
        out_cot,
    )
    (
        grad_out,
        grad_query,
        grad_key,
        grad_value,
        grad_gate,
        grad_up,
        grad_down,
        block_out,
        grad_rows,
        gate,
        grad_bias,
    ) = finish(
        att_grads.reshape(4, inner, -1),
        ff_sums[:, :share],
        block_out,
        grad_rows,
        gate,
        small,
        heads,
        buckets,
    )
    return (
        block_out,
        gate[0],
        grad_rows.T,
        small[2],
        small[3],
        small[1],
        grad_query.T,
        grad_key.T,
        grad_value.T,
        grad_out,
        grad_bias.T,
        small[0],
        grad_gate.T,
        grad_up.T,
        grad_down,
    )


def solution(mesh):
    in_specs = (
        P("rows", None),
        P(),
        P("rows"),
        P(),
        P(),
        P(),
        P(None, "tensor"),
        P(None, "tensor"),
        P(None, "tensor"),
        P("tensor", None),
        P(None, "tensor"),
        P(),
        P(None, ("rows", "tensor")),
        P(None, ("rows", "tensor")),
        P(("rows", "tensor"), None),
        P("rows", None),
        P("rows"),
    )
    out_specs = (
        P("rows", None),
        P("rows"),
        P("rows", None),
        P(),
        P(),
        P(),
        P(None, "tensor"),
        P(None, "tensor"),
        P(None, "tensor"),
        P("tensor", None),
        P(None, "tensor"),
        P(),
        P(None, ("rows", "tensor")),
        P(None, ("rows", "tensor")),
        P(("rows", "tensor"), None),
    )
    return jax.shard_map(
        per_device, mesh=mesh, in_specs=in_specs, out_specs=out_specs, check_vma=False
    )
```

```python
import functools

import jax
import jax.numpy as jnp
from jax import lax
from jax.experimental import pallas as pl
from jax.experimental.pallas import tpu as pltpu
from jax.sharding import PartitionSpec as P

MAXLEN = 1024
MARGIN = 32
EPS = 1e-06
DELETE_SCALE = -30.0
NEGATIVE = -1e30
LIMITS = (1, 2, 3, 4, 5, 6, 7, 8, 12, 16, 23, 32, 46, 64, 91)
HALF = 16
HI = 4
MESH = pl.DeviceIdType.MESH
F32 = jnp.float32
BF16 = jnp.bfloat16
VMEM_LIMIT = 63 * 1024 * 1024


def nn(a, b):
    return lax.dot_general(a, b, (((1,), (0,)), ((), ())), preferred_element_type=F32)


def nt(a, b):
    return lax.dot_general(a, b, (((1,), (1,)), ((), ())), preferred_element_type=F32)


def tn(a, b):
    return lax.dot_general(a, b, (((0,), (0,)), ((), ())), preferred_element_type=F32)


def eye(count):
    return lax.broadcasted_iota(jnp.int32, (count, count), 0) == lax.broadcasted_iota(
        jnp.int32, (count, count), 1
    )


def to_row(column, diagonal):
    return jnp.sum(jnp.where(diagonal, column, 0.0), axis=0, keepdims=True)


def to_column(row, diagonal):
    return jnp.sum(jnp.where(diagonal, row, 0.0), axis=1, keepdims=True)


def row_scale(values):
    return lax.rsqrt(jnp.mean(values * values, axis=-1, keepdims=True) + EPS)


def gate_logit(values, scale, weight):
    return scale * jnp.sum(values * weight, axis=-1, keepdims=True)


def sigmoid(value):
    return 1.0 / (1.0 + jnp.exp(-value))


def norm_back(values, gain, grad):
    scale = row_scale(values)
    scaled = grad * gain
    inner = jnp.mean(scaled * values, axis=-1, keepdims=True)
    back = scale * scaled - values * (scale * scale * scale * inner)
    return back, jnp.sum(grad * values * scale, axis=0, keepdims=True)


def reach_of(raw_count, own_rows):
    span = (MAXLEN // raw_count - 1) * own_rows + 2 * MARGIN + raw_count
    return -(-(span - 1) // own_rows)


def slots_of(reach):
    far = list(range(2, reach + 1))
    return [-d for d in reversed(far)] + far + [-1, 0, 1]


def meet_rows(rows):
    me, core = lax.axis_index("rows"), lax.axis_index("tensor")
    barrier = pltpu.get_barrier_semaphore()

    def greet(step, carry):
        pl.semaphore_signal(
            barrier, inc=1, device_id=(lax.rem(me + step, rows), core), device_id_type=MESH
        )
        return carry

    lax.fori_loop(1, rows, greet, 0)
    pl.semaphore_signal(barrier, inc=1, device_id=(me, 1 - core), device_id_type=MESH)
    pl.semaphore_wait(barrier, rows)


def send(src, dst, send_sem, recv_sem, target):
    return pltpu.make_async_remote_copy(
        src_ref=src,
        dst_ref=dst,
        send_sem=send_sem,
        recv_sem=recv_sem,
        device_id=target,
        device_id_type=MESH,
    )


class Window:
    def __init__(self, rows, offsets):
        self.rows, self.offsets = rows, offsets
        self.me, self.core = lax.axis_index("rows"), lax.axis_index("tensor")
        self.slot = {offset: number for number, offset in enumerate(offsets)}
        self.own = self.slot[0]
        side = rows // HI
        self.low = lax.rem(self.me, side)
        self.first, self.second, self.third = [], {}, []
        self.awaited = {}
        if side != 4:
            self.first = [(self.inside(d), self.own, d, self.slot[-d]) for d in offsets if d]
            self.number_all()
            return
        both = jnp.logical_and
        along_x = {1: lax.rem(self.low, 2) == 0, -1: lax.rem(self.low, 2) == 1}
        along_y = {2: self.low < 2, -2: self.low >= 2}
        beside = [*along_x.items(), *along_y.items()]
        for d in (side, -side):
            self.first.append((self.inside(d), self.own, d, self.slot[-d]))
        for step, when in beside:
            self.first.append((when, self.own, step, self.slot[-step]))
        for d in offsets:
            if abs(d) > side:
                when = self.low + d >= 2 * side if d > 0 else self.low + d < -side
                self.first.append((both(when, self.inside(d)), self.own, d, self.slot[-d]))
        for d in (side, -side):
            self.awaited[d] = [self.inside(d)]
            self.second[d] = [
                (when, self.slot[d], step, self.slot[d - step])
                for step, when in beside
                if d - step in self.slot
            ]
        for step_x, when_x in along_x.items():
            for step_y, when_y in along_y.items():
                when = both(when_x, when_y)
                entry = (when, self.slot[step_y], step_x, self.slot[step_y - step_x])
                self.third.append((step_y, entry))
                for d in (side, -side):
                    came = d + step_x
                    if came - step_y in self.slot:
                        there = both(when, self.inside(d))
                        entry = (there, self.slot[came], step_y, self.slot[came - step_y])
                        self.third.append((came, entry))
        for came, entry in self.third:
            self.awaited.setdefault(came, []).append(entry[0])
        self.number_all()

    def number_all(self):
        entries = list(self.first)
        for later in self.second.values():
            entries += later
        entries += [entry for _, entry in self.third]
        self.entries = entries

    def inside(self, offset):
        if offset < 0:
            return self.me >= -offset
        return self.me < self.rows - offset

    def copy(self, ref, sems, entry):
        _, here, step, there = entry
        number = [other is entry for other in self.entries].index(True)
        target = (self.me + step, self.core)
        return send(
            ref.at[here], ref.at[there], sems.at[0, number], sems.at[1, there], target
        )

    def arrival(self, ref, sems, offset):
        place = ref.at[self.slot[offset]]
        other = (self.me, 1 - self.core)
        return send(place, place, sems.at[0, 0], sems.at[1, self.slot[offset]], other)

    def start(self, pairs):
        for entry in self.first:

            @pl.when(entry[0])
            def _():
                for ref, sems in pairs:
                    self.copy(ref, sems, entry).start()

    def relay(self, pairs):
        for offset, entries in self.second.items():

            @pl.when(self.inside(offset))
            def _():
                for ref, sems in pairs:
                    self.arrival(ref, sems, offset).wait_recv()

                for entry in entries:

                    @pl.when(entry[0])
                    def _():
                        for ref, sems in pairs:
                            self.copy(ref, sems, entry).start()

    def relay_diagonal(self, pairs):
        for offset, entry in self.third:

            @pl.when(entry[0])
            def _():
                for ref, sems in pairs:
                    self.arrival(ref, sems, offset).wait_recv()
                    self.copy(ref, sems, entry).start()

    def finish(self, pairs):
        for offset in self.offsets:
            if offset:
                waiting = self.inside(offset)
                for when in self.awaited.get(offset, ()):
                    waiting = jnp.logical_and(waiting, jnp.logical_not(when))

                @pl.when(waiting)
                def _():
                    for ref, sems in pairs:
                        self.arrival(ref, sems, offset).wait_recv()

        for entry in self.entries:
            when = entry[0]
            for offset, entries in self.second.items():
                if any(entry is other for other in entries):
                    when = jnp.logical_and(when, self.inside(offset))

            @pl.when(when)
            def _():
                for ref, sems in pairs:
                    self.copy(ref, sems, entry).wait_send()

    def clear(self, ref, value):
        for offset in self.offsets:
            if offset:

                @pl.when(jnp.logical_not(self.inside(offset)))
                def _():
                    ref[self.slot[offset]] = jnp.full(ref.shape[1:], value, ref.dtype)


EDGE = -(-LIMITS[-1] // 16) * 16


def near_bias(gap, table_ref, head, above, below):
    if above and below:
        bias = jnp.full(gap.shape, table_ref[head, 0], F32)
    else:
        bias = jnp.full(gap.shape, table_ref[head, HALF if above else 0], F32)
    for number, limit in enumerate(LIMITS):
        if above:
            bias = jnp.where(gap >= limit, table_ref[head, HALF + number + 1], bias)
        if below:
            bias = jnp.where(gap <= -limit, table_ref[head, number + 1], bias)
    return bias


def joined_row(facts_ref, slots, line, width):
    return jnp.concatenate([facts_ref[slot, line : line + 1, :width] for slot in slots], axis=1)


GELU_A = 0.7978845608028654
GELU_B = 0.044715


def folded_row(facts_ref, slots, line, width):
    half = width // 2
    return jnp.concatenate(
        [
            facts_ref[slot, line : line + 1, begin : begin + half]
            for begin in (0, half)
            for slot in slots
        ],
        axis=1,
    )


def split3(value):
    one = value.astype(BF16).astype(F32)
    rest = value - one
    two = rest.astype(BF16).astype(F32)
    return one, two, (rest - two).astype(BF16).astype(F32)


def stacked_rows(rows, width):
    line = lax.broadcasted_iota(jnp.int32, (8, width), 0)
    result = jnp.zeros((8, width), F32)
    for number, row in enumerate(rows):
        result = jnp.where(line == number, row, result)
    return result.astype(BF16)


def layer_kernel(
    rows,
    offsets,
    lengths_ref,
    table_ref,
    byte_ref,
    keep_ref,
    vec_ref,
    gcot_ref,
    wq_ref,
    wk_ref,
    wv_ref,
    wo_ref,
    wg_ref,
    wu_ref,
    wd_ref,
    cot_ref,
    gate_ref,
    block_ref,
    rows_out_ref,
    small_ref,
    ffo_out_ref,
    attg_ref,
    ffin_ref,
    rows_ref,
    ffo_ref,
    count_ref,
    chosen_ref,
    ext_ref,
    extaux_ref,
    below_ref,
    above_ref,
    belowaux_ref,
    aboveaux_ref,
    packed_ref,
    aux_ref,
    first_ref,
    kv_ref,
    query_ref,
    facts_ref,
    dout_ref,
    facts2_ref,
    biasq_ref,
    biask_ref,
    att_ref,
    attf_ref,
    lse_ref,
    mixed_ref,
    sec_ref,
    cots_ref,
    wall_ref,
    wout_ref,
    wqkv_ref,
    mid_ref,
    dgated_ref,
    dupper_ref,
    part_ref,
    kept_ref,
    sout_ref,
    sin_ref,
    hout_ref,
    hin_ref,
    line_ref,
    dsec_ref,
    heads_ref,
    dgate_ref,
    zout_ref,
    zin_ref,
    yin_ref,
    fin_ref,
    slow_ref,
    shigh_ref,
    back_ref,
    backaux_ref,
    ffa_ref,
    ffb_ref,
    za_ref,
    zb_ref,
    count_sems,
    edge_sems,
    kv_sems,
    query_sems,
    facts_sems,
    dout_sems,
    facts2_sems,
    wall_sems,
    pair_sems,
    local_sems,
    cot_sems,
    cotf_sems,
    sec_sems,
    secf_sems,
    sib_sems,
    hi_sems,
    line_sems,
    half_sems,
    ff_sems,
    low_sems,
    high_sems,
    back_sems,
    last_sems,
    edge2_sems,
    slow_sems,
    shigh_sems,
):
    width, raw_count = byte_ref.shape
    own_rows = cot_ref.shape[0]
    inner = wq_ref.shape[0]
    heads = table_ref.shape[0]
    head_size = inner // heads
    share = wd_ref.shape[0]
    lows = rows // HI
    half = own_rows // 2
    ext_rows = own_rows + 2 * MARGIN
    me, core = lax.axis_index("rows"), lax.axis_index("tensor")
    high, low = lax.div(me, lows), lax.rem(me, lows)
    sibling = (me, 1 - core)
    mine = pl.ds(pl.multiple_of(core * half, half), half)
    theirs = pl.ds(pl.multiple_of((1 - core) * half, half), half)
    window = Window(rows, offsets)
    own = window.own
    g_delete, w_delete = vec_ref[0:1, :], vec_ref[1:2, :]
    g_attn, g_ff = vec_ref[2:3, :], vec_ref[3:4, :]

    is_square = lows == 4

    def low_other(step):
        if step == 1:
            return low + 1 - 2 * lax.rem(low, 2)
        if step == 2:
            return lax.rem(low + 2, lows)
        return lows - 1 - low

    def low_pair(step):
        return (high * lows + low_other(step), core)

    def low_peer(step):
        return (high * lows + lax.rem(low + step, lows), core)

    def low_source(step):
        return lax.rem(low + lows - step, lows)

    def high_other(step):
        if step == 0:
            return high
        if step == 1:
            return high + 1 - 2 * lax.rem(high, 2)
        if step == 2:
            return lax.rem(high + 2, HI)
        return HI - 1 - high

    def high_peer(step):
        return (high_other(step) * lows + low, core)

    middle_high = jnp.logical_and(high >= 1, high <= 2)
    end_high = jnp.logical_not(middle_high)
    upper_high = lax.div(high, 2)
    inner_high = high + 1 - 2 * upper_high
    outer_high = high - 1 + 2 * upper_high

    def line_chunk(turn):
        if turn == 0:
            return high
        if turn == 1:
            return 3 - 3 * upper_high
        if turn == 2:
            return 2 - upper_high
        return 1 - high + 4 * upper_high

    def first_half(count):
        return count // 2 // 16 * 16

    class LowGather:
        def __init__(self, source, block, count, sems):
            self.source, self.block, self.count, self.sems = source, block, count, sems
            cut = first_half(count)
            self.halves = ((0, cut), (cut, count - cut))

        def copy(self, src, dst, number, target):
            return send(src, dst, self.sems.at[0, number], self.sems.at[1, number], target)

        def direct(self, step):
            if is_square:
                target = low_pair(step)
            else:
                target = low_peer(step)
            return self.copy(self.source, self.block(low, 0, self.count), step, target)

        def arrival(self, step):
            place = self.block(low_other(step) if is_square else low_source(step), 0, self.count)
            return self.copy(place, place, step, sibling)

        def passed(self, side):
            place = self.block(low_other(2 - side), *self.halves[side])
            return self.copy(place, place, 3 + side, low_pair(1 + side))

        def start(self):
            if is_square:
                self.direct(1).start()
                self.direct(2).start()
                return

            def one(step, carry):
                self.direct(step).start()
                return carry

            lax.fori_loop(1, lows, one, 0)

        def relay(self):
            if is_square:
                for side in (1, 0):
                    self.arrival(2 - side).wait_recv()
                    self.passed(side).start()

        def finish(self):
            if is_square:
                for step in (1, 2):
                    self.direct(step).wait_send()
                for side in range(2):
                    self.passed(side).wait_send()
                    place = self.block(low_other(3), *self.halves[side])
                    self.copy(place, place, 3 + side, sibling).wait_recv()
                return

            def one(step, carry):
                self.direct(step).wait_send()
                self.arrival(step).wait_recv()
                return carry

            lax.fori_loop(1, lows, one, 0)

    class LowReduce:
        def __init__(self, part, count, relays, arrivals, sems):
            self.part, self.count, self.sems = part, count, sems
            self.relays, self.arrivals = relays, arrivals
            cut = first_half(count)
            self.halves = ((0, cut), (cut, count - cut))

        def copy(self, src, dst, number, target):
            return send(src, dst, self.sems.at[0, number], self.sems.at[1, number], target)

        def half(self, side):
            return self.copy(
                self.part(low_other(3), *self.halves[side]),
                self.relays[side],
                side,
                low_pair(2 - side),
            )

        def summed(self, side):
            return self.copy(
                self.part(low_other(1 + side), 0, self.count),
                self.arrivals.at[side],
                2 + side,
                low_pair(1 + side),
            )

        def direct(self, step):
            return self.copy(
                self.part(lax.rem(low + step, lows), 0, self.count),
                self.arrivals.at[step],
                step,
                low_peer(step),
            )

        def start(self):
            if is_square:
                for side in range(2):
                    self.half(side).start()
                return

            def one(step, carry):
                self.direct(step).start()
                return carry

            lax.fori_loop(1, lows, one, 0)

        def relay(self):
            if is_square:
                for side in range(2):
                    self.half(side).wait()
                    mine_too = self.part(low_other(1 + side), *self.halves[side])
                    both = mine_too[...].astype(F32) + self.relays[side][...].astype(F32)
                    mine_too[...] = both.astype(BF16)
                    self.summed(side).start()

        def finish(self):
            if is_square:
                for side in range(2):
                    self.summed(side).wait()
                return

            def one(step, carry):
                self.direct(step).wait()
                return carry

            lax.fori_loop(1, lows, one, 0)

    arrived = range(2) if is_square else range(1, lows)

    meet_rows(rows)

    keep = keep_ref[...].astype(F32)
    count_ref[me] = jnp.broadcast_to(jnp.sum(keep, axis=1, keepdims=True), (8, 128))

    def count_copy(step):
        return send(
            count_ref.at[me],
            count_ref.at[me],
            count_sems.at[0, step],
            count_sems.at[1, step],
            (lax.rem(me + step, rows), core),
        )

    def count_arrival(step):
        source = lax.rem(me + rows - step, rows)
        return send(
            count_ref.at[source],
            count_ref.at[source],
            count_sems.at[0, step],
            count_sems.at[1, step],
            (source, core),
        )

    def start_count(step, carry):
        count_copy(step).start()
        return carry

    lax.fori_loop(1, rows, start_count, 0)

    weight_refs = (wg_ref, wu_ref, wd_ref)
    my_share = pl.ds(pl.multiple_of(low * share, share), share)
    locals_early = [
        pltpu.make_async_copy(ref, wqkv_ref.at[core, number], local_sems.at[number])
        for number, ref in enumerate((wq_ref, wk_ref, wv_ref))
    ]
    locals_late = [
        pltpu.make_async_copy(wo_ref, wout_ref.at[core], local_sems.at[3]),
        pltpu.make_async_copy(cot_ref, cots_ref.at[high], local_sems.at[4]),
    ] + [
        pltpu.make_async_copy(ref, wall_ref.at[number, my_share], local_sems.at[5 + number])
        for number, ref in enumerate(weight_refs)
    ]
    for copy in locals_early + locals_late:
        copy.start()

    def wall_gather(place, number, start, size):
        def block(place, begin, count):
            inside = pl.ds(pl.multiple_of(place * share + start + begin, 16), count)
            return wall_ref.at[number, inside]

        source = weight_refs[number].at[pl.ds(start, size)]
        return LowGather(source, block, size, wall_sems.at[place])

    early = share * 5 // 7 // 16 * 16
    wall_cuts = [(2, 0, early), (2, early, share - early), (0, 0, share), (1, 0, share)]
    walls = [
        wall_gather(place, *cut) if cut[2] else None for place, cut in enumerate(wall_cuts)
    ]

    class Gather:
        def __init__(self, ref, sems, sems_f, offset, count, source=None):
            self.ref, self.sems, self.sems_f = ref, sems, sems_f
            self.part = pl.ds(pl.multiple_of(core * half + offset, 16), count)
            self.other = pl.ds(pl.multiple_of((1 - core) * half + offset, 16), count)
            self.source = ref.at[high] if source is None else source

        def direct(self, step):
            return send(
                self.source.at[self.part],
                self.ref.at[high, self.part],
                self.sems.at[0, step],
                self.sems.at[1, step],
                high_peer(step),
            )

        def arrival(self, step):
            place = self.ref.at[high_other(step), self.part]
            return send(
                place, place, self.sems.at[0, step], self.sems.at[1, step], high_peer(step)
            )

        def relay(self):
            place = self.ref.at[high_other(2), self.part]
            return send(place, place, self.sems.at[0, 0], self.sems.at[1, 3], high_peer(1))

        def forward(self, step, part):
            place = self.ref.at[high_other(step), part]
            return send(
                place, place, self.sems_f.at[0, step], self.sems_f.at[1, step], sibling
            )

        def start(self):
            self.direct(1).start()
            self.direct(2).start()

            @pl.when(middle_high)
            def _():
                self.direct(3).start()

        def arrived(self, step):
            self.arrival(step).wait_recv()
            if step == 2:

                @pl.when(middle_high)
                def _():
                    self.relay().start()

            self.forward(step, self.part).start()

        def forwarded(self, step):
            self.forward(step, self.other).wait_recv()

        def close(self):
            self.direct(1).wait_send()
            self.direct(2).wait_send()

            @pl.when(middle_high)
            def _():
                self.direct(3).wait_send()
                self.relay().wait_send()

            for step in range(1, HI):
                self.forward(step, self.part).wait_send()

    third = half // 3 // 16 * 16
    cot_gathers = [
        Gather(cots_ref, cot_sems.at[number], cotf_sems.at[number], begin, count, cot_ref)
        for number, (begin, count) in enumerate(((0, third), (third, half - third)))
    ]
    sec_gather = Gather(sec_ref, sec_sems, secf_sems, 0, half)

    if early:
        walls[0].start()
    cot_gathers[0].start()
    pair_early = [
        send(wo_ref, wout_ref.at[core], pair_sems.at[0, 0], pair_sems.at[1, 0], sibling)
    ] + [
        send(
            ref,
            wqkv_ref.at[core, number],
            pair_sems.at[0, 1 + number],
            pair_sems.at[1, 1 + number],
            sibling,
        )
        for number, ref in enumerate((wq_ref, wk_ref, wv_ref))
    ]
    for copy in pair_early:
        copy.start()

    gate_weight = g_delete * w_delete
    raw = byte_ref[...]
    raw_f = raw.astype(F32)
    raw_scale = lax.rsqrt(jnp.mean(raw_f * raw_f, axis=0, keepdims=True) + EPS)
    raw_logit = raw_scale * jnp.sum(
        nn(stacked_rows(split3(gate_weight), width), raw), axis=0, keepdims=True
    )
    gate_ref[...] = DELETE_SCALE * sigmoid(raw_logit)
    upper = lax.broadcasted_iota(jnp.int32, (raw_count, raw_count), 0) <= lax.broadcasted_iota(
        jnp.int32, (raw_count, raw_count), 1
    )
    rank = nn(keep.astype(BF16), jnp.where(upper, 1.0, 0.0).astype(BF16)) - 1.0
    lane = lax.broadcasted_iota(jnp.int32, (raw_count, 128), 1)
    local = lax.broadcasted_iota(jnp.int32, (raw_count, 128), 0).astype(F32)
    aux = jnp.where(lane == 0, local, jnp.where(lane == 1, me.astype(F32), 0.0)).astype(BF16)
    window.clear(kv_ref, 0.0)
    window.clear(query_ref, 0.0)
    window.clear(facts_ref, -1.0)
    window.clear(dout_ref, 0.0)
    window.clear(facts2_ref, 0.0)

    def finish_count(step, carry):
        count_copy(step).wait_send()
        count_arrival(step).wait_recv()
        return carry

    lax.fori_loop(1, rows, finish_count, 0)
    lower = lax.broadcasted_iota(jnp.int32, count_ref.shape, 0) < me
    before = jnp.sum(jnp.where(lower, count_ref[...], 0.0), axis=0)[0:1, 0:1]
    place = before + rank - (me * own_rows).astype(F32)
    place = jnp.where(keep > 0.0, place, -4096.0).astype(jnp.int32)
    chosen = place + MARGIN == lax.broadcasted_iota(jnp.int32, (ext_rows, raw_count), 0)
    chosen = jnp.where(chosen, 1.0, 0.0).astype(BF16)
    chosen_ref[...] = chosen
    ext_ref[...] = nt(chosen, raw).astype(BF16)
    extaux_ref[...] = nn(chosen, aux).astype(BF16)

    def edges(sems, downs, ups):
        def copies(pairs, offset):
            return [
                send(src, dst, sems.at[0, number], sems.at[1, number], (me + offset, core))
                for number, src, dst in pairs
            ]

        def start():
            @pl.when(me > 0)
            def _():
                for copy in copies(downs, -1):
                    copy.start()

            @pl.when(me < rows - 1)
            def _():
                for copy in copies(ups, 1):
                    copy.start()

        def finish():
            @pl.when(me > 0)
            def _():
                for copy in copies(downs, -1):
                    copy.wait_send()
                for copy in copies(ups, 1):
                    copy.wait_recv()

            @pl.when(me < rows - 1)
            def _():
                for copy in copies(ups, 1):
                    copy.wait_send()
                for copy in copies(downs, -1):
                    copy.wait_recv()

        return start, finish

    first_rows, last_rows = pl.ds(0, MARGIN), pl.ds(own_rows + MARGIN, MARGIN)
    start_edges, finish_edges = edges(
        edge_sems,
        [
            (0, ext_ref.at[first_rows], above_ref),
            (1, extaux_ref.at[first_rows], aboveaux_ref),
        ],
        [
            (2, ext_ref.at[last_rows], below_ref),
            (3, extaux_ref.at[last_rows], belowaux_ref),
        ],
    )
    start_edges()

    @pl.when(me == 0)
    def _():
        below_ref[...] = jnp.zeros(below_ref.shape, BF16)
        belowaux_ref[...] = jnp.zeros(belowaux_ref.shape, BF16)

    @pl.when(me == rows - 1)
    def _():
        above_ref[...] = jnp.zeros(above_ref.shape, BF16)
        aboveaux_ref[...] = jnp.zeros(aboveaux_ref.shape, BF16)

    packed_ref[...] = ext_ref[MARGIN : MARGIN + own_rows, :]
    aux_ref[...] = extaux_ref[MARGIN : MARGIN + own_rows, :].astype(F32)
    for copy in locals_early:
        copy.wait()
    finish_edges()
    top = own_rows - MARGIN
    packed_ref[0:MARGIN, :] = packed_ref[0:MARGIN, :] + below_ref[...]
    packed_ref[top:, :] = packed_ref[top:, :] + above_ref[...]
    aux_ref[0:MARGIN, :] = aux_ref[0:MARGIN, :] + belowaux_ref[...].astype(F32)
    aux_ref[top:, :] = aux_ref[top:, :] + aboveaux_ref[...].astype(F32)

    packed = packed_ref[...].astype(F32)
    scale = row_scale(packed)
    first = (packed * scale * g_attn).astype(BF16)
    first_ref[...] = first
    kv_ref[own, :, 0:inner] = nt(first, wqkv_ref[core, 1]).astype(BF16)
    kv_ref[own, :, inner : 2 * inner] = nt(first, wqkv_ref[core, 2]).astype(BF16)

    gate = DELETE_SCALE * sigmoid(gate_logit(packed, scale, gate_weight))
    ids = aux_ref[:, 0:1] + raw_count * aux_ref[:, 1:2]
    ids_i = ids.astype(jnp.int32)
    starts = jnp.zeros_like(ids_i)
    end = jnp.int32(0)
    for number in range(lengths_ref.shape[0]):
        end = end + lengths_ref[number]
        starts = jnp.where(ids_i >= end, end, starts)
    starts = starts.astype(F32)
    own_eye = eye(own_rows)
    facts_ref[own] = jnp.zeros(facts_ref.shape[1:], F32)
    facts_ref[own, 0:1, 0:own_rows] = to_row(gate, own_eye)
    facts_ref[own, 1:2, 0:own_rows] = to_row(ids, own_eye)
    facts_ref[own, 2:3, 0:own_rows] = to_row(starts, own_eye)
    window.start([(facts_ref, facts_sems), (kv_ref, kv_sems)])
    cot_gathers[1].start()
    def fold(ref, value):
        ref[own, :, 0:inner] = value[0:half, :]
        ref[own, :, inner : 2 * inner] = value[half:, :]

    def unfold(ref, head):
        parts = []
        for begin in (0, inner):
            cut = slice(begin + head * head_size, begin + (head + 1) * head_size)
            parts.append(ref[own, :, cut])
        return jnp.concatenate(parts, axis=0)

    def folded(ref, span, head):
        parts = []
        for begin in (0, inner):
            cut = slice(begin + head * head_size, begin + (head + 1) * head_size)
            parts.append(ref[span, :, cut].reshape(-1, head_size))
        return jnp.concatenate(parts, axis=0)

    fold(query_ref, nt(first, wqkv_ref[core, 0]).astype(BF16))

    far = (len(offsets) - 3) // 2
    segments = (range(0, far), range(far, 2 * far), range(2 * far, 2 * far + 3))
    def add_near(added_ref, pieces, rows_at, gap, extra, allowed, above, below):
        def keep(head, cut, value):
            for begin, there, count in pieces:
                added_ref[head, cut, there : there + count] = value[:, begin : begin + count]

        for head in range(heads):
            if rows_at is not None:
                rest = table_ref[head, 2 * HALF - 1 if above else HALF - 1]
                keep(head, slice(0, own_rows), jnp.where(allowed, rest + extra, NEGATIVE))
            cut = slice(0, own_rows) if rows_at is None else rows_at
            bias = near_bias(gap[cut], table_ref, head, above, below)
            more = extra if extra.shape[0] == 1 else extra[cut]
            keep(head, cut, jnp.where(allowed[cut], bias + more, NEGATIVE))

    def fact(slot, line):
        at = window.slot[slot]
        return facts_ref[at, line : line + 1, :own_rows]

    border = {-1: slice(0, EDGE), 0: None, 1: slice(own_rows - EDGE, own_rows)}

    def near_queries(slot):
        gap, allowed = fact(slot, 1) - ids, fact(slot, 2) == starts
        pieces = [(0, (1 + slot) * own_rows, own_rows)]
        add_near(
            biasq_ref, pieces, border[slot], gap, fact(slot, 0), allowed, slot >= 0, slot <= 0
        )

    def near_keys(slot):
        gap, allowed = ids - fact(slot, 1), fact(slot, 2) == starts
        pieces = [(side * half, (3 * side + 1 + slot) * half, half) for side in range(2)]
        add_near(biask_ref, pieces, border[slot], gap, gate, allowed, slot <= 0, slot >= 0)

    near_queries(0)
    window_early = [(facts_ref, facts_sems), (kv_ref, kv_sems)]
    window.relay(window_early)
    window.relay_diagonal(window_early)
    walls[1].start()
    walls[2].start()
    window.finish(window_early)
    near_queries(-1)
    near_queries(1)
    walls[3].start()
    if early:
        walls[0].relay()

    def spans(segment):
        return slice(segment[0], segment[-1] + 1)

    def far_added(segment, column, row_of=joined_row):
        allowed = row_of(facts_ref, segment, 2, own_rows) == starts
        return jnp.where(allowed, column, NEGATIVE)

    added = [
        far_added(segment, joined_row(facts_ref, segment, 0, own_rows)) for segment in segments[:2]
    ]
    fixed = (HALF - 1, 2 * HALF - 1)
    lanes = lax.broadcasted_iota(jnp.int32, lse_ref.shape, 1)
    lse_all = jnp.zeros(lse_ref.shape, F32)
    for head in range(heads):
        cut = slice(head * head_size, (head + 1) * head_size)
        cut_v = slice(inner + head * head_size, inner + (head + 1) * head_size)
        query = unfold(query_ref, head)
        parts = []
        for number, segment in enumerate(segments):
            keys = kv_ref[spans(segment), :, cut].reshape(-1, head_size)
            if number < 2:
                extra = added[number] + table_ref[head, fixed[number]]
            else:
                extra = biasq_ref[head]
            parts.append(nt(query, keys) + extra)
        most = jnp.max(parts[0], axis=1, keepdims=True)
        for part in parts[1:]:
            most = jnp.maximum(most, jnp.max(part, axis=1, keepdims=True))
        expos = [jnp.exp(part - most) for part in parts]
        total = sum(jnp.sum(expo, axis=1, keepdims=True) for expo in expos)
        lse_all = jnp.where(lanes == head, most + jnp.log(total), lse_all)
        attended = jnp.zeros((own_rows, head_size), F32)
        for segment, expo in zip(segments, expos):
            values = kv_ref[spans(segment), :, cut_v].reshape(-1, head_size)
            attended = attended + nn((expo / total).astype(BF16), values)
        attf_ref[:, cut] = attended
        att_ref[core, :, cut] = attended.astype(BF16)
    lse_ref[...] = lse_all

    att_copy = send(
        att_ref.at[core], att_ref.at[core], pair_sems.at[0, 4], pair_sems.at[1, 4], sibling
    )
    att_copy.start()
    for copy in locals_late:
        copy.wait()
    for copy in pair_early:
        copy.wait()
    att_copy.wait()
    mixed = packed_ref[...].astype(F32) + (nn(att_ref[0], wout_ref[0]) + nn(att_ref[1], wout_ref[1]))
    mixed_ref[...] = mixed
    sec_ref[high] = (mixed * row_scale(mixed) * g_ff).astype(BF16)
    sec_gather.start()

    walls[1].relay()
    walls[2].relay()
    for gather in cot_gathers:
        gather.arrived(1)
        gather.arrived(2)
    walls[3].relay()
    sec_gather.arrived(1)
    sec_gather.arrived(2)
    for wall in walls[0 if early else 1 :]:
        wall.finish()

    def sib_copy(kind, step):
        return send(
            sout_ref.at[step],
            sin_ref.at[kind, step],
            sib_sems.at[0, kind, step],
            sib_sems.at[1, kind, step],
            sibling,
        )

    def hi_copy(kind, step):
        return send(
            hout_ref.at[kind, step - 1],
            hin_ref.at[step - 1],
            hi_sems.at[0, step],
            hi_sems.at[1, step],
            high_peer(step),
        )

    def hand_over(kind, step, value):
        part_ref[...] = value
        sout_ref[step] = part_ref[theirs, :].astype(BF16)
        kept_ref[kind if step == 0 else 2 + step % 2] = part_ref[mine, :]
        sib_copy(kind, step).start()

    def pass_on(kind, step):
        sib_copy(kind, step).wait()
        both = kept_ref[2 + step % 2] + sin_ref[kind, step].astype(F32)
        hout_ref[kind, step - 1] = both.astype(BF16)

    def chunk_rows(chunk):
        return pl.ds(pl.multiple_of(chunk * own_rows, own_rows), own_rows)

    def line_copy(turn, middle):
        slot, target = turn - 1, inner_high
        if middle:
            slot = (3, 4, 0)[turn - 1]
            target = outer_high if turn == 3 else inner_high
        return send(
            hout_ref.at[0, turn - 1],
            line_ref.at[slot],
            line_sems.at[0, turn],
            line_sems.at[1, slot],
            (target * lows + low, core),
        )

    def line_arrived(slot):
        place = line_ref.at[slot]
        send(place, place, line_sems.at[0, 0], line_sems.at[1, slot], sibling).wait_recv()

    def ship_end(turn):
        @pl.when(end_high)
        def _():
            hout_ref[0, turn - 1] = kept_ref[1 + turn].astype(BF16)
            line_copy(turn, False).start()

    def ship_middle(turn):
        @pl.when(middle_high)
        def _():
            slot = (0, 1, 3)[turn - 1]
            line_arrived(slot)
            total = kept_ref[1 + turn] + line_ref[slot].astype(F32)
            hout_ref[0, turn - 1] = total.astype(BF16)
            line_copy(turn, True).start()

    for step in range(HI):
        if step:
            for gather in cot_gathers + [sec_gather]:
                if step == HI - 1:
                    gather.arrived(step)
                gather.forwarded(step)
        chunk = high_other(step)
        second = sec_ref[chunk]
        gated = nt(second, wall_ref[0])
        upper = nt(second, wall_ref[1])
        d_middle = nt(cots_ref[chunk], wall_ref[2])
        square = gated * gated
        bend = jnp.tanh(GELU_A * gated * (1.0 + GELU_B * square))
        lift = 0.5 * (1.0 + bend)
        slope = lift + 0.5 * gated * (1.0 - bend * bend) * (
            GELU_A * (1.0 + 3.0 * GELU_B * square)
        )
        gelu = gated * lift
        d_gated = (d_middle * upper * slope).astype(BF16)
        d_upper = (d_middle * gelu).astype(BF16)
        mid_ref[chunk_rows(chunk), :] = (gelu * upper).astype(BF16)
        dgated_ref[chunk_rows(chunk), :] = d_gated
        dupper_ref[chunk_rows(chunk), :] = d_upper
        hand_over(1, step, nn(d_gated, wall_ref[0]) + nn(d_upper, wall_ref[1]))
        if step == 0:
            window.start([(query_ref, query_sems)])
        if step == 2:
            window.relay([(query_ref, query_sems)])
        if step > 1:
            pass_on(1, step - 1)
            hi_copy(1, step - 1).start()
    pass_on(1, HI - 1)
    hi_copy(1, HI - 1).start()
    for gather in cot_gathers + [sec_gather]:
        gather.close()

    def ff_reduce(number):
        def part(place, begin, count):
            inside = pl.ds(pl.multiple_of(place * share + begin, 16), count)
            return wall_ref.at[number, inside]

        relays = (ffa_ref.at[number], ffb_ref.at[number])
        return LowReduce(part, share, relays, ffin_ref.at[number], ff_sems.at[number])

    reduces = [ff_reduce(number) for number in range(3)]
    hidden = wall_ref.shape[1]

    def weight_grad(number, left_ref, right_ref):
        for begin in range(0, hidden, 256):
            units = slice(begin, min(begin + 256, hidden))
            right = right_ref[...].reshape(HI * own_rows, width)
            wall_ref[number, units, :] = tn(left_ref[:, units], right).astype(BF16)

    weight_grad(0, dgated_ref, sec_ref)
    reduces[0].start()
    weight_grad(1, dupper_ref, sec_ref)
    reduces[1].start()
    window.relay_diagonal([(query_ref, query_sems)])
    sib_copy(1, 0).wait()
    for turn in (1, 2, 3, 0):
        part_ref[...] = nn(mid_ref[chunk_rows(line_chunk(turn)), :], wall_ref[2])
        sout_ref[turn] = part_ref[theirs, :].astype(BF16)
        kept_ref[1 + turn if turn else 0] = part_ref[mine, :]
        sib_copy(0, turn).start()
        if turn != 1:
            before = turn - 1 if turn else HI - 1
            sib_copy(0, before).wait()
            kept_ref[1 + before] = kept_ref[1 + before] + sin_ref[0, before].astype(F32)
    reduces[0].relay()
    weight_grad(2, mid_ref, cots_ref)
    reduces[1].relay()

    for slot in (-1, 0, 1):
        near_keys(slot)
    total = kept_ref[1] + sin_ref[1, 0].astype(F32)
    for step in range(1, HI):
        hi_copy(1, step).wait()
        total = total + hin_ref[step - 1].astype(F32)
    dsec_ref[mine, :] = total
    dsec_copy = send(
        dsec_ref.at[mine], dsec_ref.at[mine], half_sems.at[0, 0], half_sems.at[1, 0], sibling
    )
    dsec_copy.start()
    dsec_copy.wait()

    back, g_ff_grad = norm_back(mixed_ref[...], g_ff, dsec_ref[...])
    d_mixed = cots_ref[high].astype(F32) + back
    part_ref[...] = d_mixed
    d_branch = d_mixed.astype(BF16)
    d_att = nt(d_branch, wout_ref[core]).astype(BF16)
    fold(dout_ref, d_att)
    facts2_ref[own] = jnp.zeros(facts2_ref.shape[1:], F32)
    deltas = []
    products = d_att.astype(F32) * attf_ref[...]
    for head in range(heads):
        cut = slice(head * head_size, (head + 1) * head_size)
        delta = jnp.sum(products[:, cut], axis=1, keepdims=True)
        deltas.append(delta)
        facts2_ref[own, head : head + 1, 0:own_rows] = to_row(delta, own_eye)
        line = 4 + head
        facts2_ref[own, line : line + 1, 0:own_rows] = to_row(
            lse_ref[:, head : head + 1], own_eye
        )
    window.start([(facts2_ref, facts2_sems), (dout_ref, dout_sems)])
    for turn in range(1, HI):
        ship_end(turn)

    groups = zout_ref.shape[0]
    piece = zout_ref.shape[2]
    lanes_all = zout_ref.shape[3]
    quarter = lanes_all // HI

    def keep_pieces(number, value):
        for begin in range(0, inner, piece):
            group, place = divmod((number * inner + begin) // piece, lows)
            block = value[begin : begin + piece, :]
            zout_ref[group, place, :, 0:width] = block.astype(BF16)

    def quarter_of(place):
        return pl.ds(pl.multiple_of(place * quarter, 128), quarter)

    def low_sum(group):
        def part(place, begin, count):
            return zout_ref.at[group, place, pl.ds(begin, count)]

        relays = (za_ref.at[group], zb_ref.at[group])
        return LowReduce(part, piece, relays, zin_ref.at[group], low_sems.at[group])

    lows_sum = [low_sum(group) for group in range(groups)]
    early_groups, late_groups = range(groups // 2), range(groups // 2, groups)

    def high_copy(group, step, place):
        return send(
            zout_ref.at[group, low, :, quarter_of(high_other(step))],
            yin_ref.at[group, place],
            high_sems.at[0, group, step],
            high_sems.at[1, group, step],
            high_peer(step),
        )

    def share_low(group):
        lows_sum[group].finish()
        total = zout_ref[group, low].astype(F32)
        for number in arrived:
            total = total + zin_ref[group, number].astype(F32)
        zout_ref[group, low] = total.astype(BF16)
        for step in range(1, HI):
            high_copy(group, step, high).start()

    def back_copy(group, step, place):
        lanes_at = (group, slice(None), quarter_of(place))
        return send(
            fin_ref.at[lanes_at],
            fin_ref.at[lanes_at],
            back_sems.at[0, group, step],
            back_sems.at[1, group, step],
            high_peer(step),
        )

    def share_high(group):
        for step in range(1, HI):
            high_copy(group, step, high).wait_send()
            high_copy(group, step, high_other(step)).wait_recv()
        yin_ref[group, high] = zout_ref[group, low, :, quarter_of(high)]
        total = yin_ref[group, 0].astype(F32)
        for number in range(1, HI):
            total = total + yin_ref[group, number].astype(F32)
        fin_ref[group, :, quarter_of(high)] = total.astype(BF16)
        for step in range(1, HI):
            back_copy(group, step, high).start()

    def last_gather(group):
        def block(place, begin, count):
            return attg_ref.at[group, place, pl.ds(begin, count)]

        return LowGather(fin_ref.at[group], block, piece, last_sems.at[group])

    lasts = [last_gather(group) for group in range(groups)]
    own_lasts = [
        pltpu.make_async_copy(
            fin_ref.at[group], attg_ref.at[group, low], local_sems.at[8 + group]
        )
        for group in range(groups)
    ]

    def spread_low(group):
        for step in range(1, HI):
            back_copy(group, step, high).wait_send()
            back_copy(group, step, high_other(step)).wait_recv()
        lasts[group].start()
        own_lasts[group].start()

    if lanes_all > width:
        zout_ref[:, :, :, width:] = jnp.zeros(zout_ref.shape[:3] + (lanes_all - width,), BF16)
    keep_pieces(0, tn(att_ref[core], d_branch))

    lane = lax.broadcasted_iota(jnp.int32, (1, width), 1)
    bias_grad = jnp.zeros((1, width), F32)

    def add_bias(bias_grad, head, bucket, value):
        return bias_grad + jnp.where(lane == head * 2 * HALF + bucket, value, 0.0)

    def total_of(value):
        return jnp.sum(jnp.sum(value, axis=0, keepdims=True), axis=1, keepdims=True)

    for head in range(heads):
        cut = slice(head * head_size, (head + 1) * head_size)
        cut_v = slice(inner + head * head_size, inner + (head + 1) * head_size)
        query, d_head = unfold(query_ref, head), unfold(dout_ref, head)
        lse = lse_ref[:, head : head + 1]
        d_query = jnp.zeros((own_rows, head_size), F32)
        for number, segment in enumerate(segments):
            keys = kv_ref[spans(segment), :, cut].reshape(-1, head_size)
            values = kv_ref[spans(segment), :, cut_v].reshape(-1, head_size)
            if number < 2:
                extra = added[number] + table_ref[head, fixed[number]]
            else:
                extra = biasq_ref[head]
            probs = jnp.exp(nt(query, keys) + extra - lse)
            d_scores = probs * (nt(d_head, values) - deltas[head])
            d_query = d_query + nn(d_scores.astype(BF16), keys)
            if number < 2:
                bias_grad = add_bias(bias_grad, head, fixed[number], total_of(d_scores))
                continue
            for slot in (-1, 0, 1):
                lanes_at = slice((1 + slot) * own_rows, (2 + slot) * own_rows)
                block = d_scores[:, lanes_at]
                gap = fact(slot, 1) - ids
                whole = total_of(block)
                rows_at = border[slot]
                if rows_at is not None:
                    block, gap = block[rows_at], gap[rows_at]
                for sign in (1, -1):
                    if sign * slot < 0:
                        continue
                    base = HALF if sign > 0 else 0
                    sums = [
                        total_of(jnp.where(sign * gap >= limit, block, 0.0)) for limit in LIMITS
                    ]
                    if slot:
                        sums = [whole] + [value + (whole - total_of(block)) for value in sums[1:]]
                    whole = whole - sums[0]
                    for place in range(len(LIMITS)):
                        value = sums[place]
                        if place + 1 < len(LIMITS):
                            value = value - sums[place + 1]
                        bias_grad = add_bias(bias_grad, head, base + place + 1, value)
                if not slot:
                    bias_grad = add_bias(bias_grad, head, 0, whole)
        heads_ref[core, 0, :, cut] = d_query.astype(BF16)
        if head == 1:
            window.relay([(facts2_ref, facts2_sems), (dout_ref, dout_sems)])
            ship_middle(1)

    window.relay_diagonal([(facts2_ref, facts2_sems), (dout_ref, dout_sems)])
    ship_middle(2)
    keep_pieces(1, tn(heads_ref[core, 0], first_ref[...]))
    for group in early_groups:
        lows_sum[group].start()
    reduces[2].start()

    window_late = [(query_ref, query_sems), (facts2_ref, facts2_sems), (dout_ref, dout_sems)]
    window.finish(window_late)
    for group in early_groups:
        lows_sum[group].relay()
    ship_middle(3)
    d_gate = jnp.zeros((own_rows, 1), F32)
    added = [far_added(segment, gate, folded_row) for segment in segments[:2]]
    fixed = (2 * HALF - 1, HALF - 1)
    for head in range(heads):
        cut = slice(head * head_size, (head + 1) * head_size)
        cut_v = slice(inner + head * head_size, inner + (head + 1) * head_size)
        key, value = kv_ref[own, :, cut], kv_ref[own, :, cut_v]
        d_key = jnp.zeros((own_rows, head_size), F32)
        d_value = jnp.zeros((own_rows, head_size), F32)
        for number, segment in enumerate(segments):
            queries = folded(query_ref, spans(segment), head)
            d_heads = folded(dout_ref, spans(segment), head)
            if number < 2:
                extra = added[number] + table_ref[head, fixed[number]]
            else:
                extra = biask_ref[head]
            lse = folded_row(facts2_ref, segment, 4 + head, own_rows)
            delta = folded_row(facts2_ref, segment, head, own_rows)
            probs = jnp.exp(nt(key, queries) + extra - lse)
            d_scores = probs * (nt(value, d_heads) - delta)
            d_value = d_value + nn(probs.astype(BF16), d_heads)
            d_key = d_key + nn(d_scores.astype(BF16), queries)
            d_gate = d_gate + jnp.sum(d_scores, axis=1, keepdims=True)
        heads_ref[core, 1, :, cut] = d_key.astype(BF16)
        heads_ref[core, 2, :, cut] = d_value.astype(BF16)
    dgate_ref[core] = jnp.broadcast_to(d_gate, dgate_ref.shape[1:])
    pair_late = [
        send(ref.at[core], ref.at[core], pair_sems.at[0, 5 + i], pair_sems.at[1, 5 + i], sibling)
        for i, ref in enumerate((heads_ref, dgate_ref))
    ]
    for copy in pair_late:
        copy.start()
    for number in range(2):
        keep_pieces(2 + number, tn(heads_ref[core, 1 + number], first_ref[...]))
    for group in late_groups:
        lows_sum[group].start()

    for copy in pair_late:
        copy.wait()
    d_first = jnp.zeros((own_rows, width), F32)
    for side in range(2):
        for number in range(3):
            d_first = d_first + nn(heads_ref[side, number], wqkv_ref[side, number])
    back, g_attn_grad = norm_back(packed_ref[...].astype(F32), g_attn, d_first)
    inside = slice(MARGIN, MARGIN + own_rows)
    back_ref[inside, :] = (part_ref[...] + back).astype(BF16)
    d_gate = dgate_ref[0] + dgate_ref[1]
    lane_g = lax.broadcasted_iota(jnp.int32, d_gate.shape, 1)
    terms = jnp.zeros(d_gate.shape, F32)
    for number, term in enumerate(split3(d_gate)):
        terms = jnp.where(lane_g == number, term, terms)
    backaux_ref[inside, :] = terms.astype(BF16)
    down_src, down_dst = pl.ds(MARGIN, MARGIN), pl.ds(own_rows + MARGIN, MARGIN)
    up_src, up_dst = pl.ds(own_rows, MARGIN), pl.ds(0, MARGIN)
    start_edges, finish_edges = edges(
        edge2_sems,
        [
            (0, back_ref.at[down_src], back_ref.at[down_dst]),
            (1, backaux_ref.at[down_src], backaux_ref.at[down_dst]),
        ],
        [
            (2, back_ref.at[up_src], back_ref.at[up_dst]),
            (3, backaux_ref.at[up_src], backaux_ref.at[up_dst]),
        ],
    )
    start_edges()

    @pl.when(me == 0)
    def _():
        back_ref[up_dst, :] = jnp.zeros((MARGIN, width), BF16)
        backaux_ref[up_dst, :] = jnp.zeros((MARGIN, 128), BF16)

    @pl.when(me == rows - 1)
    def _():
        back_ref[down_dst, :] = jnp.zeros((MARGIN, width), BF16)
        backaux_ref[down_dst, :] = jnp.zeros((MARGIN, 128), BF16)

    gate_s = sigmoid(raw_logit)
    gate_slope = DELETE_SCALE * gate_s * (1.0 - gate_s)
    raw_scaled = gcot_ref[...] * gate_slope * raw_scale
    common = jnp.sum(
        nt(stacked_rows(split3(raw_scaled), raw_count), byte_ref[...]), axis=0, keepdims=True
    )
    packed = packed_ref[...].astype(F32)
    scale = row_scale(packed)
    own_s = sigmoid(gate_logit(packed, scale, gate_weight))
    own_scaled = d_gate[:, 0:1] * (DELETE_SCALE * own_s * (1.0 - own_s)) * scale
    common = common + jnp.sum(own_scaled * packed, axis=0, keepdims=True)
    slow_ref[low, 0:1, :] = g_ff_grad
    slow_ref[low, 1:2, :] = g_attn_grad
    slow_ref[low, 2:3, :] = common * g_delete
    slow_ref[low, 3:4, :] = common * w_delete
    slow_ref[low, 4:5, :] = bias_grad
    slow_ref[low, 5:8, :] = jnp.zeros((3, width), F32)

    def slow_copy(step, source):
        return send(
            slow_ref.at[source],
            slow_ref.at[source],
            slow_sems.at[0, step],
            slow_sems.at[1, step],
            low_peer(step),
        )

    def start_slow(step, carry):
        slow_copy(step, low).start()
        return carry

    def finish_slow(step, carry):
        slow_copy(step, low).wait_send()
        slow_copy(step, low_source(step)).wait_recv()
        return carry

    def shigh_copy(step, source):
        return send(
            shigh_ref.at[source],
            shigh_ref.at[source],
            shigh_sems.at[0, step],
            shigh_sems.at[1, step],
            high_peer(step),
        )

    lax.fori_loop(1, lows, start_slow, 0)
    for group in early_groups:
        share_low(group)
    for group in late_groups:
        lows_sum[group].relay()
    reduces[2].relay()
    for group in early_groups:
        share_high(group)
    for group in late_groups:
        share_low(group)
    lax.fori_loop(1, lows, finish_slow, 0)
    small = slow_ref[0]
    for number in range(1, lows):
        small = small + slow_ref[number]
    shigh_ref[high] = small
    for step in range(1, HI):
        shigh_copy(step, high).start()
    for group in early_groups:
        spread_low(group)
    for group in late_groups:
        share_high(group)
    for group in early_groups:
        lasts[group].relay()
    for group in late_groups:
        spread_low(group)

    finish_edges()
    spread = tn(backaux_ref[...], chosen_ref[...])
    raw_cot = gcot_ref[...] + (spread[0:1, :] + spread[1:2, :] + spread[2:3, :])
    d_logit = raw_cot * gate_slope
    scaled = d_logit * raw_scale
    along = d_logit * raw_logit * raw_scale * raw_scale * (1.0 / width)
    s1, s2, s3 = split3(scaled)
    w1, w2, w3 = split3(gate_weight)
    outer = tn(
        stacked_rows((w1, w1, w2, w2, w1, w3), width),
        stacked_rows((s1, s2, s1, s2, s3, s1), raw_count),
    )
    rows_ref[...] = outer - along * byte_ref[...].astype(F32)
    rows_ref[...] = rows_ref[...] + tn(back_ref[...], chosen_ref[...])
    stores = [pltpu.make_async_copy(rows_ref, rows_out_ref, local_sems.at[2])]
    stores[0].start()
    for step in range(1, HI):
        shigh_copy(step, high).wait_send()
        shigh_copy(step, high_other(step)).wait_recv()
    small = shigh_ref[0]
    for number in range(1, HI):
        small = small + shigh_ref[number]
    small_ref[...] = small

    sib_copy(0, 0).wait()
    part_ref[mine, :] = mixed_ref[mine, :] + (kept_ref[0] + sin_ref[0, 0].astype(F32))

    def add_line(middle):
        for slot in (2, 4) if middle else (0,):
            line_arrived(slot)
            part_ref[mine, :] = part_ref[mine, :] + line_ref[slot].astype(F32)
        for turn in range(1, HI):
            line_copy(turn, middle).wait_send()

    @pl.when(end_high)
    def _():
        add_line(False)

    @pl.when(middle_high)
    def _():
        add_line(True)

    block_ref[mine, :] = part_ref[mine, :].astype(BF16)
    block_copy = send(
        block_ref.at[mine], block_ref.at[mine], half_sems.at[0, 1], half_sems.at[1, 1], sibling
    )
    block_copy.start()

    def finish_reduce(number):
        reduces[number].finish()
        total = wall_ref[number, my_share, :].astype(F32)
        for begin in range(0, len(arrived), HI):
            loads = [
                pltpu.make_async_copy(
                    ffin_ref.at[number, slot],
                    sec_ref.at[place, pl.ds(0, share)],
                    local_sems.at[3 + place],
                )
                for place, slot in enumerate(arrived[begin : begin + HI])
            ]
            for load in loads:
                load.start()
            for load in loads:
                load.wait()
            for place in range(len(loads)):
                total = total + sec_ref[place, 0:share, :].astype(F32)
        ffo_ref[number] = total
        store = pltpu.make_async_copy(
            ffo_ref.at[number], ffo_out_ref.at[number], local_sems.at[(0, 1, 7)[number]]
        )
        store.start()
        stores.append(store)

    finish_reduce(0)
    finish_reduce(1)
    for group in late_groups:
        lasts[group].relay()
    finish_reduce(2)
    block_copy.wait()
    for store in stores:
        store.wait()
    for group in range(groups):
        lasts[group].finish()
        own_lasts[group].wait()


def layer(rows, offsets, *operands):
    lengths, table, byte_t, keep, vecs, gcot, wq, wk, wv, wo, wg, wu, wd, cot = operands
    width, raw_count = byte_t.shape
    own_rows = cot.shape[0]
    inner = wq.shape[0]
    heads = table.shape[0]
    share = wd.shape[0]
    lows = rows // HI
    hidden = lows * share
    slots = len(offsets)
    half = own_rows // 2
    groups = 4 * inner // 128
    piece = 128 // lows
    lanes = -(-width // (128 * HI)) * 128 * HI
    slots_in = 2 if lows == 4 else lows
    window_sems = 3 * slots
    ff_cut, z_cut = share // 2 // 16 * 16, piece // 2 // 16 * 16
    ext_rows = own_rows + 2 * MARGIN
    vmem = pl.BlockSpec(memory_space=pltpu.VMEM)
    smem = pl.BlockSpec(memory_space=pltpu.SMEM)
    anywhere = pl.BlockSpec(memory_space=pl.ANY)
    shape = jax.ShapeDtypeStruct
    dma = pltpu.SemaphoreType.DMA
    outs = [
        shape((1, raw_count), F32),
        shape((own_rows, width), BF16),
        shape((width, raw_count), F32),
        shape((8, width), F32),
        shape((3, share, width), F32),
        shape((groups, lows, piece, lanes), BF16),
        shape((3, slots_in, share, width), BF16),
    ]
    out_specs = [vmem, vmem, anywhere, vmem] + [anywhere] * 3
    scratch = [
        pltpu.VMEM((width, raw_count), F32),
        pltpu.VMEM((3, share, width), F32),
        pltpu.VMEM((rows, 8, 128), F32),
        pltpu.VMEM((ext_rows, raw_count), BF16),
        pltpu.VMEM((ext_rows, width), BF16),
        pltpu.VMEM((ext_rows, 128), BF16),
        pltpu.VMEM((MARGIN, width), BF16),
        pltpu.VMEM((MARGIN, width), BF16),
        pltpu.VMEM((MARGIN, 128), BF16),
        pltpu.VMEM((MARGIN, 128), BF16),
        pltpu.VMEM((own_rows, width), BF16),
        pltpu.VMEM((own_rows, 128), F32),
        pltpu.VMEM((own_rows, width), BF16),
        pltpu.VMEM((slots, own_rows, 2 * inner), BF16),
        pltpu.VMEM((slots, half, 2 * inner), BF16),
        pltpu.VMEM((slots, 8, 256), F32),
        pltpu.VMEM((slots, half, 2 * inner), BF16),
        pltpu.VMEM((slots, 8, 256), F32),
        pltpu.VMEM((heads, own_rows, 3 * own_rows), F32),
        pltpu.VMEM((heads, own_rows, 3 * own_rows), F32),
        pltpu.VMEM((2, own_rows, inner), BF16),
        pltpu.VMEM((own_rows, inner), F32),
        pltpu.VMEM((own_rows, 128), F32),
        pltpu.VMEM((own_rows, width), F32),
        pltpu.VMEM((HI, own_rows, width), BF16),
        pltpu.VMEM((HI, own_rows, width), BF16),
        pltpu.VMEM((3, hidden, width), BF16),
        pltpu.VMEM((2, inner, width), BF16),
        pltpu.VMEM((2, 3, inner, width), BF16),
        pltpu.VMEM((HI * own_rows, hidden), BF16),
        pltpu.VMEM((HI * own_rows, hidden), BF16),
        pltpu.VMEM((HI * own_rows, hidden), BF16),
        pltpu.VMEM((own_rows, width), F32),
        pltpu.VMEM((5, half, width), F32),
        pltpu.VMEM((HI, half, width), BF16),
        pltpu.VMEM((2, HI, half, width), BF16),
        pltpu.VMEM((2, HI - 1, half, width), BF16),
        pltpu.VMEM((HI - 1, half, width), BF16),
        pltpu.VMEM((5, half, width), BF16),
        pltpu.VMEM((own_rows, width), F32),
        pltpu.VMEM((2, 3, own_rows, inner), BF16),
        pltpu.VMEM((2, own_rows, 128), F32),
        pltpu.VMEM((groups, lows, piece, lanes), BF16),
        pltpu.VMEM((groups, slots_in, piece, lanes), BF16),
        pltpu.VMEM((groups, HI, piece, lanes // HI), BF16),
        pltpu.VMEM((groups, piece, lanes), BF16),
        pltpu.VMEM((lows, 8, width), F32),
        pltpu.VMEM((HI, 8, width), F32),
        pltpu.VMEM((ext_rows, width), BF16),
        pltpu.VMEM((ext_rows, 128), BF16),
        pltpu.VMEM((3, max(ff_cut, 16), width), BF16),
        pltpu.VMEM((3, share - ff_cut, width), BF16),
        pltpu.VMEM((groups, max(z_cut, 16), lanes), BF16),
        pltpu.VMEM((groups, piece - z_cut, lanes), BF16),
        dma((2, rows)),
        dma((2, 4)),
        dma((2, window_sems)),
        dma((2, window_sems)),
        dma((2, window_sems)),
        dma((2, window_sems)),
        dma((2, window_sems)),
        dma((4, 2, max(5, lows))),
        dma((2, 7)),
        dma((8 + groups,)),
        dma((2, 2, HI)),
        dma((2, 2, HI)),
        dma((2, HI)),
        dma((2, HI)),
        dma((2, 2, HI)),
        dma((2, HI)),
        dma((2, 5)),
        dma((2, 2)),
        dma((3, 2, max(5, lows))),
        dma((groups, 2, max(5, lows))),
        dma((2, groups, HI)),
        dma((2, groups, HI)),
        dma((groups, 2, max(5, lows))),
        dma((2, 4)),
        dma((2, lows)),
        dma((2, HI)),
    ]
    return pl.pallas_call(
        functools.partial(layer_kernel, rows, offsets),
        name="layer",
        out_shape=outs,
        in_specs=[smem, smem] + [vmem] * 4 + [anywhere] * 8,
        out_specs=out_specs,
        scratch_shapes=scratch,
        compiler_params=pltpu.CompilerParams(
            collective_id=0, has_side_effects=True, vmem_limit_bytes=VMEM_LIMIT
        ),
    )(*operands)


def finish_kernel(
    att_ref,
    ff_ref,
    block_ref,
    rows_ref,
    gate_ref,
    small_ref,
    out_ref,
    query_ref,
    key_ref,
    value_ref,
    ffg_ref,
    ffu_ref,
    ffd_ref,
    block_out_ref,
    rows_out_ref,
    gate_out_ref,
    bias_ref,
    load_ref,
    wide_ref,
    ff_hold_ref,
    rows_hold_ref,
    block_hold_ref,
    gate_hold_ref,
    load_sems,
    store_sems,
    pass_sems,
):
    width = out_ref.shape[1]
    heads, buckets = bias_ref.shape
    results = (out_ref, query_ref, key_ref, value_ref)
    loads = [
        pltpu.make_async_copy(att_ref.at[number], load_ref.at[number], load_sems.at[number])
        for number in range(4)
    ]
    for load in loads:
        load.start()
    holds = [
        (rows_ref, rows_hold_ref, rows_out_ref),
        (ff_ref.at[0], ff_hold_ref.at[0], ffg_ref),
        (ff_ref.at[1], ff_hold_ref.at[1], ffu_ref),
        (ff_ref.at[2], ff_hold_ref.at[2], ffd_ref),
        (block_ref, block_hold_ref, block_out_ref),
        (gate_ref, gate_hold_ref, gate_out_ref),
    ]
    fetches = [
        pltpu.make_async_copy(src, hold, pass_sems.at[0, number])
        for number, (src, hold, _) in enumerate(holds)
    ]
    for copy in fetches:
        copy.start()
    for head in range(heads):
        bias_ref[head : head + 1, :] = small_ref[4:5, head * buckets : (head + 1) * buckets]
    stores = []
    for number, (_, hold, result) in enumerate(holds):
        fetches[number].wait()
        store = pltpu.make_async_copy(hold, result, pass_sems.at[1, number])
        store.start()
        stores.append(store)
    for number, load in enumerate(loads):
        load.wait()
        wide_ref[number] = load_ref[number, :, 0:width].astype(F32)
        store = pltpu.make_async_copy(
            wide_ref.at[number], results[number], store_sems.at[number]
        )
        store.start()
        stores.append(store)
    for copy in stores:
        copy.wait()


def finish(att_grads, ff_sums, block, grad_rows, gate, small, heads, buckets):
    _, inner, lanes = att_grads.shape
    _, share, width = ff_sums.shape
    vmem = pl.BlockSpec(memory_space=pltpu.VMEM)
    anywhere = pl.BlockSpec(memory_space=pl.ANY)
    shape = jax.ShapeDtypeStruct
    dma = pltpu.SemaphoreType.DMA
    outs = [shape((inner, width), F32)] * 4 + [shape((share, width), F32)] * 3
    outs += [shape(array.shape, array.dtype) for array in (block, grad_rows, gate)]
    outs += [shape((heads, buckets), F32)]
    return pl.pallas_call(
        finish_kernel,
        name="finish",
        out_shape=outs,
        in_specs=[anywhere] * 5 + [vmem],
        out_specs=[anywhere] * 10 + [vmem],
        scratch_shapes=[
            pltpu.VMEM((4, inner, lanes), BF16),
            pltpu.VMEM((4, inner, width), F32),
            pltpu.VMEM((3, share, width), F32),
            pltpu.VMEM(grad_rows.shape, F32),
            pltpu.VMEM(block.shape, BF16),
            pltpu.VMEM(gate.shape, F32),
            dma((4,)),
            dma((4,)),
            dma((2, 6)),
        ],
        compiler_params=pltpu.CompilerParams(vmem_limit_bytes=VMEM_LIMIT),
    )(att_grads, ff_sums, block, grad_rows, gate, small)


def per_device(
    byte_rows,
    lengths,
    keep_mask,
    w_delete,
    g_delete,
    g_attn,
    w_query,
    w_key,
    w_value,
    w_out,
    rel_bias,
    g_ff,
    w_gate,
    w_up,
    w_down,
    out_cot,
    gate_cot,
):
    raw_count, width = byte_rows.shape
    own_rows = out_cot.shape[0]
    inner = w_query.shape[1]
    buckets, heads = rel_bias.shape
    rows = lax.axis_size("rows")
    share = w_down.shape[0]
    offsets = slots_of(reach_of(raw_count, own_rows))
    line = lax.broadcasted_iota(jnp.int32, (8, width), 0)
    vecs = jnp.zeros((8, width), F32)
    for number, vector in enumerate((g_delete, w_delete, g_attn, g_ff)):
        vecs = jnp.where(line == number, vector[None, :], vecs)
    spare = -share % 16
    weights = [jnp.pad(w, ((0, spare), (0, 0))) for w in (w_gate.T, w_up.T, w_down)]
    gate, block_out, grad_rows, small, ff_sums, att_grads, _ = layer(
        rows,
        offsets,
        lengths,
        rel_bias.T,
        byte_rows.T,
        keep_mask.reshape(1, -1),
        vecs,
        gate_cot.reshape(1, -1),
        w_query.T,
        w_key.T,
        w_value.T,
        w_out,
        *weights,
        out_cot,
    )
    (
        grad_out,
        grad_query,
        grad_key,
        grad_value,
        grad_gate,
        grad_up,
        grad_down,
        block_out,
        grad_rows,
        gate,
        grad_bias,
    ) = finish(
        att_grads.reshape(4, inner, -1),
        ff_sums[:, :share],
        block_out,
        grad_rows,
        gate,
        small,
        heads,
        buckets,
    )
    return (
        block_out,
        gate[0],
        grad_rows.T,
        small[2],
        small[3],
        small[1],
        grad_query.T,
        grad_key.T,
        grad_value.T,
        grad_out,
        grad_bias.T,
        small[0],
        grad_gate.T,
        grad_up.T,
        grad_down,
    )


def solution(mesh):
    in_specs = (
        P("rows", None),
        P(),
        P("rows"),
        P(),
        P(),
        P(),
        P(None, "tensor"),
        P(None, "tensor"),
        P(None, "tensor"),
        P("tensor", None),
        P(None, "tensor"),
        P(),
        P(None, ("rows", "tensor")),
        P(None, ("rows", "tensor")),
        P(("rows", "tensor"), None),
        P("rows", None),
        P("rows"),
    )
    out_specs = (
        P("rows", None),
        P("rows"),
        P("rows", None),
        P(),
        P(),
        P(),
        P(None, "tensor"),
        P(None, "tensor"),
        P(None, "tensor"),
        P("tensor", None),
        P(None, "tensor"),
        P(),
        P(None, ("rows", "tensor")),
        P(None, ("rows", "tensor")),
        P(("rows", "tensor"), None),
    )
    return jax.shard_map(
        per_device, mesh=mesh, in_specs=in_specs, out_specs=out_specs, check_vma=False
    )
```
